32 devices in a mesh: members: 2 (over y), lat: 4 (over z), lon: 4 (over x, core).
Axes of the slice: x: 2, y: 2, z: 4, core: 2. Of those that a mesh axis runs over, the one named last changes fastest.
Arguments:
- u_wind: float32 [128, 16, 3584], P(('members', 'lat'), None, 'lon'), parts along dimension 0, may hold values from -6 to 6
- v_wind: float32 [128, 16, 3584], P(('members', 'lat'), None, 'lon'), parts along dimension 0, may hold values from -6 to 6
- theta: float32 [128, 16, 3584], P(('members', 'lat'), None, 'lon'), parts along dimension 0, may hold values from -6 to 6
- geopot: float32 [128, 16, 3584], P(('members', 'lat'), None, 'lon'), parts along dimension 0, may hold values from -6 to 6
- mass: float32 [128, 3584], P(('members', 'lat'), 'lon'), parts along dimension 0, may hold values from 0.5 to 2
- cutoffs: int32 [32], replicated, may hold values from 1 to 447
Outputs:
- u_next: float32 [128, 16, 3584], P(('members', 'lat'), None, 'lon'), parts along dimension 0
- v_next: float32 [128, 16, 3584], P(('members', 'lat'), None, 'lon'), parts along dimension 0
- theta_next: float32 [128, 16, 3584], P(('members', 'lat'), None, 'lon'), parts along dimension 0
- geopot_next: float32 [128, 16, 3584], P(('members', 'lat'), None, 'lon'), parts along dimension 0
The draws below stay inside these ranges and needn't reach their ends.
There are 2 independent parts, one for each index of `members`. The reference program is written for one: setup_inputs(seed, part) draws one part's arguments, and reference() takes and returns one part's arrays. A program takes and returns all parts, laid end to end along the dimension named above; an argument that names none is the same for every part. Nothing has to cross between parts.
All inputs are finite; a program needn't handle non-finite values.
Results may differ from the reference program's by a relative error of at most 0.00005.
Values sent between devices are 32-bit elements; how exact they have to be, the bound alone decides.
No kernel may reach another device: no remote copies, remote signals or barrier semaphores. Data moves between devices by JAX's collectives and lax.ppermute only.
A program may use at most 192 MiB of HBM per device.

```python
import math
import jax
import jax.numpy as jnp
from jax import lax

LEV = 16
NLON = 3584
NLAT = 64
KMAX = 448


def plant(drawn, key, least, top_value):
    shape = drawn.shape
    index_at = [jax.random.randint(jax.random.fold_in(key, axis), (), 0, shape[axis]) for axis in range(len(shape))]
    drawn = drawn.at[tuple(index_at)].set(least)
    longest = shape.index(max(shape))
    index_at[longest] = (index_at[longest] + 1) % shape[longest]
    return drawn.at[tuple(index_at)].set(top_value)


def shard_levels(own_key, extent, pieces, low, largest):
    def one(dim, shards_of):
        steps = jax.random.uniform(jax.random.fold_in(jax.random.fold_in(own_key, 6), dim), (shards_of,), jnp.float32, low / len(pieces), largest / len(pieces))
        return jnp.repeat(jnp.exp(steps), extent[dim] // shards_of).reshape((-1,) + (1,) * (len(extent) - dim - 1))

    gain = one(*pieces[0])
    for cut in pieces[1:]:
        gain = gain * one(*cut)
    return gain


def gaussian(key, extent, deviation, reach, shards=(), kind=jnp.bfloat16):
    loudness = shard_levels(key, extent, shards, -0.22, 0.18) if shards else 1.0
    drawn = jax.random.normal(key, extent, jnp.float32) * deviation * loudness
    return jnp.minimum(jnp.maximum(drawn, -reach), reach).astype(kind)


def setup_inputs(seed: int = 0, part: int = 0) -> dict:
    streams_of = jax.random.split(jax.random.key(seed), 7)
    part_keys = jax.random.split(jax.random.fold_in(streams_of[6], part), 7)
    u_wind = gaussian(part_keys[0], (NLAT, LEV, NLON), 1.0, 6.0, ((0, 4), (2, 4)), jnp.float32)
    v_wind = gaussian(part_keys[1], (NLAT, LEV, NLON), 1.0, 6.0, ((0, 4), (2, 4)), jnp.float32)
    theta = gaussian(part_keys[2], (NLAT, LEV, NLON), 1.0, 6.0, ((0, 4), (2, 4)), jnp.float32)
    geopot = gaussian(part_keys[3], (NLAT, LEV, NLON), 1.0, 6.0, ((0, 4), (2, 4)), jnp.float32)
    mass = jnp.clip(jnp.exp(math.log(2.0) - 1.3862944 * jax.random.uniform(part_keys[4], (NLAT, NLON), jnp.float32) ** shard_levels(part_keys[4], (NLAT, NLON), ((0, 4), (1, 4)), -0.2, 0.2)), 0.5, 2.0)
    cutoffs = plant(jax.random.randint(streams_of[5], (NLAT // 2,), 1, KMAX), jax.random.fold_in(streams_of[5], 1), 1, KMAX - 1).astype(jnp.int32)
    return {"u_wind": u_wind, "v_wind": v_wind, "theta": theta, "geopot": geopot, "mass": mass, "cutoffs": cutoffs}


STEP = 0.1
SPIN = 0.5


def window(padded, offset, along, length):
    return lax.slice_in_dim(padded, 3 + offset, 3 + offset + length, axis=along)


def centered(padded, along, length):
    def pick(offset):
        return window(padded, offset, along, length)
    return (45.0 * (pick(1) - pick(-1)) - 9.0 * (pick(2) - pick(-2)) + (pick(3) - pick(-3))) / 60.0


def hyperdiff(padded, along, length):
    def pick(offset):
        return window(padded, offset, along, length)
    return (pick(3) + pick(-3) - 6.0 * (pick(2) + pick(-2)) + 15.0 * (pick(1) + pick(-1)) - 20.0 * pick(0)) / 60.0


def tendencies(padded, latitude):
    row_count = padded.shape[0] - 6
    col_count = padded.shape[2] - 6
    levels = (padded.shape[1] - 1) // 4
    across = padded[3:3 + row_count]
    upward = padded[:, :, 3:3 + col_count]
    grad_x = centered(across, 2, col_count)
    diss_x = hyperdiff(across, 2, col_count)
    grad_y = centered(upward, 0, row_count)
    diss_y = hyperdiff(upward, 0, row_count)
    centre = across[:, :, 3:3 + col_count]
    shape_four = (row_count, 4, levels, col_count)
    metric = (1.0 / jnp.cos(latitude))[:, None, None]
    spin_term = (SPIN * jnp.sin(latitude))[:, None, None]
    east = centre[:, 0:levels]
    north = centre[:, levels:2 * levels]
    potent = centre[:, 2 * levels:3 * levels]
    column = centre[:, 4 * levels:]
    slope_x = grad_x[:, :4 * levels].reshape(shape_four)
    smooth_x = diss_x[:, :4 * levels].reshape(shape_four)
    slope_y = grad_y[:, :4 * levels].reshape(shape_four)
    smooth_y = diss_y[:, :4 * levels].reshape(shape_four)
    east_all = east[:, None]
    north_all = north[:, None]
    advect = metric[:, None] * (east_all * slope_x - jnp.abs(east_all) * smooth_x) + north_all * slope_y - jnp.abs(north_all) * smooth_y
    mass_x = grad_x[:, 4 * levels:] / column
    mass_y = grad_y[:, 4 * levels:] / column
    tend_east = -advect[:, 0] + spin_term * north - metric * (slope_x[:, 3] + potent * mass_x)
    tend_north = -advect[:, 1] - spin_term * east - (slope_y[:, 3] + potent * mass_y)
    return jnp.stack([tend_east, tend_north, -advect[:, 2], -advect[:, 3]], axis=1)


def truncate(block, row_cut):
    spectrum = jnp.fft.rfft(block, axis=-1)
    wave = jnp.arange(spectrum.shape[-1]).astype(jnp.int32)
    keep = wave[None, :] <= row_cut[:, None]
    spectrum = jnp.where(keep[:, None, None, :], spectrum, jnp.zeros_like(spectrum))
    return jnp.fft.irfft(spectrum, n=block.shape[-1], axis=-1).astype(block.dtype)


def reference(u_wind, v_wind, theta, geopot, mass, cutoffs):
    stacked = jnp.concatenate([u_wind, v_wind, theta, geopot, mass[:, None, :]], axis=1)
    wide = jnp.concatenate([stacked[:, :, -3:], stacked, stacked[:, :, :3]], axis=2)
    padded = jnp.pad(wide, ((3, 3), (0, 0), (0, 0)))
    latitude = (jnp.arange(NLAT).astype(jnp.float32) + 0.5) * (math.pi / NLAT) - math.pi / 2
    tend = tendencies(padded, latitude)
    quarter = NLAT // 4
    south_rows = truncate(tend[:quarter], cutoffs[:quarter])
    north_rows = truncate(tend[NLAT - quarter:], cutoffs[quarter:])
    tend = jnp.concatenate([south_rows, tend[quarter:NLAT - quarter], north_rows], axis=0)
    updated = stacked[:, :4 * LEV].reshape(NLAT, 4, LEV, NLON) + STEP * tend
    return updated[:, 0], updated[:, 1], updated[:, 2], updated[:, 3]
```

```python
import functools
import math

import jax
import jax.numpy as jnp
import ml_dtypes
import numpy as np
from jax import lax
from jax.experimental import pallas as pl
from jax.experimental.pallas import tpu as pltpu
from jax.sharding import PartitionSpec as P

STEP = 0.1
SPIN = 0.5
LANES = 128
NEAR = 16
FAR = 8
NODES = 256
F32 = jnp.float32
BF16 = jnp.bfloat16
VMEM_LIMIT = 56 * 1024 * 1024


def pivoted(matrix, count):
    rest = np.array(matrix)
    columns = rest.shape[1]
    tilt = 1.0 + 1e-3 * np.arange(columns) / columns
    picked = []
    tri = np.zeros((count, columns))
    for step in range(count):
        size = (rest * rest).sum(axis=0)
        best = int(np.argmax(size * tilt))
        picked.append(best)
        unit = rest[:, best] / math.sqrt(size[best])
        for _ in range(2):
            part = (unit[:, None] * rest).sum(axis=0)
            rest -= unit[:, None] * part[None, :]
            tri[step] += part
        rest[:, best] = 0.0
    left = tri[:, picked].copy()
    right = tri.copy()
    for step in range(count - 1, -1, -1):
        right[step] /= left[step, step]
        right[:step] -= left[:step, step][:, None] * right[step][None, :]
    right[:, picked] = np.eye(count)
    order = np.argsort(picked)
    return np.asarray(picked)[order], right[order]


def cauchy(target, source, circle):
    gap = target[:, None] - source[None, :]
    angle = np.where(gap == 0, 0.5 * math.pi, gap * math.pi / circle)
    return np.where(gap == 0, 0.0, 1.0 / (circle * np.sin(angle)))


def halves(table):
    table = table.astype(np.float32)
    high = table.astype(ml_dtypes.bfloat16)
    low = (table - high.astype(np.float32)).astype(ml_dtypes.bfloat16)
    return np.stack([high, low])


@functools.lru_cache(maxsize=None)
def filter_tables(sector, circle):
    modes = circle // 8
    place = np.arange(sector)
    wave = np.arange(modes)
    phase = (wave[:, None] * place[None, :]) % circle * (2 * math.pi / circle)
    basis = np.concatenate([np.cos(phase), np.sin(phase[1:])], axis=0)
    nodes, spread = pivoted(basis, NODES)
    own = cauchy(nodes, nodes, circle)
    send = np.zeros((2, 4, NODES, 2 * LANES))
    take = np.zeros((3 * LANES, 4, 2, NODES))
    for name, shift, count in (("east", sector, NEAR), ("west", -sector, NEAR), ("far", 2 * sector, FAR)):
        kernel = cauchy(nodes + shift, nodes, circle)
        pick, weights = pivoted(kernel, count)
        back = kernel[:, pick].T
        for pair in range(2):
            for group in range(4):
                if name == "far":
                    first = LANES + 32 * pair + FAR * group
                    lane = 2 * LANES + 32 * pair + FAR * group
                elif name == "east":
                    first = 64 * pair + NEAR * group
                    lane = 64 * pair + NEAR * group
                else:
                    first = 64 * (1 - pair) + NEAR * group
                    lane = LANES + 64 * (1 - pair) + NEAR * group
                send[pair, group, :, first : first + count] = weights.T
                take[lane : lane + count, 2 * pair + group // 2, group % 2] = back
    return dict(
        nodes=nodes.astype(np.int32),
        spread=halves(spread.T),
        gather=halves(STEP * spread),
        own=halves(own.T),
        send=halves(send),
        take=halves(take.reshape(3 * LANES, 8 * NODES)),
    )


def split(value):
    high = value.astype(BF16)
    return high, (value - high.astype(F32)).astype(BF16)


def dot3(high, low, table_high, table_low):
    def one(a, b):
        return lax.dot_general(a, b, (((1,), (0,)), ((), ())), preferred_element_type=F32)

    return one(high, table_high) + one(low, table_high) + one(high, table_low)


def pack_kernel(*refs):
    fields = refs[:4]
    mass, south, north, west, east, edge, sems = refs[4:]
    rows = mass.shape[0]
    levels = edge.shape[3]
    columns = mass.shape[1]
    copies = []
    for f in range(4):
        copies.append(pltpu.make_async_copy(fields[f].at[:, :, 0:LANES], edge.at[0, f], sems.at[0, f]))
        copies.append(
            pltpu.make_async_copy(
                fields[f].at[:, :, columns - LANES : columns], edge.at[1, f], sems.at[1, f]
            )
        )
    for c in copies:
        c.start()
    strips = []
    for f in range(4):
        for j in range(3):
            into = pl.ds(levels * (3 * f + j), levels)
            strips.append(pltpu.make_async_copy(fields[f].at[j], south.at[into], sems.at[2 + j, f]))
            strips.append(
                pltpu.make_async_copy(fields[f].at[rows - 3 + j], north.at[into], sems.at[5 + j, f])
            )
    for c in strips:
        c.start()
    tail = 12 * levels
    blank = jnp.zeros((5, columns), F32)
    south[tail : tail + 3] = mass[0:3]
    south[tail + 3 : tail + 8] = blank
    north[tail : tail + 3] = mass[rows - 3 : rows]
    north[tail + 3 : tail + 8] = blank
    lane = lax.broadcasted_iota(jnp.int32, (levels, LANES), 1)
    west[2 * levels :] = mass[:, 0:LANES]
    east[2 * levels :] = pltpu.roll(mass[:, columns - LANES : columns], 3, 1)
    for c in copies:
        c.wait()
    for parity in range(2):
        for side, out in ((0, west), (1, east)):
            total = jnp.zeros((levels, LANES), F32)
            for r in range(parity, rows, 2):
                for f in range(4):
                    first = 16 * (r // 2) + 3 * f
                    turn = first if side == 0 else (first + 3) % LANES
                    tile = edge[side, f, r]
                    if turn:
                        tile = pltpu.roll(tile, turn, 1)
                    total = jnp.where((lane >= first) & (lane < first + 3), tile, total)
            out[parity * levels : (parity + 1) * levels] = total
    for c in strips:
        c.wait()


def stencil(center, plus, minus):
    p1, p2, p3 = plus
    m1, m2, m3 = minus
    slope = 45.0 * (p1 - m1) - 9.0 * (p2 - m2) + (p3 - m3)
    smooth = (p3 + m3) - 6.0 * (p2 + m2) + 15.0 * (p1 + m1) - 20.0 * center
    return slope, smooth


def tend_kernel(edge_rows, chained, count, *refs):
    refs = list(refs)

    def some(n):
        taken = refs[:n]
        del refs[:n]
        return taken

    (polar,) = some(1)
    metric, spin = some(2)
    fields = some(4)
    mass, west, east = some(3)
    south, north = some(2) if edge_rows else (None, None)
    cosines, sines, diagonal = some(3)
    spread, own, send = some(3)
    if chained:
        some(4)
    outs = some(4)
    local, to_east, to_west, to_far = some(4)
    ext, tend, mass_ext, mass_x, mass_y, sems = some(6)
    rows, columns = mass.shape
    levels = ext.shape[2]
    items = count * levels

    copies = []
    for f in range(4):
        if edge_rows:
            copies += [
                (fields[f].at[0:6], ext.at[f, 3:9]),
                (fields[f].at[rows - 6 : rows], ext.at[f, 9:15]),
            ]
            for j in range(3):
                rest = pl.ds(levels * (3 * f + j), levels)
                copies += [(south.at[rest], ext.at[f, j]), (north.at[rest], ext.at[f, 15 + j])]
        else:
            copies += [(fields[f], ext.at[f])]
    if edge_rows:
        tail = pl.ds(12 * levels, 8)
        copies += [(south.at[tail], mass_ext.at[0:8]), (north.at[tail], mass_ext.at[24:32])]
    copies = [pltpu.make_async_copy(a, b, sems.at[n]) for n, (a, b) in enumerate(copies)]
    for c in copies:
        c.start()
    mass_ext[8:24] = mass[...]
    if not edge_rows:
        mass_ext[0:8] = jnp.ones((8, columns), F32)
        mass_ext[24:32] = jnp.ones((8, columns), F32)
    for c in copies:
        c.wait()

    def shifted(left, body, right, axis_len):
        wide = jnp.concatenate([left, body, right], axis=1)
        whole = axis_len + 2 * LANES

        def at(k):
            return pltpu.roll(wide, (-k) % whole, 1)[:, LANES : LANES + axis_len]

        return [at(1), at(2), at(3)], [at(-1), at(-2), at(-3)]

    middle = mass[...]
    per_mass = 1.0 / (60.0 * middle)
    plus, minus = shifted(
        pltpu.roll(west[2 * levels :], LANES - 3, 1), middle, east[2 * levels :], columns
    )
    mass_x[...] = stencil(middle, plus, minus)[0] * per_mass
    if edge_rows:
        below = jnp.concatenate([mass_ext[0:3], middle, mass_ext[24:27]], axis=0)
        plus = [below[3 + k : 3 + k + rows] for k in (1, 2, 3)]
        minus = [below[3 - k : 3 - k + rows] for k in (1, 2, 3)]
    else:
        plus = [mass_ext[8 + k : 8 + k + rows] for k in (1, 2, 3)]
        minus = [mass_ext[8 - k : 8 - k + rows] for k in (1, 2, 3)]
    mass_y[...] = stencil(middle, plus, minus)[0] * per_mass

    def one_row(i, carry):
        upper = i // 3 if edge_rows else 0
        row = i + (rows - 6) * upper if edge_rows else i + 3
        at = i + 3 + 6 * upper if edge_rows else i + 3
        metric_row = metric[row]
        spin_row = spin[row]
        along = metric_row * (1.0 / 60.0)
        lead = 16 * (row // 2)
        slope_mass_x = metric_row * mass_x[pl.ds(row, 1), :]
        slope_mass_y = mass_y[pl.ds(row, 1), :]
        for first in range(0, levels, 8):
            lev = slice(first, first + 8)
            halo = pl.ds(pl.multiple_of((row % 2) * levels + first, 8), 8)
            u = ext[0, at, lev]
            v = ext[1, at, lev]
            theta = ext[2, at, lev]
            u_fast = u * along
            u_size = jnp.abs(u_fast)
            v_fast = v * (1.0 / 60.0)
            v_size = jnp.abs(v_fast)
            push_x = push_y = None
            for f in (3, 0, 1, 2):
                q = ext[f, at, lev]
                start = lead + 3 * f
                left = pltpu.roll(west[halo, :], lax.rem(LANES - 3 + LANES - start, LANES), 1)
                right = pltpu.roll(east[halo, :], lax.rem(LANES - start, LANES), 1)
                plus, minus = shifted(left, q, right, columns)
                slope_x, smooth_x = stencil(q, plus, minus)
                slope_y, smooth_y = stencil(
                    q,
                    [ext[f, at + k, lev] for k in (1, 2, 3)],
                    [ext[f, at - k, lev] for k in (1, 2, 3)],
                )
                change = (u_size * smooth_x - u_fast * slope_x) + (v_size * smooth_y - v_fast * slope_y)
                if f == 3:
                    push_x = along * slope_x + theta * slope_mass_x
                    push_y = (1.0 / 60.0) * slope_y + theta * slope_mass_y
                elif f == 0:
                    change = change + (spin_row * v - push_x)
                elif f == 1:
                    change = change - (spin_row * u + push_y)
                tend[f, i, lev] = change
        return carry

    lax.fori_loop(0, count, one_row, 0)

    @pl.when(polar[0] == 0)
    def _():
        def update(i, carry):
            at = i + 3 + 6 * (i // 3) if edge_rows else i + 3
            for f in range(4):
                tend[f, i] = ext[f, at] + STEP * tend[f, i]
            return carry

        lax.fori_loop(0, count, update, 0)
        writes = []
        for f in range(4):
            if edge_rows:
                writes += [
                    (tend.at[f, 0:3], outs[f].at[0:3]),
                    (tend.at[f, 3:6], outs[f].at[rows - 3 : rows]),
                ]
            else:
                writes += [(tend.at[f], outs[f].at[3 : rows - 3])]
        writes = [pltpu.make_async_copy(a, b, sems.at[n]) for n, (a, b) in enumerate(writes)]
        for c in writes:
            c.start()
        for c in writes:
            c.wait()

    @pl.when(polar[0] != 0)
    def _():
        def spread_out(table):
            table = table[...]
            wide = jnp.broadcast_to(table[:, None, :], (count, levels, NODES))
            return wide.reshape(items, NODES)

        c_all, s_all, d_all = spread_out(cosines), spread_out(sines), spread_out(diagonal)
        messages = [None, None]
        for f in range(4):
            high, low = split(tend[f].reshape(items, columns))
            nodal = dot3(high, low, spread[0], spread[1])
            result = d_all * nodal
            for part, factor in ((0, c_all), (1, s_all)):
                high, low = split(factor * nodal)
                moved = dot3(high, low, own[0], own[1])
                result = result + (s_all * moved if part == 0 else -(c_all * moved))
                group = 2 * (f % 2) + part
                sent = dot3(high, low, send[0, f // 2, group], send[1, f // 2, group])
                old = messages[f // 2]
                messages[f // 2] = sent if old is None else old + sent
            local[f] = result
        first, second = messages
        lane = lax.broadcasted_iota(jnp.int32, (items, LANES), 1)
        to_east[...] = jnp.where(lane < 64, first[:, :LANES], second[:, :LANES])
        to_west[...] = jnp.where(lane < 64, second[:, :LANES], first[:, :LANES])
        far = first[:, LANES:] + second[:, LANES:]
        to_far[...] = far[: items // 2] + pltpu.roll(far[items // 2 :], 64, 1)


def finish_kernel(edge_rows, count, *refs):
    polar, signs = refs[:2]
    fields = refs[2:6]
    from_west, from_east, from_far, local, cosines, sines, take, gather = refs[6:14]
    outs = refs[18:22]
    old, new, sems = refs[22:]
    rows = fields[0].shape[0]
    levels, columns = old.shape[2], old.shape[3]
    items = count * levels

    @pl.when(polar[0] != 0)
    def _():
        reads, writes = [], []
        for f in range(4):
            if edge_rows:
                parts = [((0, 3), (0, 3)), ((3, 6), (rows - 3, rows))]
            else:
                parts = [((0, count), (3, rows - 3))]
            for (a, b), (c, d) in parts:
                reads.append((fields[f].at[c:d], old.at[f, a:b]))
                writes.append((new.at[f, a:b], outs[f].at[c:d]))
        reads = [pltpu.make_async_copy(a, b, sems.at[n]) for n, (a, b) in enumerate(reads)]
        writes = [pltpu.make_async_copy(a, b, sems.at[n]) for n, (a, b) in enumerate(writes)]
        for c in reads:
            c.start()

        def spread_out(table):
            table = table[...]
            wide = jnp.broadcast_to(table[:, None, :], (count, levels, NODES))
            return wide.reshape(items, NODES)

        c_all, s_all = spread_out(cosines), spread_out(sines)
        folded = from_far[...] * signs[2]
        come = jnp.concatenate(
            [
                from_west[...] * signs[0],
                from_east[...] * signs[1],
                jnp.concatenate([folded, pltpu.roll(folded, 64, 1)], axis=0),
            ],
            axis=1,
        )
        high, low = split(come)
        for c in reads:
            c.wait()
        for f in range(4):
            span = slice(2 * f * NODES, (2 * f + 2) * NODES)
            both = dot3(high, low, take[0, :, span], take[1, :, span])
            value = local[f] + (s_all * both[:, :NODES] - c_all * both[:, NODES:])
            wide = dot3(*split(value), gather[0], gather[1])
            new[f] = old[f] + wide.reshape(count, levels, columns)
        for c in writes:
            c.start()
        for c in writes:
            c.wait()


def vmem():
    return pl.BlockSpec(memory_space=pltpu.VMEM)


def smem():
    return pl.BlockSpec(memory_space=pltpu.SMEM)


def anywhere():
    return pl.BlockSpec(memory_space=pl.ANY)


def like(*shape):
    return jax.ShapeDtypeStruct(shape, F32)


def params():
    return pltpu.CompilerParams(vmem_limit_bytes=VMEM_LIMIT)


def row_cutoffs(cutoffs, owner, row_count, lat_count):
    quarter = lat_count // 4
    first = jnp.where(
        owner < quarter, owner * row_count, owner * row_count - lat_count * row_count // 2
    )
    first = jnp.clip(first, 0, cutoffs.shape[0] - row_count)
    return lax.dynamic_slice_in_dim(cutoffs, first, row_count)


def pick_rows(table, edge_rows):
    if edge_rows:
        return jnp.concatenate([table[:3], table[-3:]], axis=0)
    return table[3:-3]


def shards(u_wind, v_wind, theta, geopot, mass, cutoffs):
    rows, levels, columns = u_wind.shape
    lat_count = lax.axis_size("lat")
    lon_count = lax.axis_size("lon")
    lat_idx = lax.axis_index("lat")
    lon_idx = lax.axis_index("lon")
    nlat_all = rows * lat_count
    circle = columns * lon_count
    tables = filter_tables(columns, circle)
    fields = (u_wind, v_wind, theta, geopot)

    strip = 12 * levels + 8
    to_south, to_north, to_west, to_east = pl.pallas_call(
        pack_kernel,
        out_shape=[like(strip, columns)] * 2 + [like(2 * levels + rows, LANES)] * 2,
        in_specs=[anywhere()] * 4 + [vmem()],
        out_specs=[vmem()] * 4,
        scratch_shapes=[
            pltpu.VMEM((2, 4, rows, levels, LANES), F32),
            pltpu.SemaphoreType.DMA((8, 4)),
        ],
        compiler_params=params(),
        name="pack_edges",
    )(*fields, mass)

    def ring(value, step):
        return lax.ppermute(value, "lon", [(i, (i + step) % lon_count) for i in range(lon_count)])

    west = ring(to_east, 1)
    east = ring(to_west, -1)
    south = lax.ppermute(to_north, "lat", [(i, i + 1) for i in range(lat_count - 1)])
    north = lax.ppermute(to_south, "lat", [(i + 1, i) for i in range(lat_count - 1)])

    row_global = lat_idx * rows + jnp.arange(rows, dtype=jnp.int32)
    latitude = (row_global.astype(F32) + 0.5) * (math.pi / nlat_all) - math.pi / 2
    metric = 1.0 / jnp.cos(latitude)
    spin = SPIN * jnp.sin(latitude)
    quarter = lat_count // 4
    polar = ((lat_idx < quarter) | (lat_idx >= lat_count - quarter)).astype(jnp.int32)[None]
    twice = 2 * row_cutoffs(cutoffs, lat_idx, rows, lat_count) + 1
    place = lon_idx * columns + jnp.asarray(tables["nodes"])
    angle = (twice[:, None] * place[None, :] % (2 * circle)).astype(F32) * (math.pi / circle)
    cosines, sines = jnp.cos(angle), jnp.sin(angle)
    diagonal = jnp.broadcast_to((twice.astype(F32) / circle)[:, None], (rows, NODES))

    def tendencies(edge_rows, old):
        count = 6 if edge_rows else rows - 6
        items = count * levels
        deep = 18 if edge_rows else rows
        halos = [south, north] if edge_rows else []
        args = (
            [polar, metric, spin, *fields, mass, west, east, *halos]
            + [pick_rows(t, edge_rows) for t in (cosines, sines, diagonal)]
            + [jnp.asarray(tables[k]) for k in ("spread", "own", "send")]
        )
        specs = (
            [smem()] * 3
            + [anywhere()] * 4
            + [vmem()] * 3
            + [anywhere()] * len(halos)
            + [vmem()] * 6
        )
        aliases = {len(args) + f: f for f in range(4)} if old else {}
        return pl.pallas_call(
            functools.partial(tend_kernel, edge_rows, bool(old), count),
            out_shape=[like(rows, levels, columns)] * 4
            + [like(4, items, NODES)]
            + [like(items, LANES)] * 2
            + [like(items // 2, LANES)],
            in_specs=specs + [anywhere()] * len(old),
            out_specs=[anywhere()] * 4 + [vmem()] * 4,
            scratch_shapes=[
                pltpu.VMEM((4, deep, levels, columns), F32),
                pltpu.VMEM((4, count, levels, columns), F32),
                pltpu.VMEM((rows + 16, columns), F32),
                pltpu.VMEM((rows, columns), F32),
                pltpu.VMEM((rows, columns), F32),
                pltpu.SemaphoreType.DMA((40,)),
            ],
            input_output_aliases=aliases,
            compiler_params=params(),
            cost_estimate=pl.CostEstimate(
                flops=items * 4 * columns * 2000, bytes_accessed=8 * items * columns * 4, transcendentals=0
            ),
            name="tend_edge" if edge_rows else "tend_inner",
        )(*args, *old)

    def exchange(east_part, west_part, far_part):
        return ring(east_part, 1), ring(west_part, -1), ring(far_part, 2)

    signs = jnp.stack(
        [
            jnp.where(lon_idx == 0, -1.0, 1.0),
            jnp.where(lon_idx == lon_count - 1, -1.0, 1.0),
            jnp.where(lon_idx < 2, -1.0, 1.0),
        ]
    ).astype(F32)

    def finish(edge_rows, received, local, old):
        count = 6 if edge_rows else rows - 6
        args = [polar, signs, *fields, *received, local]
        args += [pick_rows(t, edge_rows) for t in (cosines, sines)]
        args += [jnp.asarray(tables[k]) for k in ("take", "gather")]
        return pl.pallas_call(
            functools.partial(finish_kernel, edge_rows, count),
            out_shape=[like(rows, levels, columns)] * 4,
            in_specs=[smem()] * 2 + [anywhere()] * 4 + [vmem()] * 8 + [anywhere()] * 4,
            out_specs=[anywhere()] * 4,
            scratch_shapes=[
                pltpu.VMEM((4, count, levels, columns), F32),
                pltpu.VMEM((4, count, levels, columns), F32),
                pltpu.SemaphoreType.DMA((8,)),
            ],
            input_output_aliases={len(args) + f: f for f in range(4)},
            compiler_params=params(),
            name="finish_edge" if edge_rows else "finish_inner",
        )(*args, *old)

    *outs, local_inner, a, b, c = tendencies(False, [])
    received_inner = exchange(a, b, c)
    *outs, local_edge, a, b, c = tendencies(True, outs)
    received_edge = exchange(a, b, c)
    outs = finish(False, received_inner, local_inner, outs)
    outs = finish(True, received_edge, local_edge, outs)
    return tuple(outs)


def solution(mesh):
    return jax.shard_map(
        shards,
        mesh=mesh,
        in_specs=(
            P(("members", "lat"), None, "lon"),
            P(("members", "lat"), None, "lon"),
            P(("members", "lat"), None, "lon"),
            P(("members", "lat"), None, "lon"),
            P(("members", "lat"), "lon"),
            P(),
        ),
        out_specs=(
            P(("members", "lat"), None, "lon"),
            P(("members", "lat"), None, "lon"),
            P(("members", "lat"), None, "lon"),
            P(("members", "lat"), None, "lon"),
        ),
        check_vma=False,
    )
```

```python
import functools
import math

import jax
import jax.numpy as jnp
import ml_dtypes
import numpy as np
from jax import lax
from jax.experimental import pallas as pl
from jax.experimental.pallas import tpu as pltpu
from jax.sharding import PartitionSpec as P

STEP = 0.1
SPIN = 0.5
LANES = 128
NEAR = 16
FAR = 8
NODES = 256
F32 = jnp.float32
BF16 = jnp.bfloat16
MESSAGE = 2 * NEAR + FAR
VMEM_LIMIT = 56 * 1024 * 1024


def pivoted(matrix, count):
    rest = np.array(matrix)
    columns = rest.shape[1]
    tilt = 1.0 + 1e-3 * np.arange(columns) / columns
    picked = []
    tri = np.zeros((count, columns))
    for step in range(count):
        size = (rest * rest).sum(axis=0)
        best = int(np.argmax(size * tilt))
        picked.append(best)
        unit = rest[:, best] / math.sqrt(size[best])
        for _ in range(2):
            part = (unit[:, None] * rest).sum(axis=0)
            rest -= unit[:, None] * part[None, :]
            tri[step] += part
        rest[:, best] = 0.0
    left = tri[:, picked].copy()
    right = tri.copy()
    for step in range(count - 1, -1, -1):
        right[step] /= left[step, step]
        right[:step] -= left[:step, step][:, None] * right[step][None, :]
    right[:, picked] = np.eye(count)
    order = np.argsort(picked)
    return np.asarray(picked)[order], right[order]


def cauchy(target, source, circle):
    gap = target[:, None] - source[None, :]
    angle = np.where(gap == 0, 0.5 * math.pi, gap * math.pi / circle)
    return np.where(gap == 0, 0.0, 1.0 / (circle * np.sin(angle)))


def stacked_halves(table):
    table = table.astype(np.float32)
    high = table.astype(ml_dtypes.bfloat16)
    low = (table - high.astype(np.float32)).astype(ml_dtypes.bfloat16)
    return np.concatenate([high, high, low], axis=0)


def band_table():
    band = np.zeros((2 * LANES, 2 * LANES))
    slope = {-3: -1, -2: 9, -1: -45, 1: 45, 2: -9, 3: 1}
    smooth = {-3: 1, -2: -6, -1: 15, 0: -20, 1: 15, 2: -6, 3: 1}
    for j in range(LANES):
        for k, value in slope.items():
            band[j + 3 + k, j] = value
        for k, value in smooth.items():
            band[j + 3 + k, LANES + j] = value
    return np.concatenate([band, band], axis=0).astype(ml_dtypes.bfloat16)


@functools.lru_cache(maxsize=None)
def filter_tables(sector, circle):
    modes = circle // 8
    place = np.arange(sector)
    wave = np.arange(modes)
    phase = (wave[:, None] * place[None, :]) % circle * (2 * math.pi / circle)
    basis = np.concatenate([np.cos(phase), np.sin(phase[1:])], axis=0)
    nodes, spread = pivoted(basis, NODES)
    own = cauchy(nodes, nodes, circle)
    send = np.zeros((NODES, LANES))
    take = np.zeros((MESSAGE, NODES))
    at = 0
    for shift, count in ((sector, NEAR), (-sector, NEAR), (2 * sector, FAR)):
        kernel = cauchy(nodes + shift, nodes, circle)
        pick, weights = pivoted(kernel, count)
        send[:, at : at + count] = weights.T
        take[at : at + count] = kernel[:, pick].T
        at += count
    take = stacked_halves(take)
    take = np.concatenate([take, np.zeros((LANES - 3 * MESSAGE, NODES), take.dtype)], axis=0)
    return dict(
        nodes=nodes.astype(np.float32)[None],
        band=band_table(),
        spread=stacked_halves(spread.T),
        own=stacked_halves(own.T),
        send=stacked_halves(send),
        take=take,
        gather=stacked_halves(STEP * spread),
    )


def split(value):
    high = value.astype(BF16)
    low = (value - high.astype(F32)).astype(BF16)
    return jnp.concatenate([high, low, high], axis=1)


def dot(a, b):
    return lax.dot_general(a, b, (((1,), (0,)), ((), ())), preferred_element_type=F32)


def start_all(pairs, sems, first=0):
    copies = [pltpu.make_async_copy(a, b, sems.at[first + n]) for n, (a, b) in enumerate(pairs)]
    for c in copies:
        c.start()
    return copies


def wait_all(copies):
    for c in copies:
        c.wait()


def is_polar():
    owner = lax.axis_index("lat")
    quarter = lax.axis_size("lat") // 4
    return (owner < quarter) | (owner >= lax.axis_size("lat") - quarter)


def pack_kernel(cutoffs, *refs):
    fields = refs[:4]
    mass, nodes, south, north, west, east, waves, edge, own_mass, tails, sems = refs[4:]
    rows, columns = mass.shape
    levels = edge.shape[3]
    tail = 12 * levels
    first = start_all(
        [(mass, own_mass)]
        + [(q.at[:, :, 0:LANES], edge.at[0, f]) for f, q in enumerate(fields)]
        + [(q.at[:, :, columns - LANES : columns], edge.at[1, f]) for f, q in enumerate(fields)],
        sems,
    )
    strips = []
    for f, q in enumerate(fields):
        for j in range(3):
            into = pl.ds(levels * (3 * f + j), levels)
            strips += [(q.at[j], south.at[into]), (q.at[rows - 3 + j], north.at[into])]
    strips = start_all(strips, sems, 9)

    lat_count = lax.axis_size("lat")
    lon_count = lax.axis_size("lon")
    owner = lax.axis_index("lat")
    circle = columns * lon_count
    start = jnp.where(owner < lat_count // 4, owner * rows, owner * rows - lat_count * rows // 2)
    start = jnp.clip(start, 0, lat_count * rows // 2 - rows)
    line = lax.broadcasted_iota(jnp.int32, (rows, NODES), 0)
    twice = jnp.zeros((rows, NODES), F32)
    for r in range(rows):
        twice = jnp.where(line == r, (2 * cutoffs[start + r] + 1).astype(F32), twice)
    place = nodes[...] + (lax.axis_index("lon") * columns).astype(F32)
    turns = twice * place
    angle = (turns - 2.0 * circle * jnp.floor(turns * (0.5 / circle))) * (math.pi / circle)
    waves[0] = jnp.cos(angle)
    waves[1] = jnp.sin(angle)
    waves[2] = twice * (1.0 / circle)

    wait_all(first)
    tails[...] = jnp.zeros_like(tails)
    tails[0, 0:3] = own_mass[0:3]
    tails[1, 0:3] = own_mass[rows - 3 : rows]
    into = pl.ds(tail, 8)
    ends = start_all([(tails.at[0], south.at[into]), (tails.at[1], north.at[into])], sems, 33)
    lane = lax.broadcasted_iota(jnp.int32, (levels, LANES), 1)
    west[2 * levels :] = own_mass[:, 0:LANES]
    east[2 * levels :] = pltpu.roll(own_mass[:, columns - LANES : columns], 3, 1)
    for parity in range(2):
        for side, out in ((0, west), (1, east)):
            total = jnp.zeros((levels, LANES), F32)
            for r in range(parity, rows, 2):
                for f in range(4):
                    lead = 16 * (r // 2) + 3 * f
                    turn = lead if side == 0 else (lead + 3) % LANES
                    tile = edge[side, f, r]
                    if turn:
                        tile = pltpu.roll(tile, turn, 1)
                    total = jnp.where((lane >= lead) & (lane < lead + 3), tile, total)
            out[parity * levels : (parity + 1) * levels] = total
    wait_all(strips + ends)


def stencil(center, plus, minus):
    p1, p2, p3 = plus
    m1, m2, m3 = minus
    slope = 45.0 * (p1 - m1) - 9.0 * (p2 - m2) + (p3 - m3)
    smooth = (p3 + m3) - 6.0 * (p2 + m2) + 15.0 * (p1 + m1) - 20.0 * center
    return slope, smooth


def mass_slopes(mass, west, east, mass_ext, mass_x, mass_y, levels, edge_rows):
    rows, columns = mass.shape
    middle = mass[...]
    per_mass = 1.0 / (60.0 * middle)
    wide = jnp.concatenate(
        [pltpu.roll(west[2 * levels :], LANES - 3, 1), middle, east[2 * levels :]], axis=1
    )
    whole = columns + 2 * LANES

    def at(k):
        return pltpu.roll(wide, (-k) % whole, 1)[:, LANES : LANES + columns]

    def store(out, value):
        out[...] = jnp.broadcast_to(value[:, None, :], out.shape)

    store(mass_x, stencil(middle, [at(1), at(2), at(3)], [at(-1), at(-2), at(-3)])[0] * per_mass)
    if edge_rows:
        tall = jnp.concatenate([mass_ext[0:3], middle, mass_ext[8:11]], axis=0)
    else:
        blank = jnp.zeros((3, columns), F32)
        tall = jnp.concatenate([blank, middle, blank], axis=0)
    plus = [tall[3 + k : 3 + k + rows] for k in (1, 2, 3)]
    minus = [tall[3 - k : 3 - k + rows] for k in (1, 2, 3)]
    store(mass_y, stencil(middle, plus, minus)[0] * per_mass)


def spread_rows(table, count, levels):
    wide = jnp.broadcast_to(table[:, None, :], (count, levels, table.shape[1]))
    return wide.reshape(count * levels, table.shape[1])


def own_waves(waves, part, edge_rows):
    table = waves[part]
    rows = table.shape[0]
    if edge_rows:
        return jnp.concatenate([table[:3], table[rows - 3 :]], axis=0)
    return table[3 : rows - 3]


def tend_kernel(edge_rows, count, metric, spin, *refs):
    refs = list(refs)

    def some(n):
        taken = refs[:n]
        del refs[:n]
        return taken

    fields = some(4)
    mass_in, west_in, east_in, waves_in = some(4)
    south, north = some(2) if edge_rows else (None, None)
    band_in, spread_in, own_in, send_in = some(4)
    if edge_rows:
        some(4)
    outs = some(4)
    local, to_east, to_west, to_far = some(4)
    ext, high, low, cross, new, kept_high, kept_low = some(7)
    mass, mass_ext, mass_x, mass_y, west, east, waves = some(7)
    band, spread, own, send, sems = some(5)
    rows, columns = mass.shape
    levels = ext.shape[2]
    items = count * levels
    tiles = columns // LANES

    pairs = [(west_in, west), (east_in, east), (mass_in, mass), (band_in, band)]
    for f in range(4):
        if edge_rows:
            pairs += [
                (fields[f].at[0:6], ext.at[f, 3:9]),
                (fields[f].at[rows - 6 : rows], ext.at[f, 9:15]),
            ]
            for j in range(3):
                part = pl.ds(levels * (3 * f + j), levels)
                pairs += [(south.at[part], ext.at[f, j]), (north.at[part], ext.at[f, 15 + j])]
        else:
            pairs += [(fields[f], ext.at[f])]
    if edge_rows:
        part = pl.ds(12 * levels, 8)
        pairs += [(south.at[part], mass_ext.at[0:8]), (north.at[part], mass_ext.at[8:16])]
    first = start_all(pairs, sems)
    later = start_all(
        [(waves_in, waves), (spread_in, spread), (own_in, own), (send_in, send)], sems, len(pairs)
    )
    wait_all(first)

    mass_slopes(mass, west, east, mass_ext, mass_x, mass_y, levels, edge_rows)
    lane = lax.broadcasted_iota(jnp.int32, (levels, LANES), 1)

    def where(i):
        if edge_rows:
            return i + (rows - 6) * (i // 3), i + 3 + 6 * (i // 3)
        return i + 3, i + 3

    def cut(i, carry):
        row, at = where(i)
        halo = pl.ds(pl.multiple_of((row % 2) * levels, levels), levels)
        for f in range(4):
            lead = 16 * (row // 2) + 3 * f
            before = pltpu.roll(west[halo, :], lax.rem(LANES - lead, LANES), 1)
            for t in range(tiles + 1):
                if t < tiles:
                    tile = pltpu.roll(ext[f, at, :, t * LANES : (t + 1) * LANES], 3, 1)
                else:
                    tile = pltpu.roll(east[halo, :], lax.rem(LANES + 3 - lead, LANES), 1)
                whole = jnp.where(lane < 3, before, tile)
                top = whole.astype(BF16)
                high[f, i, :, t * LANES : (t + 1) * LANES] = top
                low[f, i, :, t * LANES : (t + 1) * LANES] = (whole - top.astype(F32)).astype(BF16)
                before = tile
        return carry

    lax.fori_loop(0, count, cut, 0)

    for t in range(tiles):
        span = slice(t * LANES, (t + 2) * LANES)
        both = jnp.concatenate(
            [high[:, :, :, span].reshape(4 * items, 2 * LANES), low[:, :, :, span].reshape(4 * items, 2 * LANES)],
            axis=1,
        )
        cross[t] = dot(both, band[...]).reshape(4, count, levels, 2 * LANES)

    start_row = lax.axis_index("lat") * rows

    def whole(lines):
        return jnp.concatenate([lines] * (levels // 8), axis=0)

    def tendency(i, t):
        row, at = where(i)
        span = slice(t * LANES, (t + 1) * LANES)
        metric_row = metric[start_row + row]
        spin_row = spin[start_row + row]
        along = metric_row * (1.0 / 60.0)
        u = ext[0, at, :, span]
        v = ext[1, at, :, span]
        theta = ext[2, at, :, span]
        u_fast = u * along
        u_size = jnp.abs(u_fast)
        v_fast = v * (1.0 / 60.0)
        v_size = jnp.abs(v_fast)
        result = [None] * 4
        for f in (3, 0, 1, 2):
            slope_x = cross[t, f, i, :, :LANES]
            smooth_x = cross[t, f, i, :, LANES:]
            slope_y, smooth_y = stencil(
                ext[f, at, :, span],
                [ext[f, at + k, :, span] for k in (1, 2, 3)],
                [ext[f, at - k, :, span] for k in (1, 2, 3)],
            )
            change = (u_size * smooth_x - u_fast * slope_x) + (v_size * smooth_y - v_fast * slope_y)
            if f == 3:
                push_x = along * slope_x + theta * (metric_row * whole(mass_x[row, :, span]))
                push_y = (1.0 / 60.0) * slope_y + theta * whole(mass_y[row, :, span])
            elif f == 0:
                change = change + (spin_row * v - push_x)
            elif f == 1:
                change = change - (spin_row * u + push_y)
            result[f] = change
        return result, at, span

    @pl.when(jnp.logical_not(is_polar()))
    def _():
        def step(i, carry):
            for t in range(tiles):
                change, at, span = tendency(i, t)
                for f in range(4):
                    new[f, i, :, span] = ext[f, at, :, span] + STEP * change[f]
            return carry

        lax.fori_loop(0, count, step, 0)
        pairs = []
        for f in range(4):
            if edge_rows:
                pairs += [
                    (new.at[f, 0:3], outs[f].at[0:3]),
                    (new.at[f, 3:6], outs[f].at[rows - 3 : rows]),
                ]
            else:
                pairs += [(new.at[f], outs[f].at[3 : rows - 3])]
        writes = start_all(pairs, sems)
        wait_all(later)
        wait_all(writes)

    @pl.when(is_polar())
    def _():
        def step(i, carry):
            for t in range(tiles):
                change, _, span = tendency(i, t)
                for f in range(4):
                    top = change[f].astype(BF16)
                    kept_high[f, i, :, span] = top
                    kept_low[f, i, :, span] = (change[f] - top.astype(F32)).astype(BF16)
            return carry

        lax.fori_loop(0, count, step, 0)
        wait_all(later)
        c_all, s_all, d_all = [
            spread_rows(own_waves(waves, part, edge_rows), count, levels) for part in range(3)
        ]
        top = kept_high[...].reshape(4 * items, columns)
        rest = kept_low[...].reshape(4 * items, columns)
        nodal = dot(jnp.concatenate([top, rest, top], axis=1), spread[...])
        turned = []
        for f in range(4):
            part = nodal[f * items : (f + 1) * items]
            turned += [c_all * part, s_all * part]
        turned = split(jnp.concatenate(turned, axis=0))
        moved = dot(turned, own[...])
        sent = dot(turned, send[...])
        for f in range(4):
            at = 2 * f * items
            local[f] = (
                s_all * moved[at : at + items]
                - c_all * moved[at + items : at + 2 * items]
                + d_all * nodal[f * items : (f + 1) * items]
            )
        wide = lax.broadcasted_iota(jnp.int32, (items, LANES), 1)
        for out, first, size in ((to_east, 0, NEAR), (to_west, NEAR, NEAR), (to_far, 2 * NEAR, FAR)):
            total = jnp.zeros((items, LANES), F32)
            for g in range(8):
                part = sent[g * items : (g + 1) * items]
                turn = (size * g - first) % LANES
                if turn:
                    part = pltpu.roll(part, turn, 1)
                total = jnp.where((wide >= size * g) & (wide < size * (g + 1)), part, total)
            if size == NEAR:
                out[...] = total
            else:
                total = total.reshape(count, 2, levels // 2, LANES)
                upper = pltpu.roll(total[:, 1].reshape(items // 2, LANES), 64, 1)
                out[...] = total[:, 0].reshape(items // 2, LANES) + upper


def finish_kernel(edge_rows, count, *refs):
    fields = refs[:4]
    from_west_in, from_east_in, from_far_in, local_in, waves_in, take_in, gather_in = refs[4:11]
    outs = refs[15:19]
    old, new, from_west, from_east, from_far, local, waves, take, gather, sems = refs[19:]
    rows = fields[0].shape[0]
    levels, columns = old.shape[2], old.shape[3]
    items = count * levels

    @pl.when(is_polar())
    def _():
        first = start_all(
            [
                (from_west_in, from_west),
                (from_east_in, from_east),
                (from_far_in, from_far),
                (waves_in, waves),
                (take_in, take),
                (local_in, local),
            ],
            sems,
        )
        reads, pairs = [(gather_in, gather)], []
        for f in range(4):
            if edge_rows:
                parts = [((0, 3), (0, 3)), ((3, 6), (rows - 3, rows))]
            else:
                parts = [((0, count), (3, rows - 3))]
            for (a, b), (c, d) in parts:
                reads.append((fields[f].at[c:d], old.at[f, a:b]))
                pairs.append((new.at[f, a:b], outs[f].at[c:d]))
        reads = start_all(reads, sems, 6)
        wait_all(first)

        place = lax.axis_index("lon")
        last = lax.axis_size("lon") - 1
        near_west = from_west[...] * jnp.where(place == 0, -1.0, 1.0)
        near_east = from_east[...] * jnp.where(place == last, -1.0, 1.0)
        far = from_far[...] * jnp.where(place < 2, -1.0, 1.0)
        far = far.reshape(count, 1, levels // 2, LANES)
        upper = pltpu.roll(far.reshape(items // 2, LANES), 64, 1).reshape(count, 1, levels // 2, LANES)
        far = jnp.concatenate([far, upper], axis=1).reshape(items, LANES)
        wide = lax.broadcasted_iota(jnp.int32, (items, LANES), 1)

        def turn(value, by):
            by = by % LANES
            return pltpu.roll(value, by, 1) if by else value

        come = []
        for g in range(8):
            part = jnp.where(wide < NEAR, turn(near_west, -NEAR * g), turn(near_east, NEAR - NEAR * g))
            part = jnp.where(wide < 2 * NEAR, part, turn(far, 2 * NEAR - FAR * g))
            part = jnp.where(wide < MESSAGE, part, 0.0)
            top = part.astype(BF16).astype(F32)
            come.append((top + turn(part - top, MESSAGE) + turn(top, 2 * MESSAGE)).astype(BF16))
        moved = dot(jnp.concatenate(come, axis=0), take[...])
        c_all, s_all = [
            spread_rows(own_waves(waves, part, edge_rows), count, levels) for part in range(2)
        ]
        value = []
        for f in range(4):
            at = 2 * f * items
            value.append(
                local[f] + (s_all * moved[at : at + items] - c_all * moved[at + items : at + 2 * items])
            )
        value = split(jnp.concatenate(value, axis=0))
        wait_all(reads)
        change = dot(value, gather[...])
        new[...] = old[...] + change.reshape(4, count, levels, columns)
        wait_all(start_all(pairs, sems))


def vmem():
    return pl.BlockSpec(memory_space=pltpu.VMEM)


def smem():
    return pl.BlockSpec(memory_space=pltpu.SMEM)


def anywhere():
    return pl.BlockSpec(memory_space=pl.ANY)


def like(*shape):
    return jax.ShapeDtypeStruct(shape, F32)


def held(value):
    return pltpu.VMEM(value.shape, value.dtype)


def params():
    return pltpu.CompilerParams(vmem_limit_bytes=VMEM_LIMIT)


def row_factors(count):
    latitude = (np.arange(count).astype(np.float32) + np.float32(0.5)) * np.float32(math.pi / count)
    latitude = latitude - np.float32(math.pi / 2)
    metric = np.float32(1.0) / np.cos(latitude)
    return metric.astype(np.float32), (np.float32(SPIN) * np.sin(latitude)).astype(np.float32)


def shards(u_wind, v_wind, theta, geopot, mass, cutoffs):
    rows, levels, columns = u_wind.shape
    lat_count = lax.axis_size("lat")
    lon_count = lax.axis_size("lon")
    tables = {k: jnp.asarray(v) for k, v in filter_tables(columns, columns * lon_count).items()}
    metric, spin = [jnp.asarray(t) for t in row_factors(rows * lat_count)]
    fields = (u_wind, v_wind, theta, geopot)

    strip = 12 * levels + 8
    edge_lines = 2 * levels + rows
    to_south, to_north, to_west, to_east, waves = pl.pallas_call(
        pack_kernel,
        out_shape=[like(strip, columns)] * 2 + [like(edge_lines, LANES)] * 2 + [like(3, rows, NODES)],
        in_specs=[smem()] + [anywhere()] * 5 + [vmem()],
        out_specs=[anywhere()] * 2 + [vmem()] * 3,
        scratch_shapes=[
            pltpu.VMEM((2, 4, rows, levels, LANES), F32),
            pltpu.VMEM((rows, columns), F32),
            pltpu.VMEM((2, 8, columns), F32),
            pltpu.SemaphoreType.DMA((35,)),
        ],
        compiler_params=params(),
        name="pack_edges",
    )(cutoffs, *fields, mass, tables["nodes"])

    def ring(value, step):
        return lax.ppermute(value, "lon", [(i, (i + step) % lon_count) for i in range(lon_count)])

    west = ring(to_east, 1)
    east = ring(to_west, -1)
    south = lax.ppermute(to_north, "lat", [(i, i + 1) for i in range(lat_count - 1)])
    north = lax.ppermute(to_south, "lat", [(i + 1, i) for i in range(lat_count - 1)])

    def tendencies(edge_rows, old):
        count = 6 if edge_rows else rows - 6
        items = count * levels
        deep = 18 if edge_rows else rows
        halos = [south, north] if edge_rows else []
        weights = [tables[k] for k in ("band", "spread", "own", "send")]
        args = [metric, spin, *fields, mass, west, east, waves, *halos, *weights]
        return pl.pallas_call(
            functools.partial(tend_kernel, edge_rows, count),
            out_shape=[like(rows, levels, columns)] * 4
            + [like(4, items, NODES)]
            + [like(items, LANES)] * 2
            + [like(items // 2, LANES)],
            in_specs=[smem()] * 2 + [anywhere()] * (len(args) - 2 + len(old)),
            out_specs=[anywhere()] * 4 + [vmem()] * 4,
            scratch_shapes=[
                pltpu.VMEM((4, deep, levels, columns), F32),
                pltpu.VMEM((4, count, levels, columns + LANES), BF16),
                pltpu.VMEM((4, count, levels, columns + LANES), BF16),
                pltpu.VMEM((columns // LANES, 4, count, levels, 2 * LANES), F32),
                pltpu.VMEM((4, count, levels, columns), F32),
                pltpu.VMEM((4, count, levels, columns), BF16),
                pltpu.VMEM((4, count, levels, columns), BF16),
                pltpu.VMEM((rows, columns), F32),
                pltpu.VMEM((16, columns), F32),
                pltpu.VMEM((rows, 8, columns), F32),
                pltpu.VMEM((rows, 8, columns), F32),
                pltpu.VMEM((edge_lines, LANES), F32),
                pltpu.VMEM((edge_lines, LANES), F32),
                pltpu.VMEM((3, rows, NODES), F32),
                *[held(w) for w in weights],
                pltpu.SemaphoreType.DMA((48,)),
            ],
            input_output_aliases={len(args) + f: f for f in range(4)} if old else {},
            compiler_params=params(),
            cost_estimate=pl.CostEstimate(
                flops=items * 4 * columns * 2000, bytes_accessed=8 * items * columns * 4, transcendentals=0
            ),
            name="tend_edge" if edge_rows else "tend_inner",
        )(*args, *old)

    def exchange(east_part, west_part, far_part):
        return ring(east_part, 1), ring(west_part, -1), ring(far_part, 2)

    def finish(edge_rows, received, local, old):
        count = 6 if edge_rows else rows - 6
        items = count * levels
        weights = [tables[k] for k in ("take", "gather")]
        args = [*fields, *received, local, waves, *weights]
        return pl.pallas_call(
            functools.partial(finish_kernel, edge_rows, count),
            out_shape=[like(rows, levels, columns)] * 4,
            in_specs=[anywhere()] * (len(args) + 4),
            out_specs=[anywhere()] * 4,
            scratch_shapes=[
                pltpu.VMEM((4, count, levels, columns), F32),
                pltpu.VMEM((4, count, levels, columns), F32),
                pltpu.VMEM((items, LANES), F32),
                pltpu.VMEM((items, LANES), F32),
                pltpu.VMEM((items // 2, LANES), F32),
                pltpu.VMEM((4, items, NODES), F32),
                pltpu.VMEM((3, rows, NODES), F32),
                *[held(w) for w in weights],
                pltpu.SemaphoreType.DMA((16,)),
            ],
            input_output_aliases={len(args) + f: f for f in range(4)},
            compiler_params=params(),
            name="finish_edge" if edge_rows else "finish_inner",
        )(*args, *old)

    *outs, local_inner, a, b, c = tendencies(False, [])
    received_inner = exchange(a, b, c)
    *outs, local_edge, a, b, c = tendencies(True, outs)
    received_edge = exchange(a, b, c)
    outs = finish(False, received_inner, local_inner, outs)
    outs = finish(True, received_edge, local_edge, outs)
    return tuple(outs)


def solution(mesh):
    return jax.shard_map(
        shards,
        mesh=mesh,
        in_specs=(
            P(("members", "lat"), None, "lon"),
            P(("members", "lat"), None, "lon"),
            P(("members", "lat"), None, "lon"),
            P(("members", "lat"), None, "lon"),
            P(("members", "lat"), "lon"),
            P(),
        ),
        out_specs=(
            P(("members", "lat"), None, "lon"),
            P(("members", "lat"), None, "lon"),
            P(("members", "lat"), None, "lon"),
            P(("members", "lat"), None, "lon"),
        ),
        check_vma=False,
    )
```

```python
import functools
import math

import jax
import jax.numpy as jnp
import ml_dtypes
import numpy as np
from jax import lax
from jax.experimental import pallas as pl
from jax.experimental.pallas import tpu as pltpu
from jax.sharding import PartitionSpec as P

STEP = 0.1
SPIN = 0.5
LANES = 128
NEAR = 16
FAR = 8
NODES = 256
F32 = jnp.float32
BF16 = jnp.bfloat16
MESSAGE = 2 * NEAR + FAR


def pivoted(matrix, count):
    rest = np.array(matrix)
    columns = rest.shape[1]
    tilt = 1.0 + 1e-3 * np.arange(columns) / columns
    picked = []
    tri = np.zeros((count, columns))
    for step in range(count):
        size = (rest * rest).sum(axis=0)
        best = int(np.argmax(size * tilt))
        picked.append(best)
        unit = rest[:, best] / math.sqrt(size[best])
        for _ in range(2):
            part = (unit[:, None] * rest).sum(axis=0)
            rest -= unit[:, None] * part[None, :]
            tri[step] += part
        rest[:, best] = 0.0
    left = tri[:, picked].copy()
    right = tri.copy()
    for step in range(count - 1, -1, -1):
        right[step] /= left[step, step]
        right[:step] -= left[:step, step][:, None] * right[step][None, :]
    right[:, picked] = np.eye(count)
    order = np.argsort(picked)
    return np.asarray(picked)[order], right[order]


def cauchy(target, source, circle):
    gap = target[:, None] - source[None, :]
    angle = np.where(gap == 0, 0.5 * math.pi, gap * math.pi / circle)
    return np.where(gap == 0, 0.0, 1.0 / (circle * np.sin(angle)))


def stacked_halves(table):
    table = table.astype(np.float32)
    high = table.astype(ml_dtypes.bfloat16)
    low = (table - high.astype(np.float32)).astype(ml_dtypes.bfloat16)
    return np.concatenate([high, high, low], axis=0)


def band_table():
    band = np.zeros((2 * LANES, 2 * LANES))
    slope = {-3: -1, -2: 9, -1: -45, 1: 45, 2: -9, 3: 1}
    smooth = {-3: 1, -2: -6, -1: 15, 0: -20, 1: 15, 2: -6, 3: 1}
    for j in range(LANES):
        for k, value in slope.items():
            band[j + 3 + k, j] = value
        for k, value in smooth.items():
            band[j + 3 + k, LANES + j] = value
    return np.concatenate([band, band], axis=0).astype(ml_dtypes.bfloat16)


@functools.lru_cache(maxsize=None)
def filter_tables(sector, circle):
    modes = circle // 8
    place = np.arange(sector)
    wave = np.arange(modes)
    phase = (wave[:, None] * place[None, :]) % circle * (2 * math.pi / circle)
    basis = np.concatenate([np.cos(phase), np.sin(phase[1:])], axis=0)
    nodes, spread = pivoted(basis, NODES)
    own = cauchy(nodes, nodes, circle)
    send = np.zeros((NODES, LANES))
    take = np.zeros((MESSAGE, NODES))
    at = 0
    for shift, count in ((sector, NEAR), (-sector, NEAR), (2 * sector, FAR)):
        kernel = cauchy(nodes + shift, nodes, circle)
        pick, weights = pivoted(kernel, count)
        send[:, at : at + count] = weights.T
        take[at : at + count] = kernel[:, pick].T
        at += count
    take = stacked_halves(take)
    take = np.concatenate([take, np.zeros((LANES - 3 * MESSAGE, NODES), take.dtype)], axis=0)
    return dict(
        nodes=nodes.astype(np.float32)[None],
        band=band_table(),
        spread=stacked_halves(spread.T),
        own=stacked_halves(own.T),
        send=stacked_halves(send),
        take=take,
        gather=stacked_halves(STEP * spread),
    )


def split(value):
    high = value.astype(BF16)
    low = (value - high.astype(F32)).astype(BF16)
    return jnp.concatenate([high, low, high], axis=1)


def dot(a, b):
    return lax.dot_general(a, b, (((1,), (0,)), ((), ())), preferred_element_type=F32)


def start_all(pairs, sems, first=0):
    copies = [pltpu.make_async_copy(a, b, sems.at[first + n]) for n, (a, b) in enumerate(pairs)]
    for c in copies:
        c.start()
    return copies


def wait_all(copies):
    for c in copies:
        c.wait()


def is_polar():
    owner = lax.axis_index("lat")
    quarter = lax.axis_size("lat") // 4
    return (owner < quarter) | (owner >= lax.axis_size("lat") - quarter)


def pack_lon_kernel(*refs):
    fields = refs[:4]
    mass, west, east, edge, own_mass, sems = refs[4:]
    rows, columns = mass.shape
    levels = edge.shape[3]
    copies = start_all(
        [(mass, own_mass)]
        + [(q.at[:, :, 0:LANES], edge.at[0, f]) for f, q in enumerate(fields)]
        + [(q.at[:, :, columns - LANES : columns], edge.at[1, f]) for f, q in enumerate(fields)],
        sems,
    )
    wait_all(copies)
    lane = lax.broadcasted_iota(jnp.int32, (levels, LANES), 1)
    west[2 * levels :] = own_mass[:, 0:LANES]
    east[2 * levels :] = pltpu.roll(own_mass[:, columns - LANES : columns], 3, 1)
    for parity in range(2):
        for side, out in ((0, west), (1, east)):
            total = jnp.zeros((levels, LANES), F32)
            for r in range(parity, rows, 2):
                for f in range(4):
                    lead = 16 * (r // 2) + 3 * f
                    turn = lead if side == 0 else (lead + 3) % LANES
                    tile = edge[side, f, r]
                    if turn:
                        tile = pltpu.roll(tile, turn, 1)
                    total = jnp.where((lane >= lead) & (lane < lead + 3), tile, total)
            out[parity * levels : (parity + 1) * levels] = total


def pack_lat_kernel(cutoffs, *refs):
    fields = refs[:4]
    mass, nodes, _, south, north, waves, strips, own_mass, sems = refs[4:]
    rows, columns = mass.shape
    levels = fields[0].shape[1]
    tail = 12 * levels
    pairs, parts = [], []
    for f, q in enumerate(fields):
        for side, first in ((0, 0), (1, rows - 3)):
            for j in range(3):
                part = pl.ds(levels * (3 * f + j), levels)
                pairs.append((q.at[first + j], strips.at[side, part]))
                parts.append((strips.at[side, part], (south, north)[side].at[part]))
    mass_copy = start_all([(mass, own_mass)], sems)
    reads = start_all(pairs, sems, 1)

    lat_count = lax.axis_size("lat")
    lon_count = lax.axis_size("lon")
    owner = lax.axis_index("lat")
    circle = columns * lon_count
    start = jnp.where(owner < lat_count // 4, owner * rows, owner * rows - lat_count * rows // 2)
    start = jnp.clip(start, 0, lat_count * rows // 2 - rows)
    line = lax.broadcasted_iota(jnp.int32, (rows, NODES), 0)
    twice = jnp.zeros((rows, NODES), F32)
    for r in range(rows):
        twice = jnp.where(line == r, (2 * cutoffs[start + r] + 1).astype(F32), twice)
    place = nodes[...] + (lax.axis_index("lon") * columns).astype(F32)
    turns = twice * place
    angle = (turns - 2.0 * circle * jnp.floor(turns * (0.5 / circle))) * (math.pi / circle)
    waves[0] = jnp.cos(angle)
    waves[1] = jnp.sin(angle)
    waves[2] = twice * (1.0 / circle)

    wait_all(mass_copy)
    for side, first in ((0, 0), (1, rows - 3)):
        strips[side, tail : tail + 3] = own_mass[first : first + 3]
        strips[side, tail + 3 : tail + 8] = jnp.zeros((5, columns), F32)
    rest = pl.ds(tail, 8)
    writes = start_all([(strips.at[0, rest], south.at[rest]), (strips.at[1, rest], north.at[rest])], sems, 25)
    for n, c in enumerate(reads):
        c.wait()
        writes += start_all([parts[n]], sems, 27 + n)
    wait_all(writes)


def stencil(center, plus, minus):
    p1, p2, p3 = plus
    m1, m2, m3 = minus
    slope = 45.0 * (p1 - m1) - 9.0 * (p2 - m2) + (p3 - m3)
    smooth = (p3 + m3) - 6.0 * (p2 + m2) + 15.0 * (p1 + m1) - 20.0 * center
    return slope, smooth


def mass_slopes(mass, west, east, mass_ext, mass_x, mass_y, levels, edge_rows):
    rows, columns = mass.shape
    middle = mass[...]
    per_mass = 1.0 / (60.0 * middle)
    wide = jnp.concatenate(
        [pltpu.roll(west[2 * levels :], LANES - 3, 1), middle, east[2 * levels :]], axis=1
    )
    whole = columns + 2 * LANES

    def at(k):
        return pltpu.roll(wide, (-k) % whole, 1)[:, LANES : LANES + columns]

    def store(out, value):
        out[...] = jnp.broadcast_to(value[:, None, :], out.shape)

    store(mass_x, stencil(middle, [at(1), at(2), at(3)], [at(-1), at(-2), at(-3)])[0] * per_mass)
    if edge_rows:
        tall = jnp.concatenate([mass_ext[0:3], middle, mass_ext[8:11]], axis=0)
    else:
        blank = jnp.zeros((3, columns), F32)
        tall = jnp.concatenate([blank, middle, blank], axis=0)
    plus = [tall[3 + k : 3 + k + rows] for k in (1, 2, 3)]
    minus = [tall[3 - k : 3 - k + rows] for k in (1, 2, 3)]
    store(mass_y, stencil(middle, plus, minus)[0] * per_mass)


def spread_rows(table, count, levels):
    wide = jnp.broadcast_to(table[:, None, :], (count, levels, table.shape[1]))
    return wide.reshape(count * levels, table.shape[1])


def own_waves(waves, part, edge_rows):
    table = waves[part]
    rows = table.shape[0]
    if edge_rows:
        return jnp.concatenate([table[:3], table[rows - 3 :]], axis=0)
    return table[3 : rows - 3]


def tend_kernel(edge_rows, count, metric, spin, *refs):
    refs = list(refs)

    def some(n):
        taken = refs[:n]
        del refs[:n]
        return taken

    fields = some(4)
    mass_in, west_in, east_in, waves_in = some(4)
    south, north = some(2) if edge_rows else (None, None)
    band_in, spread_in, own_in, send_in = some(4)
    if edge_rows:
        some(4)
    outs = some(4)
    local, to_east, to_west, to_far = some(4)
    ext, high, low, cross, new, kept_high, kept_low = some(7)
    mass, mass_ext, mass_x, mass_y, west, east, waves = some(7)
    band, spread, own, send, sems = some(5)
    rows, columns = mass.shape
    levels = ext.shape[2]
    items = count * levels
    tiles = columns // LANES

    pairs = [(west_in, west), (east_in, east), (mass_in, mass), (band_in, band)]
    for f in range(4):
        if edge_rows:
            pairs += [
                (fields[f].at[0:6], ext.at[f, 3:9]),
                (fields[f].at[rows - 6 : rows], ext.at[f, 9:15]),
            ]
            for j in range(3):
                part = pl.ds(levels * (3 * f + j), levels)
                pairs += [(south.at[part], ext.at[f, j]), (north.at[part], ext.at[f, 15 + j])]
        else:
            pairs += [(fields[f], ext.at[f])]
    if edge_rows:
        part = pl.ds(12 * levels, 8)
        pairs += [(south.at[part], mass_ext.at[0:8]), (north.at[part], mass_ext.at[8:16])]
    first = start_all(pairs, sems)
    later = start_all(
        [(waves_in, waves), (spread_in, spread), (own_in, own), (send_in, send)], sems, len(pairs)
    )
    wait_all(first)

    mass_slopes(mass, west, east, mass_ext, mass_x, mass_y, levels, edge_rows)
    lane = lax.broadcasted_iota(jnp.int32, (levels, LANES), 1)

    def where(i):
        if edge_rows:
            return i + (rows - 6) * (i // 3), i + 3 + 6 * (i // 3)
        return i + 3, i + 3

    def cut(i, carry):
        row, at = where(i)
        halo = pl.ds(pl.multiple_of((row % 2) * levels, levels), levels)
        for f in range(4):
            lead = 16 * (row // 2) + 3 * f
            before = pltpu.roll(west[halo, :], lax.rem(LANES - lead, LANES), 1)
            for t in range(tiles + 1):
                if t < tiles:
                    tile = pltpu.roll(ext[f, at, :, t * LANES : (t + 1) * LANES], 3, 1)
                else:
                    tile = pltpu.roll(east[halo, :], lax.rem(LANES + 3 - lead, LANES), 1)
                whole = jnp.where(lane < 3, before, tile)
                top = whole.astype(BF16)
                high[f, i, :, t * LANES : (t + 1) * LANES] = top
                low[f, i, :, t * LANES : (t + 1) * LANES] = (whole - top.astype(F32)).astype(BF16)
                before = tile
        return carry

    lax.fori_loop(0, count, cut, 0)

    for t in range(tiles):
        span = slice(t * LANES, (t + 2) * LANES)
        both = jnp.concatenate(
            [high[:, :, :, span].reshape(4 * items, 2 * LANES), low[:, :, :, span].reshape(4 * items, 2 * LANES)],
            axis=1,
        )
        cross[t] = dot(both, band[...]).reshape(4, count, levels, 2 * LANES)

    start_row = lax.axis_index("lat") * rows

    def whole(lines):
        return jnp.concatenate([lines] * (levels // 8), axis=0)

    def tendency(i, t):
        row, at = where(i)
        span = slice(t * LANES, (t + 1) * LANES)
        metric_row = metric[start_row + row]
        spin_row = spin[start_row + row]
        along = metric_row * (1.0 / 60.0)
        u = ext[0, at, :, span]
        v = ext[1, at, :, span]
        theta = ext[2, at, :, span]
        u_fast = u * along
        u_size = jnp.abs(u_fast)
        v_fast = v * (1.0 / 60.0)
        v_size = jnp.abs(v_fast)
        result = [None] * 4
        for f in (3, 0, 1, 2):
            slope_x = cross[t, f, i, :, :LANES]
            smooth_x = cross[t, f, i, :, LANES:]
            slope_y, smooth_y = stencil(
                ext[f, at, :, span],
                [ext[f, at + k, :, span] for k in (1, 2, 3)],
                [ext[f, at - k, :, span] for k in (1, 2, 3)],
            )
            change = (u_size * smooth_x - u_fast * slope_x) + (v_size * smooth_y - v_fast * slope_y)
            if f == 3:
                push_x = along * slope_x + theta * (metric_row * whole(mass_x[row, :, span]))
                push_y = (1.0 / 60.0) * slope_y + theta * whole(mass_y[row, :, span])
            elif f == 0:
                change = change + (spin_row * v - push_x)
            elif f == 1:
                change = change - (spin_row * u + push_y)
            result[f] = change
        return result, at, span

    @pl.when(jnp.logical_not(is_polar()))
    def _():
        def step(i, carry):
            for t in range(tiles):
                change, at, span = tendency(i, t)
                for f in range(4):
                    new[f, i, :, span] = ext[f, at, :, span] + STEP * change[f]
            return carry

        lax.fori_loop(0, count, step, 0)
        pairs = []
        for f in range(4):
            if edge_rows:
                pairs += [
                    (new.at[f, 0:3], outs[f].at[0:3]),
                    (new.at[f, 3:6], outs[f].at[rows - 3 : rows]),
                ]
            else:
                pairs += [(new.at[f], outs[f].at[3 : rows - 3])]
        writes = start_all(pairs, sems)
        wait_all(later)
        wait_all(writes)

    @pl.when(is_polar())
    def _():
        def step(i, carry):
            for t in range(tiles):
                change, _, span = tendency(i, t)
                for f in range(4):
                    top = change[f].astype(BF16)
                    kept_high[f, i, :, span] = top
                    kept_low[f, i, :, span] = (change[f] - top.astype(F32)).astype(BF16)
            return carry

        lax.fori_loop(0, count, step, 0)
        wait_all(later)
        c_all, s_all, d_all = [
            spread_rows(own_waves(waves, part, edge_rows), count, levels) for part in range(3)
        ]
        top = kept_high[...].reshape(4 * items, columns)
        rest = kept_low[...].reshape(4 * items, columns)
        nodal = dot(jnp.concatenate([top, rest, top], axis=1), spread[...])
        turned = []
        for f in range(4):
            part = nodal[f * items : (f + 1) * items]
            turned += [c_all * part, s_all * part]
        turned = split(jnp.concatenate(turned, axis=0))
        moved = dot(turned, own[...])
        sent = dot(turned, send[...])
        for f in range(4):
            at = 2 * f * items
            local[f] = (
                s_all * moved[at : at + items]
                - c_all * moved[at + items : at + 2 * items]
                + d_all * nodal[f * items : (f + 1) * items]
            )
        wide = lax.broadcasted_iota(jnp.int32, (items, LANES), 1)
        for out, first, size in ((to_east, 0, NEAR), (to_west, NEAR, NEAR), (to_far, 2 * NEAR, FAR)):
            total = jnp.zeros((items, LANES), F32)
            for g in range(8):
                part = sent[g * items : (g + 1) * items]
                turn = (size * g - first) % LANES
                if turn:
                    part = pltpu.roll(part, turn, 1)
                total = jnp.where((wide >= size * g) & (wide < size * (g + 1)), part, total)
            if size == NEAR:
                out[...] = total
            else:
                total = total.reshape(count, 2, levels // 2, LANES)
                upper = pltpu.roll(total[:, 1].reshape(items // 2, LANES), 64, 1)
                out[...] = total[:, 0].reshape(items // 2, LANES) + upper


def finish_kernel(edge_rows, count, *refs):
    fields = refs[:4]
    from_west_in, from_east_in, from_far_in, local_in, waves_in, take_in, gather_in = refs[4:11]
    outs = refs[15:19]
    old, new, from_west, from_east, from_far, local, waves, take, gather, sems = refs[19:]
    rows = fields[0].shape[0]
    levels, columns = old.shape[2], old.shape[3]
    items = count * levels

    @pl.when(is_polar())
    def _():
        first = start_all(
            [
                (from_west_in, from_west),
                (from_east_in, from_east),
                (from_far_in, from_far),
                (waves_in, waves),
                (take_in, take),
                (local_in, local),
            ],
            sems,
        )
        reads, pairs = [(gather_in, gather)], []
        for f in range(4):
            if edge_rows:
                parts = [((0, 3), (0, 3)), ((3, 6), (rows - 3, rows))]
            else:
                parts = [((0, count), (3, rows - 3))]
            for (a, b), (c, d) in parts:
                reads.append((fields[f].at[c:d], old.at[f, a:b]))
                pairs.append((new.at[f, a:b], outs[f].at[c:d]))
        reads = start_all(reads, sems, 6)
        wait_all(first)

        place = lax.axis_index("lon")
        last = lax.axis_size("lon") - 1
        near_west = from_west[...] * jnp.where(place == 0, -1.0, 1.0)
        near_east = from_east[...] * jnp.where(place == last, -1.0, 1.0)
        far = from_far[...] * jnp.where(place < 2, -1.0, 1.0)
        far = far.reshape(count, 1, levels // 2, LANES)
        upper = pltpu.roll(far.reshape(items // 2, LANES), 64, 1).reshape(count, 1, levels // 2, LANES)
        far = jnp.concatenate([far, upper], axis=1).reshape(items, LANES)
        wide = lax.broadcasted_iota(jnp.int32, (items, LANES), 1)

        def turn(value, by):
            by = by % LANES
            return pltpu.roll(value, by, 1) if by else value

        come = []
        for g in range(8):
            part = jnp.where(wide < NEAR, turn(near_west, -NEAR * g), turn(near_east, NEAR - NEAR * g))
            part = jnp.where(wide < 2 * NEAR, part, turn(far, 2 * NEAR - FAR * g))
            part = jnp.where(wide < MESSAGE, part, 0.0)
            top = part.astype(BF16).astype(F32)
            come.append((top + turn(part - top, MESSAGE) + turn(top, 2 * MESSAGE)).astype(BF16))
        moved = dot(jnp.concatenate(come, axis=0), take[...])
        c_all, s_all = [
            spread_rows(own_waves(waves, part, edge_rows), count, levels) for part in range(2)
        ]
        value = []
        for f in range(4):
            at = 2 * f * items
            value.append(
                local[f] + (s_all * moved[at : at + items] - c_all * moved[at + items : at + 2 * items])
            )
        value = split(jnp.concatenate(value, axis=0))
        wait_all(reads)
        change = dot(value, gather[...])
        new[...] = old[...] + change.reshape(4, count, levels, columns)
        wait_all(start_all(pairs, sems))


def vmem():
    return pl.BlockSpec(memory_space=pltpu.VMEM)


def smem():
    return pl.BlockSpec(memory_space=pltpu.SMEM)


def anywhere():
    return pl.BlockSpec(memory_space=pl.ANY)


def like(*shape):
    return jax.ShapeDtypeStruct(shape, F32)


def held(value):
    return pltpu.VMEM(value.shape, value.dtype)


def params(mebibytes):
    return pltpu.CompilerParams(vmem_limit_bytes=mebibytes * 1024 * 1024)


def row_factors(count):
    latitude = (np.arange(count).astype(np.float32) + np.float32(0.5)) * np.float32(math.pi / count)
    latitude = latitude - np.float32(math.pi / 2)
    metric = np.float32(1.0) / np.cos(latitude)
    return metric.astype(np.float32), (np.float32(SPIN) * np.sin(latitude)).astype(np.float32)


def shards(u_wind, v_wind, theta, geopot, mass, cutoffs):
    rows, levels, columns = u_wind.shape
    lat_count = lax.axis_size("lat")
    lon_count = lax.axis_size("lon")
    tables = {k: jnp.asarray(v) for k, v in filter_tables(columns, columns * lon_count).items()}
    metric, spin = [jnp.asarray(t) for t in row_factors(rows * lat_count)]
    fields = (u_wind, v_wind, theta, geopot)

    strip = 12 * levels + 8
    edge_lines = 2 * levels + rows
    to_west, to_east = pl.pallas_call(
        pack_lon_kernel,
        out_shape=[like(edge_lines, LANES)] * 2,
        in_specs=[anywhere()] * 5,
        out_specs=[vmem()] * 2,
        scratch_shapes=[
            pltpu.VMEM((2, 4, rows, levels, LANES), F32),
            pltpu.VMEM((rows, columns), F32),
            pltpu.SemaphoreType.DMA((9,)),
        ],
        compiler_params=params(8),
        name="pack_lon",
    )(*fields, mass)
    to_south, to_north, waves = pl.pallas_call(
        pack_lat_kernel,
        out_shape=[like(strip, columns)] * 2 + [like(3, rows, NODES)],
        in_specs=[smem()] + [anywhere()] * 5 + [vmem(), anywhere()],
        out_specs=[anywhere()] * 2 + [vmem()],
        scratch_shapes=[
            pltpu.VMEM((2, strip, columns), F32),
            pltpu.VMEM((rows, columns), F32),
            pltpu.SemaphoreType.DMA((51,)),
        ],
        compiler_params=params(8),
        name="pack_lat",
    )(cutoffs, *fields, mass, tables["nodes"], to_west)

    def ring(value, step):
        return lax.ppermute(value, "lon", [(i, (i + step) % lon_count) for i in range(lon_count)])

    west = ring(to_east, 1)
    east = ring(to_west, -1)
    south = lax.ppermute(to_north, "lat", [(i, i + 1) for i in range(lat_count - 1)])
    north = lax.ppermute(to_south, "lat", [(i + 1, i) for i in range(lat_count - 1)])

    def tendencies(edge_rows, old):
        count = 6 if edge_rows else rows - 6
        items = count * levels
        deep = 18 if edge_rows else rows
        halos = [south, north] if edge_rows else []
        weights = [tables[k] for k in ("band", "spread", "own", "send")]
        args = [metric, spin, *fields, mass, west, east, waves, *halos, *weights]
        return pl.pallas_call(
            functools.partial(tend_kernel, edge_rows, count),
            out_shape=[like(rows, levels, columns)] * 4
            + [like(4, items, NODES)]
            + [like(items, LANES)] * 2
            + [like(items // 2, LANES)],
            in_specs=[smem()] * 2 + [anywhere()] * (len(args) - 2 + len(old)),
            out_specs=[anywhere()] * 4 + [vmem()] * 4,
            scratch_shapes=[
                pltpu.VMEM((4, deep, levels, columns), F32),
                pltpu.VMEM((4, count, levels, columns + LANES), BF16),
                pltpu.VMEM((4, count, levels, columns + LANES), BF16),
                pltpu.VMEM((columns // LANES, 4, count, levels, 2 * LANES), F32),
                pltpu.VMEM((4, count, levels, columns), F32),
                pltpu.VMEM((4, count, levels, columns), BF16),
                pltpu.VMEM((4, count, levels, columns), BF16),
                pltpu.VMEM((rows, columns), F32),
                pltpu.VMEM((16, columns), F32),
                pltpu.VMEM((rows, 8, columns), F32),
                pltpu.VMEM((rows, 8, columns), F32),
                pltpu.VMEM((edge_lines, LANES), F32),
                pltpu.VMEM((edge_lines, LANES), F32),
                pltpu.VMEM((3, rows, NODES), F32),
                *[held(w) for w in weights],
                pltpu.SemaphoreType.DMA((48,)),
            ],
            input_output_aliases={len(args) + f: f for f in range(4)} if old else {},
            compiler_params=params(36),
            cost_estimate=pl.CostEstimate(
                flops=items * 4 * columns * 2000, bytes_accessed=8 * items * columns * 4, transcendentals=0
            ),
            name="tend_edge" if edge_rows else "tend_inner",
        )(*args, *old)

    def exchange(east_part, west_part, far_part):
        return ring(east_part, 1), ring(west_part, -1), ring(far_part, 2)

    def finish(edge_rows, received, local, old):
        count = 6 if edge_rows else rows - 6
        items = count * levels
        weights = [tables[k] for k in ("take", "gather")]
        args = [*fields, *received, local, waves, *weights]
        return pl.pallas_call(
            functools.partial(finish_kernel, edge_rows, count),
            out_shape=[like(rows, levels, columns)] * 4,
            in_specs=[anywhere()] * (len(args) + 4),
            out_specs=[anywhere()] * 4,
            scratch_shapes=[
                pltpu.VMEM((4, count, levels, columns), F32),
                pltpu.VMEM((4, count, levels, columns), F32),
                pltpu.VMEM((items, LANES), F32),
                pltpu.VMEM((items, LANES), F32),
                pltpu.VMEM((items // 2, LANES), F32),
                pltpu.VMEM((4, items, NODES), F32),
                pltpu.VMEM((3, rows, NODES), F32),
                *[held(w) for w in weights],
                pltpu.SemaphoreType.DMA((16,)),
            ],
            input_output_aliases={len(args) + f: f for f in range(4)},
            compiler_params=params(24),
            name="finish_edge" if edge_rows else "finish_inner",
        )(*args, *old)

    *outs, local_inner, a, b, c = tendencies(False, [])
    received_inner = exchange(a, b, c)
    *outs, local_edge, a, b, c = tendencies(True, outs)
    received_edge = exchange(a, b, c)
    outs = finish(False, received_inner, local_inner, outs)
    outs = finish(True, received_edge, local_edge, outs)
    return tuple(outs)


def solution(mesh):
    return jax.shard_map(
        shards,
        mesh=mesh,
        in_specs=(
            P(("members", "lat"), None, "lon"),
            P(("members", "lat"), None, "lon"),
            P(("members", "lat"), None, "lon"),
            P(("members", "lat"), None, "lon"),
            P(("members", "lat"), "lon"),
            P(),
        ),
        out_specs=(
            P(("members", "lat"), None, "lon"),
            P(("members", "lat"), None, "lon"),
            P(("members", "lat"), None, "lon"),
            P(("members", "lat"), None, "lon"),
        ),
        check_vma=False,
    )
```

```python
import functools
import math

import jax
import jax.numpy as jnp
import ml_dtypes
import numpy as np
from jax import lax
from jax.experimental import pallas as pl
from jax.experimental.pallas import tpu as pltpu
from jax.sharding import PartitionSpec as P

STEP = 0.1
SPIN = 0.5
LANES = 128
NEAR = 16
FAR = 8
NODES = 256
F32 = jnp.float32
BF16 = jnp.bfloat16
MESSAGE = 2 * NEAR + FAR


def pivoted(matrix, count):
    rest = np.array(matrix)
    columns = rest.shape[1]
    tilt = 1.0 + 1e-3 * np.arange(columns) / columns
    picked = []
    tri = np.zeros((count, columns))
    for step in range(count):
        size = (rest * rest).sum(axis=0)
        best = int(np.argmax(size * tilt))
        picked.append(best)
        unit = rest[:, best] / math.sqrt(size[best])
        for _ in range(2):
            part = (unit[:, None] * rest).sum(axis=0)
            rest -= unit[:, None] * part[None, :]
            tri[step] += part
        rest[:, best] = 0.0
    left = tri[:, picked].copy()
    right = tri.copy()
    for step in range(count - 1, -1, -1):
        right[step] /= left[step, step]
        right[:step] -= left[:step, step][:, None] * right[step][None, :]
    right[:, picked] = np.eye(count)
    order = np.argsort(picked)
    return np.asarray(picked)[order], right[order]


def cauchy(target, source, circle):
    gap = target[:, None] - source[None, :]
    angle = np.where(gap == 0, 0.5 * math.pi, gap * math.pi / circle)
    return np.where(gap == 0, 0.0, 1.0 / (circle * np.sin(angle)))


def stacked_halves(table):
    table = table.astype(np.float32)
    high = table.astype(ml_dtypes.bfloat16)
    low = (table - high.astype(np.float32)).astype(ml_dtypes.bfloat16)
    return np.concatenate([high, high, low], axis=0)


def band_table():
    band = np.zeros((2 * LANES, 2 * LANES))
    slope = {-3: -1, -2: 9, -1: -45, 1: 45, 2: -9, 3: 1}
    smooth = {-3: 1, -2: -6, -1: 15, 0: -20, 1: 15, 2: -6, 3: 1}
    for j in range(LANES):
        for k, value in slope.items():
            band[j + 3 + k, j] = value
        for k, value in smooth.items():
            band[j + 3 + k, LANES + j] = value
    return np.concatenate([band, band], axis=0).astype(ml_dtypes.bfloat16)


@functools.lru_cache(maxsize=None)
def filter_tables(sector, circle):
    modes = circle // 8
    place = np.arange(sector)
    wave = np.arange(modes)
    phase = (wave[:, None] * place[None, :]) % circle * (2 * math.pi / circle)
    basis = np.concatenate([np.cos(phase), np.sin(phase[1:])], axis=0)
    nodes, spread = pivoted(basis, NODES)
    own = cauchy(nodes, nodes, circle)
    send = np.zeros((NODES, LANES))
    take = np.zeros((MESSAGE, NODES))
    at = 0
    for shift, count in ((sector, NEAR), (-sector, NEAR), (2 * sector, FAR)):
        kernel = cauchy(nodes + shift, nodes, circle)
        pick, weights = pivoted(kernel, count)
        send[:, at : at + count] = weights.T
        take[at : at + count] = kernel[:, pick].T
        at += count
    take = stacked_halves(take)
    take = np.concatenate([take, np.zeros((LANES - 3 * MESSAGE, NODES), take.dtype)], axis=0)
    return dict(
        nodes=nodes.astype(np.float32)[None],
        band=band_table(),
        spread=stacked_halves(spread.T),
        own=stacked_halves(own.T),
        send=stacked_halves(send),
        take=take,
        gather=stacked_halves(STEP * spread),
    )


def split(value):
    high = value.astype(BF16)
    low = (value - high.astype(F32)).astype(BF16)
    return jnp.concatenate([high, low, high], axis=1)


def dot(a, b):
    return lax.dot_general(a, b, (((1,), (0,)), ((), ())), preferred_element_type=F32)


def start_all(pairs, sems, first=0):
    copies = [pltpu.make_async_copy(a, b, sems.at[first + n]) for n, (a, b) in enumerate(pairs)]
    for c in copies:
        c.start()
    return copies


def wait_all(copies):
    for c in copies:
        c.wait()


def is_polar():
    owner = lax.axis_index("lat")
    quarter = lax.axis_size("lat") // 4
    return (owner < quarter) | (owner >= lax.axis_size("lat") - quarter)


def pack_lon_kernel(cutoffs, *refs):
    fields = refs[:4]
    mass, nodes, _, west, east, waves, edge, own_mass, sems = refs[4:]
    rows, columns = mass.shape
    levels = edge.shape[3]
    copies = start_all(
        [(mass, own_mass)]
        + [(q.at[:, :, 0:LANES], edge.at[0, f]) for f, q in enumerate(fields)]
        + [(q.at[:, :, columns - LANES : columns], edge.at[1, f]) for f, q in enumerate(fields)],
        sems,
    )

    lat_count = lax.axis_size("lat")
    lon_count = lax.axis_size("lon")
    owner = lax.axis_index("lat")
    circle = columns * lon_count
    start = jnp.where(owner < lat_count // 4, owner * rows, owner * rows - lat_count * rows // 2)
    start = jnp.clip(start, 0, lat_count * rows // 2 - rows)
    line = lax.broadcasted_iota(jnp.int32, (rows, NODES), 0)
    twice = jnp.zeros((rows, NODES), F32)
    for r in range(rows):
        twice = jnp.where(line == r, (2 * cutoffs[start + r] + 1).astype(F32), twice)
    place = nodes[...] + (lax.axis_index("lon") * columns).astype(F32)
    turns = twice * place
    angle = (turns - 2.0 * circle * jnp.floor(turns * (0.5 / circle))) * (math.pi / circle)
    waves[0] = jnp.cos(angle)
    waves[1] = jnp.sin(angle)
    waves[2] = twice * (1.0 / circle)

    wait_all(copies)
    lane = lax.broadcasted_iota(jnp.int32, (levels, LANES), 1)
    west[2 * levels :] = own_mass[:, 0:LANES]
    east[2 * levels :] = pltpu.roll(own_mass[:, columns - LANES : columns], 3, 1)
    for parity in range(2):
        for side, out in ((0, west), (1, east)):
            total = jnp.zeros((levels, LANES), F32)
            for r in range(parity, rows, 2):
                for f in range(4):
                    lead = 16 * (r // 2) + 3 * f
                    turn = lead if side == 0 else (lead + 3) % LANES
                    tile = edge[side, f, r]
                    if turn:
                        tile = pltpu.roll(tile, turn, 1)
                    total = jnp.where((lane >= lead) & (lane < lead + 3), tile, total)
            out[parity * levels : (parity + 1) * levels] = total


def pack_lat_kernel(*refs):
    fields = refs[:4]
    mass, south, north, own_mass, sems = refs[4:]
    rows, columns = mass.shape
    levels = fields[0].shape[1]
    tail = 12 * levels
    mass_copy = start_all([(mass, own_mass)], sems)
    pairs = []
    for f, q in enumerate(fields):
        for strip, first in ((south, 0), (north, rows - 3)):
            for j in range(3):
                pairs.append((q.at[first + j], strip.at[pl.ds(levels * (3 * f + j), levels)]))
    copies = start_all(pairs, sems, 1)
    wait_all(mass_copy)
    for strip, first in ((south, 0), (north, rows - 3)):
        strip[tail : tail + 3] = own_mass[first : first + 3]
        strip[tail + 3 : tail + 8] = jnp.zeros((5, columns), F32)
    wait_all(copies)


def stencil(center, plus, minus):
    p1, p2, p3 = plus
    m1, m2, m3 = minus
    slope = 45.0 * (p1 - m1) - 9.0 * (p2 - m2) + (p3 - m3)
    smooth = (p3 + m3) - 6.0 * (p2 + m2) + 15.0 * (p1 + m1) - 20.0 * center
    return slope, smooth


def mass_slopes(mass, west, east, south, north, mass_x, mass_y, levels):
    rows, columns = mass.shape
    middle = mass[...]
    per_mass = 1.0 / (60.0 * middle)
    wide = jnp.concatenate(
        [pltpu.roll(west[2 * levels :], LANES - 3, 1), middle, east[2 * levels :]], axis=1
    )
    whole = columns + 2 * LANES

    def at(k):
        return pltpu.roll(wide, (-k) % whole, 1)[:, LANES : LANES + columns]

    def store(out, value):
        out[...] = jnp.broadcast_to(value[:, None, :], out.shape)

    store(mass_x, stencil(middle, [at(1), at(2), at(3)], [at(-1), at(-2), at(-3)])[0] * per_mass)
    tall = jnp.concatenate([south, middle, north], axis=0)
    plus = [tall[3 + k : 3 + k + rows] for k in (1, 2, 3)]
    minus = [tall[3 - k : 3 - k + rows] for k in (1, 2, 3)]
    store(mass_y, stencil(middle, plus, minus)[0] * per_mass)


def spread_rows(table, count, levels):
    wide = jnp.broadcast_to(table[:, None, :], (count, levels, table.shape[1]))
    return wide.reshape(count * levels, table.shape[1])


def own_waves(waves, part, edge_rows):
    table = waves[part]
    rows = table.shape[0]
    if edge_rows:
        return jnp.concatenate([table[:3], table[rows - 3 :]], axis=0)
    return table[3 : rows - 3]


def tend_kernel(edge_rows, count, metric, spin, *refs):
    refs = list(refs)

    def some(n):
        taken = refs[:n]
        del refs[:n]
        return taken

    fields = some(4)
    mass, west, east, waves = some(4)
    south, north = some(2) if edge_rows else (None, None)
    band, spread, own, send = some(4)
    if edge_rows:
        some(4)
    outs = some(4)
    local, to_east, to_west, to_far = some(4)
    high, low, cross, new, kept_high, kept_low, mass_x, mass_y, sems = some(9)
    rows, columns = mass.shape
    levels = fields[0].shape[1]
    items = count * levels
    tiles = columns // LANES

    tail = 12 * levels
    if edge_rows:
        mass_slopes(mass, west, east, south[tail : tail + 3], north[tail : tail + 3], mass_x, mass_y, levels)
    else:
        blank = jnp.zeros((3, columns), F32)
        mass_slopes(mass, west, east, blank, blank, mass_x, mass_y, levels)
    lane = lax.broadcasted_iota(jnp.int32, (levels, LANES), 1)

    def cut(i, carry):
        row = i + (rows - 6) * (i // 3) if edge_rows else i + 3
        halo = pl.ds(pl.multiple_of((row % 2) * levels, levels), levels)
        for f in range(4):
            lead = 16 * (row // 2) + 3 * f
            before = pltpu.roll(west[halo, :], lax.rem(LANES - lead, LANES), 1)
            for t in range(tiles + 1):
                if t < tiles:
                    tile = pltpu.roll(fields[f][row, :, t * LANES : (t + 1) * LANES], 3, 1)
                else:
                    tile = pltpu.roll(east[halo, :], lax.rem(LANES + 3 - lead, LANES), 1)
                whole = jnp.where(lane < 3, before, tile)
                top = whole.astype(BF16)
                high[f, i, :, t * LANES : (t + 1) * LANES] = top
                low[f, i, :, t * LANES : (t + 1) * LANES] = (whole - top.astype(F32)).astype(BF16)
                before = tile
        return carry

    lax.fori_loop(0, count, cut, 0)

    for t in range(tiles):
        span = slice(t * LANES, (t + 2) * LANES)
        both = jnp.concatenate(
            [high[:, :, :, span].reshape(4 * items, 2 * LANES), low[:, :, :, span].reshape(4 * items, 2 * LANES)],
            axis=1,
        )
        cross[t] = dot(both, band[...]).reshape(4, count, levels, 2 * LANES)

    start_row = lax.axis_index("lat") * rows

    def whole(lines):
        return jnp.concatenate([lines] * (levels // 8), axis=0)

    def tendency(t, first, first_row, size, row_of, emit):
        span = slice(t * LANES, (t + 1) * LANES)
        metrics = [metric[start_row + first_row + j] for j in range(size)]
        spins = [spin[start_row + first_row + j] for j in range(size)]
        centers = [[row_of(f, j, span) for j in range(size)] for f in range(3)]
        fast, fast_size, up, up_size = [], [], [], []
        for j in range(size):
            fast.append(centers[0][j] * (metrics[j] * (1.0 / 60.0)))
            fast_size.append(jnp.abs(fast[j]))
            up.append(centers[1][j] * (1.0 / 60.0))
            up_size.append(jnp.abs(up[j]))
        push_x, push_y = [None] * size, [None] * size
        for f in (3, 0, 1, 2):
            column = [row_of(f, j, span) for j in range(-3, size + 3)]
            for j in range(size):
                q = column[j + 3]
                slope_x = cross[t, f, first + j, :, :LANES]
                smooth_x = cross[t, f, first + j, :, LANES:]
                slope_y, smooth_y = stencil(q, column[j + 4 : j + 7], column[j + 2 :: -1][:3])
                change = (fast_size[j] * smooth_x - fast[j] * slope_x) + (
                    up_size[j] * smooth_y - up[j] * slope_y
                )
                if f == 3:
                    theta = centers[2][j]
                    over_x = whole(mass_x[first_row + j, :, span])
                    over_y = whole(mass_y[first_row + j, :, span])
                    push_x[j] = metrics[j] * ((1.0 / 60.0) * slope_x + theta * over_x)
                    push_y[j] = (1.0 / 60.0) * slope_y + theta * over_y
                elif f == 0:
                    change = change + (spins[j] * centers[1][j] - push_x[j])
                elif f == 1:
                    change = change - (spins[j] * centers[0][j] + push_y[j])
                emit(f, first + j, span, q, change)

    def all_rows(emit):
        if edge_rows:
            for side in range(2):
                first_row = (rows - 3) * side

                def row_of(f, j, span):
                    row = first_row + j
                    if row < 0:
                        return south[levels * (3 * f + row + 3) : levels * (3 * f + row + 4), span]
                    if row >= rows:
                        return north[levels * (3 * f + row - rows) : levels * (3 * f + row - rows + 1), span]
                    return fields[f][row, :, span]

                for t in range(tiles):
                    tendency(t, 3 * side, first_row, 3, row_of, emit)
        else:

            def step(n, carry):
                first_row = 3 + 2 * n

                def row_of(f, j, span):
                    return fields[f][first_row + j, :, span]

                for t in range(tiles):
                    tendency(t, 2 * n, first_row, 2, row_of, emit)
                return carry

            lax.fori_loop(0, count // 2, step, 0)

    @pl.when(jnp.logical_not(is_polar()))
    def _():
        def emit(f, i, span, q, change):
            new[f, i, :, span] = q + STEP * change

        all_rows(emit)
        pairs = []
        for f in range(4):
            if edge_rows:
                pairs += [
                    (new.at[f, 0:3], outs[f].at[0:3]),
                    (new.at[f, 3:6], outs[f].at[rows - 3 : rows]),
                ]
            else:
                pairs += [(new.at[f], outs[f].at[3 : rows - 3])]
        wait_all(start_all(pairs, sems))

    @pl.when(is_polar())
    def _():
        def emit(f, i, span, q, change):
            top = change.astype(BF16)
            kept_high[f, i, :, span] = top
            kept_low[f, i, :, span] = (change - top.astype(F32)).astype(BF16)

        all_rows(emit)
        c_all, s_all, d_all = [
            spread_rows(own_waves(waves, part, edge_rows), count, levels) for part in range(3)
        ]
        top = kept_high[...].reshape(4 * items, columns)
        rest = kept_low[...].reshape(4 * items, columns)
        nodal = dot(jnp.concatenate([top, rest, top], axis=1), spread[...])
        turned = []
        for f in range(4):
            part = nodal[f * items : (f + 1) * items]
            turned += [c_all * part, s_all * part]
        turned = split(jnp.concatenate(turned, axis=0))
        moved = dot(turned, own[...])
        sent = dot(turned, send[...])
        for f in range(4):
            at = 2 * f * items
            local[f] = (
                s_all * moved[at : at + items]
                - c_all * moved[at + items : at + 2 * items]
                + d_all * nodal[f * items : (f + 1) * items]
            )
        wide = lax.broadcasted_iota(jnp.int32, (items, LANES), 1)
        for out, first, size in ((to_east, 0, NEAR), (to_west, NEAR, NEAR), (to_far, 2 * NEAR, FAR)):
            total = jnp.zeros((items, LANES), F32)
            for g in range(8):
                part = sent[g * items : (g + 1) * items]
                turn = (size * g - first) % LANES
                if turn:
                    part = pltpu.roll(part, turn, 1)
                total = jnp.where((wide >= size * g) & (wide < size * (g + 1)), part, total)
            if size == NEAR:
                out[...] = total
            else:
                total = total.reshape(count, 2, levels // 2, LANES)
                upper = pltpu.roll(total[:, 1].reshape(items // 2, LANES), 64, 1)
                out[...] = total[:, 0].reshape(items // 2, LANES) + upper


def finish_kernel(edge_rows, count, *refs):
    fields = refs[:4]
    from_west, from_east, from_far, local, waves, take, gather = refs[4:11]
    outs = refs[15:19]
    new, sems = refs[19:]
    rows = fields[0].shape[0]
    levels, columns = new.shape[2], new.shape[3]
    items = count * levels

    @pl.when(is_polar())
    def _():
        place = lax.axis_index("lon")
        last = lax.axis_size("lon") - 1
        near_west = from_west[...] * jnp.where(place == 0, -1.0, 1.0)
        near_east = from_east[...] * jnp.where(place == last, -1.0, 1.0)
        far = from_far[...] * jnp.where(place < 2, -1.0, 1.0)
        far = far.reshape(count, 1, levels // 2, LANES)
        upper = pltpu.roll(far.reshape(items // 2, LANES), 64, 1).reshape(count, 1, levels // 2, LANES)
        far = jnp.concatenate([far, upper], axis=1).reshape(items, LANES)
        wide = lax.broadcasted_iota(jnp.int32, (items, LANES), 1)

        def turn(value, by):
            by = by % LANES
            return pltpu.roll(value, by, 1) if by else value

        come = []
        for g in range(8):
            part = jnp.where(wide < NEAR, turn(near_west, -NEAR * g), turn(near_east, NEAR - NEAR * g))
            part = jnp.where(wide < 2 * NEAR, part, turn(far, 2 * NEAR - FAR * g))
            part = jnp.where(wide < MESSAGE, part, 0.0)
            top = part.astype(BF16).astype(F32)
            come.append((top + turn(part - top, MESSAGE) + turn(top, 2 * MESSAGE)).astype(BF16))
        moved = dot(jnp.concatenate(come, axis=0), take[...])
        c_all, s_all = [
            spread_rows(own_waves(waves, part, edge_rows), count, levels) for part in range(2)
        ]
        writes = []
        for half in range(2):
            value = []
            for f in (2 * half, 2 * half + 1):
                at = 2 * f * items
                value.append(
                    local[f] + (s_all * moved[at : at + items] - c_all * moved[at + items : at + 2 * items])
                )
            change = dot(split(jnp.concatenate(value, axis=0)), gather[...])
            change = change.reshape(2, count, levels, columns)
            pairs = []
            for f in (2 * half, 2 * half + 1):
                if edge_rows:
                    new[f, 0:3] = fields[f][0:3] + change[f % 2, 0:3]
                    new[f, 3:6] = fields[f][rows - 3 : rows] + change[f % 2, 3:6]
                    pairs += [
                        (new.at[f, 0:3], outs[f].at[0:3]),
                        (new.at[f, 3:6], outs[f].at[rows - 3 : rows]),
                    ]
                else:
                    new[f] = fields[f][3 : rows - 3] + change[f % 2]
                    pairs += [(new.at[f], outs[f].at[3 : rows - 3])]
            writes += start_all(pairs, sems, 4 * half)
        wait_all(writes)


def vmem():
    return pl.BlockSpec(memory_space=pltpu.VMEM)


def smem():
    return pl.BlockSpec(memory_space=pltpu.SMEM)


def anywhere():
    return pl.BlockSpec(memory_space=pl.ANY)


def like(*shape):
    return jax.ShapeDtypeStruct(shape, F32)


def params(mebibytes):
    return pltpu.CompilerParams(vmem_limit_bytes=mebibytes * 1024 * 1024)


def row_factors(count):
    latitude = (np.arange(count).astype(np.float32) + np.float32(0.5)) * np.float32(math.pi / count)
    latitude = latitude - np.float32(math.pi / 2)
    metric = np.float32(1.0) / np.cos(latitude)
    return metric.astype(np.float32), (np.float32(SPIN) * np.sin(latitude)).astype(np.float32)


def shards(u_wind, v_wind, theta, geopot, mass, cutoffs):
    rows, levels, columns = u_wind.shape
    lat_count = lax.axis_size("lat")
    lon_count = lax.axis_size("lon")
    tables = {k: jnp.asarray(v) for k, v in filter_tables(columns, columns * lon_count).items()}
    metric, spin = [jnp.asarray(t) for t in row_factors(rows * lat_count)]
    fields = (u_wind, v_wind, theta, geopot)

    strip = 12 * levels + 8
    edge_lines = 2 * levels + rows
    far_fields = [pltpu.with_memory_space_constraint(q, pltpu.HBM) for q in (*fields, mass)]
    to_south, to_north = pl.pallas_call(
        pack_lat_kernel,
        out_shape=[like(strip, columns)] * 2,
        in_specs=[anywhere()] * 5,
        out_specs=[vmem()] * 2,
        scratch_shapes=[pltpu.VMEM((rows, columns), F32), pltpu.SemaphoreType.DMA((25,))],
        compiler_params=params(8),
        name="pack_lat",
    )(*far_fields)
    to_west, to_east, waves = pl.pallas_call(
        pack_lon_kernel,
        out_shape=[like(edge_lines, LANES)] * 2 + [like(3, rows, NODES)],
        in_specs=[smem()] + [anywhere()] * 5 + [vmem(), anywhere()],
        out_specs=[vmem()] * 3,
        scratch_shapes=[
            pltpu.VMEM((2, 4, rows, levels, LANES), F32),
            pltpu.VMEM((rows, columns), F32),
            pltpu.SemaphoreType.DMA((9,)),
        ],
        compiler_params=params(8),
        name="pack_lon",
    )(cutoffs, *far_fields, tables["nodes"], to_south)

    def ring(value, step):
        return lax.ppermute(value, "lon", [(i, (i + step) % lon_count) for i in range(lon_count)])

    west = ring(to_east, 1)
    east = ring(to_west, -1)
    south = lax.ppermute(to_north, "lat", [(i, i + 1) for i in range(lat_count - 1)])
    north = lax.ppermute(to_south, "lat", [(i + 1, i) for i in range(lat_count - 1)])

    def tendencies(edge_rows, old):
        count = 6 if edge_rows else rows - 6
        items = count * levels
        halos = [south, north] if edge_rows else []
        weights = [tables[k] for k in ("band", "spread", "own", "send")]
        args = [metric, spin, *fields, mass, west, east, waves, *halos, *weights]
        return pl.pallas_call(
            functools.partial(tend_kernel, edge_rows, count),
            out_shape=[like(rows, levels, columns)] * 4
            + [like(4, items, NODES)]
            + [like(items, LANES)] * 2
            + [like(items // 2, LANES)],
            in_specs=[smem()] * 2 + [vmem()] * (len(args) - 2) + [anywhere()] * len(old),
            out_specs=[anywhere()] * 4 + [vmem()] * 4,
            scratch_shapes=[
                pltpu.VMEM((4, count, levels, columns + LANES), BF16),
                pltpu.VMEM((4, count, levels, columns + LANES), BF16),
                pltpu.VMEM((columns // LANES, 4, count, levels, 2 * LANES), F32),
                pltpu.VMEM((4, count, levels, columns), F32),
                pltpu.VMEM((4, count, levels, columns), BF16),
                pltpu.VMEM((4, count, levels, columns), BF16),
                pltpu.VMEM((rows, 8, columns), F32),
                pltpu.VMEM((rows, 8, columns), F32),
                pltpu.SemaphoreType.DMA((8,)),
            ],
            input_output_aliases={len(args) + f: f for f in range(4)} if old else {},
            compiler_params=params(36),
            cost_estimate=pl.CostEstimate(
                flops=items * 4 * columns * 2000, bytes_accessed=8 * items * columns * 4, transcendentals=0
            ),
            name="tend_edge" if edge_rows else "tend_inner",
        )(*args, *old)

    def exchange(east_part, west_part, far_part):
        return ring(east_part, 1), ring(west_part, -1), ring(far_part, 2)

    def finish(edge_rows, received, local, old):
        count = 6 if edge_rows else rows - 6
        items = count * levels
        weights = [tables[k] for k in ("take", "gather")]
        args = [*fields, *received, local, waves, *weights]
        return pl.pallas_call(
            functools.partial(finish_kernel, edge_rows, count),
            out_shape=[like(rows, levels, columns)] * 4,
            in_specs=[vmem()] * len(args) + [anywhere()] * 4,
            out_specs=[anywhere()] * 4,
            scratch_shapes=[
                pltpu.VMEM((4, count, levels, columns), F32),
                pltpu.SemaphoreType.DMA((8,)),
            ],
            input_output_aliases={len(args) + f: f for f in range(4)},
            compiler_params=params(24),
            name="finish_edge" if edge_rows else "finish_inner",
        )(*args, *old)

    *outs, local_inner, a, b, c = tendencies(False, [])
    received_inner = exchange(a, b, c)
    *outs, local_edge, a, b, c = tendencies(True, outs)
    received_edge = exchange(a, b, c)
    outs = finish(False, received_inner, local_inner, outs)
    outs = finish(True, received_edge, local_edge, outs)
    return tuple(outs)


def solution(mesh):
    return jax.shard_map(
        shards,
        mesh=mesh,
        in_specs=(
            P(("members", "lat"), None, "lon"),
            P(("members", "lat"), None, "lon"),
            P(("members", "lat"), None, "lon"),
            P(("members", "lat"), None, "lon"),
            P(("members", "lat"), "lon"),
            P(),
        ),
        out_specs=(
            P(("members", "lat"), None, "lon"),
            P(("members", "lat"), None, "lon"),
            P(("members", "lat"), None, "lon"),
            P(("members", "lat"), None, "lon"),
        ),
        check_vma=False,
    )
```

```python
import functools
import math

import jax
import jax.numpy as jnp
import ml_dtypes
import numpy as np
from jax import lax
from jax.experimental import pallas as pl
from jax.experimental.pallas import tpu as pltpu
from jax.sharding import PartitionSpec as P

STEP = 0.1
SPIN = 0.5
LANES = 128
NEAR = 16
FAR = 8
NODES = 256
F32 = jnp.float32
BF16 = jnp.bfloat16
MESSAGE = 2 * NEAR + FAR


def pivoted(matrix, count):
    rest = np.array(matrix)
    columns = rest.shape[1]
    tilt = 1.0 + 1e-3 * np.arange(columns) / columns
    picked = []
    tri = np.zeros((count, columns))
    for step in range(count):
        size = (rest * rest).sum(axis=0)
        best = int(np.argmax(size * tilt))
        picked.append(best)
        unit = rest[:, best] / math.sqrt(size[best])
        for _ in range(2):
            part = (unit[:, None] * rest).sum(axis=0)
            rest -= unit[:, None] * part[None, :]
            tri[step] += part
        rest[:, best] = 0.0
    left = tri[:, picked].copy()
    right = tri.copy()
    for step in range(count - 1, -1, -1):
        right[step] /= left[step, step]
        right[:step] -= left[:step, step][:, None] * right[step][None, :]
    right[:, picked] = np.eye(count)
    order = np.argsort(picked)
    return np.asarray(picked)[order], right[order]


def cauchy(target, source, circle):
    gap = target[:, None] - source[None, :]
    angle = np.where(gap == 0, 0.5 * math.pi, gap * math.pi / circle)
    return np.where(gap == 0, 0.0, 1.0 / (circle * np.sin(angle)))


def stacked_halves(table):
    table = table.astype(np.float32)
    high = table.astype(ml_dtypes.bfloat16)
    low = (table - high.astype(np.float32)).astype(ml_dtypes.bfloat16)
    return np.concatenate([high, high, low], axis=0)


def band_table():
    band = np.zeros((2 * LANES, 2 * LANES))
    slope = {-3: -1, -2: 9, -1: -45, 1: 45, 2: -9, 3: 1}
    smooth = {-3: 1, -2: -6, -1: 15, 0: -20, 1: 15, 2: -6, 3: 1}
    for j in range(LANES):
        for k, value in slope.items():
            band[j + 3 + k, j] = value
        for k, value in smooth.items():
            band[j + 3 + k, LANES + j] = value
    return np.concatenate([band, band], axis=0).astype(ml_dtypes.bfloat16)


@functools.lru_cache(maxsize=None)
def filter_tables(sector, circle):
    modes = circle // 8
    place = np.arange(sector)
    wave = np.arange(modes)
    phase = (wave[:, None] * place[None, :]) % circle * (2 * math.pi / circle)
    basis = np.concatenate([np.cos(phase), np.sin(phase[1:])], axis=0)
    nodes, spread = pivoted(basis, NODES)
    own = cauchy(nodes, nodes, circle)
    send = np.zeros((NODES, LANES))
    take = np.zeros((MESSAGE, NODES))
    at = 0
    for shift, count in ((sector, NEAR), (-sector, NEAR), (2 * sector, FAR)):
        kernel = cauchy(nodes + shift, nodes, circle)
        pick, weights = pivoted(kernel, count)
        send[:, at : at + count] = weights.T
        take[at : at + count] = kernel[:, pick].T
        at += count
    take = stacked_halves(take)
    take = np.concatenate([take, np.zeros((LANES - 3 * MESSAGE, NODES), take.dtype)], axis=0)
    return dict(
        nodes=nodes.astype(np.float32)[None],
        band=band_table(),
        spread=stacked_halves(spread.T),
        own=stacked_halves(own.T),
        send=stacked_halves(send),
        take=take,
        gather=stacked_halves(STEP * spread),
    )


def split(value):
    high = value.astype(BF16)
    low = (value - high.astype(F32)).astype(BF16)
    return jnp.concatenate([high, low, high], axis=1)


def dot(a, b):
    return lax.dot_general(a, b, (((1,), (0,)), ((), ())), preferred_element_type=F32)


def start_all(pairs, sems, first=0):
    copies = [pltpu.make_async_copy(a, b, sems.at[first + n]) for n, (a, b) in enumerate(pairs)]
    for c in copies:
        c.start()
    return copies


def wait_all(copies):
    for c in copies:
        c.wait()


def is_polar():
    owner = lax.axis_index("lat")
    quarter = lax.axis_size("lat") // 4
    return (owner < quarter) | (owner >= lax.axis_size("lat") - quarter)


def edge_row(entry, rows):
    north = (lax.axis_index("lat") % 2 == 0) == (entry < 3)
    return jnp.where(north, rows - 1 - entry % 3, entry % 3)


def by_parity(even, odd):
    return jnp.where(lax.axis_index("lat") % 2 == 0, even, odd)


def pack_kernel(cutoffs, *refs):
    fields = refs[:4]
    mass, nodes, strip_a, strip_b, west, east, waves, edge, own_mass, sems = refs[4:]
    rows, columns = mass.shape
    levels = edge.shape[3]
    tail = 12 * levels
    small = start_all(
        [(mass, own_mass)]
        + [(q.at[:, :, 0:LANES], edge.at[0, f]) for f, q in enumerate(fields)]
        + [(q.at[:, :, columns - LANES : columns], edge.at[1, f]) for f, q in enumerate(fields)],
        sems,
    )
    pairs = []
    for entry in range(6):
        strip = strip_a if entry < 3 else strip_b
        row = edge_row(entry, rows)
        for f, q in enumerate(fields):
            pairs.append((q.at[row], strip.at[pl.ds(levels * (3 * f + entry % 3), levels)]))
    large = start_all(pairs, sems, 9)

    lat_count = lax.axis_size("lat")
    lon_count = lax.axis_size("lon")
    owner = lax.axis_index("lat")
    circle = columns * lon_count
    start = jnp.where(owner < lat_count // 4, owner * rows, owner * rows - lat_count * rows // 2)
    start = jnp.clip(start, 0, lat_count * rows // 2 - rows)
    line = lax.broadcasted_iota(jnp.int32, (rows, NODES), 0)
    twice = jnp.zeros((rows, NODES), F32)
    for r in range(rows):
        twice = jnp.where(line == r, (2 * cutoffs[start + r] + 1).astype(F32), twice)
    place = nodes[...] + (lax.axis_index("lon") * columns).astype(F32)
    turns = twice * place
    angle = (turns - 2.0 * circle * jnp.floor(turns * (0.5 / circle))) * (math.pi / circle)
    for part, table in enumerate((jnp.cos(angle), jnp.sin(angle), twice * (1.0 / circle))):
        waves[part] = jnp.broadcast_to(table[:, None, :], (rows, 8, NODES))

    wait_all(small)
    north = jnp.concatenate([own_mass[rows - 1 - m : rows - m] for m in range(3)], axis=0)
    south = own_mass[0:3]
    for strip, lines in ((strip_a, by_parity(north, south)), (strip_b, by_parity(south, north))):
        strip[tail : tail + 3] = lines
        strip[tail + 3 : tail + 8] = jnp.zeros((5, columns), F32)
    lane = lax.broadcasted_iota(jnp.int32, (levels, LANES), 1)
    west[2 * levels :] = own_mass[:, 0:LANES]
    east[2 * levels :] = pltpu.roll(own_mass[:, columns - LANES : columns], 3, 1)
    for parity in range(2):
        for side, out in ((0, west), (1, east)):
            total = jnp.zeros((levels, LANES), F32)
            for r in range(parity, rows, 2):
                for f in range(4):
                    lead = 16 * (r // 2) + 3 * f
                    turn = lead if side == 0 else (lead + 3) % LANES
                    tile = edge[side, f, r]
                    if turn:
                        tile = pltpu.roll(tile, turn, 1)
                    total = jnp.where((lane >= lead) & (lane < lead + 3), tile, total)
            out[parity * levels : (parity + 1) * levels] = total
    wait_all(large)


def stencil(center, plus, minus):
    p1, p2, p3 = plus
    m1, m2, m3 = minus
    slope = 45.0 * (p1 - m1) - 9.0 * (p2 - m2) + (p3 - m3)
    smooth = (p3 + m3) - 6.0 * (p2 + m2) + 15.0 * (p1 + m1) - 20.0 * center
    return slope, smooth


def mass_slopes(mass, west, east, south, north, mass_x, mass_y, levels):
    rows, columns = mass.shape
    middle = mass[...]
    per_mass = 1.0 / (60.0 * middle)
    wide = jnp.concatenate(
        [pltpu.roll(west[2 * levels :], LANES - 3, 1), middle, east[2 * levels :]], axis=1
    )
    whole = columns + 2 * LANES

    def at(k):
        return pltpu.roll(wide, (-k) % whole, 1)[:, LANES : LANES + columns]

    def store(out, value):
        out[...] = jnp.broadcast_to(value[:, None, :], out.shape)

    store(mass_x, stencil(middle, [at(1), at(2), at(3)], [at(-1), at(-2), at(-3)])[0] * per_mass)
    tall = jnp.concatenate([south, middle, north], axis=0)
    plus = [tall[3 + k : 3 + k + rows] for k in (1, 2, 3)]
    minus = [tall[3 - k : 3 - k + rows] for k in (1, 2, 3)]
    store(mass_y, stencil(middle, plus, minus)[0] * per_mass)


def spread_waves(waves, part, edge_rows, levels):
    rows = waves.shape[1]
    if edge_rows:
        numbers = [edge_row(entry, rows) for entry in range(6)]
    else:
        numbers = range(3, rows - 3)
    return jnp.concatenate([waves[part, n] for n in numbers for _ in range(levels // 8)], axis=0)


def tend_kernel(edge_rows, count, metric, spin, *refs):
    refs = list(refs)

    def some(n):
        taken = refs[:n]
        del refs[:n]
        return taken

    fields = some(4)
    mass, west, east, waves = some(4)
    strips = some(2) if edge_rows else None
    band, spread, own, send = some(4)
    if edge_rows:
        some(4)
    outs = some(4)
    local, to_east, to_west, to_far = some(4)
    high, low, cross, new, kept_high, kept_low, mass_x, mass_y, sems = some(9)
    rows, columns = mass.shape
    levels = fields[0].shape[1]
    items = count * levels
    tiles = columns // LANES

    if edge_rows:
        tail = 12 * levels
        lines = [strip[tail : tail + 3] for strip in strips]
        upper = by_parity(lines[0], lines[1])
        lower = by_parity(lines[1], lines[0])
        lower = jnp.concatenate([lower[2:3], lower[1:2], lower[0:1]], axis=0)
    else:
        lower = upper = jnp.zeros((3, columns), F32)
    mass_slopes(mass, west, east, lower, upper, mass_x, mass_y, levels)
    lane = lax.broadcasted_iota(jnp.int32, (levels, LANES), 1)

    def cut(i, carry):
        row = edge_row(i, rows) if edge_rows else i + 3
        halo = pl.ds(pl.multiple_of((row % 2) * levels, levels), levels)
        for f in range(4):
            lead = 16 * (row // 2) + 3 * f
            before = pltpu.roll(west[halo, :], lax.rem(LANES - lead, LANES), 1)
            for t in range(tiles + 1):
                if t < tiles:
                    tile = pltpu.roll(fields[f][row, :, t * LANES : (t + 1) * LANES], 3, 1)
                else:
                    tile = pltpu.roll(east[halo, :], lax.rem(LANES + 3 - lead, LANES), 1)
                whole = jnp.where(lane < 3, before, tile)
                top = whole.astype(BF16)
                high[f, i, :, t * LANES : (t + 1) * LANES] = top
                low[f, i, :, t * LANES : (t + 1) * LANES] = (whole - top.astype(F32)).astype(BF16)
                before = tile
        return carry

    lax.fori_loop(0, count, cut, 0)

    for t in range(tiles):
        span = slice(t * LANES, (t + 2) * LANES)
        both = jnp.concatenate(
            [high[:, :, :, span].reshape(4 * items, 2 * LANES), low[:, :, :, span].reshape(4 * items, 2 * LANES)],
            axis=1,
        )
        cross[t] = dot(both, band[...]).reshape(4, count, levels, 2 * LANES)

    start_row = lax.axis_index("lat") * rows

    def whole(lines):
        return jnp.concatenate([lines] * (levels // 8), axis=0)

    def tendency(t, first, numbers, row_of, emit, inward=1.0):
        size = len(numbers)
        span = slice(t * LANES, (t + 1) * LANES)
        metrics = [metric[start_row + n] for n in numbers]
        spins = [spin[start_row + n] for n in numbers]
        centers = [[row_of(f, j, span) for j in range(size)] for f in range(3)]
        per_row = inward * (1.0 / 60.0)
        fast, fast_size, up, up_size = [], [], [], []
        for j in range(size):
            fast.append(centers[0][j] * (metrics[j] * (1.0 / 60.0)))
            fast_size.append(jnp.abs(fast[j]))
            up.append(centers[1][j] * per_row)
            up_size.append(jnp.abs(up[j]))
        push_x, push_y = [None] * size, [None] * size
        for f in (3, 0, 1, 2):
            column = [row_of(f, j, span) for j in range(-3, size + 3)]
            for j in range(size):
                q = column[j + 3]
                slope_x = cross[t, f, first + j, :, :LANES]
                smooth_x = cross[t, f, first + j, :, LANES:]
                slope_y, smooth_y = stencil(q, column[j + 4 : j + 7], column[j + 2 :: -1][:3])
                change = (fast_size[j] * smooth_x - fast[j] * slope_x) + (
                    up_size[j] * smooth_y - up[j] * slope_y
                )
                if f == 3:
                    theta = centers[2][j]
                    over_x = whole(mass_x[numbers[j], :, span])
                    over_y = whole(mass_y[numbers[j], :, span])
                    push_x[j] = metrics[j] * ((1.0 / 60.0) * slope_x + theta * over_x)
                    push_y[j] = per_row * slope_y + theta * over_y
                elif f == 0:
                    change = change + (spins[j] * centers[1][j] - push_x[j])
                elif f == 1:
                    change = change - (spins[j] * centers[0][j] + push_y[j])
                emit(f, first + j, span, q, change)

    def all_rows(emit):
        if edge_rows:
            for side in range(2):
                edge = edge_row(3 * side, rows)
                step = jnp.where(edge == 0, 1, -1)

                def row_of(f, j, span):
                    if j < 0:
                        first = levels * (3 * f - j - 1)
                        return strips[side][first : first + levels, span]
                    return fields[f][edge + step * j, :, span]

                numbers = [edge + step * j for j in range(3)]
                for t in range(tiles):
                    tendency(t, 3 * side, numbers, row_of, emit, step.astype(F32))
        else:

            def step(n, carry):
                first_row = 3 + 2 * n

                def row_of(f, j, span):
                    return fields[f][first_row + j, :, span]

                for t in range(tiles):
                    tendency(t, 2 * n, [first_row, first_row + 1], row_of, emit)
                return carry

            lax.fori_loop(0, count // 2, step, 0)

    def write_out(f):
        if edge_rows:
            return [(new.at[f, n], outs[f].at[edge_row(n, rows)]) for n in range(6)]
        return [(new.at[f], outs[f].at[3 : rows - 3])]

    @pl.when(jnp.logical_not(is_polar()))
    def _():
        def emit(f, i, span, q, change):
            new[f, i, :, span] = q + STEP * change

        all_rows(emit)
        pairs = [pair for f in range(4) for pair in write_out(f)]
        wait_all(start_all(pairs, sems))

    @pl.when(is_polar())
    def _():
        def emit(f, i, span, q, change):
            top = change.astype(BF16)
            kept_high[f, i, :, span] = top
            kept_low[f, i, :, span] = (change - top.astype(F32)).astype(BF16)

        all_rows(emit)
        c_all, s_all, d_all = [
            spread_waves(waves, part, edge_rows, levels) for part in range(3)
        ]
        top = kept_high[...].reshape(4 * items, columns)
        rest = kept_low[...].reshape(4 * items, columns)
        nodal = dot(jnp.concatenate([top, rest, top], axis=1), spread[...])
        turned = []
        for f in range(4):
            part = nodal[f * items : (f + 1) * items]
            turned += [c_all * part, s_all * part]
        turned = split(jnp.concatenate(turned, axis=0))
        moved = dot(turned, own[...])
        sent = dot(turned, send[...])
        for f in range(4):
            at = 2 * f * items
            local[f] = (
                s_all * moved[at : at + items]
                - c_all * moved[at + items : at + 2 * items]
                + d_all * nodal[f * items : (f + 1) * items]
            )
        wide = lax.broadcasted_iota(jnp.int32, (items, LANES), 1)
        for out, first, size in ((to_east, 0, NEAR), (to_west, NEAR, NEAR), (to_far, 2 * NEAR, FAR)):
            total = jnp.zeros((items, LANES), F32)
            for g in range(8):
                part = sent[g * items : (g + 1) * items]
                turn = (size * g - first) % LANES
                if turn:
                    part = pltpu.roll(part, turn, 1)
                total = jnp.where((wide >= size * g) & (wide < size * (g + 1)), part, total)
            if size == NEAR:
                out[...] = total
            else:
                total = total.reshape(count, 2, levels // 2, LANES)
                upper = pltpu.roll(total[:, 1].reshape(items // 2, LANES), 64, 1)
                out[...] = total[:, 0].reshape(items // 2, LANES) + upper


def finish_kernel(edge_rows, count, *refs):
    fields = refs[:4]
    from_west, from_east, from_far, local, waves, take, gather = refs[4:11]
    outs = refs[15:19]
    new, sems = refs[19:]
    rows = fields[0].shape[0]
    levels, columns = new.shape[2], new.shape[3]
    items = count * levels

    @pl.when(is_polar())
    def _():
        place = lax.axis_index("lon")
        last = lax.axis_size("lon") - 1
        near_west = from_west[...] * jnp.where(place == 0, -1.0, 1.0)
        near_east = from_east[...] * jnp.where(place == last, -1.0, 1.0)
        far = from_far[...] * jnp.where(place < 2, -1.0, 1.0)
        far = far.reshape(count, 1, levels // 2, LANES)
        upper = pltpu.roll(far.reshape(items // 2, LANES), 64, 1).reshape(count, 1, levels // 2, LANES)
        far = jnp.concatenate([far, upper], axis=1).reshape(items, LANES)
        wide = lax.broadcasted_iota(jnp.int32, (items, LANES), 1)

        def turn(value, by):
            by = by % LANES
            return pltpu.roll(value, by, 1) if by else value

        come = []
        for g in range(8):
            part = jnp.where(wide < NEAR, turn(near_west, -NEAR * g), turn(near_east, NEAR - NEAR * g))
            part = jnp.where(wide < 2 * NEAR, part, turn(far, 2 * NEAR - FAR * g))
            part = jnp.where(wide < MESSAGE, part, 0.0)
            top = part.astype(BF16).astype(F32)
            come.append((top + turn(part - top, MESSAGE) + turn(top, 2 * MESSAGE)).astype(BF16))
        moved = dot(jnp.concatenate(come, axis=0), take[...])
        c_all, s_all = [spread_waves(waves, part, edge_rows, levels) for part in range(2)]
        writes = []
        for half in range(2):
            value = []
            for f in (2 * half, 2 * half + 1):
                at = 2 * f * items
                value.append(
                    local[f] + (s_all * moved[at : at + items] - c_all * moved[at + items : at + 2 * items])
                )
            change = dot(split(jnp.concatenate(value, axis=0)), gather[...])
            change = change.reshape(2, count, levels, columns)
            pairs = []
            for f in (2 * half, 2 * half + 1):
                if edge_rows:
                    for n in range(6):
                        row = edge_row(n, rows)
                        new[f, n] = fields[f][row] + change[f % 2, n]
                        pairs.append((new.at[f, n], outs[f].at[row]))
                else:
                    new[f] = fields[f][3 : rows - 3] + change[f % 2]
                    pairs.append((new.at[f], outs[f].at[3 : rows - 3]))
            writes += start_all(pairs, sems, 12 * half)
        wait_all(writes)


def vmem():
    return pl.BlockSpec(memory_space=pltpu.VMEM)


def smem():
    return pl.BlockSpec(memory_space=pltpu.SMEM)


def anywhere():
    return pl.BlockSpec(memory_space=pl.ANY)


def like(*shape):
    return jax.ShapeDtypeStruct(shape, F32)


def params(mebibytes):
    return pltpu.CompilerParams(vmem_limit_bytes=mebibytes * 1024 * 1024)


def row_factors(count):
    latitude = (np.arange(count).astype(np.float32) + np.float32(0.5)) * np.float32(math.pi / count)
    latitude = latitude - np.float32(math.pi / 2)
    metric = np.float32(1.0) / np.cos(latitude)
    return metric.astype(np.float32), (np.float32(SPIN) * np.sin(latitude)).astype(np.float32)


def shards(u_wind, v_wind, theta, geopot, mass, cutoffs):
    rows, levels, columns = u_wind.shape
    lat_count = lax.axis_size("lat")
    lon_count = lax.axis_size("lon")
    tables = {k: jnp.asarray(v) for k, v in filter_tables(columns, columns * lon_count).items()}
    metric, spin = [jnp.asarray(t) for t in row_factors(rows * lat_count)]
    fields = (u_wind, v_wind, theta, geopot)

    strip = 12 * levels + 8
    edge_lines = 2 * levels + rows
    far_fields = [pltpu.with_memory_space_constraint(q, pltpu.HBM) for q in (*fields, mass)]
    to_a, to_b, to_west, to_east, waves = pl.pallas_call(
        pack_kernel,
        out_shape=[like(strip, columns)] * 2 + [like(edge_lines, LANES)] * 2 + [like(3, rows, 8, NODES)],
        in_specs=[smem()] + [anywhere()] * 5 + [vmem()],
        out_specs=[vmem()] * 5,
        scratch_shapes=[
            pltpu.VMEM((2, 4, rows, levels, LANES), F32),
            pltpu.VMEM((rows, columns), F32),
            pltpu.SemaphoreType.DMA((33,)),
        ],
        compiler_params=params(8),
        name="pack_edges",
    )(cutoffs, *far_fields, tables["nodes"])

    def ring(value, step):
        return lax.ppermute(value, "lon", [(i, (i + step) % lon_count) for i in range(lon_count)])

    west = ring(to_east, 1)
    east = ring(to_west, -1)
    odd_up = [(i, i + 1) for i in range(1, lat_count - 1, 2)]
    strip_a = lax.ppermute(to_a, "lat", [(i, i ^ 1) for i in range(lat_count)])
    strip_b = lax.ppermute(to_b, "lat", odd_up + [(j, i) for i, j in odd_up])

    def tendencies(edge_rows, old):
        count = 6 if edge_rows else rows - 6
        items = count * levels
        halos = [strip_a, strip_b] if edge_rows else []
        weights = [tables[k] for k in ("band", "spread", "own", "send")]
        args = [metric, spin, *fields, mass, west, east, waves, *halos, *weights]
        return pl.pallas_call(
            functools.partial(tend_kernel, edge_rows, count),
            out_shape=[like(rows, levels, columns)] * 4
            + [like(4, items, NODES)]
            + [like(items, LANES)] * 2
            + [like(items // 2, LANES)],
            in_specs=[smem()] * 2 + [vmem()] * (len(args) - 2) + [anywhere()] * len(old),
            out_specs=[anywhere()] * 4 + [vmem()] * 4,
            scratch_shapes=[
                pltpu.VMEM((4, count, levels, columns + LANES), BF16),
                pltpu.VMEM((4, count, levels, columns + LANES), BF16),
                pltpu.VMEM((columns // LANES, 4, count, levels, 2 * LANES), F32),
                pltpu.VMEM((4, count, levels, columns), F32),
                pltpu.VMEM((4, count, levels, columns), BF16),
                pltpu.VMEM((4, count, levels, columns), BF16),
                pltpu.VMEM((rows, 8, columns), F32),
                pltpu.VMEM((rows, 8, columns), F32),
                pltpu.SemaphoreType.DMA((24,)),
            ],
            input_output_aliases={len(args) + f: f for f in range(4)} if old else {},
            compiler_params=params(36),
            cost_estimate=pl.CostEstimate(
                flops=items * 4 * columns * 20000, bytes_accessed=8 * items * columns * 4, transcendentals=0
            ),
            name="tend_edge" if edge_rows else "tend_inner",
        )(*args, *old)

    def exchange(east_part, west_part, far_part):
        return ring(east_part, 1), ring(west_part, -1), ring(far_part, 2)

    def finish(edge_rows, received, local, old):
        count = 6 if edge_rows else rows - 6
        items = count * levels
        weights = [tables[k] for k in ("take", "gather")]
        args = [*fields, *received, local, waves, *weights]
        return pl.pallas_call(
            functools.partial(finish_kernel, edge_rows, count),
            out_shape=[like(rows, levels, columns)] * 4,
            in_specs=[vmem()] * len(args) + [anywhere()] * 4,
            out_specs=[anywhere()] * 4,
            scratch_shapes=[
                pltpu.VMEM((4, count, levels, columns), F32),
                pltpu.SemaphoreType.DMA((24,)),
            ],
            input_output_aliases={len(args) + f: f for f in range(4)},
            compiler_params=params(24),
            name="finish_edge" if edge_rows else "finish_inner",
        )(*args, *old)

    *outs, local_inner, a, b, c = tendencies(False, [])
    received_inner = exchange(a, b, c)
    *outs, local_edge, a, b, c = tendencies(True, outs)
    received_edge = exchange(a, b, c)
    outs = finish(False, received_inner, local_inner, outs)
    outs = finish(True, received_edge, local_edge, outs)
    return tuple(outs)


def solution(mesh):
    return jax.shard_map(
        shards,
        mesh=mesh,
        in_specs=(
            P(("members", "lat"), None, "lon"),
            P(("members", "lat"), None, "lon"),
            P(("members", "lat"), None, "lon"),
            P(("members", "lat"), None, "lon"),
            P(("members", "lat"), "lon"),
            P(),
        ),
        out_specs=(
            P(("members", "lat"), None, "lon"),
            P(("members", "lat"), None, "lon"),
            P(("members", "lat"), None, "lon"),
            P(("members", "lat"), None, "lon"),
        ),
        check_vma=False,
    )
```

```python
import functools
import math

import jax
import jax.numpy as jnp
import ml_dtypes
import numpy as np
from jax import lax
from jax.experimental import pallas as pl
from jax.experimental.pallas import tpu as pltpu
from jax.sharding import PartitionSpec as P

STEP = 0.1
SPIN = 0.5
LANES = 128
NEAR = 16
FAR = 8
NODES = 256
F32 = jnp.float32
BF16 = jnp.bfloat16
MESSAGE = 2 * NEAR + FAR


def pivoted(matrix, count):
    rest = np.array(matrix)
    columns = rest.shape[1]
    tilt = 1.0 + 1e-3 * np.arange(columns) / columns
    picked = []
    tri = np.zeros((count, columns))
    for step in range(count):
        size = (rest * rest).sum(axis=0)
        best = int(np.argmax(size * tilt))
        picked.append(best)
        unit = rest[:, best] / math.sqrt(size[best])
        for _ in range(2):
            part = (unit[:, None] * rest).sum(axis=0)
            rest -= unit[:, None] * part[None, :]
            tri[step] += part
        rest[:, best] = 0.0
    left = tri[:, picked].copy()
    right = tri.copy()
    for step in range(count - 1, -1, -1):
        right[step] /= left[step, step]
        right[:step] -= left[:step, step][:, None] * right[step][None, :]
    right[:, picked] = np.eye(count)
    order = np.argsort(picked)
    return np.asarray(picked)[order], right[order]


def cauchy(target, source, circle):
    gap = target[:, None] - source[None, :]
    angle = np.where(gap == 0, 0.5 * math.pi, gap * math.pi / circle)
    return np.where(gap == 0, 0.0, 1.0 / (circle * np.sin(angle)))


def stacked_halves(table):
    table = table.astype(np.float32)
    high = table.astype(ml_dtypes.bfloat16)
    low = (table - high.astype(np.float32)).astype(ml_dtypes.bfloat16)
    return np.concatenate([high, high, low], axis=0)


def band_table():
    band = np.zeros((2 * LANES, 2 * LANES))
    slope = {-3: -1, -2: 9, -1: -45, 1: 45, 2: -9, 3: 1}
    smooth = {-3: 1, -2: -6, -1: 15, 0: -20, 1: 15, 2: -6, 3: 1}
    for j in range(LANES):
        for k, value in slope.items():
            band[j + 3 + k, j] = value
        for k, value in smooth.items():
            band[j + 3 + k, LANES + j] = value
    return np.concatenate([band, band], axis=0).astype(ml_dtypes.bfloat16)


@functools.lru_cache(maxsize=None)
def filter_tables(sector, circle):
    modes = circle // 8
    place = np.arange(sector)
    wave = np.arange(modes)
    phase = (wave[:, None] * place[None, :]) % circle * (2 * math.pi / circle)
    basis = np.concatenate([np.cos(phase), np.sin(phase[1:])], axis=0)
    nodes, spread = pivoted(basis, NODES)
    own = cauchy(nodes, nodes, circle)
    send = np.zeros((NODES, LANES))
    take = np.zeros((MESSAGE, NODES))
    at = 0
    for shift, count in ((sector, NEAR), (-sector, NEAR), (2 * sector, FAR)):
        kernel = cauchy(nodes + shift, nodes, circle)
        pick, weights = pivoted(kernel, count)
        send[:, at : at + count] = weights.T
        take[at : at + count] = kernel[:, pick].T
        at += count
    take = stacked_halves(take)
    take = np.concatenate([take, np.zeros((LANES - 3 * MESSAGE, NODES), take.dtype)], axis=0)
    return dict(
        nodes=nodes.astype(np.float32)[None],
        band=band_table(),
        spread=stacked_halves(spread.T),
        own=stacked_halves(own.T),
        send=stacked_halves(send),
        take=take,
        gather=stacked_halves(STEP * spread),
    )


def split(value):
    high = value.astype(BF16)
    low = (value - high.astype(F32)).astype(BF16)
    return jnp.concatenate([high, low, high], axis=1)


def dot(a, b):
    return lax.dot_general(a, b, (((1,), (0,)), ((), ())), preferred_element_type=F32)


def start_all(pairs, sems, first=0):
    copies = [pltpu.make_async_copy(a, b, sems.at[first + n]) for n, (a, b) in enumerate(pairs)]
    for c in copies:
        c.start()
    return copies


def wait_all(copies):
    for c in copies:
        c.wait()


def is_polar():
    owner = lax.axis_index("lat")
    quarter = lax.axis_size("lat") // 4
    return (owner < quarter) | (owner >= lax.axis_size("lat") - quarter)


def edge_row(entry, rows):
    north = (lax.axis_index("lat") % 2 == 0) == (entry < 3)
    return jnp.where(north, rows - 1 - entry % 3, entry % 3)


def by_parity(even, odd):
    return jnp.where(lax.axis_index("lat") % 2 == 0, even, odd)


def pack_kernel(*refs):
    fields = refs[:4]
    mass, cutoffs_in, nodes_in, strip_a, strip_b, west, east, waves = refs[4:12]
    edge, own_mass, cutoffs, nodes, sems = refs[12:]
    rows, columns = mass.shape
    levels = edge.shape[3]
    tail = 12 * levels
    first = start_all([(cutoffs_in, cutoffs), (nodes_in, nodes)], sems, 33)
    small = start_all(
        [(mass, own_mass)]
        + [(q.at[:, :, 0:LANES], edge.at[0, f]) for f, q in enumerate(fields)]
        + [(q.at[:, :, columns - LANES : columns], edge.at[1, f]) for f, q in enumerate(fields)],
        sems,
    )
    pairs = []
    for entry in range(6):
        strip = strip_a if entry < 3 else strip_b
        row = edge_row(entry, rows)
        for f, q in enumerate(fields):
            pairs.append((q.at[row], strip.at[pl.ds(levels * (3 * f + entry % 3), levels)]))
    large = start_all(pairs, sems, 9)

    wait_all(first)
    lat_count = lax.axis_size("lat")
    lon_count = lax.axis_size("lon")
    owner = lax.axis_index("lat")
    circle = columns * lon_count
    start = jnp.where(owner < lat_count // 4, owner * rows, owner * rows - lat_count * rows // 2)
    start = jnp.clip(start, 0, lat_count * rows // 2 - rows)
    line = lax.broadcasted_iota(jnp.int32, (rows, NODES), 0)
    twice = jnp.zeros((rows, NODES), F32)
    for r in range(rows):
        twice = jnp.where(line == r, (2 * cutoffs[start + r] + 1).astype(F32), twice)
    place = nodes[...] + (lax.axis_index("lon") * columns).astype(F32)
    turns = twice * place
    angle = (turns - 2.0 * circle * jnp.floor(turns * (0.5 / circle))) * (math.pi / circle)
    for part, table in enumerate((jnp.cos(angle), jnp.sin(angle), twice * (1.0 / circle))):
        waves[part] = jnp.broadcast_to(table[:, None, :], (rows, 8, NODES))

    wait_all(small)
    north = jnp.concatenate([own_mass[rows - 1 - m : rows - m] for m in range(3)], axis=0)
    south = own_mass[0:3]
    for strip, lines in ((strip_a, by_parity(north, south)), (strip_b, by_parity(south, north))):
        strip[tail : tail + 3] = lines
        strip[tail + 3 : tail + 8] = jnp.zeros((5, columns), F32)
    lane = lax.broadcasted_iota(jnp.int32, (levels, LANES), 1)
    west[2 * levels :] = own_mass[:, 0:LANES]
    east[2 * levels :] = pltpu.roll(own_mass[:, columns - LANES : columns], 3, 1)
    for parity in range(2):
        for side, out in ((0, west), (1, east)):
            total = jnp.zeros((levels, LANES), F32)
            for r in range(parity, rows, 2):
                for f in range(4):
                    lead = 16 * (r // 2) + 3 * f
                    turn = lead if side == 0 else (lead + 3) % LANES
                    tile = edge[side, f, r]
                    if turn:
                        tile = pltpu.roll(tile, turn, 1)
                    total = jnp.where((lane >= lead) & (lane < lead + 3), tile, total)
            out[parity * levels : (parity + 1) * levels] = total
    wait_all(large)


def stencil(center, plus, minus):
    p1, p2, p3 = plus
    m1, m2, m3 = minus
    slope = 45.0 * (p1 - m1) - 9.0 * (p2 - m2) + (p3 - m3)
    smooth = (p3 + m3) - 6.0 * (p2 + m2) + 15.0 * (p1 + m1) - 20.0 * center
    return slope, smooth


def mass_slopes(mass, west, east, south, north, mass_x, mass_y, levels):
    rows, columns = mass.shape
    middle = mass[...]
    per_mass = 1.0 / (60.0 * middle)
    wide = jnp.concatenate(
        [pltpu.roll(west[2 * levels :], LANES - 3, 1), middle, east[2 * levels :]], axis=1
    )
    whole = columns + 2 * LANES

    def at(k):
        return pltpu.roll(wide, (-k) % whole, 1)[:, LANES : LANES + columns]

    def store(out, value):
        out[...] = jnp.broadcast_to(value[:, None, :], out.shape)

    store(mass_x, stencil(middle, [at(1), at(2), at(3)], [at(-1), at(-2), at(-3)])[0] * per_mass)
    tall = jnp.concatenate([south, middle, north], axis=0)
    plus = [tall[3 + k : 3 + k + rows] for k in (1, 2, 3)]
    minus = [tall[3 - k : 3 - k + rows] for k in (1, 2, 3)]
    store(mass_y, stencil(middle, plus, minus)[0] * per_mass)


def spread_waves(waves, part, edge_rows, levels):
    rows = waves.shape[1]
    if edge_rows:
        numbers = [edge_row(entry, rows) for entry in range(6)]
    else:
        numbers = range(3, rows - 3)
    return jnp.concatenate([waves[part, n] for n in numbers for _ in range(levels // 8)], axis=0)


def tend_kernel(edge_rows, count, metric, spin, *refs):
    refs = list(refs)

    def some(n):
        taken = refs[:n]
        del refs[:n]
        return taken

    fields = some(4)
    mass, west, east, waves = some(4)
    strips = some(2) if edge_rows else None
    tables_in = some(4)
    if edge_rows:
        some(4)
    outs = some(4)
    local, to_east, to_west, to_far = some(4)
    high, low, cross, new, kept_high, kept_low, mass_x, mass_y, *tables, sems = some(13)
    band, spread, own, send = tables
    rows, columns = mass.shape
    levels = fields[0].shape[1]
    items = count * levels
    tiles = columns // LANES

    fetched = start_all(zip(tables_in, tables), sems, 24)
    if edge_rows:
        tail = 12 * levels
        lines = [strip[tail : tail + 3] for strip in strips]
        upper = by_parity(lines[0], lines[1])
        lower = by_parity(lines[1], lines[0])
        lower = jnp.concatenate([lower[2:3], lower[1:2], lower[0:1]], axis=0)
    else:
        lower = upper = jnp.zeros((3, columns), F32)
    mass_slopes(mass, west, east, lower, upper, mass_x, mass_y, levels)
    lane = lax.broadcasted_iota(jnp.int32, (levels, LANES), 1)

    def cut(i, carry):
        row = edge_row(i, rows) if edge_rows else i + 3
        halo = pl.ds(pl.multiple_of((row % 2) * levels, levels), levels)
        for f in range(4):
            lead = 16 * (row // 2) + 3 * f
            before = pltpu.roll(west[halo, :], lax.rem(LANES - lead, LANES), 1)
            for t in range(tiles + 1):
                if t < tiles:
                    tile = pltpu.roll(fields[f][row, :, t * LANES : (t + 1) * LANES], 3, 1)
                else:
                    tile = pltpu.roll(east[halo, :], lax.rem(LANES + 3 - lead, LANES), 1)
                whole = jnp.where(lane < 3, before, tile)
                top = whole.astype(BF16)
                high[f, i, :, t * LANES : (t + 1) * LANES] = top
                low[f, i, :, t * LANES : (t + 1) * LANES] = (whole - top.astype(F32)).astype(BF16)
                before = tile
        return carry

    lax.fori_loop(0, count, cut, 0)

    wait_all(fetched[:1])
    for t in range(tiles):
        span = slice(t * LANES, (t + 2) * LANES)
        both = jnp.concatenate(
            [high[:, :, :, span].reshape(4 * items, 2 * LANES), low[:, :, :, span].reshape(4 * items, 2 * LANES)],
            axis=1,
        )
        cross[t] = dot(both, band[...]).reshape(4, count, levels, 2 * LANES)

    start_row = lax.axis_index("lat") * rows

    def whole(lines):
        return jnp.concatenate([lines] * (levels // 8), axis=0)

    def tendency(t, first, numbers, row_of, emit, inward=1.0):
        size = len(numbers)
        span = slice(t * LANES, (t + 1) * LANES)
        metrics = [metric[start_row + n] for n in numbers]
        spins = [spin[start_row + n] for n in numbers]
        centers = [[row_of(f, j, span) for j in range(size)] for f in range(3)]
        per_row = inward * (1.0 / 60.0)
        fast, fast_size, up, up_size = [], [], [], []
        for j in range(size):
            fast.append(centers[0][j] * (metrics[j] * (1.0 / 60.0)))
            fast_size.append(jnp.abs(fast[j]))
            up.append(centers[1][j] * per_row)
            up_size.append(jnp.abs(up[j]))
        push_x, push_y = [None] * size, [None] * size
        for f in (3, 0, 1, 2):
            column = [row_of(f, j, span) for j in range(-3, size + 3)]
            for j in range(size):
                q = column[j + 3]
                slope_x = cross[t, f, first + j, :, :LANES]
                smooth_x = cross[t, f, first + j, :, LANES:]
                slope_y, smooth_y = stencil(q, column[j + 4 : j + 7], column[j + 2 :: -1][:3])
                change = (fast_size[j] * smooth_x - fast[j] * slope_x) + (
                    up_size[j] * smooth_y - up[j] * slope_y
                )
                if f == 3:
                    theta = centers[2][j]
                    over_x = whole(mass_x[numbers[j], :, span])
                    over_y = whole(mass_y[numbers[j], :, span])
                    push_x[j] = metrics[j] * ((1.0 / 60.0) * slope_x + theta * over_x)
                    push_y[j] = per_row * slope_y + theta * over_y
                elif f == 0:
                    change = change + (spins[j] * centers[1][j] - push_x[j])
                elif f == 1:
                    change = change - (spins[j] * centers[0][j] + push_y[j])
                emit(f, first + j, span, q, change)

    def all_rows(emit):
        if edge_rows:
            for side in range(2):
                edge = edge_row(3 * side, rows)
                step = jnp.where(edge == 0, 1, -1)

                def row_of(f, j, span):
                    if j < 0:
                        first = levels * (3 * f - j - 1)
                        return strips[side][first : first + levels, span]
                    return fields[f][edge + step * j, :, span]

                numbers = [edge + step * j for j in range(3)]
                for t in range(tiles):
                    tendency(t, 3 * side, numbers, row_of, emit, step.astype(F32))
        else:

            def step(n, carry):
                first_row = 3 + 2 * n

                def row_of(f, j, span):
                    return fields[f][first_row + j, :, span]

                for t in range(tiles):
                    tendency(t, 2 * n, [first_row, first_row + 1], row_of, emit)
                return carry

            lax.fori_loop(0, count // 2, step, 0)

    def write_out(f):
        if edge_rows:
            return [(new.at[f, n], outs[f].at[edge_row(n, rows)]) for n in range(6)]
        return [(new.at[f], outs[f].at[3 : rows - 3])]

    @pl.when(jnp.logical_not(is_polar()))
    def _():
        def emit(f, i, span, q, change):
            new[f, i, :, span] = q + STEP * change

        all_rows(emit)
        pairs = [pair for f in range(4) for pair in write_out(f)]
        wait_all(start_all(pairs, sems))
        wait_all(fetched[1:])

    @pl.when(is_polar())
    def _():
        def emit(f, i, span, q, change):
            top = change.astype(BF16)
            kept_high[f, i, :, span] = top
            kept_low[f, i, :, span] = (change - top.astype(F32)).astype(BF16)

        all_rows(emit)
        wait_all(fetched[1:])
        c_all, s_all, d_all = [
            spread_waves(waves, part, edge_rows, levels) for part in range(3)
        ]
        top = kept_high[...].reshape(4 * items, columns)
        rest = kept_low[...].reshape(4 * items, columns)
        nodal = dot(jnp.concatenate([top, rest, top], axis=1), spread[...])
        turned = []
        for f in range(4):
            part = nodal[f * items : (f + 1) * items]
            turned += [c_all * part, s_all * part]
        turned = split(jnp.concatenate(turned, axis=0))
        moved = dot(turned, own[...])
        sent = dot(turned, send[...])
        for f in range(4):
            at = 2 * f * items
            local[f] = (
                s_all * moved[at : at + items]
                - c_all * moved[at + items : at + 2 * items]
                + d_all * nodal[f * items : (f + 1) * items]
            )
        wide = lax.broadcasted_iota(jnp.int32, (items, LANES), 1)
        for out, first, size in ((to_east, 0, NEAR), (to_west, NEAR, NEAR), (to_far, 2 * NEAR, FAR)):
            total = jnp.zeros((items, LANES), F32)
            for g in range(8):
                part = sent[g * items : (g + 1) * items]
                turn = (size * g - first) % LANES
                if turn:
                    part = pltpu.roll(part, turn, 1)
                total = jnp.where((wide >= size * g) & (wide < size * (g + 1)), part, total)
            if size == NEAR:
                out[...] = total
            else:
                total = total.reshape(count, 2, levels // 2, LANES)
                upper = pltpu.roll(total[:, 1].reshape(items // 2, LANES), 64, 1)
                out[...] = total[:, 0].reshape(items // 2, LANES) + upper


def finish_kernel(edge_rows, count, *refs):
    fields = refs[:4]
    from_west, from_east, from_far, local, waves, take_in, gather_in = refs[4:11]
    outs = refs[15:19]
    new, take, gather, sems = refs[19:]
    rows = fields[0].shape[0]
    levels, columns = new.shape[2], new.shape[3]
    items = count * levels

    @pl.when(is_polar())
    def _():
        fetched = start_all([(take_in, take), (gather_in, gather)], sems, 24)

        place = lax.axis_index("lon")
        last = lax.axis_size("lon") - 1
        near_west = from_west[...] * jnp.where(place == 0, -1.0, 1.0)
        near_east = from_east[...] * jnp.where(place == last, -1.0, 1.0)
        far = from_far[...] * jnp.where(place < 2, -1.0, 1.0)
        far = far.reshape(count, 1, levels // 2, LANES)
        upper = pltpu.roll(far.reshape(items // 2, LANES), 64, 1).reshape(count, 1, levels // 2, LANES)
        far = jnp.concatenate([far, upper], axis=1).reshape(items, LANES)
        wide = lax.broadcasted_iota(jnp.int32, (items, LANES), 1)

        def turn(value, by):
            by = by % LANES
            return pltpu.roll(value, by, 1) if by else value

        come = []
        for g in range(8):
            part = jnp.where(wide < NEAR, turn(near_west, -NEAR * g), turn(near_east, NEAR - NEAR * g))
            part = jnp.where(wide < 2 * NEAR, part, turn(far, 2 * NEAR - FAR * g))
            part = jnp.where(wide < MESSAGE, part, 0.0)
            top = part.astype(BF16).astype(F32)
            come.append((top + turn(part - top, MESSAGE) + turn(top, 2 * MESSAGE)).astype(BF16))
        wait_all(fetched[:1])
        moved = dot(jnp.concatenate(come, axis=0), take[...])
        c_all, s_all = [spread_waves(waves, part, edge_rows, levels) for part in range(2)]
        wait_all(fetched[1:])
        writes = []
        for half in range(2):
            value = []
            for f in (2 * half, 2 * half + 1):
                at = 2 * f * items
                value.append(
                    local[f] + (s_all * moved[at : at + items] - c_all * moved[at + items : at + 2 * items])
                )
            change = dot(split(jnp.concatenate(value, axis=0)), gather[...])
            change = change.reshape(2, count, levels, columns)
            pairs = []
            for f in (2 * half, 2 * half + 1):
                if edge_rows:
                    for n in range(6):
                        row = edge_row(n, rows)
                        new[f, n] = fields[f][row] + change[f % 2, n]
                        pairs.append((new.at[f, n], outs[f].at[row]))
                else:
                    new[f] = fields[f][3 : rows - 3] + change[f % 2]
                    pairs.append((new.at[f], outs[f].at[3 : rows - 3]))
            writes += start_all(pairs, sems, 12 * half)
        wait_all(writes)


def vmem():
    return pl.BlockSpec(memory_space=pltpu.VMEM)


def smem():
    return pl.BlockSpec(memory_space=pltpu.SMEM)


def anywhere():
    return pl.BlockSpec(memory_space=pl.ANY)


def like(*shape):
    return jax.ShapeDtypeStruct(shape, F32)


def in_hbm(value):
    return pltpu.with_memory_space_constraint(value, pltpu.HBM)


def params(mebibytes):
    return pltpu.CompilerParams(vmem_limit_bytes=mebibytes * 1024 * 1024)


def row_factors(count):
    latitude = (np.arange(count).astype(np.float32) + np.float32(0.5)) * np.float32(math.pi / count)
    latitude = latitude - np.float32(math.pi / 2)
    metric = np.float32(1.0) / np.cos(latitude)
    return metric.astype(np.float32), (np.float32(SPIN) * np.sin(latitude)).astype(np.float32)


def shards(u_wind, v_wind, theta, geopot, mass, cutoffs):
    rows, levels, columns = u_wind.shape
    lat_count = lax.axis_size("lat")
    lon_count = lax.axis_size("lon")
    tables = filter_tables(columns, columns * lon_count)
    tables = {k: in_hbm(jnp.asarray(v)) for k, v in tables.items()}
    metric, spin = [jnp.asarray(t) for t in row_factors(rows * lat_count)]
    fields = (u_wind, v_wind, theta, geopot)

    strip = 12 * levels + 8
    edge_lines = 2 * levels + rows
    far_fields = [in_hbm(q) for q in (*fields, mass)]
    to_a, to_b, to_west, to_east, waves = pl.pallas_call(
        pack_kernel,
        out_shape=[like(strip, columns)] * 2 + [like(edge_lines, LANES)] * 2 + [like(3, rows, 8, NODES)],
        in_specs=[anywhere()] * 7,
        out_specs=[vmem()] * 5,
        scratch_shapes=[
            pltpu.VMEM((2, 4, rows, levels, LANES), F32),
            pltpu.VMEM((rows, columns), F32),
            pltpu.SMEM(cutoffs.shape, jnp.int32),
            pltpu.VMEM((1, NODES), F32),
            pltpu.SemaphoreType.DMA((35,)),
        ],
        compiler_params=params(8),
        name="pack_edges",
    )(*far_fields, in_hbm(cutoffs), tables["nodes"])

    def ring(value, step):
        return lax.ppermute(value, "lon", [(i, (i + step) % lon_count) for i in range(lon_count)])

    west = ring(to_east, 1)
    east = ring(to_west, -1)
    odd_up = [(i, i + 1) for i in range(1, lat_count - 1, 2)]
    strip_a = lax.ppermute(to_a, "lat", [(i, i ^ 1) for i in range(lat_count)])
    strip_b = lax.ppermute(to_b, "lat", odd_up + [(j, i) for i, j in odd_up])

    def tendencies(edge_rows, old):
        count = 6 if edge_rows else rows - 6
        items = count * levels
        halos = [strip_a, strip_b] if edge_rows else []
        weights = [tables[k] for k in ("band", "spread", "own", "send")]
        args = [metric, spin, *fields, mass, west, east, waves, *halos, *weights]
        return pl.pallas_call(
            functools.partial(tend_kernel, edge_rows, count),
            out_shape=[like(rows, levels, columns)] * 4
            + [like(4, items, NODES)]
            + [like(items, LANES)] * 2
            + [like(items // 2, LANES)],
            in_specs=[smem()] * 2 + [vmem()] * (len(args) - 6) + [anywhere()] * (4 + len(old)),
            out_specs=[anywhere()] * 4 + [vmem()] * 4,
            scratch_shapes=[
                pltpu.VMEM((4, count, levels, columns + LANES), BF16),
                pltpu.VMEM((4, count, levels, columns + LANES), BF16),
                pltpu.VMEM((columns // LANES, 4, count, levels, 2 * LANES), F32),
                pltpu.VMEM((4, count, levels, columns), F32),
                pltpu.VMEM((4, count, levels, columns), BF16),
                pltpu.VMEM((4, count, levels, columns), BF16),
                pltpu.VMEM((rows, 8, columns), F32),
                pltpu.VMEM((rows, 8, columns), F32),
                *[pltpu.VMEM(w.shape, w.dtype) for w in weights],
                pltpu.SemaphoreType.DMA((28,)),
            ],
            input_output_aliases={len(args) + f: f for f in range(4)} if old else {},
            compiler_params=params(36),
            cost_estimate=pl.CostEstimate(
                flops=items * 4 * columns * 20000, bytes_accessed=8 * items * columns * 4, transcendentals=0
            ),
            name="tend_edge" if edge_rows else "tend_inner",
        )(*args, *old)

    def exchange(east_part, west_part, far_part):
        return ring(east_part, 1), ring(west_part, -1), ring(far_part, 2)

    def finish(edge_rows, received, local, old):
        count = 6 if edge_rows else rows - 6
        items = count * levels
        weights = [tables[k] for k in ("take", "gather")]
        args = [*fields, *received, local, waves, *weights]
        return pl.pallas_call(
            functools.partial(finish_kernel, edge_rows, count),
            out_shape=[like(rows, levels, columns)] * 4,
            in_specs=[vmem()] * (len(args) - 2) + [anywhere()] * 6,
            out_specs=[anywhere()] * 4,
            scratch_shapes=[
                pltpu.VMEM((4, count, levels, columns), F32),
                *[pltpu.VMEM(w.shape, w.dtype) for w in weights],
                pltpu.SemaphoreType.DMA((26,)),
            ],
            input_output_aliases={len(args) + f: f for f in range(4)},
            compiler_params=params(24),
            name="finish_edge" if edge_rows else "finish_inner",
        )(*args, *old)

    *outs, local_inner, a, b, c = tendencies(False, [])
    received_inner = exchange(a, b, c)
    *outs, local_edge, a, b, c = tendencies(True, outs)
    received_edge = exchange(a, b, c)
    outs = finish(False, received_inner, local_inner, outs)
    outs = finish(True, received_edge, local_edge, outs)
    return tuple(outs)


def solution(mesh):
    return jax.shard_map(
        shards,
        mesh=mesh,
        in_specs=(
            P(("members", "lat"), None, "lon"),
            P(("members", "lat"), None, "lon"),
            P(("members", "lat"), None, "lon"),
            P(("members", "lat"), None, "lon"),
            P(("members", "lat"), "lon"),
            P(),
        ),
        out_specs=(
            P(("members", "lat"), None, "lon"),
            P(("members", "lat"), None, "lon"),
            P(("members", "lat"), None, "lon"),
            P(("members", "lat"), None, "lon"),
        ),
        check_vma=False,
    )
```

```python
import functools
import math

import jax
import jax.numpy as jnp
import ml_dtypes
import numpy as np
from jax import lax
from jax.experimental import pallas as pl
from jax.experimental.pallas import tpu as pltpu
from jax.sharding import PartitionSpec as P

STEP = 0.1
SPIN = 0.5
LANES = 128
NEAR = 16
FAR = 8
NODES = 256
F32 = jnp.float32
BF16 = jnp.bfloat16
MESSAGE = 2 * NEAR + FAR


def pivoted(matrix, count):
    rest = np.array(matrix)
    columns = rest.shape[1]
    tilt = 1.0 + 1e-3 * np.arange(columns) / columns
    picked = []
    tri = np.zeros((count, columns))
    for step in range(count):
        size = (rest * rest).sum(axis=0)
        best = int(np.argmax(size * tilt))
        picked.append(best)
        unit = rest[:, best] / math.sqrt(size[best])
        for _ in range(2):
            part = (unit[:, None] * rest).sum(axis=0)
            rest -= unit[:, None] * part[None, :]
            tri[step] += part
        rest[:, best] = 0.0
    left = tri[:, picked].copy()
    right = tri.copy()
    for step in range(count - 1, -1, -1):
        right[step] /= left[step, step]
        right[:step] -= left[:step, step][:, None] * right[step][None, :]
    right[:, picked] = np.eye(count)
    order = np.argsort(picked)
    return np.asarray(picked)[order], right[order]


def cauchy(target, source, circle):
    gap = target[:, None] - source[None, :]
    angle = np.where(gap == 0, 0.5 * math.pi, gap * math.pi / circle)
    return np.where(gap == 0, 0.0, 1.0 / (circle * np.sin(angle)))


def stacked_halves(table):
    table = table.astype(np.float32)
    high = table.astype(ml_dtypes.bfloat16)
    low = (table - high.astype(np.float32)).astype(ml_dtypes.bfloat16)
    return np.concatenate([high, high, low], axis=0)


def band_table():
    band = np.zeros((2 * LANES, 2 * LANES))
    slope = {-3: -1, -2: 9, -1: -45, 1: 45, 2: -9, 3: 1}
    smooth = {-3: 1, -2: -6, -1: 15, 0: -20, 1: 15, 2: -6, 3: 1}
    for j in range(LANES):
        for k, value in slope.items():
            band[j + 3 + k, j] = value
        for k, value in smooth.items():
            band[j + 3 + k, LANES + j] = value
    return np.concatenate([band, band], axis=0).astype(ml_dtypes.bfloat16)


@functools.lru_cache(maxsize=None)
def filter_tables(sector, circle):
    modes = circle // 8
    place = np.arange(sector)
    wave = np.arange(modes)
    phase = (wave[:, None] * place[None, :]) % circle * (2 * math.pi / circle)
    basis = np.concatenate([np.cos(phase), np.sin(phase[1:])], axis=0)
    nodes, spread = pivoted(basis, NODES)
    own = cauchy(nodes, nodes, circle)
    send = np.zeros((NODES, LANES))
    take = np.zeros((MESSAGE, NODES))
    at = 0
    for shift, count in ((sector, NEAR), (-sector, NEAR), (2 * sector, FAR)):
        kernel = cauchy(nodes + shift, nodes, circle)
        pick, weights = pivoted(kernel, count)
        send[:, at : at + count] = weights.T
        take[at : at + count] = kernel[:, pick].T
        at += count
    take = stacked_halves(take)
    take = np.concatenate([take, np.zeros((LANES - 3 * MESSAGE, NODES), take.dtype)], axis=0)
    return dict(
        nodes=nodes.astype(np.float32)[None],
        band=band_table(),
        spread=stacked_halves(spread.T),
        own=stacked_halves(own.T),
        send=stacked_halves(send),
        take=take,
        gather=stacked_halves(STEP * spread),
    )


def split(value):
    high = value.astype(BF16)
    low = (value - high.astype(F32)).astype(BF16)
    return jnp.concatenate([high, low, high], axis=1)


def dot(a, b):
    return lax.dot_general(a, b, (((1,), (0,)), ((), ())), preferred_element_type=F32)


def start_all(pairs, sems, first=0):
    copies = [pltpu.make_async_copy(a, b, sems.at[first + n]) for n, (a, b) in enumerate(pairs)]
    for c in copies:
        c.start()
    return copies


def wait_all(copies):
    for c in copies:
        c.wait()


def is_polar():
    owner = lax.axis_index("lat")
    quarter = lax.axis_size("lat") // 4
    return (owner < quarter) | (owner >= lax.axis_size("lat") - quarter)


def edge_row(entry, rows):
    north = (lax.axis_index("lat") % 2 == 0) == (entry < 3)
    return jnp.where(north, rows - 1 - entry % 3, entry % 3)


def entry_row(inner, entry, rows):
    if not inner:
        return edge_row(entry, rows)
    if isinstance(entry, int):
        return entry + 3 if entry < rows - 6 else edge_row(entry - (rows - 6) + 3, rows)
    return jnp.where(entry < rows - 6, entry + 3, edge_row(entry - (rows - 6) + 3, rows))


def by_parity(even, odd):
    return jnp.where(lax.axis_index("lat") % 2 == 0, even, odd)


def pack_kernel(*refs):
    fields = refs[:4]
    mass, cutoffs_in, nodes_in, strip_a, strip_b, west, east, waves = refs[4:12]
    edge, own_mass, cutoffs, nodes, sems = refs[12:]
    rows, columns = mass.shape
    levels = edge.shape[3]
    tail = 12 * levels
    first = start_all([(cutoffs_in, cutoffs), (nodes_in, nodes)], sems, 33)
    small = start_all(
        [(mass, own_mass)]
        + [(q.at[:, :, 0:LANES], edge.at[0, f]) for f, q in enumerate(fields)]
        + [(q.at[:, :, columns - LANES : columns], edge.at[1, f]) for f, q in enumerate(fields)],
        sems,
    )
    pairs = []
    for entry in range(6):
        strip = strip_a if entry < 3 else strip_b
        row = edge_row(entry, rows)
        for f, q in enumerate(fields):
            pairs.append((q.at[row], strip.at[pl.ds(levels * (3 * f + entry % 3), levels)]))
    large = start_all(pairs, sems, 9)

    wait_all(first)
    lat_count = lax.axis_size("lat")
    lon_count = lax.axis_size("lon")
    owner = lax.axis_index("lat")
    circle = columns * lon_count
    start = jnp.where(owner < lat_count // 4, owner * rows, owner * rows - lat_count * rows // 2)
    start = jnp.clip(start, 0, lat_count * rows // 2 - rows)
    line = lax.broadcasted_iota(jnp.int32, (rows, NODES), 0)
    twice = jnp.zeros((rows, NODES), F32)
    for r in range(rows):
        twice = jnp.where(line == r, (2 * cutoffs[start + r] + 1).astype(F32), twice)
    place = nodes[...] + (lax.axis_index("lon") * columns).astype(F32)
    turns = twice * place
    angle = (turns - 2.0 * circle * jnp.floor(turns * (0.5 / circle))) * (math.pi / circle)
    for part, table in enumerate((jnp.cos(angle), jnp.sin(angle), twice * (1.0 / circle))):
        waves[part] = jnp.broadcast_to(table[:, None, :], (rows, 8, NODES))

    wait_all(small)
    north = jnp.concatenate([own_mass[rows - 1 - m : rows - m] for m in range(3)], axis=0)
    south = own_mass[0:3]
    for strip, lines in ((strip_a, by_parity(north, south)), (strip_b, by_parity(south, north))):
        strip[tail : tail + 3] = lines
        strip[tail + 3 : tail + 8] = jnp.zeros((5, columns), F32)
    lane = lax.broadcasted_iota(jnp.int32, (levels, LANES), 1)
    west[2 * levels :] = own_mass[:, 0:LANES]
    east[2 * levels :] = pltpu.roll(own_mass[:, columns - LANES : columns], 3, 1)
    for parity in range(2):
        for side, out in ((0, west), (1, east)):
            total = jnp.zeros((levels, LANES), F32)
            for r in range(parity, rows, 2):
                for f in range(4):
                    lead = 16 * (r // 2) + 3 * f
                    turn = lead if side == 0 else (lead + 3) % LANES
                    tile = edge[side, f, r]
                    if turn:
                        tile = pltpu.roll(tile, turn, 1)
                    total = jnp.where((lane >= lead) & (lane < lead + 3), tile, total)
            out[parity * levels : (parity + 1) * levels] = total
    wait_all(large)


def stencil(center, plus, minus):
    p1, p2, p3 = plus
    m1, m2, m3 = minus
    slope = 45.0 * (p1 - m1) - 9.0 * (p2 - m2) + (p3 - m3)
    smooth = (p3 + m3) - 6.0 * (p2 + m2) + 15.0 * (p1 + m1) - 20.0 * center
    return slope, smooth


def mass_slopes(mass, west, east, south, north, mass_x, mass_y, levels):
    rows, columns = mass.shape
    middle = mass[...]
    per_mass = 1.0 / (60.0 * middle)
    wide = jnp.concatenate(
        [pltpu.roll(west[2 * levels :], LANES - 3, 1), middle, east[2 * levels :]], axis=1
    )
    whole = columns + 2 * LANES

    def at(k):
        return pltpu.roll(wide, (-k) % whole, 1)[:, LANES : LANES + columns]

    def store(out, value):
        out[...] = jnp.broadcast_to(value[:, None, :], out.shape)

    store(mass_x, stencil(middle, [at(1), at(2), at(3)], [at(-1), at(-2), at(-3)])[0] * per_mass)
    tall = jnp.concatenate([south, middle, north], axis=0)
    plus = [tall[3 + k : 3 + k + rows] for k in (1, 2, 3)]
    minus = [tall[3 - k : 3 - k + rows] for k in (1, 2, 3)]
    store(mass_y, stencil(middle, plus, minus)[0] * per_mass)


def spread_waves(waves, part, inner, kept, levels):
    rows = waves.shape[1]
    numbers = [entry_row(inner, entry, rows) for entry in range(kept)]
    return jnp.concatenate([waves[part, n] for n in numbers for _ in range(levels // 8)], axis=0)


def tend_kernel(inner, count, kept, metric, spin, *refs):
    edge_rows = not inner
    refs = list(refs)

    def some(n):
        taken = refs[:n]
        del refs[:n]
        return taken

    fields = some(4)
    mass, west, east, waves = some(4)
    strips = some(2) if edge_rows else None
    tables_in = some(4)
    if edge_rows:
        some(4)
    outs = some(4)
    local, to_east, to_west, to_far = some(4)
    high, low, cross, new, kept_high, kept_low, mass_x, mass_y, sems = some(9)
    tables = refs if inner else tables_in
    band, spread, own, send = tables
    rows, columns = mass.shape
    levels = fields[0].shape[1]
    items = count * levels
    kept_items = kept * levels
    tiles = columns // LANES

    fetched = start_all(zip(tables_in, tables), sems, 24) if inner else []
    if edge_rows:
        tail = 12 * levels
        lines = [strip[tail : tail + 3] for strip in strips]
        upper = by_parity(lines[0], lines[1])
        lower = by_parity(lines[1], lines[0])
        lower = jnp.concatenate([lower[2:3], lower[1:2], lower[0:1]], axis=0)
    else:
        lower = upper = jnp.zeros((3, columns), F32)
    mass_slopes(mass, west, east, lower, upper, mass_x, mass_y, levels)
    lane = lax.broadcasted_iota(jnp.int32, (levels, LANES), 1)

    def cut(i, carry):
        row = entry_row(inner, i, rows)
        halo = pl.ds(pl.multiple_of((row % 2) * levels, levels), levels)
        for f in range(4):
            lead = 16 * (row // 2) + 3 * f
            before = pltpu.roll(west[halo, :], lax.rem(LANES - lead, LANES), 1)
            for t in range(tiles + 1):
                if t < tiles:
                    tile = pltpu.roll(fields[f][row, :, t * LANES : (t + 1) * LANES], 3, 1)
                else:
                    tile = pltpu.roll(east[halo, :], lax.rem(LANES + 3 - lead, LANES), 1)
                whole = jnp.where(lane < 3, before, tile)
                top = whole.astype(BF16)
                high[f, i, :, t * LANES : (t + 1) * LANES] = top
                low[f, i, :, t * LANES : (t + 1) * LANES] = (whole - top.astype(F32)).astype(BF16)
                before = tile
        return carry

    lax.fori_loop(0, count, cut, 0)

    wait_all(fetched[:1])
    for t in range(tiles):
        span = slice(t * LANES, (t + 2) * LANES)
        both = jnp.concatenate(
            [high[:, :, :, span].reshape(4 * items, 2 * LANES), low[:, :, :, span].reshape(4 * items, 2 * LANES)],
            axis=1,
        )
        cross[t] = dot(both, band[...]).reshape(4, count, levels, 2 * LANES)

    start_row = lax.axis_index("lat") * rows

    def whole(lines):
        return jnp.concatenate([lines] * (levels // 8), axis=0)

    def tendency(t, first, numbers, row_of, emit, inward=1.0):
        size = len(numbers)
        span = slice(t * LANES, (t + 1) * LANES)
        metrics = [metric[start_row + n] for n in numbers]
        spins = [spin[start_row + n] for n in numbers]
        centers = [[row_of(f, j, span) for j in range(size)] for f in range(3)]
        per_row = inward * (1.0 / 60.0)
        fast, fast_size, up, up_size = [], [], [], []
        for j in range(size):
            fast.append(centers[0][j] * (metrics[j] * (1.0 / 60.0)))
            fast_size.append(jnp.abs(fast[j]))
            up.append(centers[1][j] * per_row)
            up_size.append(jnp.abs(up[j]))
        push_x, push_y = [None] * size, [None] * size
        for f in (3, 0, 1, 2):
            column = [row_of(f, j, span) for j in range(-3, size + 3)]
            for j in range(size):
                q = column[j + 3]
                slope_x = cross[t, f, first + j, :, :LANES]
                smooth_x = cross[t, f, first + j, :, LANES:]
                slope_y, smooth_y = stencil(q, column[j + 4 : j + 7], column[j + 2 :: -1][:3])
                change = (fast_size[j] * smooth_x - fast[j] * slope_x) + (
                    up_size[j] * smooth_y - up[j] * slope_y
                )
                if f == 3:
                    theta = centers[2][j]
                    over_x = whole(mass_x[numbers[j], :, span])
                    over_y = whole(mass_y[numbers[j], :, span])
                    push_x[j] = metrics[j] * ((1.0 / 60.0) * slope_x + theta * over_x)
                    push_y[j] = per_row * slope_y + theta * over_y
                elif f == 0:
                    change = change + (spins[j] * centers[1][j] - push_x[j])
                elif f == 1:
                    change = change - (spins[j] * centers[0][j] + push_y[j])
                emit(f, first + j, span, q, change)

    def edge_side(side, first, emit):
        edge = edge_row(3 * side, rows)
        step = jnp.where(edge == 0, 1, -1)

        def row_of(f, j, span):
            if j >= 0:
                return fields[f][edge + step * j, :, span]
            if inner:
                return jnp.zeros((levels, LANES), F32)
            start = levels * (3 * f - j - 1)
            return strips[side][start : start + levels, span]

        numbers = [edge + step * j for j in range(3)]
        for t in range(tiles):
            tendency(t, first, numbers, row_of, emit, step.astype(F32))

    def inner_rows(emit):
        def step(n, carry):
            first_row = 3 + 2 * n

            def row_of(f, j, span):
                return fields[f][first_row + j, :, span]

            for t in range(tiles):
                tendency(t, 2 * n, [first_row, first_row + 1], row_of, emit)
            return carry

        lax.fori_loop(0, (rows - 6) // 2, step, 0)

    def write_out(f):
        if edge_rows:
            return [(new.at[f, n], outs[f].at[edge_row(n, rows)]) for n in range(6)]
        return [(new.at[f, 0 : rows - 6], outs[f].at[3 : rows - 3])]

    @pl.when(jnp.logical_not(is_polar()))
    def _():
        def emit(f, i, span, q, change):
            new[f, i, :, span] = q + STEP * change

        if inner:
            inner_rows(emit)
        else:
            edge_side(0, 0, emit)
            edge_side(1, 3, emit)
        pairs = [pair for f in range(4) for pair in write_out(f)]
        wait_all(start_all(pairs, sems))
        wait_all(fetched[1:])

    @pl.when(is_polar())
    def _():
        def emit(f, i, span, q, change):
            top = change.astype(BF16)
            kept_high[f, i, :, span] = top
            kept_low[f, i, :, span] = (change - top.astype(F32)).astype(BF16)

        if inner:
            inner_rows(emit)
            if kept > rows - 6:
                edge_side(1, rows - 6, emit)
        else:
            edge_side(0, 0, emit)
            if kept > 3:
                edge_side(1, 3, emit)
        wait_all(fetched[1:])
        c_all, s_all, d_all = [
            spread_waves(waves, part, inner, kept, levels) for part in range(3)
        ]
        top = kept_high[...].reshape(4 * kept_items, columns)
        rest = kept_low[...].reshape(4 * kept_items, columns)
        nodal = dot(jnp.concatenate([top, rest, top], axis=1), spread[...])
        turned = []
        for f in range(4):
            part = nodal[f * kept_items : (f + 1) * kept_items]
            turned += [c_all * part, s_all * part]
        turned = split(jnp.concatenate(turned, axis=0))
        moved = dot(turned, own[...])
        sent = dot(turned, send[...])
        for f in range(4):
            at = 2 * f * kept_items
            local[f] = (
                s_all * moved[at : at + kept_items]
                - c_all * moved[at + kept_items : at + 2 * kept_items]
                + d_all * nodal[f * kept_items : (f + 1) * kept_items]
            )
        wide = lax.broadcasted_iota(jnp.int32, (kept_items, LANES), 1)
        for out, first, size in ((to_east, 0, NEAR), (to_west, NEAR, NEAR), (to_far, 2 * NEAR, FAR)):
            total = jnp.zeros((kept_items, LANES), F32)
            for g in range(8):
                part = sent[g * kept_items : (g + 1) * kept_items]
                turn = (size * g - first) % LANES
                if turn:
                    part = pltpu.roll(part, turn, 1)
                total = jnp.where((wide >= size * g) & (wide < size * (g + 1)), part, total)
            if size == NEAR:
                out[...] = total
            else:
                total = total.reshape(kept, 2, levels // 2, LANES)
                upper = pltpu.roll(total[:, 1].reshape(kept_items // 2, LANES), 64, 1)
                out[...] = total[:, 0].reshape(kept_items // 2, LANES) + upper


def finish_kernel(inner, count, *refs):
    fields = refs[:4]
    from_west, from_east, from_far, local, waves, take, gather = refs[4:11]
    outs = refs[15:19]
    new, sems = refs[19:]
    rows = fields[0].shape[0]
    levels, columns = new.shape[2], new.shape[3]
    items = count * levels

    @pl.when(is_polar())
    def _():
        place = lax.axis_index("lon")
        last = lax.axis_size("lon") - 1
        near_west = from_west[...] * jnp.where(place == 0, -1.0, 1.0)
        near_east = from_east[...] * jnp.where(place == last, -1.0, 1.0)
        far = from_far[...] * jnp.where(place < 2, -1.0, 1.0)
        far = far.reshape(count, 1, levels // 2, LANES)
        upper = pltpu.roll(far.reshape(items // 2, LANES), 64, 1).reshape(count, 1, levels // 2, LANES)
        far = jnp.concatenate([far, upper], axis=1).reshape(items, LANES)
        wide = lax.broadcasted_iota(jnp.int32, (items, LANES), 1)

        def turn(value, by):
            by = by % LANES
            return pltpu.roll(value, by, 1) if by else value

        come = []
        for g in range(8):
            part = jnp.where(wide < NEAR, turn(near_west, -NEAR * g), turn(near_east, NEAR - NEAR * g))
            part = jnp.where(wide < 2 * NEAR, part, turn(far, 2 * NEAR - FAR * g))
            part = jnp.where(wide < MESSAGE, part, 0.0)
            top = part.astype(BF16).astype(F32)
            come.append((top + turn(part - top, MESSAGE) + turn(top, 2 * MESSAGE)).astype(BF16))
        moved = dot(jnp.concatenate(come, axis=0), take[...])
        c_all, s_all = [spread_waves(waves, part, inner, count, levels) for part in range(2)]
        writes = []
        for half in range(2):
            value = []
            for f in (2 * half, 2 * half + 1):
                at = 2 * f * items
                value.append(
                    local[f] + (s_all * moved[at : at + items] - c_all * moved[at + items : at + 2 * items])
                )
            change = dot(split(jnp.concatenate(value, axis=0)), gather[...])
            change = change.reshape(2, count, levels, columns)
            pairs = []
            for f in (2 * half, 2 * half + 1):
                for n in range(count):
                    new[f, n] = fields[f][entry_row(inner, n, rows)] + change[f % 2, n]
                off_edge = rows - 6 if inner else 0
                if inner:
                    pairs.append((new.at[f, 0:off_edge], outs[f].at[3 : rows - 3]))
                for n in range(off_edge, count):
                    pairs.append((new.at[f, n], outs[f].at[entry_row(inner, n, rows)]))
            writes += start_all(pairs, sems, 12 * half)
        wait_all(writes)


def vmem():
    return pl.BlockSpec(memory_space=pltpu.VMEM)


def smem():
    return pl.BlockSpec(memory_space=pltpu.SMEM)


def anywhere():
    return pl.BlockSpec(memory_space=pl.ANY)


def like(*shape):
    return jax.ShapeDtypeStruct(shape, F32)


def in_hbm(value):
    return pltpu.with_memory_space_constraint(value, pltpu.HBM)


def params(mebibytes):
    return pltpu.CompilerParams(vmem_limit_bytes=mebibytes * 1024 * 1024)


def row_factors(count):
    latitude = (np.arange(count).astype(np.float32) + np.float32(0.5)) * np.float32(math.pi / count)
    latitude = latitude - np.float32(math.pi / 2)
    metric = np.float32(1.0) / np.cos(latitude)
    return metric.astype(np.float32), (np.float32(SPIN) * np.sin(latitude)).astype(np.float32)


def shards(u_wind, v_wind, theta, geopot, mass, cutoffs):
    rows, levels, columns = u_wind.shape
    lat_count = lax.axis_size("lat")
    lon_count = lax.axis_size("lon")
    tables = filter_tables(columns, columns * lon_count)
    tables = {k: jnp.asarray(v) for k, v in tables.items()}
    metric, spin = [jnp.asarray(t) for t in row_factors(rows * lat_count)]
    fields = (u_wind, v_wind, theta, geopot)

    strip = 12 * levels + 8
    edge_lines = 2 * levels + rows
    far_fields = [in_hbm(q) for q in (*fields, mass)]
    to_a, to_b, to_west, to_east, waves = pl.pallas_call(
        pack_kernel,
        out_shape=[like(strip, columns)] * 2 + [like(edge_lines, LANES)] * 2 + [like(3, rows, 8, NODES)],
        in_specs=[anywhere()] * 7,
        out_specs=[vmem()] * 5,
        scratch_shapes=[
            pltpu.VMEM((2, 4, rows, levels, LANES), F32),
            pltpu.VMEM((rows, columns), F32),
            pltpu.SMEM(cutoffs.shape, jnp.int32),
            pltpu.VMEM((1, NODES), F32),
            pltpu.SemaphoreType.DMA((35,)),
        ],
        compiler_params=params(8),
        name="pack_edges",
    )(*far_fields, in_hbm(cutoffs), in_hbm(tables["nodes"]))

    def ring(value, step):
        return lax.ppermute(value, "lon", [(i, (i + step) % lon_count) for i in range(lon_count)])

    west = ring(to_east, 1)
    east = ring(to_west, -1)
    odd_up = [(i, i + 1) for i in range(1, lat_count - 1, 2)]
    strip_a = lax.ppermute(to_a, "lat", [(i, i ^ 1) for i in range(lat_count)])
    strip_b = lax.ppermute(to_b, "lat", odd_up + [(j, i) for i, j in odd_up])

    at_poles = lat_count == 4
    inner_count = rows - 3 if at_poles else rows - 6
    edge_kept = 3 if at_poles else 6

    def tendencies(inner, old):
        count, kept = (inner_count, inner_count) if inner else (6, edge_kept)
        kept_items = kept * levels
        halos = [] if inner else [strip_a, strip_b]
        weights = [tables[k] for k in ("band", "spread", "own", "send")]
        if inner:
            weights = [in_hbm(w) for w in weights]
        args = [metric, spin, *fields, mass, west, east, waves, *halos, *weights]
        return pl.pallas_call(
            functools.partial(tend_kernel, inner, count, kept),
            out_shape=[like(rows, levels, columns)] * 4
            + [like(4, kept_items, NODES)]
            + [like(kept_items, LANES)] * 2
            + [like(kept_items // 2, LANES)],
            in_specs=[smem()] * 2
            + [vmem()] * (len(args) - 6)
            + [anywhere() if inner else vmem()] * 4
            + [anywhere()] * len(old),
            out_specs=[anywhere()] * 4 + [vmem()] * 4,
            scratch_shapes=[
                pltpu.VMEM((4, count, levels, columns + LANES), BF16),
                pltpu.VMEM((4, count, levels, columns + LANES), BF16),
                pltpu.VMEM((columns // LANES, 4, count, levels, 2 * LANES), F32),
                pltpu.VMEM((4, count, levels, columns), F32),
                pltpu.VMEM((4, kept, levels, columns), BF16),
                pltpu.VMEM((4, kept, levels, columns), BF16),
                pltpu.VMEM((rows, 8, columns), F32),
                pltpu.VMEM((rows, 8, columns), F32),
                pltpu.SemaphoreType.DMA((28,)),
                *[pltpu.VMEM(w.shape, w.dtype) for w in weights if inner],
            ],
            input_output_aliases={len(args) + f: f for f in range(4)} if old else {},
            compiler_params=params(40),
            cost_estimate=pl.CostEstimate(
                flops=count * levels * 4 * columns * 20000, bytes_accessed=2**22, transcendentals=0
            ),
            name="tend_inner" if inner else "tend_edge",
        )(*args, *old)

    def exchange(east_part, west_part, far_part):
        return ring(east_part, 1), ring(west_part, -1), ring(far_part, 2)

    def finish(inner, received, local, old):
        count = inner_count if inner else edge_kept
        weights = [tables[k] for k in ("take", "gather")]
        args = [*fields, *received, local, waves, *weights]
        return pl.pallas_call(
            functools.partial(finish_kernel, inner, count),
            out_shape=[like(rows, levels, columns)] * 4,
            in_specs=[vmem()] * len(args) + [anywhere()] * 4,
            out_specs=[anywhere()] * 4,
            scratch_shapes=[
                pltpu.VMEM((4, count, levels, columns), F32),
                pltpu.SemaphoreType.DMA((24,)),
            ],
            input_output_aliases={len(args) + f: f for f in range(4)},
            compiler_params=params(24),
            name="finish_inner" if inner else "finish_edge",
        )(*args, *old)

    *outs, local_inner, a, b, c = tendencies(True, [])
    received_inner = exchange(a, b, c)
    *outs, local_edge, a, b, c = tendencies(False, outs)
    received_edge = exchange(a, b, c)
    outs = finish(True, received_inner, local_inner, outs)
    outs = finish(False, received_edge, local_edge, outs)
    return tuple(outs)


def solution(mesh):
    return jax.shard_map(
        shards,
        mesh=mesh,
        in_specs=(
            P(("members", "lat"), None, "lon"),
            P(("members", "lat"), None, "lon"),
            P(("members", "lat"), None, "lon"),
            P(("members", "lat"), None, "lon"),
            P(("members", "lat"), "lon"),
            P(),
        ),
        out_specs=(
            P(("members", "lat"), None, "lon"),
            P(("members", "lat"), None, "lon"),
            P(("members", "lat"), None, "lon"),
            P(("members", "lat"), None, "lon"),
        ),
        check_vma=False,
    )
```

```python
import functools
import math

import jax
import jax.numpy as jnp
import ml_dtypes
import numpy as np
from jax import lax
from jax.experimental import pallas as pl
from jax.experimental.pallas import tpu as pltpu
from jax.sharding import PartitionSpec as P

STEP = 0.1
SPIN = 0.5
LANES = 128
NEAR = 16
FAR = 8
NODES = 256
F32 = jnp.float32
BF16 = jnp.bfloat16
MESSAGE = 2 * NEAR + FAR


def pivoted(matrix, count):
    rest = np.array(matrix)
    columns = rest.shape[1]
    tilt = 1.0 + 1e-3 * np.arange(columns) / columns
    picked = []
    tri = np.zeros((count, columns))
    for step in range(count):
        size = (rest * rest).sum(axis=0)
        best = int(np.argmax(size * tilt))
        picked.append(best)
        unit = rest[:, best] / math.sqrt(size[best])
        for _ in range(2):
            part = (unit[:, None] * rest).sum(axis=0)
            rest -= unit[:, None] * part[None, :]
            tri[step] += part
        rest[:, best] = 0.0
    left = tri[:, picked].copy()
    right = tri.copy()
    for step in range(count - 1, -1, -1):
        right[step] /= left[step, step]
        right[:step] -= left[:step, step][:, None] * right[step][None, :]
    right[:, picked] = np.eye(count)
    order = np.argsort(picked)
    return np.asarray(picked)[order], right[order]


def cauchy(target, source, circle):
    gap = target[:, None] - source[None, :]
    angle = np.where(gap == 0, 0.5 * math.pi, gap * math.pi / circle)
    return np.where(gap == 0, 0.0, 1.0 / (circle * np.sin(angle)))


def stacked_halves(table):
    table = table.astype(np.float32)
    high = table.astype(ml_dtypes.bfloat16)
    low = (table - high.astype(np.float32)).astype(ml_dtypes.bfloat16)
    return np.concatenate([high, high, low], axis=0)


def band_table():
    band = np.zeros((2 * LANES, 2 * LANES))
    slope = {-3: -1, -2: 9, -1: -45, 1: 45, 2: -9, 3: 1}
    smooth = {-3: 1, -2: -6, -1: 15, 0: -20, 1: 15, 2: -6, 3: 1}
    for j in range(LANES):
        for k, value in slope.items():
            band[j + 3 + k, j] = value
        for k, value in smooth.items():
            band[j + 3 + k, LANES + j] = value
    return np.concatenate([band, band], axis=0).astype(ml_dtypes.bfloat16)


@functools.lru_cache(maxsize=None)
def filter_tables(sector, circle):
    modes = circle // 8
    place = np.arange(sector)
    wave = np.arange(modes)
    phase = (wave[:, None] * place[None, :]) % circle * (2 * math.pi / circle)
    basis = np.concatenate([np.cos(phase), np.sin(phase[1:])], axis=0)
    nodes, spread = pivoted(basis, NODES)
    own = cauchy(nodes, nodes, circle)
    send = np.zeros((NODES, LANES))
    take = np.zeros((MESSAGE, NODES))
    at = 0
    for shift, count in ((sector, NEAR), (-sector, NEAR), (2 * sector, FAR)):
        kernel = cauchy(nodes + shift, nodes, circle)
        pick, weights = pivoted(kernel, count)
        send[:, at : at + count] = weights.T
        take[at : at + count] = kernel[:, pick].T
        at += count
    take = stacked_halves(take)
    take = np.concatenate([take, np.zeros((LANES - 3 * MESSAGE, NODES), take.dtype)], axis=0)
    return dict(
        nodes=nodes.astype(np.float32)[None],
        band=band_table(),
        spread=stacked_halves(spread.T),
        own=stacked_halves(own.T),
        send=stacked_halves(send),
        take=take,
        gather=stacked_halves(STEP * spread),
    )


def split(value):
    high = value.astype(BF16)
    low = (value - high.astype(F32)).astype(BF16)
    return jnp.concatenate([high, low, high], axis=1)


def dot(a, b):
    return lax.dot_general(a, b, (((1,), (0,)), ((), ())), preferred_element_type=F32)


def start_all(pairs, sems, first=0):
    copies = [pltpu.make_async_copy(a, b, sems.at[first + n]) for n, (a, b) in enumerate(pairs)]
    for c in copies:
        c.start()
    return copies


def wait_all(copies):
    for c in copies:
        c.wait()


def is_polar():
    owner = lax.axis_index("lat")
    quarter = lax.axis_size("lat") // 4
    return (owner < quarter) | (owner >= lax.axis_size("lat") - quarter)


def edge_row(entry, rows):
    north = (lax.axis_index("lat") % 2 == 0) == (entry < 3)
    return jnp.where(north, rows - 1 - entry % 3, entry % 3)


def entry_row(inner, entry, rows):
    if not inner:
        return edge_row(entry, rows)
    if isinstance(entry, int):
        return entry + 3 if entry < rows - 6 else edge_row(entry - (rows - 6) + 3, rows)
    return jnp.where(entry < rows - 6, entry + 3, edge_row(entry - (rows - 6) + 3, rows))


def by_parity(even, odd):
    return jnp.where(lax.axis_index("lat") % 2 == 0, even, odd)


def pack_kernel(*refs):
    fields = refs[:4]
    mass, cutoffs_in, nodes_in, strip_a, strip_b, west, east, waves = refs[4:12]
    edge, own_mass, cutoffs, nodes, sems = refs[12:]
    rows, columns = mass.shape
    levels = edge.shape[3]
    tail = 12 * levels
    first = start_all([(cutoffs_in, cutoffs), (nodes_in, nodes)], sems, 33)
    small = start_all(
        [(mass, own_mass)]
        + [(q.at[:, :, 0:LANES], edge.at[0, f]) for f, q in enumerate(fields)]
        + [(q.at[:, :, columns - LANES : columns], edge.at[1, f]) for f, q in enumerate(fields)],
        sems,
    )
    pairs = []
    for entry in range(6):
        strip = strip_a if entry < 3 else strip_b
        row = edge_row(entry, rows)
        for f, q in enumerate(fields):
            pairs.append((q.at[row], strip.at[pl.ds(levels * (3 * f + entry % 3), levels)]))
    large = start_all(pairs, sems, 9)

    wait_all(first)
    lat_count = lax.axis_size("lat")
    lon_count = lax.axis_size("lon")
    owner = lax.axis_index("lat")
    circle = columns * lon_count
    start = jnp.where(owner < lat_count // 4, owner * rows, owner * rows - lat_count * rows // 2)
    start = jnp.clip(start, 0, lat_count * rows // 2 - rows)
    line = lax.broadcasted_iota(jnp.int32, (rows, NODES), 0)
    twice = jnp.zeros((rows, NODES), F32)
    for r in range(rows):
        twice = jnp.where(line == r, (2 * cutoffs[start + r] + 1).astype(F32), twice)
    place = nodes[...] + (lax.axis_index("lon") * columns).astype(F32)
    turns = twice * place
    angle = (turns - 2.0 * circle * jnp.floor(turns * (0.5 / circle))) * (math.pi / circle)
    for part, table in enumerate((jnp.cos(angle), jnp.sin(angle), twice * (1.0 / circle))):
        waves[part] = jnp.broadcast_to(table[:, None, :], (rows, 8, NODES))

    wait_all(small)
    north = jnp.concatenate([own_mass[rows - 1 - m : rows - m] for m in range(3)], axis=0)
    south = own_mass[0:3]
    for strip, lines in ((strip_a, by_parity(north, south)), (strip_b, by_parity(south, north))):
        strip[tail : tail + 3] = lines
        strip[tail + 3 : tail + 8] = jnp.zeros((5, columns), F32)
    lane = lax.broadcasted_iota(jnp.int32, (levels, LANES), 1)
    west[2 * levels :] = own_mass[:, 0:LANES]
    east[2 * levels :] = pltpu.roll(own_mass[:, columns - LANES : columns], 3, 1)
    for parity in range(2):
        for side, out in ((0, west), (1, east)):
            total = jnp.zeros((levels, LANES), F32)
            for r in range(parity, rows, 2):
                for f in range(4):
                    lead = 16 * (r // 2) + 3 * f
                    turn = lead if side == 0 else (lead + 3) % LANES
                    tile = edge[side, f, r]
                    if turn:
                        tile = pltpu.roll(tile, turn, 1)
                    total = jnp.where((lane >= lead) & (lane < lead + 3), tile, total)
            out[parity * levels : (parity + 1) * levels] = total
    wait_all(large)


def stencil(center, plus, minus):
    p1, p2, p3 = plus
    m1, m2, m3 = minus
    slope = 45.0 * (p1 - m1) - 9.0 * (p2 - m2) + (p3 - m3)
    smooth = (p3 + m3) - 6.0 * (p2 + m2) + 15.0 * (p1 + m1) - 20.0 * center
    return slope, smooth


def mass_slopes(mass, west, east, south, north, mass_x, mass_y, levels):
    rows, columns = mass.shape
    middle = mass[...]
    per_mass = 1.0 / (60.0 * middle)
    wide = jnp.concatenate(
        [pltpu.roll(west[2 * levels :], LANES - 3, 1), middle, east[2 * levels :]], axis=1
    )
    whole = columns + 2 * LANES

    def at(k):
        return pltpu.roll(wide, (-k) % whole, 1)[:, LANES : LANES + columns]

    def store(out, value):
        out[...] = jnp.broadcast_to(value[:, None, :], out.shape)

    store(mass_x, stencil(middle, [at(1), at(2), at(3)], [at(-1), at(-2), at(-3)])[0] * per_mass)
    tall = jnp.concatenate([south, middle, north], axis=0)
    plus = [tall[3 + k : 3 + k + rows] for k in (1, 2, 3)]
    minus = [tall[3 - k : 3 - k + rows] for k in (1, 2, 3)]
    store(mass_y, stencil(middle, plus, minus)[0] * per_mass)


def spread_waves(waves, part, inner, kept, levels):
    rows = waves.shape[1]
    numbers = [entry_row(inner, entry, rows) for entry in range(kept)]
    return jnp.concatenate([waves[part, n] for n in numbers for _ in range(levels // 8)], axis=0)


def tend_kernel(inner, count, kept, metric, spin, *refs):
    edge_rows = not inner
    refs = list(refs)

    def some(n):
        taken = refs[:n]
        del refs[:n]
        return taken

    fields = some(4)
    mass, west, east, waves = some(4)
    strips = some(2) if edge_rows else None
    tables_in = some(4)
    if edge_rows:
        some(4)
    outs = some(4)
    local, messages = some(2)
    high, low, cross, new, kept_high, kept_low, mass_x, mass_y, sems = some(9)
    tables = refs if inner else tables_in
    band, spread, own, send = tables
    rows, columns = mass.shape
    levels = fields[0].shape[1]
    items = count * levels
    kept_items = kept * levels
    tiles = columns // LANES

    fetched = start_all(zip(tables_in, tables), sems, 24) if inner else []
    if edge_rows:
        tail = 12 * levels
        lines = [strip[tail : tail + 3] for strip in strips]
        upper = by_parity(lines[0], lines[1])
        lower = by_parity(lines[1], lines[0])
        lower = jnp.concatenate([lower[2:3], lower[1:2], lower[0:1]], axis=0)
    else:
        lower = upper = jnp.zeros((3, columns), F32)
    mass_slopes(mass, west, east, lower, upper, mass_x, mass_y, levels)
    lane = lax.broadcasted_iota(jnp.int32, (levels, LANES), 1)

    def cut(i, carry):
        row = entry_row(inner, i, rows)
        halo = pl.ds(pl.multiple_of((row % 2) * levels, levels), levels)
        for f in range(4):
            lead = 16 * (row // 2) + 3 * f
            before = pltpu.roll(west[halo, :], lax.rem(LANES - lead, LANES), 1)
            for t in range(tiles + 1):
                if t < tiles:
                    tile = pltpu.roll(fields[f][row, :, t * LANES : (t + 1) * LANES], 3, 1)
                else:
                    tile = pltpu.roll(east[halo, :], lax.rem(LANES + 3 - lead, LANES), 1)
                whole = jnp.where(lane < 3, before, tile)
                top = whole.astype(BF16)
                high[f, i, :, t * LANES : (t + 1) * LANES] = top
                low[f, i, :, t * LANES : (t + 1) * LANES] = (whole - top.astype(F32)).astype(BF16)
                before = tile
        return carry

    lax.fori_loop(0, count, cut, 0)

    wait_all(fetched[:1])
    for t in range(tiles):
        span = slice(t * LANES, (t + 2) * LANES)
        both = jnp.concatenate(
            [high[:, :, :, span].reshape(4 * items, 2 * LANES), low[:, :, :, span].reshape(4 * items, 2 * LANES)],
            axis=1,
        )
        cross[t] = dot(both, band[...]).reshape(4, count, levels, 2 * LANES)

    start_row = lax.axis_index("lat") * rows

    def whole(lines):
        return jnp.concatenate([lines] * (levels // 8), axis=0)

    def tendency(t, first, numbers, row_of, emit, inward=1.0):
        size = len(numbers)
        span = slice(t * LANES, (t + 1) * LANES)
        metrics = [metric[start_row + n] for n in numbers]
        spins = [spin[start_row + n] for n in numbers]
        centers = [[row_of(f, j, span) for j in range(size)] for f in range(3)]
        per_row = inward * (1.0 / 60.0)
        fast, fast_size, up, up_size = [], [], [], []
        for j in range(size):
            fast.append(centers[0][j] * (metrics[j] * (1.0 / 60.0)))
            fast_size.append(jnp.abs(fast[j]))
            up.append(centers[1][j] * per_row)
            up_size.append(jnp.abs(up[j]))
        push_x, push_y = [None] * size, [None] * size
        for f in (3, 0, 1, 2):
            column = [row_of(f, j, span) for j in range(-3, size + 3)]
            for j in range(size):
                q = column[j + 3]
                slope_x = cross[t, f, first + j, :, :LANES]
                smooth_x = cross[t, f, first + j, :, LANES:]
                slope_y, smooth_y = stencil(q, column[j + 4 : j + 7], column[j + 2 :: -1][:3])
                change = (fast_size[j] * smooth_x - fast[j] * slope_x) + (
                    up_size[j] * smooth_y - up[j] * slope_y
                )
                if f == 3:
                    theta = centers[2][j]
                    over_x = whole(mass_x[numbers[j], :, span])
                    over_y = whole(mass_y[numbers[j], :, span])
                    push_x[j] = metrics[j] * ((1.0 / 60.0) * slope_x + theta * over_x)
                    push_y[j] = per_row * slope_y + theta * over_y
                elif f == 0:
                    change = change + (spins[j] * centers[1][j] - push_x[j])
                elif f == 1:
                    change = change - (spins[j] * centers[0][j] + push_y[j])
                emit(f, first + j, span, q, change)

    def edge_side(side, first, emit):
        edge = edge_row(3 * side, rows)
        step = jnp.where(edge == 0, 1, -1)

        def row_of(f, j, span):
            if j >= 0:
                return fields[f][edge + step * j, :, span]
            if inner:
                return jnp.zeros((levels, LANES), F32)
            start = levels * (3 * f - j - 1)
            return strips[side][start : start + levels, span]

        numbers = [edge + step * j for j in range(3)]
        for t in range(tiles):
            tendency(t, first, numbers, row_of, emit, step.astype(F32))

    def inner_rows(emit):
        def step(n, carry):
            first_row = 3 + 2 * n

            def row_of(f, j, span):
                return fields[f][first_row + j, :, span]

            for t in range(tiles):
                tendency(t, 2 * n, [first_row, first_row + 1], row_of, emit)
            return carry

        lax.fori_loop(0, (rows - 6) // 2, step, 0)

    def write_out(f):
        if edge_rows:
            return [(new.at[f, n], outs[f].at[edge_row(n, rows)]) for n in range(6)]
        return [(new.at[f, 0 : rows - 6], outs[f].at[3 : rows - 3])]

    @pl.when(jnp.logical_not(is_polar()))
    def _():
        def emit(f, i, span, q, change):
            new[f, i, :, span] = q + STEP * change

        if inner:
            inner_rows(emit)
        else:
            edge_side(0, 0, emit)
            edge_side(1, 3, emit)
        pairs = [pair for f in range(4) for pair in write_out(f)]
        wait_all(start_all(pairs, sems))
        wait_all(fetched[1:])

    @pl.when(is_polar())
    def _():
        def emit(f, i, span, q, change):
            top = change.astype(BF16)
            kept_high[f, i, :, span] = top
            kept_low[f, i, :, span] = (change - top.astype(F32)).astype(BF16)

        if inner:
            inner_rows(emit)
            if kept > rows - 6:
                edge_side(1, rows - 6, emit)
        else:
            edge_side(0, 0, emit)
            if kept > 3:
                edge_side(1, 3, emit)
        wait_all(fetched[1:])
        c_all, s_all, d_all = [
            spread_waves(waves, part, inner, kept, levels) for part in range(3)
        ]
        top = kept_high[...].reshape(4 * kept_items, columns)
        rest = kept_low[...].reshape(4 * kept_items, columns)
        nodal = dot(jnp.concatenate([top, rest, top], axis=1), spread[...])
        turned = []
        for f in range(4):
            part = nodal[f * kept_items : (f + 1) * kept_items]
            turned += [c_all * part, s_all * part]
        turned = split(jnp.concatenate(turned, axis=0))
        moved = dot(turned, own[...])
        sent = dot(turned, send[...])
        for f in range(4):
            at = 2 * f * kept_items
            local[f] = (
                s_all * moved[at : at + kept_items]
                - c_all * moved[at + kept_items : at + 2 * kept_items]
                + d_all * nodal[f * kept_items : (f + 1) * kept_items]
            )
        wide = lax.broadcasted_iota(jnp.int32, (kept_items, LANES), 1)
        place = lax.axis_index("lon")
        for ahead, first, size in ((1, 0, NEAR), (3, NEAR, NEAR), (2, 2 * NEAR, FAR)):
            total = jnp.zeros((kept_items, LANES), F32)
            for g in range(8):
                part = sent[g * kept_items : (g + 1) * kept_items]
                turn = (size * g - first) % LANES
                if turn:
                    part = pltpu.roll(part, turn, 1)
                total = jnp.where((wide >= size * g) & (wide < size * (g + 1)), part, total)
            messages[lax.rem(place + ahead, 4)] = total


def finish_kernel(inner, count, *refs):
    fields = refs[:4]
    messages, local, waves, take, gather = refs[4:9]
    outs = refs[13:17]
    new, sems = refs[17:]
    rows = fields[0].shape[0]
    levels, columns = new.shape[2], new.shape[3]
    items = count * levels

    @pl.when(is_polar())
    def _():
        place = lax.axis_index("lon")
        near_west = messages[lax.rem(place + 3, 4)] * jnp.where(place == 0, -1.0, 1.0)
        near_east = messages[lax.rem(place + 1, 4)] * jnp.where(place == 3, -1.0, 1.0)
        far = messages[lax.rem(place + 2, 4)] * jnp.where(place < 2, -1.0, 1.0)
        wide = lax.broadcasted_iota(jnp.int32, (items, LANES), 1)

        def turn(value, by):
            by = by % LANES
            return pltpu.roll(value, by, 1) if by else value

        come = []
        for g in range(8):
            part = jnp.where(wide < NEAR, turn(near_west, -NEAR * g), turn(near_east, NEAR - NEAR * g))
            part = jnp.where(wide < 2 * NEAR, part, turn(far, 2 * NEAR - FAR * g))
            part = jnp.where(wide < MESSAGE, part, 0.0)
            top = part.astype(BF16).astype(F32)
            come.append((top + turn(part - top, MESSAGE) + turn(top, 2 * MESSAGE)).astype(BF16))
        moved = dot(jnp.concatenate(come, axis=0), take[...])
        c_all, s_all = [spread_waves(waves, part, inner, count, levels) for part in range(2)]
        writes = []
        for half in range(2):
            value = []
            for f in (2 * half, 2 * half + 1):
                at = 2 * f * items
                value.append(
                    local[f] + (s_all * moved[at : at + items] - c_all * moved[at + items : at + 2 * items])
                )
            change = dot(split(jnp.concatenate(value, axis=0)), gather[...])
            change = change.reshape(2, count, levels, columns)
            pairs = []
            for f in (2 * half, 2 * half + 1):
                for n in range(count):
                    new[f, n] = fields[f][entry_row(inner, n, rows)] + change[f % 2, n]
                off_edge = rows - 6 if inner else 0
                if inner:
                    pairs.append((new.at[f, 0:off_edge], outs[f].at[3 : rows - 3]))
                for n in range(off_edge, count):
                    pairs.append((new.at[f, n], outs[f].at[entry_row(inner, n, rows)]))
            writes += start_all(pairs, sems, 12 * half)
        wait_all(writes)


def vmem():
    return pl.BlockSpec(memory_space=pltpu.VMEM)


def smem():
    return pl.BlockSpec(memory_space=pltpu.SMEM)


def anywhere():
    return pl.BlockSpec(memory_space=pl.ANY)


def like(*shape):
    return jax.ShapeDtypeStruct(shape, F32)


def in_hbm(value):
    return pltpu.with_memory_space_constraint(value, pltpu.HBM)


def params(mebibytes):
    return pltpu.CompilerParams(vmem_limit_bytes=mebibytes * 1024 * 1024)


def row_factors(count):
    latitude = (np.arange(count).astype(np.float32) + np.float32(0.5)) * np.float32(math.pi / count)
    latitude = latitude - np.float32(math.pi / 2)
    metric = np.float32(1.0) / np.cos(latitude)
    return metric.astype(np.float32), (np.float32(SPIN) * np.sin(latitude)).astype(np.float32)


def shards(u_wind, v_wind, theta, geopot, mass, cutoffs):
    rows, levels, columns = u_wind.shape
    lat_count = lax.axis_size("lat")
    lon_count = lax.axis_size("lon")
    tables = filter_tables(columns, columns * lon_count)
    tables = {k: jnp.asarray(v) for k, v in tables.items()}
    metric, spin = [jnp.asarray(t) for t in row_factors(rows * lat_count)]
    fields = (u_wind, v_wind, theta, geopot)

    strip = 12 * levels + 8
    edge_lines = 2 * levels + rows
    far_fields = [in_hbm(q) for q in (*fields, mass)]
    to_a, to_b, to_west, to_east, waves = pl.pallas_call(
        pack_kernel,
        out_shape=[like(strip, columns)] * 2 + [like(edge_lines, LANES)] * 2 + [like(3, rows, 8, NODES)],
        in_specs=[anywhere()] * 7,
        out_specs=[vmem()] * 5,
        scratch_shapes=[
            pltpu.VMEM((2, 4, rows, levels, LANES), F32),
            pltpu.VMEM((rows, columns), F32),
            pltpu.SMEM(cutoffs.shape, jnp.int32),
            pltpu.VMEM((1, NODES), F32),
            pltpu.SemaphoreType.DMA((35,)),
        ],
        compiler_params=params(8),
        name="pack_edges",
    )(*far_fields, in_hbm(cutoffs), in_hbm(tables["nodes"]))

    def ring(value, step):
        return lax.ppermute(value, "lon", [(i, (i + step) % lon_count) for i in range(lon_count)])

    west = ring(to_east, 1)
    east = ring(to_west, -1)
    odd_up = [(i, i + 1) for i in range(1, lat_count - 1, 2)]
    strip_a = lax.ppermute(to_a, "lat", [(i, i ^ 1) for i in range(lat_count)])
    strip_b = lax.ppermute(to_b, "lat", odd_up + [(j, i) for i, j in odd_up])

    at_poles = lat_count == 4
    inner_count = rows - 3 if at_poles else rows - 6
    edge_kept = 3 if at_poles else 6

    def tendencies(inner, old):
        count, kept = (inner_count, inner_count) if inner else (6, edge_kept)
        kept_items = kept * levels
        halos = [] if inner else [strip_a, strip_b]
        weights = [tables[k] for k in ("band", "spread", "own", "send")]
        if inner:
            weights = [in_hbm(w) for w in weights]
        args = [metric, spin, *fields, mass, west, east, waves, *halos, *weights]
        return pl.pallas_call(
            functools.partial(tend_kernel, inner, count, kept),
            out_shape=[like(rows, levels, columns)] * 4
            + [like(4, kept_items, NODES)]
            + [like(lon_count, kept_items, LANES)],
            in_specs=[smem()] * 2
            + [vmem()] * (len(args) - 6)
            + [anywhere() if inner else vmem()] * 4
            + [anywhere()] * len(old),
            out_specs=[anywhere()] * 4 + [vmem()] * 2,
            scratch_shapes=[
                pltpu.VMEM((4, count, levels, columns + LANES), BF16),
                pltpu.VMEM((4, count, levels, columns + LANES), BF16),
                pltpu.VMEM((columns // LANES, 4, count, levels, 2 * LANES), F32),
                pltpu.VMEM((4, count, levels, columns), F32),
                pltpu.VMEM((4, kept, levels, columns), BF16),
                pltpu.VMEM((4, kept, levels, columns), BF16),
                pltpu.VMEM((rows, 8, columns), F32),
                pltpu.VMEM((rows, 8, columns), F32),
                pltpu.SemaphoreType.DMA((28,)),
                *[pltpu.VMEM(w.shape, w.dtype) for w in weights if inner],
            ],
            input_output_aliases={len(args) + f: f for f in range(4)} if old else {},
            compiler_params=params(40),
            cost_estimate=pl.CostEstimate(
                flops=count * levels * 4 * columns * 20000, bytes_accessed=2**22, transcendentals=0
            ),
            name="tend_inner" if inner else "tend_edge",
        )(*args, *old)

    def exchange(messages):
        return lax.all_to_all(messages, "lon", split_axis=0, concat_axis=0, tiled=True)

    def finish(inner, received, local, old):
        count = inner_count if inner else edge_kept
        weights = [tables[k] for k in ("take", "gather")]
        args = [*fields, received, local, waves, *weights]
        return pl.pallas_call(
            functools.partial(finish_kernel, inner, count),
            out_shape=[like(rows, levels, columns)] * 4,
            in_specs=[vmem()] * len(args) + [anywhere()] * 4,
            out_specs=[anywhere()] * 4,
            scratch_shapes=[
                pltpu.VMEM((4, count, levels, columns), F32),
                pltpu.SemaphoreType.DMA((24,)),
            ],
            input_output_aliases={len(args) + f: f for f in range(4)},
            compiler_params=params(24),
            name="finish_inner" if inner else "finish_edge",
        )(*args, *old)

    *outs, local_inner, messages = tendencies(True, [])
    received_inner = exchange(messages)
    *outs, local_edge, messages = tendencies(False, outs)
    received_edge = exchange(messages)
    outs = finish(True, received_inner, local_inner, outs)
    outs = finish(False, received_edge, local_edge, outs)
    return tuple(outs)


def solution(mesh):
    return jax.shard_map(
        shards,
        mesh=mesh,
        in_specs=(
            P(("members", "lat"), None, "lon"),
            P(("members", "lat"), None, "lon"),
            P(("members", "lat"), None, "lon"),
            P(("members", "lat"), None, "lon"),
            P(("members", "lat"), "lon"),
            P(),
        ),
        out_specs=(
            P(("members", "lat"), None, "lon"),
            P(("members", "lat"), None, "lon"),
            P(("members", "lat"), None, "lon"),
            P(("members", "lat"), None, "lon"),
        ),
        check_vma=False,
    )
```

```python
import functools
import math

import jax
import jax.numpy as jnp
import ml_dtypes
import numpy as np
from jax import lax
from jax.experimental import pallas as pl
from jax.experimental.pallas import tpu as pltpu
from jax.sharding import PartitionSpec as P

STEP = 0.1
SPIN = 0.5
LANES = 128
NEAR = 16
FAR = 8
NODES = 256
F32 = jnp.float32
BF16 = jnp.bfloat16
MESSAGE = 2 * NEAR + FAR


def pivoted(matrix, count):
    rest = np.array(matrix)
    columns = rest.shape[1]
    tilt = 1.0 + 1e-3 * np.arange(columns) / columns
    picked = []
    tri = np.zeros((count, columns))
    for step in range(count):
        size = (rest * rest).sum(axis=0)
        best = int(np.argmax(size * tilt))
        picked.append(best)
        unit = rest[:, best] / math.sqrt(size[best])
        for _ in range(2):
            part = (unit[:, None] * rest).sum(axis=0)
            rest -= unit[:, None] * part[None, :]
            tri[step] += part
        rest[:, best] = 0.0
    left = tri[:, picked].copy()
    right = tri.copy()
    for step in range(count - 1, -1, -1):
        right[step] /= left[step, step]
        right[:step] -= left[:step, step][:, None] * right[step][None, :]
    right[:, picked] = np.eye(count)
    order = np.argsort(picked)
    return np.asarray(picked)[order], right[order]


def cauchy(target, source, circle):
    gap = target[:, None] - source[None, :]
    angle = np.where(gap == 0, 0.5 * math.pi, gap * math.pi / circle)
    return np.where(gap == 0, 0.0, 1.0 / (circle * np.sin(angle)))


def stacked_halves(table):
    table = table.astype(np.float32)
    high = table.astype(ml_dtypes.bfloat16)
    low = (table - high.astype(np.float32)).astype(ml_dtypes.bfloat16)
    return np.concatenate([high, high, low], axis=0)


def band_table():
    band = np.zeros((3 * LANES, 2 * LANES))
    slope = {-3: -1, -2: 9, -1: -45, 1: 45, 2: -9, 3: 1}
    smooth = {-3: 1, -2: -6, -1: 15, 0: -20, 1: 15, 2: -6, 3: 1}
    for j in range(LANES):
        for k, value in slope.items():
            band[LANES + j + k, j] = value
        for k, value in smooth.items():
            band[LANES + j + k, LANES + j] = value
    return np.concatenate([band, band], axis=0).astype(ml_dtypes.bfloat16)


@functools.lru_cache(maxsize=None)
def filter_tables(sector, circle):
    modes = circle // 8
    place = np.arange(sector)
    wave = np.arange(modes)
    phase = (wave[:, None] * place[None, :]) % circle * (2 * math.pi / circle)
    basis = np.concatenate([np.cos(phase), np.sin(phase[1:])], axis=0)
    nodes, spread = pivoted(basis, NODES)
    own = cauchy(nodes, nodes, circle)
    send = np.zeros((NODES, LANES))
    take = np.zeros((MESSAGE, NODES))
    at = 0
    for shift, count in ((sector, NEAR), (-sector, NEAR), (2 * sector, FAR)):
        kernel = cauchy(nodes + shift, nodes, circle)
        pick, weights = pivoted(kernel, count)
        send[:, at : at + count] = weights.T
        take[at : at + count] = kernel[:, pick].T
        at += count
    take = stacked_halves(take)
    take = np.concatenate([take, np.zeros((LANES - 3 * MESSAGE, NODES), take.dtype)], axis=0)
    return dict(
        nodes=nodes.astype(np.float32)[None],
        band=band_table(),
        spread=stacked_halves(spread.T),
        own=stacked_halves(own.T),
        send=stacked_halves(send),
        take=take,
        gather=stacked_halves(STEP * spread),
    )


def split(value):
    high = value.astype(BF16)
    low = (value - high.astype(F32)).astype(BF16)
    return jnp.concatenate([high, low, high], axis=1)


def dot(a, b):
    return lax.dot_general(a, b, (((1,), (0,)), ((), ())), preferred_element_type=F32)


def start_all(pairs, sems, first=0):
    copies = [pltpu.make_async_copy(a, b, sems.at[first + n]) for n, (a, b) in enumerate(pairs)]
    for c in copies:
        c.start()
    return copies


def wait_all(copies):
    for c in copies:
        c.wait()


def is_polar():
    owner = lax.axis_index("lat")
    quarter = lax.axis_size("lat") // 4
    return (owner < quarter) | (owner >= lax.axis_size("lat") - quarter)


def edge_row(entry, rows):
    north = (lax.axis_index("lat") % 2 == 0) == (entry < 3)
    return jnp.where(north, rows - 1 - entry % 3, entry % 3)


def entry_row(inner, entry, rows):
    if not inner:
        return edge_row(entry, rows)
    if isinstance(entry, int):
        return entry + 3 if entry < rows - 6 else edge_row(entry - (rows - 6) + 3, rows)
    return jnp.where(entry < rows - 6, entry + 3, edge_row(entry - (rows - 6) + 3, rows))


def by_parity(even, odd):
    return jnp.where(lax.axis_index("lat") % 2 == 0, even, odd)


def pack_kernel(*refs):
    fields = refs[:4]
    mass, cutoffs_in, nodes_in, strip_a, strip_b, west, east, waves = refs[4:12]
    edge, own_mass, cutoffs, nodes, sems = refs[12:]
    rows, columns = mass.shape
    levels = edge.shape[3]
    tail = 12 * levels
    first = start_all([(cutoffs_in, cutoffs), (nodes_in, nodes)], sems, 33)
    small = start_all(
        [(mass, own_mass)]
        + [(q.at[:, :, 0:LANES], edge.at[0, f]) for f, q in enumerate(fields)]
        + [(q.at[:, :, columns - LANES : columns], edge.at[1, f]) for f, q in enumerate(fields)],
        sems,
    )
    pairs = []
    for entry in range(6):
        strip = strip_a if entry < 3 else strip_b
        row = edge_row(entry, rows)
        for f, q in enumerate(fields):
            pairs.append((q.at[row], strip.at[pl.ds(levels * (3 * f + entry % 3), levels)]))
    large = start_all(pairs, sems, 9)

    wait_all(first)
    lat_count = lax.axis_size("lat")
    lon_count = lax.axis_size("lon")
    owner = lax.axis_index("lat")
    circle = columns * lon_count
    start = jnp.where(owner < lat_count // 4, owner * rows, owner * rows - lat_count * rows // 2)
    start = jnp.clip(start, 0, lat_count * rows // 2 - rows)
    line = lax.broadcasted_iota(jnp.int32, (rows, NODES), 0)
    twice = jnp.zeros((rows, NODES), F32)
    for r in range(rows):
        twice = jnp.where(line == r, (2 * cutoffs[start + r] + 1).astype(F32), twice)
    place = nodes[...] + (lax.axis_index("lon") * columns).astype(F32)
    turns = twice * place
    angle = (turns - 2.0 * circle * jnp.floor(turns * (0.5 / circle))) * (math.pi / circle)
    for part, table in enumerate((jnp.cos(angle), jnp.sin(angle), twice * (1.0 / circle))):
        waves[part] = jnp.broadcast_to(table[:, None, :], (rows, 8, NODES))

    wait_all(small)
    north = jnp.concatenate([own_mass[rows - 1 - m : rows - m] for m in range(3)], axis=0)
    south = own_mass[0:3]
    for strip, lines in ((strip_a, by_parity(north, south)), (strip_b, by_parity(south, north))):
        strip[tail : tail + 3] = lines
        strip[tail + 3 : tail + 8] = jnp.zeros((5, columns), F32)
    lane = lax.broadcasted_iota(jnp.int32, (levels, LANES), 1)
    west[2 * levels :] = own_mass[:, 0:LANES]
    east[2 * levels :] = pltpu.roll(own_mass[:, columns - LANES : columns], 3, 1)
    for parity in range(2):
        for side, out in ((0, west), (1, east)):
            total = jnp.zeros((levels, LANES), F32)
            for r in range(parity, rows, 2):
                for f in range(4):
                    lead = 16 * (r // 2) + 3 * f
                    turn = lead if side == 0 else (lead + 3) % LANES
                    tile = edge[side, f, r]
                    if turn:
                        tile = pltpu.roll(tile, turn, 1)
                    total = jnp.where((lane >= lead) & (lane < lead + 3), tile, total)
            out[parity * levels : (parity + 1) * levels] = total
    wait_all(large)


def stencil(center, plus, minus):
    p1, p2, p3 = plus
    m1, m2, m3 = minus
    slope = 45.0 * (p1 - m1) - 9.0 * (p2 - m2) + (p3 - m3)
    smooth = (p3 + m3) - 6.0 * (p2 + m2) + 15.0 * (p1 + m1) - 20.0 * center
    return slope, smooth


def over_levels(value):
    return jnp.broadcast_to(value[:, None, :], (value.shape[0], 8, value.shape[1]))


def mass_slope_x(mass, west, east, levels):
    columns = mass.shape[1]
    middle = mass[...]
    wide = jnp.concatenate(
        [pltpu.roll(west[2 * levels :], LANES - 3, 1), middle, east[2 * levels :]], axis=1
    )
    whole = columns + 2 * LANES

    def at(k):
        return pltpu.roll(wide, (-k) % whole, 1)[:, LANES : LANES + columns]

    slope = stencil(middle, [at(1), at(2), at(3)], [at(-1), at(-2), at(-3)])[0]
    return over_levels(slope / (60.0 * middle))


def mass_slope_y(tall):
    size = tall.shape[0] - 6
    plus = [tall[3 + k : 3 + k + size] for k in (1, 2, 3)]
    minus = [tall[3 - k : 3 - k + size] for k in (1, 2, 3)]
    middle = tall[3 : 3 + size]
    return over_levels(stencil(middle, plus, minus)[0] / (60.0 * middle))


def spread_waves(waves, part, inner, kept, levels):
    rows = waves.shape[1]
    numbers = [entry_row(inner, entry, rows) for entry in range(kept)]
    return jnp.concatenate([waves[part, n] for n in numbers for _ in range(levels // 8)], axis=0)


def tend_kernel(inner, count, kept, metric, spin, *refs):
    edge_rows = not inner
    refs = list(refs)

    def some(n):
        taken = refs[:n]
        del refs[:n]
        return taken

    fields = some(4)
    mass, west, east, waves = some(4)
    strips = some(2) if edge_rows else None
    mass_x = some(1)[0] if edge_rows else None
    tables_in = some(4)
    if edge_rows:
        some(4)
    outs = some(4)
    local, to_east, to_west, to_far = some(4)
    mass_x = some(1)[0] if inner else mass_x
    high, low, cross, new, kept_high, kept_low, mass_y, sems = some(8)
    tables = refs if inner else tables_in
    band, spread, own, send = tables
    rows, columns = mass.shape
    levels = fields[0].shape[1]
    items = count * levels
    kept_items = kept * levels
    tiles = columns // LANES

    fetched = start_all(zip(tables_in, tables), sems, 24) if inner else []
    if edge_rows:
        tail = 12 * levels
        lines = [strip[tail : tail + 3] for strip in strips]
        upper = by_parity(lines[0], lines[1])
        lower = by_parity(lines[1], lines[0])
        lower = jnp.concatenate([lower[2:3], lower[1:2], lower[0:1]], axis=0)
        mass_y[0:3] = mass_slope_y(jnp.concatenate([lower, mass[0:6]], axis=0))
        mass_y[rows - 3 :] = mass_slope_y(jnp.concatenate([mass[rows - 6 :], upper], axis=0))
    else:
        blank = jnp.zeros((3, columns), F32)
        mass_x[...] = mass_slope_x(mass, west, east, levels)
        mass_y[...] = mass_slope_y(jnp.concatenate([blank, mass[...], blank], axis=0))

    def cut(i, carry):
        row = entry_row(inner, i, rows)
        halo = pl.ds(pl.multiple_of((row % 2) * levels, levels), levels)
        for f in range(4):
            lead = 16 * (row // 2) + 3 * f
            for t in range(tiles + 2):
                if t == 0:
                    tile = pltpu.roll(west[halo, :], lax.rem(2 * LANES - 3 - lead, LANES), 1)
                elif t <= tiles:
                    tile = fields[f][row, :, (t - 1) * LANES : t * LANES]
                else:
                    tile = pltpu.roll(east[halo, :], lax.rem(LANES - lead, LANES), 1)
                top = tile.astype(BF16)
                high[f, i, :, t * LANES : (t + 1) * LANES] = top
                low[f, i, :, t * LANES : (t + 1) * LANES] = (tile - top.astype(F32)).astype(BF16)
        return carry

    def slopes_x(first, size):
        lax.fori_loop(first, first + size, cut, 0)
        wait_all(fetched[:1])
        for t in range(tiles):
            span = slice(t * LANES, (t + 3) * LANES)
            some_rows = slice(first, first + size)
            both = jnp.concatenate(
                [
                    table[:, some_rows, :, span].reshape(4 * size * levels, 3 * LANES)
                    for table in (high, low)
                ],
                axis=1,
            )
            cross[t, :, some_rows] = dot(both, band[...]).reshape(4, size, levels, 2 * LANES)

    start_row = lax.axis_index("lat") * rows

    def whole(lines):
        return jnp.concatenate([lines] * (levels // 8), axis=0)

    def tendency(t, first, numbers, row_of, emit, inward=1.0):
        size = len(numbers)
        span = slice(t * LANES, (t + 1) * LANES)
        metrics = [metric[start_row + n] for n in numbers]
        spins = [spin[start_row + n] for n in numbers]
        centers = [[row_of(f, j, span) for j in range(size)] for f in range(3)]
        per_row = inward * (1.0 / 60.0)
        fast, fast_size, up, up_size = [], [], [], []
        for j in range(size):
            fast.append(centers[0][j] * (metrics[j] * (1.0 / 60.0)))
            fast_size.append(jnp.abs(fast[j]))
            up.append(centers[1][j] * per_row)
            up_size.append(jnp.abs(up[j]))
        push_x, push_y = [None] * size, [None] * size
        for f in (3, 0, 1, 2):
            column = [row_of(f, j, span) for j in range(-3, size + 3)]
            for j in range(size):
                q = column[j + 3]
                slope_x = cross[t, f, first + j, :, :LANES]
                smooth_x = cross[t, f, first + j, :, LANES:]
                slope_y, smooth_y = stencil(q, column[j + 4 : j + 7], column[j + 2 :: -1][:3])
                change = (fast_size[j] * smooth_x - fast[j] * slope_x) + (
                    up_size[j] * smooth_y - up[j] * slope_y
                )
                if f == 3:
                    theta = centers[2][j]
                    over_x = whole(mass_x[numbers[j], :, span])
                    over_y = whole(mass_y[numbers[j], :, span])
                    push_x[j] = metrics[j] * ((1.0 / 60.0) * slope_x + theta * over_x)
                    push_y[j] = per_row * slope_y + theta * over_y
                elif f == 0:
                    change = change + (spins[j] * centers[1][j] - push_x[j])
                elif f == 1:
                    change = change - (spins[j] * centers[0][j] + push_y[j])
                emit(f, first + j, span, q, change)

    def edge_side(side, first, emit):
        edge = edge_row(3 * side, rows)
        step = jnp.where(edge == 0, 1, -1)

        def row_of(f, j, span):
            if j >= 0:
                return fields[f][edge + step * j, :, span]
            if inner:
                return jnp.zeros((levels, LANES), F32)
            start = levels * (3 * f - j - 1)
            return strips[side][start : start + levels, span]

        numbers = [edge + step * j for j in range(3)]
        for t in range(tiles):
            tendency(t, first, numbers, row_of, emit, step.astype(F32))

    def inner_rows(emit):
        def step(n, carry):
            first_row = 3 + 2 * n

            def row_of(f, j, span):
                return fields[f][first_row + j, :, span]

            for t in range(tiles):
                tendency(t, 2 * n, [first_row, first_row + 1], row_of, emit)
            return carry

        lax.fori_loop(0, (rows - 6) // 2, step, 0)

    def write_out(f):
        if edge_rows:
            return [(new.at[f, n], outs[f].at[edge_row(n, rows)]) for n in range(6)]
        return [(new.at[f, 0 : rows - 6], outs[f].at[3 : rows - 3])]

    @pl.when(jnp.logical_not(is_polar()))
    def _():
        def emit(f, i, span, q, change):
            new[f, i, :, span] = q + STEP * change

        if inner:
            slopes_x(0, rows - 6)
            inner_rows(emit)
        else:
            slopes_x(0, 6)
            edge_side(0, 0, emit)
            edge_side(1, 3, emit)
        pairs = [pair for f in range(4) for pair in write_out(f)]
        wait_all(start_all(pairs, sems))
        wait_all(fetched[1:])

    @pl.when(is_polar())
    def _():
        def emit(f, i, span, q, change):
            top = change.astype(BF16)
            kept_high[f, i, :, span] = top
            kept_low[f, i, :, span] = (change - top.astype(F32)).astype(BF16)

        slopes_x(0, kept)
        if inner:
            inner_rows(emit)
            if kept > rows - 6:
                edge_side(1, rows - 6, emit)
        else:
            edge_side(0, 0, emit)
            if kept > 3:
                edge_side(1, 3, emit)
        wait_all(fetched[1:])
        c_all, s_all, d_all = [
            spread_waves(waves, part, inner, kept, levels) for part in range(3)
        ]
        top = kept_high[...].reshape(4 * kept_items, columns)
        rest = kept_low[...].reshape(4 * kept_items, columns)
        nodal = dot(jnp.concatenate([top, rest, top], axis=1), spread[...])
        turned = []
        for f in range(4):
            part = nodal[f * kept_items : (f + 1) * kept_items]
            turned += [c_all * part, s_all * part]
        turned = split(jnp.concatenate(turned, axis=0))
        moved = dot(turned, own[...])
        sent = dot(turned, send[...])
        for f in range(4):
            at = 2 * f * kept_items
            local[f] = (
                s_all * moved[at : at + kept_items]
                - c_all * moved[at + kept_items : at + 2 * kept_items]
                + d_all * nodal[f * kept_items : (f + 1) * kept_items]
            )
        wide = lax.broadcasted_iota(jnp.int32, (kept_items, LANES), 1)
        for out, first, size in ((to_east, 0, NEAR), (to_west, NEAR, NEAR), (to_far, 2 * NEAR, FAR)):
            total = jnp.zeros((kept_items, LANES), F32)
            for g in range(8):
                part = sent[g * kept_items : (g + 1) * kept_items]
                turn = (size * g - first) % LANES
                if turn:
                    part = pltpu.roll(part, turn, 1)
                total = jnp.where((wide >= size * g) & (wide < size * (g + 1)), part, total)
            if size == NEAR:
                out[...] = total
            else:
                total = total.reshape(kept, 2, levels // 2, LANES)
                upper = pltpu.roll(total[:, 1].reshape(kept_items // 2, LANES), 64, 1)
                out[...] = total[:, 0].reshape(kept_items // 2, LANES) + upper


def finish_kernel(inner, count, *refs):
    fields = refs[:4]
    from_west, from_east, from_far, local, waves, take, gather = refs[4:11]
    outs = refs[15:19]
    new, sems = refs[19:]
    rows = fields[0].shape[0]
    levels, columns = new.shape[2], new.shape[3]
    items = count * levels

    @pl.when(is_polar())
    def _():
        place = lax.axis_index("lon")
        last = lax.axis_size("lon") - 1
        near_west = from_west[...] * jnp.where(place == 0, -1.0, 1.0)
        near_east = from_east[...] * jnp.where(place == last, -1.0, 1.0)
        far = from_far[...] * jnp.where(place < 2, -1.0, 1.0)
        far = far.reshape(count, 1, levels // 2, LANES)
        upper = pltpu.roll(far.reshape(items // 2, LANES), 64, 1).reshape(count, 1, levels // 2, LANES)
        far = jnp.concatenate([far, upper], axis=1).reshape(items, LANES)
        wide = lax.broadcasted_iota(jnp.int32, (items, LANES), 1)

        def turn(value, by):
            by = by % LANES
            return pltpu.roll(value, by, 1) if by else value

        come = []
        for g in range(8):
            part = jnp.where(wide < NEAR, turn(near_west, -NEAR * g), turn(near_east, NEAR - NEAR * g))
            part = jnp.where(wide < 2 * NEAR, part, turn(far, 2 * NEAR - FAR * g))
            part = jnp.where(wide < MESSAGE, part, 0.0)
            top = part.astype(BF16).astype(F32)
            come.append((top + turn(part - top, MESSAGE) + turn(top, 2 * MESSAGE)).astype(BF16))
        moved = dot(jnp.concatenate(come, axis=0), take[...])
        c_all, s_all = [spread_waves(waves, part, inner, count, levels) for part in range(2)]
        writes = []
        for half in range(2):
            value = []
            for f in (2 * half, 2 * half + 1):
                at = 2 * f * items
                value.append(
                    local[f] + (s_all * moved[at : at + items] - c_all * moved[at + items : at + 2 * items])
                )
            change = dot(split(jnp.concatenate(value, axis=0)), gather[...])
            change = change.reshape(2, count, levels, columns)
            pairs = []
            for f in (2 * half, 2 * half + 1):
                for n in range(count):
                    new[f, n] = fields[f][entry_row(inner, n, rows)] + change[f % 2, n]
                off_edge = rows - 6 if inner else 0
                if inner:
                    pairs.append((new.at[f, 0:off_edge], outs[f].at[3 : rows - 3]))
                for n in range(off_edge, count):
                    pairs.append((new.at[f, n], outs[f].at[entry_row(inner, n, rows)]))
            writes += start_all(pairs, sems, 12 * half)
        wait_all(writes)


def vmem():
    return pl.BlockSpec(memory_space=pltpu.VMEM)


def smem():
    return pl.BlockSpec(memory_space=pltpu.SMEM)


def anywhere():
    return pl.BlockSpec(memory_space=pl.ANY)


def like(*shape):
    return jax.ShapeDtypeStruct(shape, F32)


def in_hbm(value):
    return pltpu.with_memory_space_constraint(value, pltpu.HBM)


def params(mebibytes):
    return pltpu.CompilerParams(vmem_limit_bytes=mebibytes * 1024 * 1024)


def row_factors(count):
    latitude = (np.arange(count).astype(np.float32) + np.float32(0.5)) * np.float32(math.pi / count)
    latitude = latitude - np.float32(math.pi / 2)
    metric = np.float32(1.0) / np.cos(latitude)
    return metric.astype(np.float32), (np.float32(SPIN) * np.sin(latitude)).astype(np.float32)


def shards(u_wind, v_wind, theta, geopot, mass, cutoffs):
    rows, levels, columns = u_wind.shape
    lat_count = lax.axis_size("lat")
    lon_count = lax.axis_size("lon")
    tables = filter_tables(columns, columns * lon_count)
    tables = {k: jnp.asarray(v) for k, v in tables.items()}
    metric, spin = [jnp.asarray(t) for t in row_factors(rows * lat_count)]
    fields = (u_wind, v_wind, theta, geopot)

    strip = 12 * levels + 8
    edge_lines = 2 * levels + rows
    far_fields = [in_hbm(q) for q in (*fields, mass)]
    to_a, to_b, to_west, to_east, waves = pl.pallas_call(
        pack_kernel,
        out_shape=[like(strip, columns)] * 2 + [like(edge_lines, LANES)] * 2 + [like(3, rows, 8, NODES)],
        in_specs=[anywhere()] * 7,
        out_specs=[vmem()] * 5,
        scratch_shapes=[
            pltpu.VMEM((2, 4, rows, levels, LANES), F32),
            pltpu.VMEM((rows, columns), F32),
            pltpu.SMEM(cutoffs.shape, jnp.int32),
            pltpu.VMEM((1, NODES), F32),
            pltpu.SemaphoreType.DMA((35,)),
        ],
        compiler_params=params(8),
        name="pack_edges",
    )(*far_fields, in_hbm(cutoffs), in_hbm(tables["nodes"]))

    def ring(value, step):
        return lax.ppermute(value, "lon", [(i, (i + step) % lon_count) for i in range(lon_count)])

    west = ring(to_east, 1)
    east = ring(to_west, -1)
    odd_up = [(i, i + 1) for i in range(1, lat_count - 1, 2)]
    strip_a = lax.ppermute(to_a, "lat", [(i, i ^ 1) for i in range(lat_count)])
    strip_b = lax.ppermute(to_b, "lat", odd_up + [(j, i) for i, j in odd_up])

    at_poles = lat_count == 4
    inner_count = rows - 3 if at_poles else rows - 6
    edge_kept = 3 if at_poles else 6

    def tendencies(inner, old):
        count, kept = (inner_count, inner_count) if inner else (6, edge_kept)
        kept_items = kept * levels
        weights = [tables[k] for k in ("band", "spread", "own", "send")]
        if inner:
            weights = [in_hbm(w) for w in weights]
        halos = [] if inner else [strip_a, strip_b, *old[4:]]
        old = old[:4]
        args = [metric, spin, *fields, mass, west, east, waves, *halos, *weights]
        return pl.pallas_call(
            functools.partial(tend_kernel, inner, count, kept),
            out_shape=[like(rows, levels, columns)] * 4
            + [like(4, kept_items, NODES)]
            + [like(kept_items, LANES)] * 2
            + [like(kept_items // 2, LANES)]
            + [like(rows, 8, columns)] * inner,
            in_specs=[smem()] * 2
            + [vmem()] * (len(args) - 6)
            + [anywhere() if inner else vmem()] * 4
            + [anywhere()] * len(old),
            out_specs=[anywhere()] * 4 + [vmem()] * (4 + inner),
            scratch_shapes=[
                pltpu.VMEM((4, count, levels, columns + 2 * LANES), BF16),
                pltpu.VMEM((4, count, levels, columns + 2 * LANES), BF16),
                pltpu.VMEM((columns // LANES, 4, count, levels, 2 * LANES), F32),
                pltpu.VMEM((4, count, levels, columns), F32),
                pltpu.VMEM((4, kept, levels, columns), BF16),
                pltpu.VMEM((4, kept, levels, columns), BF16),
                pltpu.VMEM((rows, 8, columns), F32),
                pltpu.SemaphoreType.DMA((28,)),
                *[pltpu.VMEM(w.shape, w.dtype) for w in weights if inner],
            ],
            input_output_aliases={len(args) + f: f for f in range(4)} if old else {},
            compiler_params=params(40),
            cost_estimate=pl.CostEstimate(
                flops=count * levels * 4 * columns * 20000, bytes_accessed=2**22, transcendentals=0
            ),
            name="tend_inner" if inner else "tend_edge",
        )(*args, *old)

    quarter = lat_count // 4
    polar_bands = [*range(quarter), *range(lat_count - quarter, lat_count)]

    def polar_ring(value, step):
        pairs = []
        for band in polar_bands:
            first = band * lon_count
            pairs += [(first + i, first + (i + step) % lon_count) for i in range(lon_count)]
        return lax.ppermute(value, ("lat", "lon"), pairs)

    def exchange(east_part, west_part, far_part):
        return polar_ring(east_part, 1), polar_ring(west_part, -1), polar_ring(far_part, 2)

    def finish(inner, received, local, old):
        count = inner_count if inner else edge_kept
        weights = [tables[k] for k in ("take", "gather")]
        args = [*fields, *received, local, waves, *weights]
        return pl.pallas_call(
            functools.partial(finish_kernel, inner, count),
            out_shape=[like(rows, levels, columns)] * 4,
            in_specs=[vmem()] * len(args) + [anywhere()] * 4,
            out_specs=[anywhere()] * 4,
            scratch_shapes=[
                pltpu.VMEM((4, count, levels, columns), F32),
                pltpu.SemaphoreType.DMA((24,)),
            ],
            input_output_aliases={len(args) + f: f for f in range(4)},
            compiler_params=params(24),
            name="finish_inner" if inner else "finish_edge",
        )(*args, *old)

    *outs, local_inner, a, b, c, mass_x = tendencies(True, [])
    received_inner = exchange(a, b, c)
    outs = [*outs, mass_x]
    *outs, local_edge, a, b, c = tendencies(False, outs)
    received_edge = exchange(a, b, c)
    outs = finish(True, received_inner, local_inner, outs)
    outs = finish(False, received_edge, local_edge, outs)
    return tuple(outs)


def solution(mesh):
    return jax.shard_map(
        shards,
        mesh=mesh,
        in_specs=(
            P(("members", "lat"), None, "lon"),
            P(("members", "lat"), None, "lon"),
            P(("members", "lat"), None, "lon"),
            P(("members", "lat"), None, "lon"),
            P(("members", "lat"), "lon"),
            P(),
        ),
        out_specs=(
            P(("members", "lat"), None, "lon"),
            P(("members", "lat"), None, "lon"),
            P(("members", "lat"), None, "lon"),
            P(("members", "lat"), None, "lon"),
        ),
        check_vma=False,
    )
```

```python
import functools
import math

import jax
import jax.numpy as jnp
import ml_dtypes
import numpy as np
from jax import lax
from jax.experimental import pallas as pl
from jax.experimental.pallas import tpu as pltpu
from jax.sharding import PartitionSpec as P

STEP = 0.1
SPIN = 0.5
LANES = 128
NEAR = 16
FAR = 8
NODES = 256
F32 = jnp.float32
BF16 = jnp.bfloat16
MESSAGE = 2 * NEAR + FAR


def pivoted(matrix, count):
    rest = np.array(matrix)
    columns = rest.shape[1]
    tilt = 1.0 + 1e-3 * np.arange(columns) / columns
    picked = []
    tri = np.zeros((count, columns))
    for step in range(count):
        size = (rest * rest).sum(axis=0)
        best = int(np.argmax(size * tilt))
        picked.append(best)
        unit = rest[:, best] / math.sqrt(size[best])
        for _ in range(2):
            part = (unit[:, None] * rest).sum(axis=0)
            rest -= unit[:, None] * part[None, :]
            tri[step] += part
        rest[:, best] = 0.0
    left = tri[:, picked].copy()
    right = tri.copy()
    for step in range(count - 1, -1, -1):
        right[step] /= left[step, step]
        right[:step] -= left[:step, step][:, None] * right[step][None, :]
    right[:, picked] = np.eye(count)
    order = np.argsort(picked)
    return np.asarray(picked)[order], right[order]


def cauchy(target, source, circle):
    gap = target[:, None] - source[None, :]
    angle = np.where(gap == 0, 0.5 * math.pi, gap * math.pi / circle)
    return np.where(gap == 0, 0.0, 1.0 / (circle * np.sin(angle)))


def stacked_halves(table):
    table = table.astype(np.float32)
    high = table.astype(ml_dtypes.bfloat16)
    low = (table - high.astype(np.float32)).astype(ml_dtypes.bfloat16)
    return np.concatenate([high, high, low], axis=0)


def band_table():
    band = np.zeros((2 * LANES, 2 * LANES))
    slope = {-3: -1, -2: 9, -1: -45, 1: 45, 2: -9, 3: 1}
    smooth = {-3: 1, -2: -6, -1: 15, 0: -20, 1: 15, 2: -6, 3: 1}
    for j in range(LANES):
        for k, value in slope.items():
            band[j + 3 + k, j] = value
        for k, value in smooth.items():
            band[j + 3 + k, LANES + j] = value
    return np.concatenate([band, band], axis=0).astype(ml_dtypes.bfloat16)


@functools.lru_cache(maxsize=None)
def filter_tables(sector, circle):
    modes = circle // 8
    place = np.arange(sector)
    wave = np.arange(modes)
    phase = (wave[:, None] * place[None, :]) % circle * (2 * math.pi / circle)
    basis = np.concatenate([np.cos(phase), np.sin(phase[1:])], axis=0)
    nodes, spread = pivoted(basis, NODES)
    own = cauchy(nodes, nodes, circle)
    send = np.zeros((NODES, LANES))
    take = np.zeros((MESSAGE, NODES))
    at = 0
    for shift, count in ((sector, NEAR), (-sector, NEAR), (2 * sector, FAR)):
        kernel = cauchy(nodes + shift, nodes, circle)
        pick, weights = pivoted(kernel, count)
        send[:, at : at + count] = weights.T
        take[at : at + count] = kernel[:, pick].T
        at += count
    take = stacked_halves(take)
    take = np.concatenate([take, np.zeros((LANES - 3 * MESSAGE, NODES), take.dtype)], axis=0)
    return dict(
        nodes=nodes.astype(np.float32)[None],
        band=band_table(),
        spread=stacked_halves(spread.T),
        own=stacked_halves(np.concatenate([own.T, send, np.zeros((NODES, LANES))], axis=1)),
        take=take,
        gather=stacked_halves(STEP * spread),
    )


def split(value):
    high = value.astype(BF16)
    low = (value - high.astype(F32)).astype(BF16)
    return jnp.concatenate([high, low, high], axis=1)


def dot(a, b):
    return lax.dot_general(a, b, (((1,), (0,)), ((), ())), preferred_element_type=F32)


def start_all(pairs, sems, first=0):
    copies = [pltpu.make_async_copy(a, b, sems.at[first + n]) for n, (a, b) in enumerate(pairs)]
    for c in copies:
        c.start()
    return copies


def wait_all(copies):
    for c in copies:
        c.wait()


def is_polar():
    owner = lax.axis_index("lat")
    quarter = lax.axis_size("lat") // 4
    return (owner < quarter) | (owner >= lax.axis_size("lat") - quarter)


def edge_row(entry, rows):
    north = (lax.axis_index("lat") % 2 == 0) == (entry < 3)
    return jnp.where(north, rows - 1 - entry % 3, entry % 3)


def entry_row(inner, entry, rows):
    if not inner:
        return edge_row(entry, rows)
    if isinstance(entry, int):
        return entry + 3 if entry < rows - 6 else edge_row(entry - (rows - 6) + 3, rows)
    return jnp.where(entry < rows - 6, entry + 3, edge_row(entry - (rows - 6) + 3, rows))


def by_parity(even, odd):
    return jnp.where(lax.axis_index("lat") % 2 == 0, even, odd)


def pack_kernel(*refs):
    fields = refs[:4]
    mass, cutoffs_in, nodes_in, strip_a, strip_b, west, east, waves = refs[4:12]
    edge, own_mass, cutoffs, nodes, sems = refs[12:]
    rows, columns = mass.shape
    levels = edge.shape[3]
    tail = 12 * levels
    first = start_all([(cutoffs_in, cutoffs), (nodes_in, nodes)], sems, 33)
    small = start_all(
        [(mass, own_mass)]
        + [(q.at[:, :, 0:LANES], edge.at[0, f]) for f, q in enumerate(fields)]
        + [(q.at[:, :, columns - LANES : columns], edge.at[1, f]) for f, q in enumerate(fields)],
        sems,
    )
    pairs = []
    for entry in range(6):
        strip = strip_a if entry < 3 else strip_b
        row = edge_row(entry, rows)
        for f, q in enumerate(fields):
            pairs.append((q.at[row], strip.at[pl.ds(levels * (3 * f + entry % 3), levels)]))
    large = start_all(pairs, sems, 9)

    wait_all(first)
    lat_count = lax.axis_size("lat")
    lon_count = lax.axis_size("lon")
    owner = lax.axis_index("lat")
    circle = columns * lon_count
    start = jnp.where(owner < lat_count // 4, owner * rows, owner * rows - lat_count * rows // 2)
    start = jnp.clip(start, 0, lat_count * rows // 2 - rows)
    line = lax.broadcasted_iota(jnp.int32, (rows, NODES), 0)
    twice = jnp.zeros((rows, NODES), F32)
    for r in range(rows):
        twice = jnp.where(line == r, (2 * cutoffs[start + r] + 1).astype(F32), twice)
    place = nodes[...] + (lax.axis_index("lon") * columns).astype(F32)
    turns = twice * place
    angle = (turns - 2.0 * circle * jnp.floor(turns * (0.5 / circle))) * (math.pi / circle)
    for part, table in enumerate((jnp.cos(angle), jnp.sin(angle), twice * (1.0 / circle))):
        waves[part] = jnp.broadcast_to(table[:, None, :], (rows, 8, NODES))

    wait_all(small)
    north = jnp.concatenate([own_mass[rows - 1 - m : rows - m] for m in range(3)], axis=0)
    south = own_mass[0:3]
    for strip, lines in ((strip_a, by_parity(north, south)), (strip_b, by_parity(south, north))):
        strip[tail : tail + 3] = lines
        strip[tail + 3 : tail + 8] = jnp.zeros((5, columns), F32)
    lane = lax.broadcasted_iota(jnp.int32, (levels, LANES), 1)
    west[2 * levels :] = own_mass[:, 0:LANES]
    east[2 * levels :] = pltpu.roll(own_mass[:, columns - LANES : columns], 3, 1)
    for parity in range(2):
        for side, out in ((0, west), (1, east)):
            total = jnp.zeros((levels, LANES), F32)
            for r in range(parity, rows, 2):
                for f in range(4):
                    lead = 16 * (r // 2) + 3 * f
                    turn = lead if side == 0 else (lead + 3) % LANES
                    tile = edge[side, f, r]
                    if turn:
                        tile = pltpu.roll(tile, turn, 1)
                    total = jnp.where((lane >= lead) & (lane < lead + 3), tile, total)
            out[parity * levels : (parity + 1) * levels] = total
    wait_all(large)


def stencil(center, plus, minus):
    p1, p2, p3 = plus
    m1, m2, m3 = minus
    slope = 45.0 * (p1 - m1) - 9.0 * (p2 - m2) + (p3 - m3)
    smooth = (p3 + m3) - 6.0 * (p2 + m2) + 15.0 * (p1 + m1) - 20.0 * center
    return slope, smooth


def over_levels(value):
    return jnp.broadcast_to(value[:, None, :], (value.shape[0], 8, value.shape[1]))


def mass_slope_x(mass, west, east, levels):
    columns = mass.shape[1]
    middle = mass[...]
    wide = jnp.concatenate(
        [pltpu.roll(west[2 * levels :], LANES - 3, 1), middle, east[2 * levels :]], axis=1
    )
    whole = columns + 2 * LANES

    def at(k):
        return pltpu.roll(wide, (-k) % whole, 1)[:, LANES : LANES + columns]

    slope = stencil(middle, [at(1), at(2), at(3)], [at(-1), at(-2), at(-3)])[0]
    return over_levels(slope / (60.0 * middle))


def mass_slope_y(tall):
    size = tall.shape[0] - 6
    plus = [tall[3 + k : 3 + k + size] for k in (1, 2, 3)]
    minus = [tall[3 - k : 3 - k + size] for k in (1, 2, 3)]
    middle = tall[3 : 3 + size]
    return over_levels(stencil(middle, plus, minus)[0] / (60.0 * middle))


def spread_waves(waves, part, inner, kept, levels):
    rows = waves.shape[1]
    numbers = [entry_row(inner, entry, rows) for entry in range(kept)]
    return jnp.concatenate([waves[part, n] for n in numbers for _ in range(levels // 8)], axis=0)


def tend_kernel(inner, count, kept, metric, spin, *refs):
    edge_rows = not inner
    refs = list(refs)

    def some(n):
        taken = refs[:n]
        del refs[:n]
        return taken

    fields = some(4)
    mass, west, east, waves = some(4)
    strips = some(2) if edge_rows else None
    mass_x = some(1)[0] if edge_rows else None
    tables_in = some(3)
    if edge_rows:
        some(4)
    outs = some(4)
    local, to_east, to_west, to_far = some(4)
    mass_x = some(1)[0] if inner else mass_x
    high, low, cross, new, kept_parts, mass_y, sems = some(7)
    tables = refs if inner else tables_in
    band, spread, own = tables
    rows, columns = mass.shape
    levels = fields[0].shape[1]
    items = count * levels
    kept_items = kept * levels
    tiles = columns // LANES

    fetched = start_all(zip(tables_in, tables), sems, 24) if inner else []
    if edge_rows:
        tail = 12 * levels
        lines = [strip[tail : tail + 3] for strip in strips]
        upper = by_parity(lines[0], lines[1])
        lower = by_parity(lines[1], lines[0])
        lower = jnp.concatenate([lower[2:3], lower[1:2], lower[0:1]], axis=0)
        mass_y[0:3] = mass_slope_y(jnp.concatenate([lower, mass[0:6]], axis=0))
        mass_y[rows - 3 :] = mass_slope_y(jnp.concatenate([mass[rows - 6 :], upper], axis=0))
    else:
        blank = jnp.zeros((3, columns), F32)
        mass_x[...] = mass_slope_x(mass, west, east, levels)
        mass_y[...] = mass_slope_y(jnp.concatenate([blank, mass[...], blank], axis=0))

    lane = lax.broadcasted_iota(jnp.int32, (levels, LANES), 1)

    def cut(i, carry):
        row = entry_row(inner, i, rows)
        halo = pl.ds(pl.multiple_of((row % 2) * levels, levels), levels)
        for f in range(4):
            lead = 16 * (row // 2) + 3 * f
            before = pltpu.roll(west[halo, :], lax.rem(LANES - lead, LANES), 1)
            for t in range(tiles + 1):
                if t < tiles:
                    tile = pltpu.roll(fields[f][row, :, t * LANES : (t + 1) * LANES], 3, 1)
                else:
                    tile = pltpu.roll(east[halo, :], lax.rem(LANES + 3 - lead, LANES), 1)
                whole = jnp.where(lane < 3, before, tile)
                top = whole.astype(BF16)
                high[f, i, :, t * LANES : (t + 1) * LANES] = top
                low[f, i, :, t * LANES : (t + 1) * LANES] = (whole - top.astype(F32)).astype(BF16)
                before = tile
        return carry

    def slopes_x(first, size):
        lax.fori_loop(first, first + size, cut, 0)
        wait_all(fetched[:1])
        for t in range(tiles):
            span = slice(t * LANES, (t + 2) * LANES)
            some_rows = slice(first, first + size)
            both = jnp.concatenate(
                [
                    table[:, some_rows, :, span].reshape(4 * size * levels, 2 * LANES)
                    for table in (high, low)
                ],
                axis=1,
            )
            cross[t, :, some_rows] = dot(both, band[...]).reshape(4, size, levels, 2 * LANES)

    start_row = lax.axis_index("lat") * rows

    def whole(lines):
        return jnp.concatenate([lines] * (levels // 8), axis=0)

    def tendency(t, first, numbers, row_of, emit, inward=1.0):
        size = len(numbers)
        span = slice(t * LANES, (t + 1) * LANES)
        metrics = [metric[start_row + n] for n in numbers]
        spins = [spin[start_row + n] for n in numbers]
        centers = [[row_of(f, j, span) for j in range(size)] for f in range(3)]
        per_row = inward * (1.0 / 60.0)
        fast, fast_size, up, up_size = [], [], [], []
        for j in range(size):
            fast.append(centers[0][j] * (metrics[j] * (1.0 / 60.0)))
            fast_size.append(jnp.abs(fast[j]))
            up.append(centers[1][j] * per_row)
            up_size.append(jnp.abs(up[j]))
        push_x, push_y = [None] * size, [None] * size
        for f in (3, 0, 1, 2):
            column = [row_of(f, j, span) for j in range(-3, size + 3)]
            for j in range(size):
                q = column[j + 3]
                slope_x = cross[t, f, first + j, :, :LANES]
                smooth_x = cross[t, f, first + j, :, LANES:]
                slope_y, smooth_y = stencil(q, column[j + 4 : j + 7], column[j + 2 :: -1][:3])
                change = (fast_size[j] * smooth_x - fast[j] * slope_x) + (
                    up_size[j] * smooth_y - up[j] * slope_y
                )
                if f == 3:
                    theta = centers[2][j]
                    over_x = whole(mass_x[numbers[j], :, span])
                    over_y = whole(mass_y[numbers[j], :, span])
                    push_x[j] = metrics[j] * ((1.0 / 60.0) * slope_x + theta * over_x)
                    push_y[j] = per_row * slope_y + theta * over_y
                elif f == 0:
                    change = change + (spins[j] * centers[1][j] - push_x[j])
                elif f == 1:
                    change = change - (spins[j] * centers[0][j] + push_y[j])
                emit(f, first + j, span, q, change)

    def edge_side(side, first, emit):
        edge = edge_row(3 * side, rows)
        step = jnp.where(edge == 0, 1, -1)

        def row_of(f, j, span):
            if j >= 0:
                return fields[f][edge + step * j, :, span]
            if inner:
                return jnp.zeros((levels, LANES), F32)
            start = levels * (3 * f - j - 1)
            return strips[side][start : start + levels, span]

        numbers = [edge + step * j for j in range(3)]
        for t in range(tiles):
            tendency(t, first, numbers, row_of, emit, step.astype(F32))

    def inner_rows(emit):
        def step(n, carry):
            first_row = 3 + 2 * n

            def row_of(f, j, span):
                return fields[f][first_row + j, :, span]

            for t in range(tiles):
                tendency(t, 2 * n, [first_row, first_row + 1], row_of, emit)
            return carry

        lax.fori_loop(0, (rows - 6) // 2, step, 0)

    def write_out(f):
        if edge_rows:
            return [(new.at[f, n], outs[f].at[edge_row(n, rows)]) for n in range(6)]
        return [(new.at[f, 0 : rows - 6], outs[f].at[3 : rows - 3])]

    @pl.when(jnp.logical_not(is_polar()))
    def _():
        def emit(f, i, span, q, change):
            new[f, i, :, span] = q + STEP * change

        if inner:
            slopes_x(0, rows - 6)
            inner_rows(emit)
        else:
            slopes_x(0, 6)
            edge_side(0, 0, emit)
            edge_side(1, 3, emit)
        pairs = [pair for f in range(4) for pair in write_out(f)]
        wait_all(start_all(pairs, sems))
        wait_all(fetched[1:])

    @pl.when(is_polar())
    def _():
        def emit(f, i, span, q, change):
            top = change.astype(BF16)
            first = span.start
            kept_parts[f, i, :, first : first + LANES] = top
            kept_parts[f, i, :, 2 * columns + first : 2 * columns + first + LANES] = top
            rest = (change - top.astype(F32)).astype(BF16)
            kept_parts[f, i, :, columns + first : columns + first + LANES] = rest

        slopes_x(0, kept)
        if inner:
            inner_rows(emit)
            if kept > rows - 6:
                edge_side(1, rows - 6, emit)
        else:
            edge_side(0, 0, emit)
            if kept > 3:
                edge_side(1, 3, emit)
        wait_all(fetched[1:])
        c_all, s_all, d_all = [
            spread_waves(waves, part, inner, kept, levels) for part in range(3)
        ]
        nodal = dot(kept_parts[...].reshape(4 * kept_items, 3 * columns), spread[...])
        turned = []
        for f in range(4):
            part = nodal[f * kept_items : (f + 1) * kept_items]
            turned += [c_all * part, s_all * part]
        turned = split(jnp.concatenate(turned, axis=0))
        moved = dot(turned, own[...])
        sent = moved[:, NODES : NODES + LANES]
        moved = moved[:, :NODES]
        for f in range(4):
            at = 2 * f * kept_items
            local[f] = (
                s_all * moved[at : at + kept_items]
                - c_all * moved[at + kept_items : at + 2 * kept_items]
                + d_all * nodal[f * kept_items : (f + 1) * kept_items]
            )
        wide = lax.broadcasted_iota(jnp.int32, (kept_items, LANES), 1)
        for out, first, size in ((to_east, 0, NEAR), (to_west, NEAR, NEAR), (to_far, 2 * NEAR, FAR)):
            total = jnp.zeros((kept_items, LANES), F32)
            for g in range(8):
                part = sent[g * kept_items : (g + 1) * kept_items]
                turn = (size * g - first) % LANES
                if turn:
                    part = pltpu.roll(part, turn, 1)
                total = jnp.where((wide >= size * g) & (wide < size * (g + 1)), part, total)
            if size == NEAR:
                out[...] = total
            else:
                total = total.reshape(kept, 2, levels // 2, LANES)
                upper = pltpu.roll(total[:, 1].reshape(kept_items // 2, LANES), 64, 1)
                out[...] = total[:, 0].reshape(kept_items // 2, LANES) + upper


def finish_kernel(inner, count, *refs):
    fields = refs[:4]
    from_west, from_east, from_far, local, waves, take, gather = refs[4:11]
    outs = refs[15:19]
    new, sems = refs[19:]
    rows = fields[0].shape[0]
    levels, columns = new.shape[2], new.shape[3]
    items = count * levels

    @pl.when(is_polar())
    def _():
        place = lax.axis_index("lon")
        last = lax.axis_size("lon") - 1
        near_west = from_west[...] * jnp.where(place == 0, -1.0, 1.0)
        near_east = from_east[...] * jnp.where(place == last, -1.0, 1.0)
        far = from_far[...] * jnp.where(place < 2, -1.0, 1.0)
        far = far.reshape(count, 1, levels // 2, LANES)
        upper = pltpu.roll(far.reshape(items // 2, LANES), 64, 1).reshape(count, 1, levels // 2, LANES)
        far = jnp.concatenate([far, upper], axis=1).reshape(items, LANES)
        wide = lax.broadcasted_iota(jnp.int32, (items, LANES), 1)

        def turn(value, by):
            by = by % LANES
            return pltpu.roll(value, by, 1) if by else value

        come = []
        for g in range(8):
            part = jnp.where(wide < NEAR, turn(near_west, -NEAR * g), turn(near_east, NEAR - NEAR * g))
            part = jnp.where(wide < 2 * NEAR, part, turn(far, 2 * NEAR - FAR * g))
            part = jnp.where(wide < MESSAGE, part, 0.0)
            top = part.astype(BF16).astype(F32)
            come.append((top + turn(part - top, MESSAGE) + turn(top, 2 * MESSAGE)).astype(BF16))
        moved = dot(jnp.concatenate(come, axis=0), take[...])
        c_all, s_all = [spread_waves(waves, part, inner, count, levels) for part in range(2)]
        writes = []
        for half in range(2):
            value = []
            for f in (2 * half, 2 * half + 1):
                at = 2 * f * items
                value.append(
                    local[f] + (s_all * moved[at : at + items] - c_all * moved[at + items : at + 2 * items])
                )
            change = dot(split(jnp.concatenate(value, axis=0)), gather[...])
            change = change.reshape(2, count, levels, columns)
            pairs = []
            for f in (2 * half, 2 * half + 1):
                for n in range(count):
                    new[f, n] = fields[f][entry_row(inner, n, rows)] + change[f % 2, n]
                off_edge = rows - 6 if inner else 0
                if inner:
                    pairs.append((new.at[f, 0:off_edge], outs[f].at[3 : rows - 3]))
                for n in range(off_edge, count):
                    pairs.append((new.at[f, n], outs[f].at[entry_row(inner, n, rows)]))
            writes += start_all(pairs, sems, 12 * half)
        wait_all(writes)


def vmem():
    return pl.BlockSpec(memory_space=pltpu.VMEM)


def smem():
    return pl.BlockSpec(memory_space=pltpu.SMEM)


def anywhere():
    return pl.BlockSpec(memory_space=pl.ANY)


def like(*shape):
    return jax.ShapeDtypeStruct(shape, F32)


def in_hbm(value):
    return pltpu.with_memory_space_constraint(value, pltpu.HBM)


def params(mebibytes):
    return pltpu.CompilerParams(vmem_limit_bytes=mebibytes * 1024 * 1024)


def row_factors(count):
    latitude = (np.arange(count).astype(np.float32) + np.float32(0.5)) * np.float32(math.pi / count)
    latitude = latitude - np.float32(math.pi / 2)
    metric = np.float32(1.0) / np.cos(latitude)
    return metric.astype(np.float32), (np.float32(SPIN) * np.sin(latitude)).astype(np.float32)


def shards(u_wind, v_wind, theta, geopot, mass, cutoffs):
    rows, levels, columns = u_wind.shape
    lat_count = lax.axis_size("lat")
    lon_count = lax.axis_size("lon")
    tables = filter_tables(columns, columns * lon_count)
    tables = {k: jnp.asarray(v) for k, v in tables.items()}
    metric, spin = [jnp.asarray(t) for t in row_factors(rows * lat_count)]
    fields = (u_wind, v_wind, theta, geopot)

    strip = 12 * levels + 8
    edge_lines = 2 * levels + rows
    far_fields = [in_hbm(q) for q in (*fields, mass)]
    to_a, to_b, to_west, to_east, waves = pl.pallas_call(
        pack_kernel,
        out_shape=[like(strip, columns)] * 2 + [like(edge_lines, LANES)] * 2 + [like(3, rows, 8, NODES)],
        in_specs=[anywhere()] * 7,
        out_specs=[vmem()] * 5,
        scratch_shapes=[
            pltpu.VMEM((2, 4, rows, levels, LANES), F32),
            pltpu.VMEM((rows, columns), F32),
            pltpu.SMEM(cutoffs.shape, jnp.int32),
            pltpu.VMEM((1, NODES), F32),
            pltpu.SemaphoreType.DMA((35,)),
        ],
        compiler_params=params(8),
        name="pack_edges",
    )(*far_fields, in_hbm(cutoffs), in_hbm(tables["nodes"]))

    def ring(value, step):
        return lax.ppermute(value, "lon", [(i, (i + step) % lon_count) for i in range(lon_count)])

    west = ring(to_east, 1)
    east = ring(to_west, -1)
    odd_up = [(i, i + 1) for i in range(1, lat_count - 1, 2)]
    strip_a = lax.ppermute(to_a, "lat", [(i, i ^ 1) for i in range(lat_count)])
    strip_b = lax.ppermute(to_b, "lat", odd_up + [(j, i) for i, j in odd_up])

    at_poles = lat_count == 4
    inner_count = rows - 3 if at_poles else rows - 6
    edge_kept = 3 if at_poles else 6

    def tendencies(inner, old):
        count, kept = (inner_count, inner_count) if inner else (6, edge_kept)
        kept_items = kept * levels
        weights = [tables[k] for k in ("band", "spread", "own")]
        if inner:
            weights = [in_hbm(w) for w in weights]
        halos = [] if inner else [strip_a, strip_b, *old[4:]]
        old = old[:4]
        args = [metric, spin, *fields, mass, west, east, waves, *halos, *weights]
        return pl.pallas_call(
            functools.partial(tend_kernel, inner, count, kept),
            out_shape=[like(rows, levels, columns)] * 4
            + [like(4, kept_items, NODES)]
            + [like(kept_items, LANES)] * 2
            + [like(kept_items // 2, LANES)]
            + [like(rows, 8, columns)] * inner,
            in_specs=[smem()] * 2
            + [vmem()] * (len(args) - 5)
            + [anywhere() if inner else vmem()] * 3
            + [anywhere()] * len(old),
            out_specs=[anywhere()] * 4 + [vmem()] * (4 + inner),
            scratch_shapes=[
                pltpu.VMEM((4, count, levels, columns + LANES), BF16),
                pltpu.VMEM((4, count, levels, columns + LANES), BF16),
                pltpu.VMEM((columns // LANES, 4, count, levels, 2 * LANES), F32),
                pltpu.VMEM((4, count, levels, columns), F32),
                pltpu.VMEM((4, kept, levels, 3 * columns), BF16),
                pltpu.VMEM((rows, 8, columns), F32),
                pltpu.SemaphoreType.DMA((28,)),
                *[pltpu.VMEM(w.shape, w.dtype) for w in weights if inner],
            ],
            input_output_aliases={len(args) + f: f for f in range(4)} if old else {},
            compiler_params=params(40),
            cost_estimate=pl.CostEstimate(
                flops=count * levels * 4 * columns * 20000, bytes_accessed=2**22, transcendentals=0
            ),
            name="tend_inner" if inner else "tend_edge",
        )(*args, *old)

    def exchange(east_part, west_part, far_part):
        return ring(east_part, 1), ring(west_part, -1), ring(far_part, 2)

    def finish(inner, received, local, old):
        count = inner_count if inner else edge_kept
        weights = [tables[k] for k in ("take", "gather")]
        args = [*fields, *received, local, waves, *weights]
        return pl.pallas_call(
            functools.partial(finish_kernel, inner, count),
            out_shape=[like(rows, levels, columns)] * 4,
            in_specs=[vmem()] * len(args) + [anywhere()] * 4,
            out_specs=[anywhere()] * 4,
            scratch_shapes=[
                pltpu.VMEM((4, count, levels, columns), F32),
                pltpu.SemaphoreType.DMA((24,)),
            ],
            input_output_aliases={len(args) + f: f for f in range(4)},
            compiler_params=params(24),
            name="finish_inner" if inner else "finish_edge",
        )(*args, *old)

    *outs, local_inner, a, b, c, mass_x = tendencies(True, [])
    received_inner = exchange(a, b, c)
    outs = [*outs, mass_x]
    *outs, local_edge, a, b, c = tendencies(False, outs)
    received_edge = exchange(a, b, c)
    outs = finish(True, received_inner, local_inner, outs)
    outs = finish(False, received_edge, local_edge, outs)
    return tuple(outs)


def solution(mesh):
    return jax.shard_map(
        shards,
        mesh=mesh,
        in_specs=(
            P(("members", "lat"), None, "lon"),
            P(("members", "lat"), None, "lon"),
            P(("members", "lat"), None, "lon"),
            P(("members", "lat"), None, "lon"),
            P(("members", "lat"), "lon"),
            P(),
        ),
        out_specs=(
            P(("members", "lat"), None, "lon"),
            P(("members", "lat"), None, "lon"),
            P(("members", "lat"), None, "lon"),
            P(("members", "lat"), None, "lon"),
        ),
        check_vma=False,
    )
```

```python
import functools
import math

import jax
import jax.numpy as jnp
import ml_dtypes
import numpy as np
from jax import lax
from jax.experimental import pallas as pl
from jax.experimental.pallas import tpu as pltpu
from jax.sharding import PartitionSpec as P

STEP = 0.1
SPIN = 0.5
LANES = 128
NEAR = 16
FAR = 8
NODES = 256
F32 = jnp.float32
BF16 = jnp.bfloat16
MESSAGE = 2 * NEAR + FAR


def pivoted(matrix, count):
    rest = np.array(matrix)
    columns = rest.shape[1]
    tilt = 1.0 + 1e-3 * np.arange(columns) / columns
    picked = []
    tri = np.zeros((count, columns))
    for step in range(count):
        size = (rest * rest).sum(axis=0)
        best = int(np.argmax(size * tilt))
        picked.append(best)
        unit = rest[:, best] / math.sqrt(size[best])
        for _ in range(2):
            part = (unit[:, None] * rest).sum(axis=0)
            rest -= unit[:, None] * part[None, :]
            tri[step] += part
        rest[:, best] = 0.0
    left = tri[:, picked].copy()
    right = tri.copy()
    for step in range(count - 1, -1, -1):
        right[step] /= left[step, step]
        right[:step] -= left[:step, step][:, None] * right[step][None, :]
    right[:, picked] = np.eye(count)
    order = np.argsort(picked)
    return np.asarray(picked)[order], right[order]


def cauchy(target, source, circle):
    gap = target[:, None] - source[None, :]
    angle = np.where(gap == 0, 0.5 * math.pi, gap * math.pi / circle)
    return np.where(gap == 0, 0.0, 1.0 / (circle * np.sin(angle)))


def stacked_halves(table):
    table = table.astype(np.float32)
    high = table.astype(ml_dtypes.bfloat16)
    low = (table - high.astype(np.float32)).astype(ml_dtypes.bfloat16)
    return np.concatenate([high, high, low], axis=0)


def band_table():
    band = np.zeros((2 * LANES, 2 * LANES))
    slope = {-3: -1, -2: 9, -1: -45, 1: 45, 2: -9, 3: 1}
    smooth = {-3: 1, -2: -6, -1: 15, 0: -20, 1: 15, 2: -6, 3: 1}
    for j in range(LANES):
        for k, value in slope.items():
            band[j + 3 + k, j] = value
        for k, value in smooth.items():
            band[j + 3 + k, LANES + j] = value
    return np.concatenate([band, band], axis=0).astype(ml_dtypes.bfloat16)


@functools.lru_cache(maxsize=None)
def filter_tables(sector, circle):
    modes = circle // 8
    place = np.arange(sector)
    wave = np.arange(modes)
    phase = (wave[:, None] * place[None, :]) % circle * (2 * math.pi / circle)
    basis = np.concatenate([np.cos(phase), np.sin(phase[1:])], axis=0)
    nodes, spread = pivoted(basis, NODES)
    own = cauchy(nodes, nodes, circle)
    send = np.zeros((NODES, LANES))
    take = np.zeros((MESSAGE, NODES))
    at = 0
    for shift, count in ((sector, NEAR), (-sector, NEAR), (2 * sector, FAR)):
        kernel = cauchy(nodes + shift, nodes, circle)
        pick, weights = pivoted(kernel, count)
        send[:, at : at + count] = weights.T
        take[at : at + count] = kernel[:, pick].T
        at += count
    take = stacked_halves(take)
    take = np.concatenate([take, np.zeros((LANES - 3 * MESSAGE, NODES), take.dtype)], axis=0)
    return dict(
        nodes=nodes.astype(np.float32)[None],
        band=band_table(),
        spread=np.stack(
            [stacked_halves(spread.T[t : t + LANES]) for t in range(0, sector, LANES)]
        ),
        own=stacked_halves(np.concatenate([own.T, send, np.zeros((NODES, LANES))], axis=1)),
        take=take,
        gather=stacked_halves(STEP * spread),
    )


def split(value):
    high = value.astype(BF16)
    low = (value - high.astype(F32)).astype(BF16)
    return jnp.concatenate([high, low, high], axis=1)


def dot(a, b):
    return lax.dot_general(a, b, (((1,), (0,)), ((), ())), preferred_element_type=F32)


def start_all(pairs, sems, first=0):
    copies = [pltpu.make_async_copy(a, b, sems.at[first + n]) for n, (a, b) in enumerate(pairs)]
    for c in copies:
        c.start()
    return copies


def wait_all(copies):
    for c in copies:
        c.wait()


def is_polar():
    owner = lax.axis_index("lat")
    quarter = lax.axis_size("lat") // 4
    return (owner < quarter) | (owner >= lax.axis_size("lat") - quarter)


def edge_row(entry, rows):
    north = (lax.axis_index("lat") % 2 == 0) == (entry < 3)
    return jnp.where(north, rows - 1 - entry % 3, entry % 3)


def entry_row(inner, entry, rows):
    if not inner:
        return edge_row(entry, rows)
    if isinstance(entry, int):
        return entry + 3 if entry < rows - 6 else edge_row(entry - (rows - 6) + 3, rows)
    return jnp.where(entry < rows - 6, entry + 3, edge_row(entry - (rows - 6) + 3, rows))


def by_parity(even, odd):
    return jnp.where(lax.axis_index("lat") % 2 == 0, even, odd)


def pack_kernel(*refs):
    fields = refs[:4]
    mass, cutoffs_in, nodes_in, strip_a, strip_b, west, east, waves = refs[4:12]
    edge, own_mass, cutoffs, nodes, sems = refs[12:]
    rows, columns = mass.shape
    levels = edge.shape[3]
    tail = 12 * levels
    first = start_all([(cutoffs_in, cutoffs), (nodes_in, nodes)], sems, 33)
    small = start_all(
        [(mass, own_mass)]
        + [(q.at[:, :, 0:LANES], edge.at[0, f]) for f, q in enumerate(fields)]
        + [(q.at[:, :, columns - LANES : columns], edge.at[1, f]) for f, q in enumerate(fields)],
        sems,
    )
    pairs = []
    for entry in range(6):
        strip = strip_a if entry < 3 else strip_b
        row = edge_row(entry, rows)
        for f, q in enumerate(fields):
            pairs.append((q.at[row], strip.at[pl.ds(levels * (3 * f + entry % 3), levels)]))
    large = start_all(pairs, sems, 9)

    wait_all(first)
    lat_count = lax.axis_size("lat")
    lon_count = lax.axis_size("lon")
    owner = lax.axis_index("lat")
    circle = columns * lon_count
    start = jnp.where(owner < lat_count // 4, owner * rows, owner * rows - lat_count * rows // 2)
    start = jnp.clip(start, 0, lat_count * rows // 2 - rows)
    line = lax.broadcasted_iota(jnp.int32, (rows, NODES), 0)
    twice = jnp.zeros((rows, NODES), F32)
    for r in range(rows):
        twice = jnp.where(line == r, (2 * cutoffs[start + r] + 1).astype(F32), twice)
    place = nodes[...] + (lax.axis_index("lon") * columns).astype(F32)
    turns = twice * place
    angle = (turns - 2.0 * circle * jnp.floor(turns * (0.5 / circle))) * (math.pi / circle)
    for part, table in enumerate((jnp.cos(angle), jnp.sin(angle), twice * (1.0 / circle))):
        waves[part] = jnp.broadcast_to(table[:, None, :], (rows, 8, NODES))

    wait_all(small)
    north = jnp.concatenate([own_mass[rows - 1 - m : rows - m] for m in range(3)], axis=0)
    south = own_mass[0:3]
    for strip, lines in ((strip_a, by_parity(north, south)), (strip_b, by_parity(south, north))):
        strip[tail : tail + 3] = lines
        strip[tail + 3 : tail + 8] = jnp.zeros((5, columns), F32)
    lane = lax.broadcasted_iota(jnp.int32, (levels, LANES), 1)
    west[2 * levels :] = own_mass[:, 0:LANES]
    east[2 * levels :] = pltpu.roll(own_mass[:, columns - LANES : columns], 3, 1)
    for parity in range(2):
        for side, out in ((0, west), (1, east)):
            total = jnp.zeros((levels, LANES), F32)
            for r in range(parity, rows, 2):
                for f in range(4):
                    lead = 16 * (r // 2) + 3 * f
                    turn = lead if side == 0 else (lead + 3) % LANES
                    tile = edge[side, f, r]
                    if turn:
                        tile = pltpu.roll(tile, turn, 1)
                    total = jnp.where((lane >= lead) & (lane < lead + 3), tile, total)
            out[parity * levels : (parity + 1) * levels] = total
    wait_all(large)


def stencil(center, plus, minus):
    p1, p2, p3 = plus
    m1, m2, m3 = minus
    slope = 45.0 * (p1 - m1) - 9.0 * (p2 - m2) + (p3 - m3)
    smooth = (p3 + m3) - 6.0 * (p2 + m2) + 15.0 * (p1 + m1) - 20.0 * center
    return slope, smooth


def over_levels(value):
    return jnp.broadcast_to(value[:, None, :], (value.shape[0], 8, value.shape[1]))


def mass_slope_x(mass, west, east, levels):
    columns = mass.shape[1]
    middle = mass[...]
    wide = jnp.concatenate(
        [pltpu.roll(west[2 * levels :], LANES - 3, 1), middle, east[2 * levels :]], axis=1
    )
    whole = columns + 2 * LANES

    def at(k):
        return pltpu.roll(wide, (-k) % whole, 1)[:, LANES : LANES + columns]

    slope = stencil(middle, [at(1), at(2), at(3)], [at(-1), at(-2), at(-3)])[0]
    return over_levels(slope / (60.0 * middle))


def mass_slope_y(tall):
    size = tall.shape[0] - 6
    plus = [tall[3 + k : 3 + k + size] for k in (1, 2, 3)]
    minus = [tall[3 - k : 3 - k + size] for k in (1, 2, 3)]
    middle = tall[3 : 3 + size]
    return over_levels(stencil(middle, plus, minus)[0] / (60.0 * middle))


def spread_waves(waves, part, inner, kept, levels):
    rows = waves.shape[1]
    numbers = [entry_row(inner, entry, rows) for entry in range(kept)]
    return jnp.concatenate([waves[part, n] for n in numbers for _ in range(levels // 8)], axis=0)


def sizes_of_groups(inner, count):
    if not inner:
        return [3] * (count // 3)
    at_pole = 3 if count % 2 else 0
    half = (count - at_pole) // 2
    return [half, half] + [3] * (at_pole // 3)


def tend_kernel(inner, count, kept, metric, spin, *refs):
    edge_rows = not inner
    refs = list(refs)

    def some(n):
        taken = refs[:n]
        del refs[:n]
        return taken

    fields = some(4)
    mass, west, east, waves = some(4)
    strips = some(2) if edge_rows else None
    mass_x = some(1)[0] if edge_rows else None
    tables_in = some(3)
    if edge_rows:
        some(4)
    outs = some(4)
    local, to_east, to_west, to_far = some(4)
    mass_x = some(1)[0] if inner else mass_x
    high, low, new, mass_y, sems = some(5)
    group_sizes = sizes_of_groups(inner, count)
    crosses, kept_parts, nodals = [some(len(group_sizes)) for _ in range(3)]
    tables = refs if inner else tables_in
    band, spread, own = tables
    rows, columns = mass.shape
    levels = fields[0].shape[1]
    items = count * levels
    kept_items = kept * levels
    tiles = columns // LANES

    fetched = start_all(zip(tables_in, tables), sems, 24) if inner else []
    if edge_rows:
        tail = 12 * levels
        lines = [strip[tail : tail + 3] for strip in strips]
        upper = by_parity(lines[0], lines[1])
        lower = by_parity(lines[1], lines[0])
        lower = jnp.concatenate([lower[2:3], lower[1:2], lower[0:1]], axis=0)
        mass_y[0:3] = mass_slope_y(jnp.concatenate([lower, mass[0:6]], axis=0))
        mass_y[rows - 3 :] = mass_slope_y(jnp.concatenate([mass[rows - 6 :], upper], axis=0))
    else:
        blank = jnp.zeros((3, columns), F32)
        mass_x[...] = mass_slope_x(mass, west, east, levels)
        mass_y[...] = mass_slope_y(jnp.concatenate([blank, mass[...], blank], axis=0))

    lane = lax.broadcasted_iota(jnp.int32, (levels, LANES), 1)

    def cut(i, carry):
        row = entry_row(inner, i, rows)
        halo = pl.ds(pl.multiple_of((row % 2) * levels, levels), levels)
        for f in range(4):
            lead = 16 * (row // 2) + 3 * f
            before = pltpu.roll(west[halo, :], lax.rem(LANES - lead, LANES), 1)
            for t in range(tiles + 1):
                if t < tiles:
                    tile = pltpu.roll(fields[f][row, :, t * LANES : (t + 1) * LANES], 3, 1)
                else:
                    tile = pltpu.roll(east[halo, :], lax.rem(LANES + 3 - lead, LANES), 1)
                whole = jnp.where(lane < 3, before, tile)
                top = whole.astype(BF16)
                high[f, i, :, t * LANES : (t + 1) * LANES] = top
                low[f, i, :, t * LANES : (t + 1) * LANES] = (whole - top.astype(F32)).astype(BF16)
                before = tile
        return carry

    def columns_of(t, width=1):
        return pl.ds(pl.multiple_of(t * LANES, LANES), width * LANES)

    def slopes_x(g, first, t):
        size = group_sizes[g]
        parts = [
            table[:, first : first + size, :, columns_of(t, 2)].reshape(4 * size * levels, 2 * LANES)
            for table in (high, low)
        ]
        product = dot(jnp.concatenate(parts, axis=1), band[...])
        crosses[g][t] = product.reshape(4, size, levels, 2 * LANES)

    def to_nodes(g, t):
        size = group_sizes[g]
        part = dot(kept_parts[g][t].reshape(4 * size * levels, 3 * LANES), spread[t])
        nodals[g][...] += part.reshape(4, size * levels, NODES)

    start_row = lax.axis_index("lat") * rows

    def whole(lines):
        return jnp.concatenate([lines] * (levels // 8), axis=0)

    def tendency(t, g, first, numbers, row_of, emit, inward=1.0):
        size = len(numbers)
        span = columns_of(t)
        metrics = [metric[start_row + n] for n in numbers]
        spins = [spin[start_row + n] for n in numbers]
        centers = [[row_of(f, j, span) for j in range(size)] for f in range(3)]
        per_row = inward * (1.0 / 60.0)
        fast, fast_size, up, up_size = [], [], [], []
        for j in range(size):
            fast.append(centers[0][j] * (metrics[j] * (1.0 / 60.0)))
            fast_size.append(jnp.abs(fast[j]))
            up.append(centers[1][j] * per_row)
            up_size.append(jnp.abs(up[j]))
        push_x, push_y = [None] * size, [None] * size
        for f in (3, 0, 1, 2):
            column = [row_of(f, j, span) for j in range(-3, size + 3)]
            for j in range(size):
                q = column[j + 3]
                slope_x = crosses[g][t, f, j, :, :LANES]
                smooth_x = crosses[g][t, f, j, :, LANES:]
                slope_y, smooth_y = stencil(q, column[j + 4 : j + 7], column[j + 2 :: -1][:3])
                change = (fast_size[j] * smooth_x - fast[j] * slope_x) + (
                    up_size[j] * smooth_y - up[j] * slope_y
                )
                if f == 3:
                    theta = centers[2][j]
                    over_x = whole(mass_x[numbers[j], :, span])
                    over_y = whole(mass_y[numbers[j], :, span])
                    push_x[j] = metrics[j] * ((1.0 / 60.0) * slope_x + theta * over_x)
                    push_y[j] = per_row * slope_y + theta * over_y
                elif f == 0:
                    change = change + (spins[j] * centers[1][j] - push_x[j])
                elif f == 1:
                    change = change - (spins[j] * centers[0][j] + push_y[j])
                emit(g, f, j, first + j, t, q, change)

    def edge_group(side):
        edge = edge_row(3 * side, rows)
        step = jnp.where(edge == 0, 1, -1)

        def row_of(f, j, span):
            if j >= 0:
                return fields[f][edge + step * j, :, span]
            if inner:
                return jnp.zeros((levels, LANES), F32)
            start = levels * (3 * f - j - 1)
            return strips[side][start : start + levels, span]

        return [edge + step * j for j in range(3)], row_of, step.astype(F32)

    def inner_group(g):
        size = group_sizes[0]
        first_row = 3 + size * g

        def row_of(f, j, span):
            return fields[f][first_row + j, :, span]

        return [first_row + j for j in range(size)], row_of, 1.0

    def run(groups, emit, filtered):
        starts = [sum(group_sizes[:g]) for g in range(len(groups) + 1)]
        lax.fori_loop(0, starts[-1], cut, 0)
        wait_all(fetched[:1])

        def prepare(t, carry):
            slopes_x(0, 0, t)
            return carry

        lax.fori_loop(0, tiles, prepare, 0)
        if filtered:
            wait_all(fetched[1:])
        for g, (numbers, row_of, inward) in enumerate(groups):

            def step(t, carry):
                if g + 1 < len(groups):
                    slopes_x(g + 1, starts[g + 1], t)
                if filtered and g > 0:
                    to_nodes(g - 1, t)
                tendency(t, g, starts[g], numbers, row_of, emit, inward)
                return carry

            if filtered:
                nodals[g][...] = jnp.zeros(nodals[g].shape, F32)
            lax.fori_loop(0, tiles, step, 0)

        def complete(t, carry):
            to_nodes(len(groups) - 1, t)
            return carry

        if filtered:
            lax.fori_loop(0, tiles, complete, 0)

    def write_out(f):
        if edge_rows:
            return [(new.at[f, n], outs[f].at[edge_row(n, rows)]) for n in range(6)]
        return [(new.at[f, 0 : rows - 6], outs[f].at[3 : rows - 3])]

    @pl.when(jnp.logical_not(is_polar()))
    def _():
        def emit(g, f, j, i, t, q, change):
            new[f, i, :, columns_of(t)] = q + STEP * change

        groups = [inner_group(0), inner_group(1)] if inner else [edge_group(0), edge_group(1)]
        run(groups, emit, False)
        pairs = [pair for f in range(4) for pair in write_out(f)]
        wait_all(start_all(pairs, sems))
        wait_all(fetched[1:])

    @pl.when(is_polar())
    def _():
        def emit(g, f, j, i, t, q, change):
            top = change.astype(BF16)
            rest = (change - top.astype(F32)).astype(BF16)
            kept_parts[g][t, f, j] = jnp.concatenate([top, rest, top], axis=1)

        if inner:
            groups = [inner_group(0), inner_group(1)] + [edge_group(1)] * (kept > rows - 6)
        else:
            groups = [edge_group(side) for side in range(kept // 3)]
        run(groups, emit, True)
        c_all, s_all, d_all = [
            spread_waves(waves, part, inner, kept, levels) for part in range(3)
        ]
        nodal = [
            jnp.concatenate([nodals[g][f] for g in range(len(groups))], axis=0) for f in range(4)
        ]
        turned = []
        for f in range(4):
            turned += [c_all * nodal[f], s_all * nodal[f]]
        turned = split(jnp.concatenate(turned, axis=0))
        moved = dot(turned, own[...])
        sent = moved[:, NODES : NODES + LANES]
        moved = moved[:, :NODES]
        for f in range(4):
            at = 2 * f * kept_items
            local[f] = (
                s_all * moved[at : at + kept_items]
                - c_all * moved[at + kept_items : at + 2 * kept_items]
                + d_all * nodal[f]
            )
        wide = lax.broadcasted_iota(jnp.int32, (kept_items, LANES), 1)
        for out, first, size in ((to_east, 0, NEAR), (to_west, NEAR, NEAR), (to_far, 2 * NEAR, FAR)):
            total = jnp.zeros((kept_items, LANES), F32)
            for g in range(8):
                part = sent[g * kept_items : (g + 1) * kept_items]
                turn = (size * g - first) % LANES
                if turn:
                    part = pltpu.roll(part, turn, 1)
                total = jnp.where((wide >= size * g) & (wide < size * (g + 1)), part, total)
            if size == NEAR:
                out[...] = total
            else:
                total = total.reshape(kept, 2, levels // 2, LANES)
                upper = pltpu.roll(total[:, 1].reshape(kept_items // 2, LANES), 64, 1)
                out[...] = total[:, 0].reshape(kept_items // 2, LANES) + upper


def finish_kernel(inner, count, *refs):
    fields = refs[:4]
    from_west, from_east, from_far, local, waves, take, gather = refs[4:11]
    outs = refs[15:19]
    new, sems = refs[19:]
    rows = fields[0].shape[0]
    levels, columns = new.shape[2], new.shape[3]
    items = count * levels

    @pl.when(is_polar())
    def _():
        place = lax.axis_index("lon")
        last = lax.axis_size("lon") - 1
        near_west = from_west[...] * jnp.where(place == 0, -1.0, 1.0)
        near_east = from_east[...] * jnp.where(place == last, -1.0, 1.0)
        far = from_far[...] * jnp.where(place < 2, -1.0, 1.0)
        far = far.reshape(count, 1, levels // 2, LANES)
        upper = pltpu.roll(far.reshape(items // 2, LANES), 64, 1).reshape(count, 1, levels // 2, LANES)
        far = jnp.concatenate([far, upper], axis=1).reshape(items, LANES)
        wide = lax.broadcasted_iota(jnp.int32, (items, LANES), 1)

        def turn(value, by):
            by = by % LANES
            return pltpu.roll(value, by, 1) if by else value

        come = []
        for g in range(8):
            part = jnp.where(wide < NEAR, turn(near_west, -NEAR * g), turn(near_east, NEAR - NEAR * g))
            part = jnp.where(wide < 2 * NEAR, part, turn(far, 2 * NEAR - FAR * g))
            part = jnp.where(wide < MESSAGE, part, 0.0)
            top = part.astype(BF16).astype(F32)
            come.append((top + turn(part - top, MESSAGE) + turn(top, 2 * MESSAGE)).astype(BF16))
        moved = dot(jnp.concatenate(come, axis=0), take[...])
        c_all, s_all = [spread_waves(waves, part, inner, count, levels) for part in range(2)]
        writes = []
        for half in range(2):
            value = []
            for f in (2 * half, 2 * half + 1):
                at = 2 * f * items
                value.append(
                    local[f] + (s_all * moved[at : at + items] - c_all * moved[at + items : at + 2 * items])
                )
            change = dot(split(jnp.concatenate(value, axis=0)), gather[...])
            change = change.reshape(2, count, levels, columns)
            pairs = []
            for f in (2 * half, 2 * half + 1):
                for n in range(count):
                    new[f, n] = fields[f][entry_row(inner, n, rows)] + change[f % 2, n]
                off_edge = rows - 6 if inner else 0
                if inner:
                    pairs.append((new.at[f, 0:off_edge], outs[f].at[3 : rows - 3]))
                for n in range(off_edge, count):
                    pairs.append((new.at[f, n], outs[f].at[entry_row(inner, n, rows)]))
            writes += start_all(pairs, sems, 12 * half)
        wait_all(writes)


def vmem():
    return pl.BlockSpec(memory_space=pltpu.VMEM)


def smem():
    return pl.BlockSpec(memory_space=pltpu.SMEM)


def anywhere():
    return pl.BlockSpec(memory_space=pl.ANY)


def like(*shape):
    return jax.ShapeDtypeStruct(shape, F32)


def in_hbm(value):
    return pltpu.with_memory_space_constraint(value, pltpu.HBM)


def params(mebibytes):
    return pltpu.CompilerParams(vmem_limit_bytes=mebibytes * 1024 * 1024)


def row_factors(count):
    latitude = (np.arange(count).astype(np.float32) + np.float32(0.5)) * np.float32(math.pi / count)
    latitude = latitude - np.float32(math.pi / 2)
    metric = np.float32(1.0) / np.cos(latitude)
    return metric.astype(np.float32), (np.float32(SPIN) * np.sin(latitude)).astype(np.float32)


def shards(u_wind, v_wind, theta, geopot, mass, cutoffs):
    rows, levels, columns = u_wind.shape
    lat_count = lax.axis_size("lat")
    lon_count = lax.axis_size("lon")
    tables = filter_tables(columns, columns * lon_count)
    tables = {k: jnp.asarray(v) for k, v in tables.items()}
    metric, spin = [jnp.asarray(t) for t in row_factors(rows * lat_count)]
    fields = (u_wind, v_wind, theta, geopot)

    strip = 12 * levels + 8
    edge_lines = 2 * levels + rows
    far_fields = [in_hbm(q) for q in (*fields, mass)]
    to_a, to_b, to_west, to_east, waves = pl.pallas_call(
        pack_kernel,
        out_shape=[like(strip, columns)] * 2 + [like(edge_lines, LANES)] * 2 + [like(3, rows, 8, NODES)],
        in_specs=[anywhere()] * 7,
        out_specs=[vmem()] * 5,
        scratch_shapes=[
            pltpu.VMEM((2, 4, rows, levels, LANES), F32),
            pltpu.VMEM((rows, columns), F32),
            pltpu.SMEM(cutoffs.shape, jnp.int32),
            pltpu.VMEM((1, NODES), F32),
            pltpu.SemaphoreType.DMA((35,)),
        ],
        compiler_params=params(8),
        name="pack_edges",
    )(*far_fields, in_hbm(cutoffs), in_hbm(tables["nodes"]))

    def ring(value, step):
        return lax.ppermute(value, "lon", [(i, (i + step) % lon_count) for i in range(lon_count)])

    west = ring(to_east, 1)
    east = ring(to_west, -1)
    odd_up = [(i, i + 1) for i in range(1, lat_count - 1, 2)]
    strip_a = lax.ppermute(to_a, "lat", [(i, i ^ 1) for i in range(lat_count)])
    strip_b = lax.ppermute(to_b, "lat", odd_up + [(j, i) for i, j in odd_up])

    at_poles = lat_count == 4
    inner_count = rows - 3 if at_poles else rows - 6
    edge_kept = 3 if at_poles else 6

    def tendencies(inner, old):
        count, kept = (inner_count, inner_count) if inner else (6, edge_kept)
        kept_items = kept * levels
        tiles = columns // LANES
        group_sizes = sizes_of_groups(inner, count)
        weights = [tables[k] for k in ("band", "spread", "own")]
        if inner:
            weights = [in_hbm(w) for w in weights]
        halos = [] if inner else [strip_a, strip_b, *old[4:]]
        old = old[:4]
        args = [metric, spin, *fields, mass, west, east, waves, *halos, *weights]
        return pl.pallas_call(
            functools.partial(tend_kernel, inner, count, kept),
            out_shape=[like(rows, levels, columns)] * 4
            + [like(4, kept_items, NODES)]
            + [like(kept_items, LANES)] * 2
            + [like(kept_items // 2, LANES)]
            + [like(rows, 8, columns)] * inner,
            in_specs=[smem()] * 2
            + [vmem()] * (len(args) - 5)
            + [anywhere() if inner else vmem()] * 3
            + [anywhere()] * len(old),
            out_specs=[anywhere()] * 4 + [vmem()] * (4 + inner),
            scratch_shapes=[
                pltpu.VMEM((4, count, levels, columns + LANES), BF16),
                pltpu.VMEM((4, count, levels, columns + LANES), BF16),
                pltpu.VMEM((4, count, levels, columns), F32),
                pltpu.VMEM((rows, 8, columns), F32),
                pltpu.SemaphoreType.DMA((28,)),
                *[pltpu.VMEM((tiles, 4, n, levels, 2 * LANES), F32) for n in group_sizes],
                *[pltpu.VMEM((tiles, 4, n, levels, 3 * LANES), BF16) for n in group_sizes],
                *[pltpu.VMEM((4, n * levels, NODES), F32) for n in group_sizes],
                *[pltpu.VMEM(w.shape, w.dtype) for w in weights if inner],
            ],
            input_output_aliases={len(args) + f: f for f in range(4)} if old else {},
            compiler_params=params(40),
            cost_estimate=pl.CostEstimate(
                flops=count * levels * 4 * columns * 20000, bytes_accessed=2**22, transcendentals=0
            ),
            name="tend_inner" if inner else "tend_edge",
        )(*args, *old)

    def exchange(east_part, west_part, far_part):
        return ring(east_part, 1), ring(west_part, -1), ring(far_part, 2)

    def finish(inner, received, local, old):
        count = inner_count if inner else edge_kept
        weights = [tables[k] for k in ("take", "gather")]
        args = [*fields, *received, local, waves, *weights]
        return pl.pallas_call(
            functools.partial(finish_kernel, inner, count),
            out_shape=[like(rows, levels, columns)] * 4,
            in_specs=[vmem()] * len(args) + [anywhere()] * 4,
            out_specs=[anywhere()] * 4,
            scratch_shapes=[
                pltpu.VMEM((4, count, levels, columns), F32),
                pltpu.SemaphoreType.DMA((24,)),
            ],
            input_output_aliases={len(args) + f: f for f in range(4)},
            compiler_params=params(24),
            name="finish_inner" if inner else "finish_edge",
        )(*args, *old)

    *outs, local_inner, a, b, c, mass_x = tendencies(True, [])
    received_inner = exchange(a, b, c)
    outs = [*outs, mass_x]
    *outs, local_edge, a, b, c = tendencies(False, outs)
    received_edge = exchange(a, b, c)
    outs = finish(True, received_inner, local_inner, outs)
    outs = finish(False, received_edge, local_edge, outs)
    return tuple(outs)


def solution(mesh):
    return jax.shard_map(
        shards,
        mesh=mesh,
        in_specs=(
            P(("members", "lat"), None, "lon"),
            P(("members", "lat"), None, "lon"),
            P(("members", "lat"), None, "lon"),
            P(("members", "lat"), None, "lon"),
            P(("members", "lat"), "lon"),
            P(),
        ),
        out_specs=(
            P(("members", "lat"), None, "lon"),
            P(("members", "lat"), None, "lon"),
            P(("members", "lat"), None, "lon"),
            P(("members", "lat"), None, "lon"),
        ),
        check_vma=False,
    )
```

```python
import functools
import math

import jax
import jax.numpy as jnp
import ml_dtypes
import numpy as np
from jax import lax
from jax.experimental import pallas as pl
from jax.experimental.pallas import tpu as pltpu
from jax.sharding import PartitionSpec as P

STEP = 0.1
SPIN = 0.5
LANES = 128
NEAR = 16
FAR = 8
NODES = 256
F32 = jnp.float32
BF16 = jnp.bfloat16
MESSAGE = 2 * NEAR + FAR


def pivoted(matrix, count):
    rest = np.array(matrix)
    columns = rest.shape[1]
    tilt = 1.0 + 1e-3 * np.arange(columns) / columns
    picked = []
    tri = np.zeros((count, columns))
    for step in range(count):
        size = (rest * rest).sum(axis=0)
        best = int(np.argmax(size * tilt))
        picked.append(best)
        unit = rest[:, best] / math.sqrt(size[best])
        for _ in range(2):
            part = (unit[:, None] * rest).sum(axis=0)
            rest -= unit[:, None] * part[None, :]
            tri[step] += part
        rest[:, best] = 0.0
    left = tri[:, picked].copy()
    right = tri.copy()
    for step in range(count - 1, -1, -1):
        right[step] /= left[step, step]
        right[:step] -= left[:step, step][:, None] * right[step][None, :]
    right[:, picked] = np.eye(count)
    order = np.argsort(picked)
    return np.asarray(picked)[order], right[order]


def cauchy(target, source, circle):
    gap = target[:, None] - source[None, :]
    angle = np.where(gap == 0, 0.5 * math.pi, gap * math.pi / circle)
    return np.where(gap == 0, 0.0, 1.0 / (circle * np.sin(angle)))


def stacked_halves(table):
    table = table.astype(np.float32)
    high = table.astype(ml_dtypes.bfloat16)
    low = (table - high.astype(np.float32)).astype(ml_dtypes.bfloat16)
    return np.concatenate([high, high, low], axis=0)


def band_table():
    band = np.zeros((2 * LANES, 2 * LANES))
    slope = {-3: -1, -2: 9, -1: -45, 1: 45, 2: -9, 3: 1}
    smooth = {-3: 1, -2: -6, -1: 15, 0: -20, 1: 15, 2: -6, 3: 1}
    for j in range(LANES):
        for k, value in slope.items():
            band[j + 3 + k, j] = value
        for k, value in smooth.items():
            band[j + 3 + k, LANES + j] = value
    return np.concatenate([band, band], axis=0).astype(ml_dtypes.bfloat16)


@functools.lru_cache(maxsize=None)
def filter_tables(sector, circle):
    modes = circle // 8
    place = np.arange(sector)
    wave = np.arange(modes)
    phase = (wave[:, None] * place[None, :]) % circle * (2 * math.pi / circle)
    basis = np.concatenate([np.cos(phase), np.sin(phase[1:])], axis=0)
    nodes, spread = pivoted(basis, NODES)
    own = cauchy(nodes, nodes, circle)
    send = np.zeros((NODES, LANES))
    take = np.zeros((MESSAGE, NODES))
    at = 0
    for shift, count in ((sector, NEAR), (-sector, NEAR), (2 * sector, FAR)):
        kernel = cauchy(nodes + shift, nodes, circle)
        pick, weights = pivoted(kernel, count)
        send[:, at : at + count] = weights.T
        take[at : at + count] = kernel[:, pick].T
        at += count
    take = stacked_halves(take)
    take = np.concatenate([take, np.zeros((LANES - 3 * MESSAGE, NODES), take.dtype)], axis=0)
    return dict(
        nodes=nodes.astype(np.float32)[None],
        band=band_table(),
        spread=stacked_halves(spread.T),
        own=stacked_halves(np.concatenate([own.T, send, np.zeros((NODES, LANES))], axis=1)),
        take=take,
        gather=stacked_halves(STEP * spread),
    )


def split(value):
    high = value.astype(BF16)
    low = (value - high.astype(F32)).astype(BF16)
    return jnp.concatenate([high, low, high], axis=1)


def dot(a, b):
    return lax.dot_general(a, b, (((1,), (0,)), ((), ())), preferred_element_type=F32)


def start_all(pairs, sems, first=0):
    copies = [pltpu.make_async_copy(a, b, sems.at[first + n]) for n, (a, b) in enumerate(pairs)]
    for c in copies:
        c.start()
    return copies


def wait_all(copies):
    for c in copies:
        c.wait()


def is_polar():
    owner = lax.axis_index("lat")
    quarter = lax.axis_size("lat") // 4
    return (owner < quarter) | (owner >= lax.axis_size("lat") - quarter)


def edge_row(entry, rows):
    north = (lax.axis_index("lat") % 2 == 0) == (entry < 3)
    return jnp.where(north, rows - 1 - entry % 3, entry % 3)


def entry_row(inner, entry, rows):
    if not inner:
        return edge_row(entry, rows)
    if isinstance(entry, int):
        return entry + 3 if entry < rows - 6 else edge_row(entry - (rows - 6) + 3, rows)
    return jnp.where(entry < rows - 6, entry + 3, edge_row(entry - (rows - 6) + 3, rows))


def by_parity(even, odd):
    return jnp.where(lax.axis_index("lat") % 2 == 0, even, odd)


def pack_kernel(*refs):
    fields = refs[:4]
    mass, cutoffs_in, nodes_in, strip_a, strip_b, west, east, waves = refs[4:12]
    edge, own_mass, cutoffs, nodes, sems = refs[12:]
    rows, columns = mass.shape
    levels = edge.shape[3]
    tail = 12 * levels
    first = start_all([(cutoffs_in, cutoffs), (nodes_in, nodes)], sems, 33)
    small = start_all(
        [(mass, own_mass)]
        + [(q.at[:, :, 0:LANES], edge.at[0, f]) for f, q in enumerate(fields)]
        + [(q.at[:, :, columns - LANES : columns], edge.at[1, f]) for f, q in enumerate(fields)],
        sems,
    )
    pairs = []
    for entry in range(6):
        strip = strip_a if entry < 3 else strip_b
        row = edge_row(entry, rows)
        for f, q in enumerate(fields):
            pairs.append((q.at[row], strip.at[pl.ds(levels * (3 * f + entry % 3), levels)]))
    large = start_all(pairs, sems, 9)

    wait_all(first)
    lat_count = lax.axis_size("lat")
    lon_count = lax.axis_size("lon")
    owner = lax.axis_index("lat")
    circle = columns * lon_count
    start = jnp.where(owner < lat_count // 4, owner * rows, owner * rows - lat_count * rows // 2)
    start = jnp.clip(start, 0, lat_count * rows // 2 - rows)
    line = lax.broadcasted_iota(jnp.int32, (rows, NODES), 0)
    twice = jnp.zeros((rows, NODES), F32)
    for r in range(rows):
        twice = jnp.where(line == r, (2 * cutoffs[start + r] + 1).astype(F32), twice)
    place = nodes[...] + (lax.axis_index("lon") * columns).astype(F32)
    turns = twice * place
    angle = (turns - 2.0 * circle * jnp.floor(turns * (0.5 / circle))) * (math.pi / circle)
    for part, table in enumerate((jnp.cos(angle), jnp.sin(angle), twice * (1.0 / circle))):
        waves[part] = jnp.broadcast_to(table[:, None, :], (rows, 8, NODES))

    wait_all(small)
    north = jnp.concatenate([own_mass[rows - 1 - m : rows - m] for m in range(3)], axis=0)
    south = own_mass[0:3]
    for strip, lines in ((strip_a, by_parity(north, south)), (strip_b, by_parity(south, north))):
        strip[tail : tail + 3] = lines
        strip[tail + 3 : tail + 8] = jnp.zeros((5, columns), F32)
    lane = lax.broadcasted_iota(jnp.int32, (levels, LANES), 1)
    west[2 * levels :] = own_mass[:, 0:LANES]
    east[2 * levels :] = pltpu.roll(own_mass[:, columns - LANES : columns], 3, 1)
    for parity in range(2):
        for side, out in ((0, west), (1, east)):
            total = jnp.zeros((levels, LANES), F32)
            for r in range(parity, rows, 2):
                for f in range(4):
                    lead = 16 * (r // 2) + 3 * f
                    turn = lead if side == 0 else (lead + 3) % LANES
                    tile = edge[side, f, r]
                    if turn:
                        tile = pltpu.roll(tile, turn, 1)
                    total = jnp.where((lane >= lead) & (lane < lead + 3), tile, total)
            out[parity * levels : (parity + 1) * levels] = total
    wait_all(large)


def stencil(center, plus, minus):
    p1, p2, p3 = plus
    m1, m2, m3 = minus
    slope = 45.0 * (p1 - m1) - 9.0 * (p2 - m2) + (p3 - m3)
    smooth = (p3 + m3) - 6.0 * (p2 + m2) + 15.0 * (p1 + m1) - 20.0 * center
    return slope, smooth


def over_levels(value):
    return jnp.broadcast_to(value[:, None, :], (value.shape[0], 8, value.shape[1]))


def mass_slope_x(mass, west, east, levels):
    columns = mass.shape[1]
    middle = mass[...]
    wide = jnp.concatenate(
        [pltpu.roll(west[2 * levels :], LANES - 3, 1), middle, east[2 * levels :]], axis=1
    )
    whole = columns + 2 * LANES

    def at(k):
        return pltpu.roll(wide, (-k) % whole, 1)[:, LANES : LANES + columns]

    slope = stencil(middle, [at(1), at(2), at(3)], [at(-1), at(-2), at(-3)])[0]
    return over_levels(slope / (60.0 * middle))


def mass_slope_y(tall):
    size = tall.shape[0] - 6
    plus = [tall[3 + k : 3 + k + size] for k in (1, 2, 3)]
    minus = [tall[3 - k : 3 - k + size] for k in (1, 2, 3)]
    middle = tall[3 : 3 + size]
    return over_levels(stencil(middle, plus, minus)[0] / (60.0 * middle))


def spread_waves(waves, part, inner, kept, levels):
    rows = waves.shape[1]
    numbers = [entry_row(inner, entry, rows) for entry in range(kept)]
    return jnp.concatenate([waves[part, n] for n in numbers for _ in range(levels // 8)], axis=0)


def tend_kernel(inner, count, kept, metric, spin, *refs):
    edge_rows = not inner
    refs = list(refs)

    def some(n):
        taken = refs[:n]
        del refs[:n]
        return taken

    fields = some(4)
    mass, west, east, waves = some(4)
    strips = some(2) if edge_rows else None
    mass_x = some(1)[0] if edge_rows else None
    tables_in = some(3)
    if edge_rows:
        some(4)
    outs = some(4)
    local, to_east, to_west, to_far = some(4)
    mass_x = some(1)[0] if inner else mass_x
    high, low, new, kept_parts, mass_y, sems = some(6)
    crosses = some(mass.shape[1] // LANES)
    tables = refs if inner else tables_in
    band, spread, own = tables
    rows, columns = mass.shape
    levels = fields[0].shape[1]
    items = count * levels
    kept_items = kept * levels
    tiles = columns // LANES

    fetched = start_all(zip(tables_in, tables), sems, 24) if inner else []
    if edge_rows:
        tail = 12 * levels
        lines = [strip[tail : tail + 3] for strip in strips]
        upper = by_parity(lines[0], lines[1])
        lower = by_parity(lines[1], lines[0])
        lower = jnp.concatenate([lower[2:3], lower[1:2], lower[0:1]], axis=0)
        mass_y[0:3] = mass_slope_y(jnp.concatenate([lower, mass[0:6]], axis=0))
        mass_y[rows - 3 :] = mass_slope_y(jnp.concatenate([mass[rows - 6 :], upper], axis=0))
    else:
        blank = jnp.zeros((3, columns), F32)
        mass_x[...] = mass_slope_x(mass, west, east, levels)
        mass_y[...] = mass_slope_y(jnp.concatenate([blank, mass[...], blank], axis=0))

    lane = lax.broadcasted_iota(jnp.int32, (levels, LANES), 1)

    def cut(i, carry):
        row = entry_row(inner, i, rows)
        halo = pl.ds(pl.multiple_of((row % 2) * levels, levels), levels)
        for f in range(4):
            lead = 16 * (row // 2) + 3 * f
            before = pltpu.roll(west[halo, :], lax.rem(LANES - lead, LANES), 1)
            for t in range(tiles + 1):
                if t < tiles:
                    tile = pltpu.roll(fields[f][row, :, t * LANES : (t + 1) * LANES], 3, 1)
                else:
                    tile = pltpu.roll(east[halo, :], lax.rem(LANES + 3 - lead, LANES), 1)
                whole = jnp.where(lane < 3, before, tile)
                top = whole.astype(BF16)
                high[f, i, :, t * LANES : (t + 1) * LANES] = top
                low[f, i, :, t * LANES : (t + 1) * LANES] = (whole - top.astype(F32)).astype(BF16)
                before = tile
        return carry

    def slopes_x(t, size):
        span = slice(t * LANES, (t + 2) * LANES)
        parts = [table[:, 0:size, :, span].reshape(4 * size * levels, 2 * LANES) for table in (high, low)]
        product = dot(jnp.concatenate(parts, axis=1), band[...])
        crosses[t][:, 0:size] = product.reshape(4, size, levels, 2 * LANES)

    start_row = lax.axis_index("lat") * rows

    def whole(lines):
        return jnp.concatenate([lines] * (levels // 8), axis=0)

    def tendency(t, first, numbers, row_of, emit, inward=1.0):
        size = len(numbers)
        span = slice(t * LANES, (t + 1) * LANES)
        metrics = [metric[start_row + n] for n in numbers]
        spins = [spin[start_row + n] for n in numbers]
        centers = [[row_of(f, j, span) for j in range(size)] for f in range(3)]
        per_row = inward * (1.0 / 60.0)
        fast, fast_size, up, up_size = [], [], [], []
        for j in range(size):
            fast.append(centers[0][j] * (metrics[j] * (1.0 / 60.0)))
            fast_size.append(jnp.abs(fast[j]))
            up.append(centers[1][j] * per_row)
            up_size.append(jnp.abs(up[j]))
        push_x, push_y = [None] * size, [None] * size
        for f in (3, 0, 1, 2):
            column = [row_of(f, j, span) for j in range(-3, size + 3)]
            for j in range(size):
                q = column[j + 3]
                slope_x = crosses[t][f, first + j, :, :LANES]
                smooth_x = crosses[t][f, first + j, :, LANES:]
                slope_y, smooth_y = stencil(q, column[j + 4 : j + 7], column[j + 2 :: -1][:3])
                change = (fast_size[j] * smooth_x - fast[j] * slope_x) + (
                    up_size[j] * smooth_y - up[j] * slope_y
                )
                if f == 3:
                    theta = centers[2][j]
                    over_x = whole(mass_x[numbers[j], :, span])
                    over_y = whole(mass_y[numbers[j], :, span])
                    push_x[j] = metrics[j] * ((1.0 / 60.0) * slope_x + theta * over_x)
                    push_y[j] = per_row * slope_y + theta * over_y
                elif f == 0:
                    change = change + (spins[j] * centers[1][j] - push_x[j])
                elif f == 1:
                    change = change - (spins[j] * centers[0][j] + push_y[j])
                emit(f, first + j, span, q, change)

    def edge_group(side, first):
        edge = edge_row(3 * side, rows)
        step = jnp.where(edge == 0, 1, -1)

        def row_of(f, j, span):
            if j >= 0:
                return fields[f][edge + step * j, :, span]
            if inner:
                return jnp.zeros((levels, LANES), F32)
            start = levels * (3 * f - j - 1)
            return strips[side][start : start + levels, span]

        return first, [edge + step * j for j in range(3)], row_of, step.astype(F32)

    def inner_group(first, size):
        def row_of(f, j, span):
            return fields[f][3 + first + j, :, span]

        return first, [3 + first + j for j in range(size)], row_of, 1.0

    def run(groups, size, emit):
        lax.fori_loop(0, size, cut, 0)
        wait_all(fetched[:1])
        slopes_x(0, size)
        for t in range(tiles):
            if t + 1 < tiles:
                slopes_x(t + 1, size)
            for first, numbers, row_of, inward in groups:
                tendency(t, first, numbers, row_of, emit, inward)

    half = (rows - 6) // 2
    inner_groups = [inner_group(0, half), inner_group(half, rows - 6 - half)]

    def write_out(f):
        if edge_rows:
            return [(new.at[f, n], outs[f].at[edge_row(n, rows)]) for n in range(6)]
        return [(new.at[f, 0 : rows - 6], outs[f].at[3 : rows - 3])]

    @pl.when(jnp.logical_not(is_polar()))
    def _():
        def emit(f, i, span, q, change):
            new[f, i, :, span] = q + STEP * change

        if inner:
            run(inner_groups, rows - 6, emit)
        else:
            run([edge_group(0, 0), edge_group(1, 3)], 6, emit)
        pairs = [pair for f in range(4) for pair in write_out(f)]
        wait_all(start_all(pairs, sems))
        wait_all(fetched[1:])

    @pl.when(is_polar())
    def _():
        def emit(f, i, span, q, change):
            top = change.astype(BF16)
            first = span.start
            kept_parts[f, i, :, first : first + LANES] = top
            kept_parts[f, i, :, 2 * columns + first : 2 * columns + first + LANES] = top
            rest = (change - top.astype(F32)).astype(BF16)
            kept_parts[f, i, :, columns + first : columns + first + LANES] = rest

        if inner:
            run(inner_groups + [edge_group(1, rows - 6)] * (kept > rows - 6), kept, emit)
        else:
            run([edge_group(side, 3 * side) for side in range(kept // 3)], kept, emit)
        wait_all(fetched[1:])
        c_all, s_all, d_all = [
            spread_waves(waves, part, inner, kept, levels) for part in range(3)
        ]
        nodal = dot(kept_parts[...].reshape(4 * kept_items, 3 * columns), spread[...])
        turned = []
        for f in range(4):
            part = nodal[f * kept_items : (f + 1) * kept_items]
            turned += [c_all * part, s_all * part]
        turned = split(jnp.concatenate(turned, axis=0))
        moved = dot(turned, own[...])
        sent = moved[:, NODES : NODES + LANES]
        moved = moved[:, :NODES]
        for f in range(4):
            at = 2 * f * kept_items
            local[f] = (
                s_all * moved[at : at + kept_items]
                - c_all * moved[at + kept_items : at + 2 * kept_items]
                + d_all * nodal[f * kept_items : (f + 1) * kept_items]
            )
        wide = lax.broadcasted_iota(jnp.int32, (kept_items, LANES), 1)
        for out, first, size in ((to_east, 0, NEAR), (to_west, NEAR, NEAR), (to_far, 2 * NEAR, FAR)):
            total = jnp.zeros((kept_items, LANES), F32)
            for g in range(8):
                part = sent[g * kept_items : (g + 1) * kept_items]
                turn = (size * g - first) % LANES
                if turn:
                    part = pltpu.roll(part, turn, 1)
                total = jnp.where((wide >= size * g) & (wide < size * (g + 1)), part, total)
            if size == NEAR:
                out[...] = total
            else:
                total = total.reshape(kept, 2, levels // 2, LANES)
                upper = pltpu.roll(total[:, 1].reshape(kept_items // 2, LANES), 64, 1)
                out[...] = total[:, 0].reshape(kept_items // 2, LANES) + upper


def finish_kernel(inner, count, *refs):
    fields = refs[:4]
    from_west, from_east, from_far, local, waves, take, gather = refs[4:11]
    outs = refs[15:19]
    new, sems = refs[19:]
    rows = fields[0].shape[0]
    levels, columns = new.shape[2], new.shape[3]
    items = count * levels

    @pl.when(is_polar())
    def _():
        place = lax.axis_index("lon")
        last = lax.axis_size("lon") - 1
        near_west = from_west[...] * jnp.where(place == 0, -1.0, 1.0)
        near_east = from_east[...] * jnp.where(place == last, -1.0, 1.0)
        far = from_far[...] * jnp.where(place < 2, -1.0, 1.0)
        far = far.reshape(count, 1, levels // 2, LANES)
        upper = pltpu.roll(far.reshape(items // 2, LANES), 64, 1).reshape(count, 1, levels // 2, LANES)
        far = jnp.concatenate([far, upper], axis=1).reshape(items, LANES)
        wide = lax.broadcasted_iota(jnp.int32, (items, LANES), 1)

        def turn(value, by):
            by = by % LANES
            return pltpu.roll(value, by, 1) if by else value

        come = []
        for g in range(8):
            part = jnp.where(wide < NEAR, turn(near_west, -NEAR * g), turn(near_east, NEAR - NEAR * g))
            part = jnp.where(wide < 2 * NEAR, part, turn(far, 2 * NEAR - FAR * g))
            part = jnp.where(wide < MESSAGE, part, 0.0)
            top = part.astype(BF16).astype(F32)
            come.append((top + turn(part - top, MESSAGE) + turn(top, 2 * MESSAGE)).astype(BF16))
        moved = dot(jnp.concatenate(come, axis=0), take[...])
        c_all, s_all = [spread_waves(waves, part, inner, count, levels) for part in range(2)]
        writes = []
        for half in range(2):
            value = []
            for f in (2 * half, 2 * half + 1):
                at = 2 * f * items
                value.append(
                    local[f] + (s_all * moved[at : at + items] - c_all * moved[at + items : at + 2 * items])
                )
            change = dot(split(jnp.concatenate(value, axis=0)), gather[...])
            change = change.reshape(2, count, levels, columns)
            pairs = []
            for f in (2 * half, 2 * half + 1):
                for n in range(count):
                    new[f, n] = fields[f][entry_row(inner, n, rows)] + change[f % 2, n]
                off_edge = rows - 6 if inner else 0
                if inner:
                    pairs.append((new.at[f, 0:off_edge], outs[f].at[3 : rows - 3]))
                for n in range(off_edge, count):
                    pairs.append((new.at[f, n], outs[f].at[entry_row(inner, n, rows)]))
            writes += start_all(pairs, sems, 12 * half)
        wait_all(writes)


def vmem():
    return pl.BlockSpec(memory_space=pltpu.VMEM)


def smem():
    return pl.BlockSpec(memory_space=pltpu.SMEM)


def anywhere():
    return pl.BlockSpec(memory_space=pl.ANY)


def like(*shape):
    return jax.ShapeDtypeStruct(shape, F32)


def in_hbm(value):
    return pltpu.with_memory_space_constraint(value, pltpu.HBM)


def params(mebibytes):
    return pltpu.CompilerParams(vmem_limit_bytes=mebibytes * 1024 * 1024)


def row_factors(count):
    latitude = (np.arange(count).astype(np.float32) + np.float32(0.5)) * np.float32(math.pi / count)
    latitude = latitude - np.float32(math.pi / 2)
    metric = np.float32(1.0) / np.cos(latitude)
    return metric.astype(np.float32), (np.float32(SPIN) * np.sin(latitude)).astype(np.float32)


def shards(u_wind, v_wind, theta, geopot, mass, cutoffs):
    rows, levels, columns = u_wind.shape
    lat_count = lax.axis_size("lat")
    lon_count = lax.axis_size("lon")
    tables = filter_tables(columns, columns * lon_count)
    tables = {k: jnp.asarray(v) for k, v in tables.items()}
    metric, spin = [jnp.asarray(t) for t in row_factors(rows * lat_count)]
    fields = (u_wind, v_wind, theta, geopot)

    strip = 12 * levels + 8
    edge_lines = 2 * levels + rows
    far_fields = [in_hbm(q) for q in (*fields, mass)]
    to_a, to_b, to_west, to_east, waves = pl.pallas_call(
        pack_kernel,
        out_shape=[like(strip, columns)] * 2 + [like(edge_lines, LANES)] * 2 + [like(3, rows, 8, NODES)],
        in_specs=[anywhere()] * 7,
        out_specs=[vmem()] * 5,
        scratch_shapes=[
            pltpu.VMEM((2, 4, rows, levels, LANES), F32),
            pltpu.VMEM((rows, columns), F32),
            pltpu.SMEM(cutoffs.shape, jnp.int32),
            pltpu.VMEM((1, NODES), F32),
            pltpu.SemaphoreType.DMA((35,)),
        ],
        compiler_params=params(8),
        name="pack_edges",
    )(*far_fields, in_hbm(cutoffs), in_hbm(tables["nodes"]))

    def ring(value, step):
        return lax.ppermute(value, "lon", [(i, (i + step) % lon_count) for i in range(lon_count)])

    west = ring(to_east, 1)
    east = ring(to_west, -1)
    odd_up = [(i, i + 1) for i in range(1, lat_count - 1, 2)]
    strip_a = lax.ppermute(to_a, "lat", [(i, i ^ 1) for i in range(lat_count)])
    strip_b = lax.ppermute(to_b, "lat", odd_up + [(j, i) for i, j in odd_up])

    at_poles = lat_count == 4
    inner_count = rows - 3 if at_poles else rows - 6
    edge_kept = 3 if at_poles else 6

    def tendencies(inner, old):
        count, kept = (inner_count, inner_count) if inner else (6, edge_kept)
        kept_items = kept * levels
        weights = [tables[k] for k in ("band", "spread", "own")]
        if inner:
            weights = [in_hbm(w) for w in weights]
        halos = [] if inner else [strip_a, strip_b, *old[4:]]
        old = old[:4]
        args = [metric, spin, *fields, mass, west, east, waves, *halos, *weights]
        return pl.pallas_call(
            functools.partial(tend_kernel, inner, count, kept),
            out_shape=[like(rows, levels, columns)] * 4
            + [like(4, kept_items, NODES)]
            + [like(kept_items, LANES)] * 2
            + [like(kept_items // 2, LANES)]
            + [like(rows, 8, columns)] * inner,
            in_specs=[smem()] * 2
            + [vmem()] * (len(args) - 5)
            + [anywhere() if inner else vmem()] * 3
            + [anywhere()] * len(old),
            out_specs=[anywhere()] * 4 + [vmem()] * (4 + inner),
            scratch_shapes=[
                pltpu.VMEM((4, count, levels, columns + LANES), BF16),
                pltpu.VMEM((4, count, levels, columns + LANES), BF16),
                pltpu.VMEM((4, count, levels, columns), F32),
                pltpu.VMEM((4, kept, levels, 3 * columns), BF16),
                pltpu.VMEM((rows, 8, columns), F32),
                pltpu.SemaphoreType.DMA((28,)),
                *[pltpu.VMEM((4, count, levels, 2 * LANES), F32)] * (columns // LANES),
                *[pltpu.VMEM(w.shape, w.dtype) for w in weights if inner],
            ],
            input_output_aliases={len(args) + f: f for f in range(4)} if old else {},
            compiler_params=params(40),
            cost_estimate=pl.CostEstimate(
                flops=count * levels * 4 * columns * 20000, bytes_accessed=2**22, transcendentals=0
            ),
            name="tend_inner" if inner else "tend_edge",
        )(*args, *old)

    def exchange(east_part, west_part, far_part):
        return ring(east_part, 1), ring(west_part, -1), ring(far_part, 2)

    def finish(inner, received, local, old):
        count = inner_count if inner else edge_kept
        weights = [tables[k] for k in ("take", "gather")]
        args = [*fields, *received, local, waves, *weights]
        return pl.pallas_call(
            functools.partial(finish_kernel, inner, count),
            out_shape=[like(rows, levels, columns)] * 4,
            in_specs=[vmem()] * len(args) + [anywhere()] * 4,
            out_specs=[anywhere()] * 4,
            scratch_shapes=[
                pltpu.VMEM((4, count, levels, columns), F32),
                pltpu.SemaphoreType.DMA((24,)),
            ],
            input_output_aliases={len(args) + f: f for f in range(4)},
            compiler_params=params(24),
            name="finish_inner" if inner else "finish_edge",
        )(*args, *old)

    *outs, local_inner, a, b, c, mass_x = tendencies(True, [])
    received_inner = exchange(a, b, c)
    outs = [*outs, mass_x]
    *outs, local_edge, a, b, c = tendencies(False, outs)
    received_edge = exchange(a, b, c)
    outs = finish(True, received_inner, local_inner, outs)
    outs = finish(False, received_edge, local_edge, outs)
    return tuple(outs)


def solution(mesh):
    return jax.shard_map(
        shards,
        mesh=mesh,
        in_specs=(
            P(("members", "lat"), None, "lon"),
            P(("members", "lat"), None, "lon"),
            P(("members", "lat"), None, "lon"),
            P(("members", "lat"), None, "lon"),
            P(("members", "lat"), "lon"),
            P(),
        ),
        out_specs=(
            P(("members", "lat"), None, "lon"),
            P(("members", "lat"), None, "lon"),
            P(("members", "lat"), None, "lon"),
            P(("members", "lat"), None, "lon"),
        ),
        check_vma=False,
    )
```

```python
import functools
import math

import jax
import jax.numpy as jnp
import ml_dtypes
import numpy as np
from jax import lax
from jax.experimental import pallas as pl
from jax.experimental.pallas import tpu as pltpu
from jax.sharding import PartitionSpec as P

STEP = 0.1
SPIN = 0.5
LANES = 128
NEAR = 16
FAR = 8
NODES = 256
F32 = jnp.float32
BF16 = jnp.bfloat16
MESSAGE = 2 * NEAR + FAR


def pivoted(matrix, count):
    rest = np.array(matrix)
    columns = rest.shape[1]
    tilt = 1.0 + 1e-3 * np.arange(columns) / columns
    picked = []
    tri = np.zeros((count, columns))
    for step in range(count):
        size = (rest * rest).sum(axis=0)
        best = int(np.argmax(size * tilt))
        picked.append(best)
        unit = rest[:, best] / math.sqrt(size[best])
        for _ in range(2):
            part = (unit[:, None] * rest).sum(axis=0)
            rest -= unit[:, None] * part[None, :]
            tri[step] += part
        rest[:, best] = 0.0
    left = tri[:, picked].copy()
    right = tri.copy()
    for step in range(count - 1, -1, -1):
        right[step] /= left[step, step]
        right[:step] -= left[:step, step][:, None] * right[step][None, :]
    right[:, picked] = np.eye(count)
    order = np.argsort(picked)
    return np.asarray(picked)[order], right[order]


def cauchy(target, source, circle):
    gap = target[:, None] - source[None, :]
    angle = np.where(gap == 0, 0.5 * math.pi, gap * math.pi / circle)
    return np.where(gap == 0, 0.0, 1.0 / (circle * np.sin(angle)))


def stacked_halves(table):
    table = table.astype(np.float32)
    high = table.astype(ml_dtypes.bfloat16)
    low = (table - high.astype(np.float32)).astype(ml_dtypes.bfloat16)
    return np.concatenate([high, high, low], axis=0)


def band_table():
    band = np.zeros((2 * LANES, 2 * LANES))
    slope = {-3: -1, -2: 9, -1: -45, 1: 45, 2: -9, 3: 1}
    smooth = {-3: 1, -2: -6, -1: 15, 0: -20, 1: 15, 2: -6, 3: 1}
    for j in range(LANES):
        for k, value in slope.items():
            band[j + 3 + k, j] = value
        for k, value in smooth.items():
            band[j + 3 + k, LANES + j] = value
    return np.concatenate([band, band], axis=0).astype(ml_dtypes.bfloat16)


@functools.lru_cache(maxsize=None)
def filter_tables(sector, circle):
    modes = circle // 8
    place = np.arange(sector)
    wave = np.arange(modes)
    phase = (wave[:, None] * place[None, :]) % circle * (2 * math.pi / circle)
    basis = np.concatenate([np.cos(phase), np.sin(phase[1:])], axis=0)
    nodes, spread = pivoted(basis, NODES)
    own = cauchy(nodes, nodes, circle)
    send = np.zeros((NODES, LANES))
    take = np.zeros((MESSAGE, NODES))
    at = 0
    for shift, count in ((sector, NEAR), (-sector, NEAR), (2 * sector, FAR)):
        kernel = cauchy(nodes + shift, nodes, circle)
        pick, weights = pivoted(kernel, count)
        send[:, at : at + count] = weights.T
        take[at : at + count] = kernel[:, pick].T
        at += count
    take = stacked_halves(take)
    take = np.concatenate([take, np.zeros((LANES - 3 * MESSAGE, NODES), take.dtype)], axis=0)
    return dict(
        nodes=nodes.astype(np.float32)[None],
        band=band_table(),
        spread=stacked_halves(spread.T),
        own=stacked_halves(np.concatenate([own.T, send, np.zeros((NODES, LANES))], axis=1)),
        take=take,
        gather=stacked_halves(STEP * spread),
    )


def split(value):
    high = value.astype(BF16)
    low = (value - high.astype(F32)).astype(BF16)
    return jnp.concatenate([high, low, high], axis=1)


def dot(a, b):
    return lax.dot_general(a, b, (((1,), (0,)), ((), ())), preferred_element_type=F32)


def start_all(pairs, sems, first=0):
    copies = [pltpu.make_async_copy(a, b, sems.at[first + n]) for n, (a, b) in enumerate(pairs)]
    for c in copies:
        c.start()
    return copies


def wait_all(copies):
    for c in copies:
        c.wait()


def is_polar():
    owner = lax.axis_index("lat")
    quarter = lax.axis_size("lat") // 4
    return (owner < quarter) | (owner >= lax.axis_size("lat") - quarter)


def edge_row(entry, rows):
    north = (lax.axis_index("lat") % 2 == 0) == (entry < 3)
    return jnp.where(north, rows - 1 - entry % 3, entry % 3)


def entry_row(sides, entry, rows):
    if sides:
        return edge_row(entry + 3 * sides[0], rows)
    if isinstance(entry, int):
        return entry + 3 if entry < rows - 6 else edge_row((entry - (rows - 6) + 3) % 6, rows)
    return jnp.where(entry < rows - 6, entry + 3, edge_row((entry - (rows - 6) + 3) % 6, rows))


def by_parity(even, odd):
    return jnp.where(lax.axis_index("lat") % 2 == 0, even, odd)


def pack_kernel(*refs):
    fields = refs[:4]
    mass, cutoffs_in, nodes_in, strip_a, strip_b, west, east, waves = refs[4:12]
    edge, own_mass, cutoffs, nodes, sems = refs[12:]
    rows, columns = mass.shape
    levels = edge.shape[3]
    tail = 12 * levels
    first = start_all([(cutoffs_in, cutoffs), (nodes_in, nodes)], sems, 33)
    small = start_all(
        [(mass, own_mass)]
        + [(q.at[:, :, 0:LANES], edge.at[0, f]) for f, q in enumerate(fields)]
        + [(q.at[:, :, columns - LANES : columns], edge.at[1, f]) for f, q in enumerate(fields)],
        sems,
    )
    pairs = []
    for entry in range(6):
        strip = strip_a if entry < 3 else strip_b
        row = edge_row(entry, rows)
        for f, q in enumerate(fields):
            pairs.append((q.at[row], strip.at[pl.ds(levels * (3 * f + entry % 3), levels)]))
    large = start_all(pairs, sems, 9)

    wait_all(first)
    lat_count = lax.axis_size("lat")
    lon_count = lax.axis_size("lon")
    owner = lax.axis_index("lat")
    circle = columns * lon_count
    start = jnp.where(owner < lat_count // 4, owner * rows, owner * rows - lat_count * rows // 2)
    start = jnp.clip(start, 0, lat_count * rows // 2 - rows)
    line = lax.broadcasted_iota(jnp.int32, (rows, NODES), 0)
    twice = jnp.zeros((rows, NODES), F32)
    for r in range(rows):
        twice = jnp.where(line == r, (2 * cutoffs[start + r] + 1).astype(F32), twice)
    place = nodes[...] + (lax.axis_index("lon") * columns).astype(F32)
    turns = twice * place
    angle = (turns - 2.0 * circle * jnp.floor(turns * (0.5 / circle))) * (math.pi / circle)
    for part, table in enumerate((jnp.cos(angle), jnp.sin(angle), twice * (1.0 / circle))):
        waves[part] = jnp.broadcast_to(table[:, None, :], (rows, 8, NODES))

    wait_all(small)
    north = jnp.concatenate([own_mass[rows - 1 - m : rows - m] for m in range(3)], axis=0)
    south = own_mass[0:3]
    for strip, lines in ((strip_a, by_parity(north, south)), (strip_b, by_parity(south, north))):
        strip[tail : tail + 3] = lines
        strip[tail + 3 : tail + 8] = jnp.zeros((5, columns), F32)
    lane = lax.broadcasted_iota(jnp.int32, (levels, LANES), 1)
    west[2 * levels :] = own_mass[:, 0:LANES]
    east[2 * levels :] = pltpu.roll(own_mass[:, columns - LANES : columns], 3, 1)
    for parity in range(2):
        for side, out in ((0, west), (1, east)):
            total = jnp.zeros((levels, LANES), F32)
            for r in range(parity, rows, 2):
                for f in range(4):
                    lead = 16 * (r // 2) + 3 * f
                    turn = lead if side == 0 else (lead + 3) % LANES
                    tile = edge[side, f, r]
                    if turn:
                        tile = pltpu.roll(tile, turn, 1)
                    total = jnp.where((lane >= lead) & (lane < lead + 3), tile, total)
            out[parity * levels : (parity + 1) * levels] = total
    wait_all(large)


def stencil(center, plus, minus):
    p1, p2, p3 = plus
    m1, m2, m3 = minus
    slope = 45.0 * (p1 - m1) - 9.0 * (p2 - m2) + (p3 - m3)
    smooth = (p3 + m3) - 6.0 * (p2 + m2) + 15.0 * (p1 + m1) - 20.0 * center
    return slope, smooth


def over_levels(value):
    return jnp.broadcast_to(value[:, None, :], (value.shape[0], 8, value.shape[1]))


def mass_slope_x(mass, west, east, levels):
    columns = mass.shape[1]
    middle = mass[...]
    wide = jnp.concatenate(
        [pltpu.roll(west[2 * levels :], LANES - 3, 1), middle, east[2 * levels :]], axis=1
    )
    whole = columns + 2 * LANES

    def at(k):
        return pltpu.roll(wide, (-k) % whole, 1)[:, LANES : LANES + columns]

    slope = stencil(middle, [at(1), at(2), at(3)], [at(-1), at(-2), at(-3)])[0]
    return over_levels(slope / (60.0 * middle))


def mass_slope_y(tall):
    size = tall.shape[0] - 6
    plus = [tall[3 + k : 3 + k + size] for k in (1, 2, 3)]
    minus = [tall[3 - k : 3 - k + size] for k in (1, 2, 3)]
    middle = tall[3 : 3 + size]
    return over_levels(stencil(middle, plus, minus)[0] / (60.0 * middle))


def spread_waves(waves, part, sides, kept, levels):
    rows = waves.shape[1]
    numbers = [entry_row(sides, entry, rows) for entry in range(kept)]
    return jnp.concatenate([waves[part, n] for n in numbers for _ in range(levels // 8)], axis=0)


PAIRS = ((3, 0), (1, 2))


def tend_kernel(sides, count, kept, metric, spin, *refs):
    inner = not sides
    refs = list(refs)

    def some(n):
        taken = refs[:n]
        del refs[:n]
        return taken

    fields = some(4)
    mass, west, east, waves = some(4)
    strips = dict(zip(sides, some(len(sides))))
    mass_x, edge_cross = (None, None) if inner else some(2)
    tables_in = some(3)
    if not inner:
        some(2 if kept else 0)
        some(4)
    outs = some(4)
    if kept:
        local, to_east, to_west, to_far = some(4)
    mass_x, edge_cross = some(2) if inner else (mass_x, edge_cross)
    new, mass_y, push, sems = some(4)
    kept_parts = some(2) if kept else None
    if inner:
        high, low, cross_all = some(3)
        crosses = some(mass.shape[1] // LANES)
    tables = refs if inner else tables_in
    band, spread, own = tables
    rows, columns = mass.shape
    levels = fields[0].shape[1]
    kept_items = kept * levels
    tiles = columns // LANES

    fetched = start_all(zip(tables_in, tables), sems, 24) if inner else []
    if inner:
        blank = jnp.zeros((3, columns), F32)
        mass_x[...] = mass_slope_x(mass, west, east, levels)
        mass_y[...] = mass_slope_y(jnp.concatenate([blank, mass[...], blank], axis=0))

    def edge_mass():
        for n, side in enumerate(sides):
            lines = [strips[side][12 * levels + m : 12 * levels + m + 1] for m in (2, 1, 0)]
            north = edge_row(3 * side, rows) != 0
            for m in range(6):
                lines.append(jnp.where(north, mass[rows - 1 - m : rows - m], mass[m : m + 1]))
            slope = mass_slope_y(jnp.concatenate(lines, axis=0))
            mass_y[3 * n : 3 * n + 3] = slope * jnp.where(north, -1.0, 1.0)

    lane = lax.broadcasted_iota(jnp.int32, (levels, LANES), 1)

    def cut(i, carry):
        row = entry_row(sides, i, rows)
        halo = pl.ds(pl.multiple_of((row % 2) * levels, levels), levels)
        for f in range(4):
            lead = 16 * (row // 2) + 3 * f
            before = pltpu.roll(west[halo, :], lax.rem(LANES - lead, LANES), 1)
            for t in range(tiles + 1):
                if t < tiles:
                    tile = pltpu.roll(fields[f][row, :, t * LANES : (t + 1) * LANES], 3, 1)
                else:
                    tile = pltpu.roll(east[halo, :], lax.rem(LANES + 3 - lead, LANES), 1)
                whole = jnp.where(lane < 3, before, tile)
                top = whole.astype(BF16)
                high[f, i, :, t * LANES : (t + 1) * LANES] = top
                low[f, i, :, t * LANES : (t + 1) * LANES] = (whole - top.astype(F32)).astype(BF16)
                before = tile
        return carry

    def columns_of(t, width=1):
        if isinstance(t, int):
            return slice(t * LANES, (t + width) * LANES)
        return pl.ds(pl.multiple_of(t * LANES, LANES), width * LANES)

    def slopes_x(t):
        span = columns_of(t, 2)
        parts = [table[:, :, :, span].reshape(4 * rows * levels, 2 * LANES) for table in (high, low)]
        product = dot(jnp.concatenate(parts, axis=1), band[...]).reshape(4, rows, levels, 2 * LANES)
        if isinstance(t, int):
            crosses[t][...] = product[:, : rows - 6]
        else:
            cross_all[t] = product[:, : rows - 6]
        edge_cross[t] = product[:, rows - 6 :]

    def cross_of(t, f, entry):
        if inner and entry < rows - 6:
            return (crosses[t], (f, entry)) if isinstance(t, int) else (cross_all, (t, f, entry))
        if inner:
            return edge_cross, (t, f, entry - (rows - 6))
        return edge_cross, (t, f, (entry + 3 * sides[0] + 3) % 6)

    start_row = lax.axis_index("lat") * rows

    def whole(lines):
        return jnp.concatenate([lines] * (levels // 8), axis=0)

    def tendency(pair, t, first, numbers, lines, row_of, emit, inward=1.0):
        size = len(numbers)
        span = columns_of(t)
        metrics = [metric[start_row + n] for n in numbers]
        spins = [spin[start_row + n] for n in numbers]
        centers = [[row_of(f, j, span) for j in range(size)] for f in range(3)]
        per_row = inward * (1.0 / 60.0)
        fast, fast_size, up, up_size = [], [], [], []
        for j in range(size):
            fast.append(centers[0][j] * (metrics[j] * (1.0 / 60.0)))
            fast_size.append(jnp.abs(fast[j]))
            up.append(centers[1][j] * per_row)
            up_size.append(jnp.abs(up[j]))
        push_x = [None] * size
        for f in PAIRS[pair]:
            column = [row_of(f, j, span) for j in range(-3, size + 3)]
            for j in range(size):
                q = column[j + 3]
                table, place = cross_of(t, f, first + j)
                slope_x = table[(*place, slice(None), slice(0, LANES))]
                smooth_x = table[(*place, slice(None), slice(LANES, 2 * LANES))]
                slope_y, smooth_y = stencil(q, column[j + 4 : j + 7], column[j + 2 :: -1][:3])
                change = (fast_size[j] * smooth_x - fast[j] * slope_x) + (
                    up_size[j] * smooth_y - up[j] * slope_y
                )
                if f == 3:
                    theta = centers[2][j]
                    over_x = whole(mass_x[numbers[j], :, span])
                    over_y = whole(mass_y[lines[j], :, span])
                    push_x[j] = metrics[j] * ((1.0 / 60.0) * slope_x + theta * over_x)
                    push[first + j, :, span] = per_row * slope_y + theta * over_y
                elif f == 0:
                    change = change + (spins[j] * centers[1][j] - push_x[j])
                elif f == 1:
                    change = change - (spins[j] * centers[0][j] + push[first + j, :, span])
                emit(f, first + j, t, q, change)

    def edge_group(side, first):
        edge = edge_row(3 * side, rows)
        step = jnp.where(edge == 0, 1, -1)

        def row_of(f, j, span):
            if j >= 0:
                return fields[f][edge + step * j, :, span]
            if inner:
                return jnp.zeros((levels, LANES), F32)
            start = levels * (3 * f - j - 1)
            return strips[side][start : start + levels, span]

        numbers = [edge + step * j for j in range(3)]
        lines = numbers if inner else [first + j for j in range(3)]
        return first, numbers, lines, row_of, step.astype(F32)

    def inner_group(first, size):
        def row_of(f, j, span):
            return fields[f][3 + first + j, :, span]

        numbers = [3 + first + j for j in range(size)]
        return first, numbers, numbers, row_of, 1.0

    def run(groups, emit, then=None):
        if inner:
            lax.fori_loop(0, rows, cut, 0)
            wait_all(fetched[:1])
            slopes_x(0)
        else:
            edge_mass()
        for pair in range(2):
            for t in range(tiles):
                if inner and pair == 0 and t + 1 < tiles:
                    slopes_x(t + 1)
                for first, numbers, lines, row_of, inward in groups:
                    tendency(pair, t, first, numbers, lines, row_of, emit, inward)
            if then:
                then(pair)

    def run_rolled(groups, emit):
        if inner:
            lax.fori_loop(0, rows, cut, 0)
            wait_all(fetched[:1])
        else:
            edge_mass()

        def step(t, carry):
            if inner:
                slopes_x(t)
            for pair in range(2):
                for first, numbers, lines, row_of, inward in groups:
                    tendency(pair, t, first, numbers, lines, row_of, emit, inward)
            return carry

        lax.fori_loop(0, tiles, step, 0)

    half = (rows - 6) // 2
    inner_groups = [inner_group(0, half), inner_group(half, rows - 6 - half)]

    def write_out(f):
        if not inner:
            return [(new.at[f, n], outs[f].at[entry_row(sides, n, rows)]) for n in range(count)]
        return [(new.at[f, 0 : rows - 6], outs[f].at[3 : rows - 3])]

    @pl.when(jnp.logical_not(is_polar()))
    def _():
        def emit(f, i, t, q, change):
            new[f, i, :, columns_of(t)] = q + STEP * change

        if inner:
            run_rolled(inner_groups, emit)
        else:
            run_rolled([edge_group(side, 3 * n) for n, side in enumerate(sides)], emit)
        pairs = [pair for f in range(4) for pair in write_out(f)]
        wait_all(start_all(pairs, sems))
        wait_all(fetched[1:])

    if not kept:
        return

    @pl.when(is_polar())
    def _():
        def emit(f, i, t, q, change):
            pair = 0 if f in PAIRS[0] else 1
            n = PAIRS[pair].index(f)
            top = change.astype(BF16)
            first = t * LANES
            kept_parts[pair][n, i, :, first : first + LANES] = top
            kept_parts[pair][n, i, :, 2 * columns + first : 2 * columns + first + LANES] = top
            rest = (change - top.astype(F32)).astype(BF16)
            kept_parts[pair][n, i, :, columns + first : columns + first + LANES] = rest

        nodal = [None] * 4
        c_all, s_all, d_all = [
            spread_waves(waves, part, sides, kept, levels) for part in range(3)
        ]

        def to_nodes(pair):
            if pair == 0:
                wait_all(fetched[1:])
            if not inner and pair == 0:
                return
            ready = [pair] if inner else [0, 1]
            parts = [kept_parts[n][...].reshape(2 * kept_items, 3 * columns) for n in ready]
            both = dot(jnp.concatenate(parts, axis=0), spread[...])
            for n, f in enumerate([f for n in ready for f in PAIRS[n]]):
                nodal[f] = both[n * kept_items : (n + 1) * kept_items]

        if inner:
            groups = inner_groups + [edge_group(1, rows - 6)] * (kept > rows - 6)
        else:
            groups = [edge_group(side, 3 * n) for n, side in enumerate(sides)]
        run(groups, emit, to_nodes)
        sent = [None] * 8
        for ready in PAIRS if inner else (PAIRS[0] + PAIRS[1],):
            turned = []
            for f in ready:
                turned += [c_all * nodal[f], s_all * nodal[f]]
            moved = dot(split(jnp.concatenate(turned, axis=0)), own[...])
            for n, f in enumerate(ready):
                of_cos = moved[2 * n * kept_items : (2 * n + 1) * kept_items]
                of_sin = moved[(2 * n + 1) * kept_items : (2 * n + 2) * kept_items]
                local[f] = s_all * of_cos[:, :NODES] - c_all * of_sin[:, :NODES] + d_all * nodal[f]
                sent[2 * f] = of_cos[:, NODES : NODES + LANES]
                sent[2 * f + 1] = of_sin[:, NODES : NODES + LANES]
        wide = lax.broadcasted_iota(jnp.int32, (kept_items, LANES), 1)
        for out, first, size in ((to_east, 0, NEAR), (to_west, NEAR, NEAR), (to_far, 2 * NEAR, FAR)):
            total = jnp.zeros((kept_items, LANES), F32)
            for g in range(7, -1, -1):
                part = sent[g]
                turn = (size * g - first) % LANES
                if turn:
                    part = pltpu.roll(part, turn, 1)
                total = jnp.where(wide < size * (g + 1), part, total)
            if size == NEAR:
                out[...] = total
            else:
                total = total.reshape(kept, 2, levels // 2, LANES)
                upper = pltpu.roll(total[:, 1].reshape(kept_items // 2, LANES), 64, 1)
                out[...] = total[:, 0].reshape(kept_items // 2, LANES) + upper


def finish_kernel(sides, count, *refs):
    inner = not sides
    fields = refs[:4]
    from_west, from_east, from_far, local, waves, take, gather = refs[4:11]
    outs = refs[15:19]
    new, sems = refs[19:]
    rows = fields[0].shape[0]
    levels, columns = new.shape[2], new.shape[3]
    items = count * levels

    @pl.when(is_polar())
    def _():
        place = lax.axis_index("lon")
        last = lax.axis_size("lon") - 1
        near_west = from_west[...] * jnp.where(place == 0, -1.0, 1.0)
        near_east = from_east[...] * jnp.where(place == last, -1.0, 1.0)
        far = from_far[...] * jnp.where(place < 2, -1.0, 1.0)
        far = far.reshape(count, 1, levels // 2, LANES)
        upper = pltpu.roll(far.reshape(items // 2, LANES), 64, 1).reshape(count, 1, levels // 2, LANES)
        far = jnp.concatenate([far, upper], axis=1).reshape(items, LANES)
        wide = lax.broadcasted_iota(jnp.int32, (items, LANES), 1)

        def turn(value, by):
            by = by % LANES
            return pltpu.roll(value, by, 1) if by else value

        come = []
        for g in range(8):
            part = jnp.where(wide < NEAR, turn(near_west, -NEAR * g), turn(near_east, NEAR - NEAR * g))
            part = jnp.where(wide < 2 * NEAR, part, turn(far, 2 * NEAR - FAR * g))
            part = jnp.where(wide < MESSAGE, part, 0.0)
            top = part.astype(BF16).astype(F32)
            come.append((top + turn(part - top, MESSAGE) + turn(top, 2 * MESSAGE)).astype(BF16))
        moved = dot(jnp.concatenate(come, axis=0), take[...])
        c_all, s_all = [spread_waves(waves, part, sides, count, levels) for part in range(2)]
        writes = []
        for half in range(2):
            value = []
            for f in (2 * half, 2 * half + 1):
                at = 2 * f * items
                value.append(
                    local[f] + (s_all * moved[at : at + items] - c_all * moved[at + items : at + 2 * items])
                )
            change = dot(split(jnp.concatenate(value, axis=0)), gather[...])
            change = change.reshape(2, count, levels, columns)
            pairs = []
            for f in (2 * half, 2 * half + 1):
                for n in range(count):
                    new[f, n] = fields[f][entry_row(sides, n, rows)] + change[f % 2, n]
                off_edge = rows - 6 if inner else 0
                if inner:
                    pairs.append((new.at[f, 0:off_edge], outs[f].at[3 : rows - 3]))
                for n in range(off_edge, count):
                    pairs.append((new.at[f, n], outs[f].at[entry_row(sides, n, rows)]))
            writes += start_all(pairs, sems, 12 * half)
        wait_all(writes)


def vmem():
    return pl.BlockSpec(memory_space=pltpu.VMEM)


def smem():
    return pl.BlockSpec(memory_space=pltpu.SMEM)


def anywhere():
    return pl.BlockSpec(memory_space=pl.ANY)


def like(*shape):
    return jax.ShapeDtypeStruct(shape, F32)


def in_hbm(value):
    return pltpu.with_memory_space_constraint(value, pltpu.HBM)


def params(mebibytes):
    return pltpu.CompilerParams(vmem_limit_bytes=mebibytes * 1024 * 1024)


def row_factors(count):
    latitude = (np.arange(count).astype(np.float32) + np.float32(0.5)) * np.float32(math.pi / count)
    latitude = latitude - np.float32(math.pi / 2)
    metric = np.float32(1.0) / np.cos(latitude)
    return metric.astype(np.float32), (np.float32(SPIN) * np.sin(latitude)).astype(np.float32)


def shards(u_wind, v_wind, theta, geopot, mass, cutoffs):
    rows, levels, columns = u_wind.shape
    lat_count = lax.axis_size("lat")
    lon_count = lax.axis_size("lon")
    tables = filter_tables(columns, columns * lon_count)
    tables = {k: jnp.asarray(v) for k, v in tables.items()}
    metric, spin = [jnp.asarray(t) for t in row_factors(rows * lat_count)]
    fields = (u_wind, v_wind, theta, geopot)

    strip = 12 * levels + 8
    edge_lines = 2 * levels + rows
    far_fields = [in_hbm(q) for q in (*fields, mass)]
    to_a, to_b, to_west, to_east, waves = pl.pallas_call(
        pack_kernel,
        out_shape=[like(strip, columns)] * 2 + [like(edge_lines, LANES)] * 2 + [like(3, rows, 8, NODES)],
        in_specs=[anywhere()] * 7,
        out_specs=[vmem()] * 5,
        scratch_shapes=[
            pltpu.VMEM((2, 4, rows, levels, LANES), F32),
            pltpu.VMEM((rows, columns), F32),
            pltpu.SMEM(cutoffs.shape, jnp.int32),
            pltpu.VMEM((1, NODES), F32),
            pltpu.SemaphoreType.DMA((35,)),
        ],
        compiler_params=params(8),
        name="pack_edges",
    )(*far_fields, in_hbm(cutoffs), in_hbm(tables["nodes"]))

    def ring(value, step):
        return lax.ppermute(value, "lon", [(i, (i + step) % lon_count) for i in range(lon_count)])

    west = ring(to_east, 1)
    east = ring(to_west, -1)
    odd_up = [(i, i + 1) for i in range(1, lat_count - 1, 2)]
    strip_a = lax.ppermute(to_a, "lat", [(i, i ^ 1) for i in range(lat_count)])
    strip_b = lax.ppermute(to_b, "lat", odd_up + [(j, i) for i, j in odd_up])

    at_poles = lat_count == 4
    inner_count = rows - 3 if at_poles else rows - 6

    def tendencies(sides, kept, old=(), shared=()):
        inner = not sides
        count = kept if inner else 3 * len(sides)
        kept_items = kept * levels
        halos = [] if inner else [*[(strip_a, strip_b)[side] for side in sides], *shared]
        weights = [tables[k] for k in ("band", "spread", "own")]
        if inner:
            weights = [in_hbm(w) for w in weights]
        args = [metric, spin, *fields, mass, west, east, waves, *halos, *weights]
        ahead = [tables["take"], tables["gather"]] if kept and not inner else []
        sent = [like(4, kept_items, NODES)] + [like(kept_items, LANES)] * 2 + [like(kept_items // 2, LANES)]
        tiles = columns // LANES
        results = sent * (kept > 0)
        if inner:
            results += [like(rows, 8, columns), like(tiles, 4, 6, levels, 2 * LANES)]
        part = pltpu.VMEM((2, kept, levels, 3 * columns), BF16)
        return pl.pallas_call(
            functools.partial(tend_kernel, sides, count, kept),
            out_shape=[like(rows, levels, columns)] * 4 + results,
            in_specs=[smem()] * 2
            + [vmem()] * (len(args) - 5)
            + [anywhere() if inner else vmem()] * 3
            + [vmem()] * len(ahead)
            + [anywhere()] * len(old),
            out_specs=[anywhere()] * 4 + [vmem()] * len(results),
            scratch_shapes=[
                pltpu.VMEM((4, count, levels, columns), F32),
                pltpu.VMEM((rows if inner else count, 8, columns), F32),
                pltpu.VMEM((count, levels, columns), F32),
                pltpu.SemaphoreType.DMA((28,)),
                *[part] * (2 if kept else 0),
                *[pltpu.VMEM((4, rows, levels, columns + LANES), BF16)] * (2 if inner else 0),
                *[pltpu.VMEM((tiles, 4, rows - 6, levels, 2 * LANES), F32)] * inner,
                *[pltpu.VMEM((4, rows - 6, levels, 2 * LANES), F32)] * (tiles if inner else 0),
                *[pltpu.VMEM(w.shape, w.dtype) for w in weights if inner],
            ],
            input_output_aliases={len(args) + len(ahead) + f: f for f in range(4)} if old else {},
            compiler_params=params(40),
            cost_estimate=pl.CostEstimate(
                flops=count * levels * 4 * columns * 20000, bytes_accessed=2**22, transcendentals=0
            ),
            name="tend_inner" if inner else "tend_edge",
        )(*args, *ahead, *old)

    def exchange(east_part, west_part, far_part):
        return ring(east_part, 1), ring(west_part, -1), ring(far_part, 2)

    def finish(sides, count, received, local, old):
        weights = [tables[k] for k in ("take", "gather")]
        args = [*fields, *received, local, waves, *weights]
        return pl.pallas_call(
            functools.partial(finish_kernel, sides, count),
            out_shape=[like(rows, levels, columns)] * 4,
            in_specs=[vmem()] * len(args) + [anywhere()] * 4,
            out_specs=[anywhere()] * 4,
            scratch_shapes=[
                pltpu.VMEM((4, count, levels, columns), F32),
                pltpu.SemaphoreType.DMA((24,)),
            ],
            input_output_aliases={len(args) + f: f for f in range(4)},
            compiler_params=params(24),
            name="finish_edge" if sides else "finish_inner",
        )(*args, *old)

    *outs, local_inner, a, b, c, mass_x, edge_cross = tendencies((), inner_count)
    shared = (mass_x, edge_cross)
    received_inner = exchange(a, b, c)
    sides = (0,) if at_poles else (0, 1)
    kept = 3 * len(sides)
    *outs, local_edge, a, b, c = tendencies(sides, kept, outs, shared)
    received_edge = exchange(a, b, c)
    if at_poles:
        outs = tendencies((1,), 0, outs, shared)
    outs = finish((), inner_count, received_inner, local_inner, outs)
    outs = finish(sides, kept, received_edge, local_edge, outs)
    return tuple(outs)


def solution(mesh):
    return jax.shard_map(
        shards,
        mesh=mesh,
        in_specs=(
            P(("members", "lat"), None, "lon"),
            P(("members", "lat"), None, "lon"),
            P(("members", "lat"), None, "lon"),
            P(("members", "lat"), None, "lon"),
            P(("members", "lat"), "lon"),
            P(),
        ),
        out_specs=(
            P(("members", "lat"), None, "lon"),
            P(("members", "lat"), None, "lon"),
            P(("members", "lat"), None, "lon"),
            P(("members", "lat"), None, "lon"),
        ),
        check_vma=False,
    )
```

```python
import functools
import math

import jax
import jax.numpy as jnp
import ml_dtypes
import numpy as np
from jax import lax
from jax.experimental import pallas as pl
from jax.experimental.pallas import tpu as pltpu
from jax.sharding import PartitionSpec as P

STEP = 0.1
SPIN = 0.5
LANES = 128
NEAR = 16
FAR = 8
NODES = 256
F32 = jnp.float32
BF16 = jnp.bfloat16
MESSAGE = 2 * NEAR + FAR


def pivoted(matrix, count):
    rest = np.array(matrix)
    columns = rest.shape[1]
    tilt = 1.0 + 1e-3 * np.arange(columns) / columns
    picked = []
    tri = np.zeros((count, columns))
    for step in range(count):
        size = (rest * rest).sum(axis=0)
        best = int(np.argmax(size * tilt))
        picked.append(best)
        unit = rest[:, best] / math.sqrt(size[best])
        for _ in range(2):
            part = (unit[:, None] * rest).sum(axis=0)
            rest -= unit[:, None] * part[None, :]
            tri[step] += part
        rest[:, best] = 0.0
    left = tri[:, picked].copy()
    right = tri.copy()
    for step in range(count - 1, -1, -1):
        right[step] /= left[step, step]
        right[:step] -= left[:step, step][:, None] * right[step][None, :]
    right[:, picked] = np.eye(count)
    order = np.argsort(picked)
    return np.asarray(picked)[order], right[order]


def cauchy(target, source, circle):
    gap = target[:, None] - source[None, :]
    angle = np.where(gap == 0, 0.5 * math.pi, gap * math.pi / circle)
    return np.where(gap == 0, 0.0, 1.0 / (circle * np.sin(angle)))


def stacked_halves(table):
    table = table.astype(np.float32)
    high = table.astype(ml_dtypes.bfloat16)
    low = (table - high.astype(np.float32)).astype(ml_dtypes.bfloat16)
    return np.concatenate([high, high, low], axis=0)


def band_table():
    band = np.zeros((2 * LANES, 2 * LANES))
    slope = {-3: -1, -2: 9, -1: -45, 1: 45, 2: -9, 3: 1}
    smooth = {-3: 1, -2: -6, -1: 15, 0: -20, 1: 15, 2: -6, 3: 1}
    for j in range(LANES):
        for k, value in slope.items():
            band[j + 3 + k, j] = value
        for k, value in smooth.items():
            band[j + 3 + k, LANES + j] = value
    return np.concatenate([band, band], axis=0).astype(ml_dtypes.bfloat16)


@functools.lru_cache(maxsize=None)
def filter_tables(sector, circle):
    modes = circle // 8
    place = np.arange(sector)
    wave = np.arange(modes)
    phase = (wave[:, None] * place[None, :]) % circle * (2 * math.pi / circle)
    basis = np.concatenate([np.cos(phase), np.sin(phase[1:])], axis=0)
    nodes, spread = pivoted(basis, NODES)
    own = cauchy(nodes, nodes, circle)
    send = np.zeros((NODES, LANES))
    take = np.zeros((MESSAGE, NODES))
    at = 0
    for shift, count in ((sector, NEAR), (-sector, NEAR), (2 * sector, FAR)):
        kernel = cauchy(nodes + shift, nodes, circle)
        pick, weights = pivoted(kernel, count)
        send[:, at : at + count] = weights.T
        take[at : at + count] = kernel[:, pick].T
        at += count
    take = stacked_halves(take)
    take = np.concatenate([take, np.zeros((LANES - 3 * MESSAGE, NODES), take.dtype)], axis=0)
    return dict(
        nodes=nodes.astype(np.float32)[None],
        band=band_table(),
        spread=stacked_halves(spread.T),
        own=stacked_halves(np.concatenate([own.T, send, np.zeros((NODES, LANES))], axis=1)),
        take=take,
        gather=stacked_halves(STEP * spread),
    )


def split(value):
    high = value.astype(BF16)
    low = (value - high.astype(F32)).astype(BF16)
    return jnp.concatenate([high, low, high], axis=1)


def dot(a, b):
    return lax.dot_general(a, b, (((1,), (0,)), ((), ())), preferred_element_type=F32)


def start_all(pairs, sems, first=0):
    copies = [pltpu.make_async_copy(a, b, sems.at[first + n]) for n, (a, b) in enumerate(pairs)]
    for c in copies:
        c.start()
    return copies


def wait_all(copies):
    for c in copies:
        c.wait()


def is_polar():
    owner = lax.axis_index("lat")
    quarter = lax.axis_size("lat") // 4
    return (owner < quarter) | (owner >= lax.axis_size("lat") - quarter)


def edge_row(entry, rows):
    north = (lax.axis_index("lat") % 2 == 0) == (entry < 3)
    return jnp.where(north, rows - 1 - entry % 3, entry % 3)


def entry_row(sides, entry, rows):
    if sides:
        return edge_row(entry + 3 * sides[0], rows)
    if isinstance(entry, int):
        return entry + 3 if entry < rows - 6 else edge_row((entry - (rows - 6) + 3) % 6, rows)
    return jnp.where(entry < rows - 6, entry + 3, edge_row((entry - (rows - 6) + 3) % 6, rows))


def by_parity(even, odd):
    return jnp.where(lax.axis_index("lat") % 2 == 0, even, odd)


def strip_copies(fields, strip, side):
    rows, levels = fields[0].shape[:2]
    pairs = []
    for m in range(3):
        row = edge_row(3 * side + m, rows)
        for f, q in enumerate(fields):
            pairs.append((q.at[row], strip.at[pl.ds(levels * (3 * f + m), levels)]))
    return pairs


def mass_tail(mass, strip, side, levels):
    rows, columns = mass.shape
    tail = 12 * levels
    north = jnp.concatenate([mass[rows - 1 - m : rows - m] for m in range(3)], axis=0)
    strip[tail : tail + 3] = jnp.where(edge_row(3 * side, rows) != 0, north, mass[0:3])
    strip[tail + 3 : tail + 8] = jnp.zeros((5, columns), F32)


def pack_b_kernel(*refs):
    fields = refs[:4]
    mass, _, strip, own_mass, sems = refs[4:]
    owner = lax.axis_index("lat")

    @pl.when((owner > 0) & (owner < lax.axis_size("lat") - 1))
    def _():
        copies = start_all([(mass, own_mass)], sems)
        copies += start_all(strip_copies(fields, strip, 1), sems, 1)
        wait_all(copies[:1])
        mass_tail(own_mass, strip, 1, fields[0].shape[1])
        wait_all(copies[1:])


def pack_kernel(*refs):
    fields = refs[:4]
    mass, cutoffs_in, metric_in, spin_in, nodes_in, strip, west, east, waves, factors = refs[4:14]
    edge, own_mass, cutoffs, metric, spin, nodes, sems = refs[14:]
    rows, columns = mass.shape
    levels = edge.shape[3]
    first = start_all(
        [(cutoffs_in, cutoffs), (nodes_in, nodes), (metric_in, metric), (spin_in, spin)], sems, 33
    )
    small = start_all(
        [(mass, own_mass)]
        + [(q.at[:, :, 0:LANES], edge.at[0, f]) for f, q in enumerate(fields)]
        + [(q.at[:, :, columns - LANES : columns], edge.at[1, f]) for f, q in enumerate(fields)],
        sems,
    )
    large = start_all(strip_copies(fields, strip, 0), sems, 9)

    wait_all(first)
    lat_count = lax.axis_size("lat")
    lon_count = lax.axis_size("lon")
    owner = lax.axis_index("lat")
    circle = columns * lon_count
    start = jnp.where(owner < lat_count // 4, owner * rows, owner * rows - lat_count * rows // 2)
    start = jnp.clip(start, 0, lat_count * rows // 2 - rows)
    line = lax.broadcasted_iota(jnp.int32, (rows, NODES), 0)
    twice = jnp.zeros((rows, NODES), F32)
    for r in range(rows):
        twice = jnp.where(line == r, (2 * cutoffs[start + r] + 1).astype(F32), twice)
    place = nodes[...] + (lax.axis_index("lon") * columns).astype(F32)
    turns = twice * place
    angle = (turns - 2.0 * circle * jnp.floor(turns * (0.5 / circle))) * (math.pi / circle)
    for part, table in enumerate((jnp.cos(angle), jnp.sin(angle), twice * (1.0 / circle))):
        waves[part] = jnp.broadcast_to(table[:, None, :], (rows, 8, NODES))
    for r in range(rows):
        row = owner * rows + r
        factors[0, r] = jnp.full((8, LANES), metric[row] * (1.0 / 60.0))
        factors[1, r] = jnp.full((8, LANES), spin[row])

    wait_all(small)
    mass_tail(own_mass, strip, 0, levels)
    lane = lax.broadcasted_iota(jnp.int32, (levels, LANES), 1)
    west[2 * levels :] = own_mass[:, 0:LANES]
    east[2 * levels :] = pltpu.roll(own_mass[:, columns - LANES : columns], 3, 1)
    for parity in range(2):
        for side, out in ((0, west), (1, east)):
            total = jnp.zeros((levels, LANES), F32)
            for r in range(parity, rows, 2):
                for f in range(4):
                    lead = 16 * (r // 2) + 3 * f
                    turn = lead if side == 0 else (lead + 3) % LANES
                    tile = edge[side, f, r]
                    if turn:
                        tile = pltpu.roll(tile, turn, 1)
                    total = jnp.where((lane >= lead) & (lane < lead + 3), tile, total)
            out[parity * levels : (parity + 1) * levels] = total
    wait_all(large)


def stencil(center, plus, minus):
    p1, p2, p3 = plus
    m1, m2, m3 = minus
    slope = 45.0 * (p1 - m1) - 9.0 * (p2 - m2) + (p3 - m3)
    smooth = (p3 + m3) - 6.0 * (p2 + m2) + 15.0 * (p1 + m1) - 20.0 * center
    return slope, smooth


def over_levels(value):
    return jnp.broadcast_to(value[:, None, :], (value.shape[0], 8, value.shape[1]))


def mass_slope_x(mass, west, east, levels):
    columns = mass.shape[1]
    middle = mass[...]
    wide = jnp.concatenate(
        [pltpu.roll(west[2 * levels :], LANES - 3, 1), middle, east[2 * levels :]], axis=1
    )
    whole = columns + 2 * LANES

    def at(k):
        return pltpu.roll(wide, (-k) % whole, 1)[:, LANES : LANES + columns]

    slope = stencil(middle, [at(1), at(2), at(3)], [at(-1), at(-2), at(-3)])[0]
    return over_levels(slope / middle)


def mass_slope_y(tall):
    size = tall.shape[0] - 6
    plus = [tall[3 + k : 3 + k + size] for k in (1, 2, 3)]
    minus = [tall[3 - k : 3 - k + size] for k in (1, 2, 3)]
    middle = tall[3 : 3 + size]
    return over_levels(stencil(middle, plus, minus)[0] / middle)


def spread_waves(waves, part, sides, kept, levels):
    rows = waves.shape[1]
    numbers = [entry_row(sides, entry, rows) for entry in range(kept)]
    return jnp.concatenate([waves[part, n] for n in numbers for _ in range(levels // 8)], axis=0)


PAIRS = ((3, 0), (1, 2))


def tend_kernel(sides, count, kept, *refs):
    inner = not sides
    refs = list(refs)

    def some(n):
        taken = refs[:n]
        del refs[:n]
        return taken

    fields = some(4)
    mass, west, east, waves, factors = some(5)
    strips = dict(zip(sides, some(len(sides))))
    mass_x, edge_cross = (None, None) if inner else some(2)
    tables_in = some(3)
    if not inner:
        some(2 if kept else 0)
        some(4)
    outs = some(4)
    if kept:
        local, to_east, to_west, to_far = some(4)
    mass_x, edge_cross = some(2) if inner else (mass_x, edge_cross)
    new, mass_y, push, sems = some(4)
    kept_parts = some(2) if kept else None
    if inner:
        high, low, cross_all = some(3)
        crosses = some(mass.shape[1] // LANES)
    tables = refs if inner else tables_in
    band, spread, own = tables
    rows, columns = mass.shape
    levels = fields[0].shape[1]
    kept_items = kept * levels
    tiles = columns // LANES

    fetched = start_all(zip(tables_in, tables), sems, 24) if inner else []
    if inner:
        blank = jnp.zeros((3, columns), F32)
        mass_x[...] = mass_slope_x(mass, west, east, levels)
        mass_y[...] = mass_slope_y(jnp.concatenate([blank, mass[...], blank], axis=0))

    def edge_mass():
        for n, side in enumerate(sides):
            lines = [strips[side][12 * levels + m : 12 * levels + m + 1] for m in (2, 1, 0)]
            north = edge_row(3 * side, rows) != 0
            for m in range(6):
                lines.append(jnp.where(north, mass[rows - 1 - m : rows - m], mass[m : m + 1]))
            mass_y[3 * n : 3 * n + 3] = mass_slope_y(jnp.concatenate(lines, axis=0))

    lane = lax.broadcasted_iota(jnp.int32, (levels, LANES), 1)

    def cut(i, carry):
        row = entry_row(sides, i, rows)
        halo = pl.ds(pl.multiple_of((row % 2) * levels, levels), levels)
        for f in range(4):
            lead = 16 * (row // 2) + 3 * f
            before = pltpu.roll(west[halo, :], lax.rem(LANES - lead, LANES), 1)
            for t in range(tiles + 1):
                if t < tiles:
                    tile = pltpu.roll(fields[f][row, :, t * LANES : (t + 1) * LANES], 3, 1)
                else:
                    tile = pltpu.roll(east[halo, :], lax.rem(LANES + 3 - lead, LANES), 1)
                whole = jnp.where(lane < 3, before, tile)
                top = whole.astype(BF16)
                high[f, i, :, t * LANES : (t + 1) * LANES] = top
                low[f, i, :, t * LANES : (t + 1) * LANES] = (whole - top.astype(F32)).astype(BF16)
                before = tile
        return carry

    def columns_of(t, width=1):
        if isinstance(t, int):
            return slice(t * LANES, (t + width) * LANES)
        return pl.ds(pl.multiple_of(t * LANES, LANES), width * LANES)

    def slopes_x(t):
        span = columns_of(t, 2)
        parts = [table[:, :, :, span].reshape(4 * rows * levels, 2 * LANES) for table in (high, low)]
        product = dot(jnp.concatenate(parts, axis=1), band[...]).reshape(4, rows, levels, 2 * LANES)
        if isinstance(t, int):
            crosses[t][...] = product[:, : rows - 6]
        else:
            cross_all[t] = product[:, : rows - 6]
        edge_cross[t] = product[:, rows - 6 :]

    def cross_of(t, f, entry):
        if inner and entry < rows - 6:
            return (crosses[t], (f, entry)) if isinstance(t, int) else (cross_all, (t, f, entry))
        if inner:
            return edge_cross, (t, f, entry - (rows - 6))
        return edge_cross, (t, f, (entry + 3 * sides[0] + 3) % 6)

    def whole(lines):
        return jnp.concatenate([lines] * (levels // 8), axis=0)

    def tendency(pair, t, first, numbers, lines, row_of, emit, inward=1.0):
        size = len(numbers)
        span = columns_of(t)
        along = [whole(factors[0, n]) for n in numbers]
        centers = [[row_of(f, j, span) for j in range(size)] for f in range(3)]
        per_row = inward * (1.0 / 60.0)
        fast, fast_size, up, up_size = [], [], [], []
        for j in range(size):
            fast.append(centers[0][j] * along[j])
            fast_size.append(jnp.abs(fast[j]))
            up.append(centers[1][j] * per_row)
            up_size.append(jnp.abs(up[j]))
        push_x = [None] * size
        for f in PAIRS[pair]:
            column = [row_of(f, j, span) for j in range(-3, size + 3)]
            for j in range(size):
                q = column[j + 3]
                table, place = cross_of(t, f, first + j)
                slope_x = table[(*place, slice(None), slice(0, LANES))]
                smooth_x = table[(*place, slice(None), slice(LANES, 2 * LANES))]
                slope_y, smooth_y = stencil(q, column[j + 4 : j + 7], column[j + 2 :: -1][:3])
                change = (fast_size[j] * smooth_x - fast[j] * slope_x) + (
                    up_size[j] * smooth_y - up[j] * slope_y
                )
                if f == 3:
                    theta = centers[2][j]
                    over_x = whole(mass_x[numbers[j], :, span])
                    over_y = whole(mass_y[lines[j], :, span])
                    if inner and not isinstance(inward, float):
                        over_y = over_y * inward
                    push_x[j] = along[j] * (slope_x + theta * over_x)
                    push[first + j, :, span] = per_row * (slope_y + theta * over_y)
                elif f == 0:
                    change = change + (whole(factors[1, numbers[j]]) * centers[1][j] - push_x[j])
                elif f == 1:
                    change = change - (whole(factors[1, numbers[j]]) * centers[0][j] + push[first + j, :, span])
                emit(f, first + j, t, q, change)

    def edge_group(side, first):
        edge = edge_row(3 * side, rows)
        step = jnp.where(edge == 0, 1, -1)

        def row_of(f, j, span):
            if j >= 0:
                return fields[f][edge + step * j, :, span]
            if inner:
                return jnp.zeros((levels, LANES), F32)
            start = levels * (3 * f - j - 1)
            return strips[side][start : start + levels, span]

        numbers = [edge + step * j for j in range(3)]
        lines = numbers if inner else [first + j for j in range(3)]
        return first, numbers, lines, row_of, step.astype(F32)

    def inner_group(first, size):
        def row_of(f, j, span):
            return fields[f][3 + first + j, :, span]

        numbers = [3 + first + j for j in range(size)]
        return first, numbers, numbers, row_of, 1.0

    def run(groups, emit, then=None):
        if inner:
            lax.fori_loop(0, rows, cut, 0)
            wait_all(fetched[:1])
            slopes_x(0)
        else:
            edge_mass()
        for pair in range(2):
            for t in range(tiles):
                if inner and pair == 0 and t + 1 < tiles:
                    slopes_x(t + 1)
                for first, numbers, lines, row_of, inward in groups:
                    tendency(pair, t, first, numbers, lines, row_of, emit, inward)
            if then:
                then(pair)

    def run_rolled(groups, emit):
        if inner:
            lax.fori_loop(0, rows, cut, 0)
            wait_all(fetched[:1])
        else:
            edge_mass()

        def step(t, carry):
            if inner:
                slopes_x(t)
            for pair in range(2):
                for first, numbers, lines, row_of, inward in groups:
                    tendency(pair, t, first, numbers, lines, row_of, emit, inward)
            return carry

        lax.fori_loop(0, tiles, step, 0)

    half = (rows - 6) // 2
    inner_groups = [inner_group(0, half), inner_group(half, rows - 6 - half)]

    def write_out(f):
        if not inner:
            return [(new.at[f, n], outs[f].at[entry_row(sides, n, rows)]) for n in range(count)]
        return [(new.at[f, 0 : rows - 6], outs[f].at[3 : rows - 3])]

    @pl.when(jnp.logical_not(is_polar()))
    def _():
        def emit(f, i, t, q, change):
            new[f, i, :, columns_of(t)] = q + STEP * change

        if inner:
            run_rolled(inner_groups, emit)
        else:
            run_rolled([edge_group(side, 3 * n) for n, side in enumerate(sides)], emit)
        pairs = [pair for f in range(4) for pair in write_out(f)]
        wait_all(start_all(pairs, sems))
        wait_all(fetched[1:])

    if not kept:
        return

    @pl.when(is_polar())
    def _():
        def emit(f, i, t, q, change):
            pair = 0 if f in PAIRS[0] else 1
            n = PAIRS[pair].index(f)
            top = change.astype(BF16)
            first = t * LANES
            kept_parts[pair][n, i, :, first : first + LANES] = top
            kept_parts[pair][n, i, :, 2 * columns + first : 2 * columns + first + LANES] = top
            rest = (change - top.astype(F32)).astype(BF16)
            kept_parts[pair][n, i, :, columns + first : columns + first + LANES] = rest

        nodal = [None] * 4
        c_all, s_all, d_all = [
            spread_waves(waves, part, sides, kept, levels) for part in range(3)
        ]

        def to_nodes(pair):
            if pair == 0:
                wait_all(fetched[1:])
            if not inner and pair == 0:
                return
            ready = [pair] if inner else [0, 1]
            parts = [kept_parts[n][...].reshape(2 * kept_items, 3 * columns) for n in ready]
            both = dot(jnp.concatenate(parts, axis=0), spread[...])
            for n, f in enumerate([f for n in ready for f in PAIRS[n]]):
                nodal[f] = both[n * kept_items : (n + 1) * kept_items]

        if inner:
            groups = inner_groups + [edge_group(1, rows - 6)] * (kept > rows - 6)
        else:
            groups = [edge_group(side, 3 * n) for n, side in enumerate(sides)]
        run(groups, emit, to_nodes)
        sent = [None] * 8
        for ready in PAIRS if inner else (PAIRS[0] + PAIRS[1],):
            turned = []
            for f in ready:
                turned += [c_all * nodal[f], s_all * nodal[f]]
            moved = dot(split(jnp.concatenate(turned, axis=0)), own[...])
            for n, f in enumerate(ready):
                of_cos = moved[2 * n * kept_items : (2 * n + 1) * kept_items]
                of_sin = moved[(2 * n + 1) * kept_items : (2 * n + 2) * kept_items]
                local[f] = s_all * of_cos[:, :NODES] - c_all * of_sin[:, :NODES] + d_all * nodal[f]
                sent[2 * f] = of_cos[:, NODES : NODES + LANES]
                sent[2 * f + 1] = of_sin[:, NODES : NODES + LANES]
        wide = lax.broadcasted_iota(jnp.int32, (kept_items, LANES), 1)
        for out, first, size in ((to_east, 0, NEAR), (to_west, NEAR, NEAR), (to_far, 2 * NEAR, FAR)):
            total = jnp.zeros((kept_items, LANES), F32)
            for g in range(7, -1, -1):
                part = sent[g]
                turn = (size * g - first) % LANES
                if turn:
                    part = pltpu.roll(part, turn, 1)
                total = jnp.where(wide < size * (g + 1), part, total)
            if size == NEAR:
                out[...] = total
            else:
                total = total.reshape(kept, 2, levels // 2, LANES)
                upper = pltpu.roll(total[:, 1].reshape(kept_items // 2, LANES), 64, 1)
                out[...] = total[:, 0].reshape(kept_items // 2, LANES) + upper


def finish_kernel(sides, count, *refs):
    inner = not sides
    fields = refs[:4]
    from_west, from_east, from_far, local, waves, take, gather = refs[4:11]
    outs = refs[15:19]
    new, sems = refs[19:]
    rows = fields[0].shape[0]
    levels, columns = new.shape[2], new.shape[3]
    items = count * levels

    @pl.when(is_polar())
    def _():
        place = lax.axis_index("lon")
        last = lax.axis_size("lon") - 1
        near_west = from_west[...] * jnp.where(place == 0, -1.0, 1.0)
        near_east = from_east[...] * jnp.where(place == last, -1.0, 1.0)
        far = from_far[...] * jnp.where(place < 2, -1.0, 1.0)
        far = far.reshape(count, 1, levels // 2, LANES)
        upper = pltpu.roll(far.reshape(items // 2, LANES), 64, 1).reshape(count, 1, levels // 2, LANES)
        far = jnp.concatenate([far, upper], axis=1).reshape(items, LANES)
        wide = lax.broadcasted_iota(jnp.int32, (items, LANES), 1)

        def turn(value, by):
            by = by % LANES
            return pltpu.roll(value, by, 1) if by else value

        come = []
        for g in range(8):
            part = jnp.where(wide < NEAR, turn(near_west, -NEAR * g), turn(near_east, NEAR - NEAR * g))
            part = jnp.where(wide < 2 * NEAR, part, turn(far, 2 * NEAR - FAR * g))
            part = jnp.where(wide < MESSAGE, part, 0.0)
            top = part.astype(BF16).astype(F32)
            come.append((top + turn(part - top, MESSAGE) + turn(top, 2 * MESSAGE)).astype(BF16))
        moved = dot(jnp.concatenate(come, axis=0), take[...])
        c_all, s_all = [spread_waves(waves, part, sides, count, levels) for part in range(2)]
        writes = []
        chunks = [(f,) for f in range(4)] if inner else [(0, 1, 2, 3)]
        for chunk in chunks:
            value = []
            for f in chunk:
                at = 2 * f * items
                value.append(
                    local[f] + (s_all * moved[at : at + items] - c_all * moved[at + items : at + 2 * items])
                )
            change = dot(split(jnp.concatenate(value, axis=0)), gather[...])
            change = change.reshape(len(chunk), count, levels, columns)
            pairs = []
            for k, f in enumerate(chunk):
                for n in range(count):
                    new[f, n] = fields[f][entry_row(sides, n, rows)] + change[k, n]
                off_edge = rows - 6 if inner else 0
                if inner:
                    pairs.append((new.at[f, 0:off_edge], outs[f].at[3 : rows - 3]))
                for n in range(off_edge, count):
                    pairs.append((new.at[f, n], outs[f].at[entry_row(sides, n, rows)]))
            writes += start_all(pairs, sems, len(writes))
        wait_all(writes)


def vmem():
    return pl.BlockSpec(memory_space=pltpu.VMEM)


def anywhere():
    return pl.BlockSpec(memory_space=pl.ANY)


def like(*shape):
    return jax.ShapeDtypeStruct(shape, F32)


def in_hbm(value):
    return pltpu.with_memory_space_constraint(value, pltpu.HBM)


def params(mebibytes):
    return pltpu.CompilerParams(vmem_limit_bytes=mebibytes * 1024 * 1024)


def row_factors(count):
    latitude = (np.arange(count).astype(np.float32) + np.float32(0.5)) * np.float32(math.pi / count)
    latitude = latitude - np.float32(math.pi / 2)
    metric = np.float32(1.0) / np.cos(latitude)
    return metric.astype(np.float32), (np.float32(SPIN) * np.sin(latitude)).astype(np.float32)


def shards(u_wind, v_wind, theta, geopot, mass, cutoffs):
    rows, levels, columns = u_wind.shape
    lat_count = lax.axis_size("lat")
    lon_count = lax.axis_size("lon")
    tables = filter_tables(columns, columns * lon_count)
    tables = {k: jnp.asarray(v) for k, v in tables.items()}
    metric, spin = [jnp.asarray(t) for t in row_factors(rows * lat_count)]
    fields = (u_wind, v_wind, theta, geopot)

    strip = 12 * levels + 8
    edge_lines = 2 * levels + rows
    far_fields = [in_hbm(q) for q in (*fields, mass)]
    to_a, to_west, to_east, waves, factors = pl.pallas_call(
        pack_kernel,
        out_shape=[
            like(strip, columns),
            *[like(edge_lines, LANES)] * 2,
            like(3, rows, 8, NODES),
            like(2, rows, 8, LANES),
        ],
        in_specs=[anywhere()] * 9,
        out_specs=[vmem()] * 5,
        scratch_shapes=[
            pltpu.VMEM((2, 4, rows, levels, LANES), F32),
            pltpu.VMEM((rows, columns), F32),
            pltpu.SMEM(cutoffs.shape, jnp.int32),
            pltpu.SMEM(metric.shape, F32),
            pltpu.SMEM(spin.shape, F32),
            pltpu.VMEM((1, NODES), F32),
            pltpu.SemaphoreType.DMA((37,)),
        ],
        compiler_params=params(8),
        name="pack_edges",
    )(*far_fields, in_hbm(cutoffs), in_hbm(metric), in_hbm(spin), in_hbm(tables["nodes"]))
    to_b = pl.pallas_call(
        pack_b_kernel,
        out_shape=like(strip, columns),
        in_specs=[anywhere()] * 6,
        out_specs=vmem(),
        scratch_shapes=[pltpu.VMEM((rows, columns), F32), pltpu.SemaphoreType.DMA((13,))],
        compiler_params=params(8),
        name="pack_b",
    )(*far_fields, to_west)

    def ring(value, step):
        return lax.ppermute(value, "lon", [(i, (i + step) % lon_count) for i in range(lon_count)])

    west = ring(to_east, 1)
    east = ring(to_west, -1)
    odd_up = [(i, i + 1) for i in range(1, lat_count - 1, 2)]
    strip_a = lax.ppermute(to_a, "lat", [(i, i ^ 1) for i in range(lat_count)])
    strip_b = lax.ppermute(to_b, "lat", odd_up + [(j, i) for i, j in odd_up])

    at_poles = lat_count == 4
    inner_count = rows - 3 if at_poles else rows - 6

    def tendencies(sides, kept, old=(), shared=()):
        inner = not sides
        count = kept if inner else 3 * len(sides)
        kept_items = kept * levels
        halos = [] if inner else [*[(strip_a, strip_b)[side] for side in sides], *shared]
        weights = [tables[k] for k in ("band", "spread", "own")]
        if inner:
            weights = [in_hbm(w) for w in weights]
        args = [*fields, mass, west, east, waves, factors, *halos, *weights]
        ahead = [tables["take"], tables["gather"]] if kept and not inner else []
        sent = [like(4, kept_items, NODES)] + [like(kept_items, LANES)] * 2 + [like(kept_items // 2, LANES)]
        tiles = columns // LANES
        results = sent * (kept > 0)
        if inner:
            results += [like(rows, 8, columns), like(tiles, 4, 6, levels, 2 * LANES)]
        part = pltpu.VMEM((2, kept, levels, 3 * columns), BF16)
        return pl.pallas_call(
            functools.partial(tend_kernel, sides, count, kept),
            out_shape=[like(rows, levels, columns)] * 4 + results,
            in_specs=[vmem()] * (len(args) - 3)
            + [anywhere() if inner else vmem()] * 3
            + [vmem()] * len(ahead)
            + [anywhere()] * len(old),
            out_specs=[anywhere()] * 4 + [vmem()] * len(results),
            scratch_shapes=[
                pltpu.VMEM((4, count, levels, columns), F32),
                pltpu.VMEM((rows if inner else count, 8, columns), F32),
                pltpu.VMEM((count, levels, columns), F32),
                pltpu.SemaphoreType.DMA((28,)),
                *[part] * (2 if kept else 0),
                *[pltpu.VMEM((4, rows, levels, columns + LANES), BF16)] * (2 if inner else 0),
                *[pltpu.VMEM((tiles, 4, rows - 6, levels, 2 * LANES), F32)] * inner,
                *[pltpu.VMEM((4, rows - 6, levels, 2 * LANES), F32)] * (tiles if inner else 0),
                *[pltpu.VMEM(w.shape, w.dtype) for w in weights if inner],
            ],
            input_output_aliases={len(args) + len(ahead) + f: f for f in range(4)} if old else {},
            compiler_params=params(40),
            cost_estimate=pl.CostEstimate(
                flops=count * levels * 4 * columns * 20000, bytes_accessed=2**22, transcendentals=0
            ),
            name="tend_inner" if inner else "tend_edge",
        )(*args, *ahead, *old)

    def exchange(east_part, west_part, far_part):
        return ring(east_part, 1), ring(west_part, -1), ring(far_part, 2)

    def finish(sides, count, received, local, old):
        weights = [tables[k] for k in ("take", "gather")]
        args = [*fields, *received, local, waves, *weights]
        return pl.pallas_call(
            functools.partial(finish_kernel, sides, count),
            out_shape=[like(rows, levels, columns)] * 4,
            in_specs=[vmem()] * len(args) + [anywhere()] * 4,
            out_specs=[anywhere()] * 4,
            scratch_shapes=[
                pltpu.VMEM((4, count, levels, columns), F32),
                pltpu.SemaphoreType.DMA((24,)),
            ],
            input_output_aliases={len(args) + f: f for f in range(4)},
            compiler_params=params(24),
            name="finish_edge" if sides else "finish_inner",
        )(*args, *old)

    *outs, local_inner, a, b, c, mass_x, edge_cross = tendencies((), inner_count)
    shared = (mass_x, edge_cross)
    received_inner = exchange(a, b, c)
    sides = (0,) if at_poles else (0, 1)
    kept = 3 * len(sides)
    *outs, local_edge, a, b, c = tendencies(sides, kept, outs, shared)
    received_edge = exchange(a, b, c)
    if at_poles:
        outs = tendencies((1,), 0, outs, shared)
    outs = finish((), inner_count, received_inner, local_inner, outs)
    outs = finish(sides, kept, received_edge, local_edge, outs)
    return tuple(outs)


def solution(mesh):
    return jax.shard_map(
        shards,
        mesh=mesh,
        in_specs=(
            P(("members", "lat"), None, "lon"),
            P(("members", "lat"), None, "lon"),
            P(("members", "lat"), None, "lon"),
            P(("members", "lat"), None, "lon"),
            P(("members", "lat"), "lon"),
            P(),
        ),
        out_specs=(
            P(("members", "lat"), None, "lon"),
            P(("members", "lat"), None, "lon"),
            P(("members", "lat"), None, "lon"),
            P(("members", "lat"), None, "lon"),
        ),
        check_vma=False,
    )
```

```python
import functools
import math

import jax
import jax.numpy as jnp
import ml_dtypes
import numpy as np
from jax import lax
from jax.experimental import pallas as pl
from jax.experimental.pallas import tpu as pltpu
from jax.sharding import PartitionSpec as P

STEP = 0.1
SPIN = 0.5
LANES = 128
NEAR = 16
FAR = 8
NODES = 256
F32 = jnp.float32
BF16 = jnp.bfloat16
MESSAGE = 2 * NEAR + FAR


def pivoted(matrix, count):
    rest = np.array(matrix)
    columns = rest.shape[1]
    tilt = 1.0 + 1e-3 * np.arange(columns) / columns
    picked = []
    tri = np.zeros((count, columns))
    for step in range(count):
        size = (rest * rest).sum(axis=0)
        best = int(np.argmax(size * tilt))
        picked.append(best)
        unit = rest[:, best] / math.sqrt(size[best])
        for _ in range(2):
            part = (unit[:, None] * rest).sum(axis=0)
            rest -= unit[:, None] * part[None, :]
            tri[step] += part
        rest[:, best] = 0.0
    left = tri[:, picked].copy()
    right = tri.copy()
    for step in range(count - 1, -1, -1):
        right[step] /= left[step, step]
        right[:step] -= left[:step, step][:, None] * right[step][None, :]
    right[:, picked] = np.eye(count)
    order = np.argsort(picked)
    return np.asarray(picked)[order], right[order]


def cauchy(target, source, circle):
    gap = target[:, None] - source[None, :]
    angle = np.where(gap == 0, 0.5 * math.pi, gap * math.pi / circle)
    return np.where(gap == 0, 0.0, 1.0 / (circle * np.sin(angle)))


def stacked_halves(table):
    table = table.astype(np.float32)
    high = table.astype(ml_dtypes.bfloat16)
    low = (table - high.astype(np.float32)).astype(ml_dtypes.bfloat16)
    return np.concatenate([high, high, low], axis=0)


def band_table():
    band = np.zeros((2 * LANES, 2 * LANES))
    slope = {-3: -1, -2: 9, -1: -45, 1: 45, 2: -9, 3: 1}
    smooth = {-3: 1, -2: -6, -1: 15, 0: -20, 1: 15, 2: -6, 3: 1}
    for j in range(LANES):
        for k, value in slope.items():
            band[j + 3 + k, j] = value
        for k, value in smooth.items():
            band[j + 3 + k, LANES + j] = value
    return np.concatenate([band, band], axis=0).astype(ml_dtypes.bfloat16)


@functools.lru_cache(maxsize=None)
def filter_tables(sector, circle):
    modes = circle // 8
    place = np.arange(sector)
    wave = np.arange(modes)
    phase = (wave[:, None] * place[None, :]) % circle * (2 * math.pi / circle)
    basis = np.concatenate([np.cos(phase), np.sin(phase[1:])], axis=0)
    nodes, spread = pivoted(basis, NODES)
    own = cauchy(nodes, nodes, circle)
    send = np.zeros((NODES, LANES))
    take = np.zeros((MESSAGE, NODES))
    at = 0
    for shift, count in ((sector, NEAR), (-sector, NEAR), (2 * sector, FAR)):
        kernel = cauchy(nodes + shift, nodes, circle)
        pick, weights = pivoted(kernel, count)
        send[:, at : at + count] = weights.T
        take[at : at + count] = kernel[:, pick].T
        at += count
    take = stacked_halves(take)
    take = np.concatenate([take, np.zeros((LANES - 3 * MESSAGE, NODES), take.dtype)], axis=0)
    return dict(
        nodes=nodes.astype(np.float32)[None],
        band=band_table(),
        spread=stacked_halves(spread.T),
        own=stacked_halves(np.concatenate([own.T, send, np.zeros((NODES, LANES))], axis=1)),
        take=take,
        gather=stacked_halves(STEP * spread),
    )


def split(value):
    high = value.astype(BF16)
    low = (value - high.astype(F32)).astype(BF16)
    return jnp.concatenate([high, low, high], axis=1)


def dot(a, b):
    return lax.dot_general(a, b, (((1,), (0,)), ((), ())), preferred_element_type=F32)


def start_all(pairs, sems, first=0):
    copies = [pltpu.make_async_copy(a, b, sems.at[first + n]) for n, (a, b) in enumerate(pairs)]
    for c in copies:
        c.start()
    return copies


def wait_all(copies):
    for c in copies:
        c.wait()


def is_polar():
    owner = lax.axis_index("lat")
    quarter = lax.axis_size("lat") // 4
    return (owner < quarter) | (owner >= lax.axis_size("lat") - quarter)


def edge_row(entry, rows):
    north = (lax.axis_index("lat") % 2 == 0) == (entry < 3)
    return jnp.where(north, rows - 1 - entry % 3, entry % 3)


def entry_row(sides, entry, rows):
    if sides:
        return edge_row(entry + 3 * sides[0], rows)
    if isinstance(entry, int):
        return entry + 3 if entry < rows - 6 else edge_row((entry - (rows - 6) + 3) % 6, rows)
    return jnp.where(entry < rows - 6, entry + 3, edge_row((entry - (rows - 6) + 3) % 6, rows))


def by_parity(even, odd):
    return jnp.where(lax.axis_index("lat") % 2 == 0, even, odd)


def strip_copies(fields, strip, side):
    rows, levels = fields[0].shape[:2]
    pairs = []
    for m in range(3):
        row = edge_row(3 * side + m, rows)
        for f, q in enumerate(fields):
            pairs.append((q.at[row], strip.at[pl.ds(levels * (3 * f + m), levels)]))
    return pairs


def mass_tail(mass, strip, side, levels):
    rows, columns = mass.shape
    tail = 12 * levels
    north = jnp.concatenate([mass[rows - 1 - m : rows - m] for m in range(3)], axis=0)
    strip[tail : tail + 3] = jnp.where(edge_row(3 * side, rows) != 0, north, mass[0:3])
    strip[tail + 3 : tail + 8] = jnp.zeros((5, columns), F32)


def pack_b_kernel(*refs):
    fields = refs[:4]
    mass, _, strip, own_mass, sems = refs[4:]
    owner = lax.axis_index("lat")

    @pl.when((owner > 0) & (owner < lax.axis_size("lat") - 1))
    def _():
        copies = start_all([(mass, own_mass)], sems)
        copies += start_all(strip_copies(fields, strip, 1), sems, 1)
        wait_all(copies[:1])
        mass_tail(own_mass, strip, 1, fields[0].shape[1])
        wait_all(copies[1:])


def pack_kernel(*refs):
    fields = refs[:4]
    mass, cutoffs_in, metric_in, spin_in, nodes_in, strip, west, east, waves, factors = refs[4:14]
    edge, own_mass, cutoffs, metric, spin, nodes, sems = refs[14:]
    rows, columns = mass.shape
    levels = edge.shape[3]
    first = start_all(
        [(cutoffs_in, cutoffs), (nodes_in, nodes), (metric_in, metric), (spin_in, spin)], sems, 33
    )
    small = start_all(
        [(mass, own_mass)]
        + [(q.at[:, :, 0:LANES], edge.at[0, f]) for f, q in enumerate(fields)]
        + [(q.at[:, :, columns - LANES : columns], edge.at[1, f]) for f, q in enumerate(fields)],
        sems,
    )
    large = start_all(strip_copies(fields, strip, 0), sems, 9)

    wait_all(first)
    lat_count = lax.axis_size("lat")
    lon_count = lax.axis_size("lon")
    owner = lax.axis_index("lat")
    circle = columns * lon_count
    start = jnp.where(owner < lat_count // 4, owner * rows, owner * rows - lat_count * rows // 2)
    start = jnp.clip(start, 0, lat_count * rows // 2 - rows)
    line = lax.broadcasted_iota(jnp.int32, (rows, NODES), 0)
    twice = jnp.zeros((rows, NODES), F32)
    for r in range(rows):
        twice = jnp.where(line == r, (2 * cutoffs[start + r] + 1).astype(F32), twice)
    place = nodes[...] + (lax.axis_index("lon") * columns).astype(F32)
    turns = twice * place
    angle = (turns - 2.0 * circle * jnp.floor(turns * (0.5 / circle))) * (math.pi / circle)
    for part, table in enumerate((jnp.cos(angle), jnp.sin(angle), twice * (1.0 / circle))):
        waves[part] = jnp.broadcast_to(table[:, None, :], (rows, 8, NODES))
    for r in range(rows):
        row = owner * rows + r
        factors[0, r] = jnp.full((8, LANES), metric[row] * (1.0 / 60.0))
        factors[1, r] = jnp.full((8, LANES), spin[row])

    wait_all(small)
    mass_tail(own_mass, strip, 0, levels)
    lane = lax.broadcasted_iota(jnp.int32, (levels, LANES), 1)
    west[2 * levels :] = own_mass[:, 0:LANES]
    east[2 * levels :] = pltpu.roll(own_mass[:, columns - LANES : columns], 3, 1)
    for parity in range(2):
        for side, out in ((0, west), (1, east)):
            total = jnp.zeros((levels, LANES), F32)
            for r in range(parity, rows, 2):
                for f in range(4):
                    lead = 16 * (r // 2) + 3 * f
                    turn = lead if side == 0 else (lead + 3) % LANES
                    tile = edge[side, f, r]
                    if turn:
                        tile = pltpu.roll(tile, turn, 1)
                    total = jnp.where((lane >= lead) & (lane < lead + 3), tile, total)
            out[parity * levels : (parity + 1) * levels] = total
    wait_all(large)


def stencil(center, plus, minus):
    p1, p2, p3 = plus
    m1, m2, m3 = minus
    slope = 45.0 * (p1 - m1) - 9.0 * (p2 - m2) + (p3 - m3)
    smooth = (p3 + m3) - 6.0 * (p2 + m2) + 15.0 * (p1 + m1) - 20.0 * center
    return slope, smooth


def over_levels(value):
    return jnp.broadcast_to(value[:, None, :], (value.shape[0], 8, value.shape[1]))


def mass_slope_x(mass, west, east, levels):
    columns = mass.shape[1]
    middle = mass[...]
    wide = jnp.concatenate(
        [pltpu.roll(west[2 * levels :], LANES - 3, 1), middle, east[2 * levels :]], axis=1
    )
    whole = columns + 2 * LANES

    def at(k):
        return pltpu.roll(wide, (-k) % whole, 1)[:, LANES : LANES + columns]

    slope = stencil(middle, [at(1), at(2), at(3)], [at(-1), at(-2), at(-3)])[0]
    return over_levels(slope / middle)


def mass_slope_y(tall):
    size = tall.shape[0] - 6
    plus = [tall[3 + k : 3 + k + size] for k in (1, 2, 3)]
    minus = [tall[3 - k : 3 - k + size] for k in (1, 2, 3)]
    middle = tall[3 : 3 + size]
    return over_levels(stencil(middle, plus, minus)[0] / middle)


def spread_waves(waves, part, sides, kept, levels):
    rows = waves.shape[1]
    numbers = [entry_row(sides, entry, rows) for entry in range(kept)]
    return jnp.concatenate([waves[part, n] for n in numbers for _ in range(levels // 8)], axis=0)


PAIRS = ((3, 0), (1, 2))


def tend_kernel(sides, count, kept, *refs):
    inner = not sides
    refs = list(refs)

    def some(n):
        taken = refs[:n]
        del refs[:n]
        return taken

    fields = some(4)
    mass, west, east, waves, factors = some(5)
    strips = dict(zip(sides, some(len(sides))))
    mass_x, edge_cross = (None, None) if inner else some(2)
    tables_in = some(3)
    if not inner:
        some(2 if kept else 0)
        some(4)
    outs = some(4)
    if kept:
        local, to_east, to_west, to_far = some(4)
    mass_x, edge_cross = some(2) if inner else (mass_x, edge_cross)
    new, mass_y, push, sems = some(4)
    kept_parts = some(2) if kept else None
    if inner:
        high, low, cross_all = some(3)
        crosses = some(mass.shape[1] // LANES)
    tables = refs if inner else tables_in
    band, spread, own = tables
    rows, columns = mass.shape
    levels = fields[0].shape[1]
    kept_items = kept * levels
    tiles = columns // LANES

    fetched = start_all(zip(tables_in, tables), sems, 24) if inner else []
    if inner:
        blank = jnp.zeros((3, columns), F32)
        mass_x[...] = mass_slope_x(mass, west, east, levels)
        mass_y[...] = mass_slope_y(jnp.concatenate([blank, mass[...], blank], axis=0))

    def edge_mass():
        for n, side in enumerate(sides):
            lines = [strips[side][12 * levels + m : 12 * levels + m + 1] for m in (2, 1, 0)]
            north = edge_row(3 * side, rows) != 0
            for m in range(6):
                lines.append(jnp.where(north, mass[rows - 1 - m : rows - m], mass[m : m + 1]))
            mass_y[3 * n : 3 * n + 3] = mass_slope_y(jnp.concatenate(lines, axis=0))

    lane = lax.broadcasted_iota(jnp.int32, (levels, LANES), 1)

    def cut(i, carry):
        row = entry_row(sides, i, rows)
        halo = pl.ds(pl.multiple_of((row % 2) * levels, levels), levels)
        for f in range(4):
            lead = 16 * (row // 2) + 3 * f
            before = pltpu.roll(west[halo, :], lax.rem(LANES - lead, LANES), 1)
            for t in range(tiles + 1):
                if t < tiles:
                    tile = pltpu.roll(fields[f][row, :, t * LANES : (t + 1) * LANES], 3, 1)
                else:
                    tile = pltpu.roll(east[halo, :], lax.rem(LANES + 3 - lead, LANES), 1)
                whole = jnp.where(lane < 3, before, tile)
                top = whole.astype(BF16)
                high[f, i, :, t * LANES : (t + 1) * LANES] = top
                low[f, i, :, t * LANES : (t + 1) * LANES] = (whole - top.astype(F32)).astype(BF16)
                before = tile
        return carry

    def cut_tile(t):
        for i in range(rows):
            row = entry_row(sides, i, rows)
            first = (row % 2) * levels
            if not isinstance(row, int):
                first = pl.multiple_of(first, levels)
            halo = pl.ds(first, levels)

            def shifted(f, n):
                lead = 16 * (row // 2) + 3 * f
                if n < 0:
                    return pltpu.roll(west[halo, :], (LANES - lead) % LANES, 1)
                if n == tiles:
                    return pltpu.roll(east[halo, :], (LANES + 3 - lead) % LANES, 1)
                return pltpu.roll(fields[f][row, :, n * LANES : (n + 1) * LANES], 3, 1)

            for f in range(4):
                whole = jnp.where(lane < 3, shifted(f, t - 1), shifted(f, t))
                top = whole.astype(BF16)
                high[f, i, :, t * LANES : (t + 1) * LANES] = top
                low[f, i, :, t * LANES : (t + 1) * LANES] = (whole - top.astype(F32)).astype(BF16)

    def columns_of(t, width=1):
        if isinstance(t, int):
            return slice(t * LANES, (t + width) * LANES)
        return pl.ds(pl.multiple_of(t * LANES, LANES), width * LANES)

    def slopes_x(t):
        span = columns_of(t, 2)
        parts = [table[:, :, :, span].reshape(4 * rows * levels, 2 * LANES) for table in (high, low)]
        product = dot(jnp.concatenate(parts, axis=1), band[...]).reshape(4, rows, levels, 2 * LANES)
        if isinstance(t, int):
            crosses[t][...] = product[:, : rows - 6]
        else:
            cross_all[t] = product[:, : rows - 6]
        edge_cross[t] = product[:, rows - 6 :]

    def cross_of(t, f, entry):
        if inner and entry < rows - 6:
            return (crosses[t], (f, entry)) if isinstance(t, int) else (cross_all, (t, f, entry))
        if inner:
            return edge_cross, (t, f, entry - (rows - 6))
        return edge_cross, (t, f, (entry + 3 * sides[0] + 3) % 6)

    def whole(lines):
        return jnp.concatenate([lines] * (levels // 8), axis=0)

    def tendency(pair, t, first, numbers, lines, row_of, emit, inward=1.0):
        size = len(numbers)
        span = columns_of(t)
        along = [whole(factors[0, n]) for n in numbers]
        centers = [[row_of(f, j, span) for j in range(size)] for f in range(3)]
        per_row = inward * (1.0 / 60.0)
        fast, fast_size, up, up_size = [], [], [], []
        for j in range(size):
            fast.append(centers[0][j] * along[j])
            fast_size.append(jnp.abs(fast[j]))
            up.append(centers[1][j] * per_row)
            up_size.append(jnp.abs(up[j]))
        push_x = [None] * size
        for f in PAIRS[pair]:
            column = [row_of(f, j, span) for j in range(-3, size + 3)]
            for j in range(size):
                q = column[j + 3]
                table, place = cross_of(t, f, first + j)
                slope_x = table[(*place, slice(None), slice(0, LANES))]
                smooth_x = table[(*place, slice(None), slice(LANES, 2 * LANES))]
                slope_y, smooth_y = stencil(q, column[j + 4 : j + 7], column[j + 2 :: -1][:3])
                change = (fast_size[j] * smooth_x - fast[j] * slope_x) + (
                    up_size[j] * smooth_y - up[j] * slope_y
                )
                if f == 3:
                    theta = centers[2][j]
                    over_x = whole(mass_x[numbers[j], :, span])
                    over_y = whole(mass_y[lines[j], :, span])
                    if inner and not isinstance(inward, float):
                        over_y = over_y * inward
                    push_x[j] = along[j] * (slope_x + theta * over_x)
                    push[first + j, :, span] = per_row * (slope_y + theta * over_y)
                elif f == 0:
                    change = change + (whole(factors[1, numbers[j]]) * centers[1][j] - push_x[j])
                elif f == 1:
                    change = change - (whole(factors[1, numbers[j]]) * centers[0][j] + push[first + j, :, span])
                emit(f, first + j, t, q, change)

    def edge_group(side, first):
        edge = edge_row(3 * side, rows)
        step = jnp.where(edge == 0, 1, -1)

        def row_of(f, j, span):
            if j >= 0:
                return fields[f][edge + step * j, :, span]
            if inner:
                return jnp.zeros((levels, LANES), F32)
            start = levels * (3 * f - j - 1)
            return strips[side][start : start + levels, span]

        numbers = [edge + step * j for j in range(3)]
        lines = numbers if inner else [first + j for j in range(3)]
        return first, numbers, lines, row_of, step.astype(F32)

    def inner_group(first, size):
        def row_of(f, j, span):
            return fields[f][3 + first + j, :, span]

        numbers = [3 + first + j for j in range(size)]
        return first, numbers, numbers, row_of, 1.0

    def run(groups, emit, then=None):
        if inner:
            cut_tile(0)
            cut_tile(1)
            wait_all(fetched[:1])
            slopes_x(0)
            cut_tile(2)
        else:
            edge_mass()
        for pair in range(2):
            for t in range(tiles):
                if inner and pair == 0 and t + 1 < tiles:
                    slopes_x(t + 1)
                    if t + 3 <= tiles:
                        cut_tile(t + 3)
                for first, numbers, lines, row_of, inward in groups:
                    tendency(pair, t, first, numbers, lines, row_of, emit, inward)
            if then:
                then(pair)

    def run_rolled(groups, emit):
        if inner:
            lax.fori_loop(0, rows, cut, 0)
            wait_all(fetched[:1])
        else:
            edge_mass()

        def step(t, carry):
            if inner:
                slopes_x(t)
            for pair in range(2):
                for first, numbers, lines, row_of, inward in groups:
                    tendency(pair, t, first, numbers, lines, row_of, emit, inward)
            return carry

        lax.fori_loop(0, tiles, step, 0)

    half = (rows - 6) // 2
    inner_groups = [inner_group(0, half), inner_group(half, rows - 6 - half)]

    def write_out(f):
        if not inner:
            return [(new.at[f, n], outs[f].at[entry_row(sides, n, rows)]) for n in range(count)]
        return [(new.at[f, 0 : rows - 6], outs[f].at[3 : rows - 3])]

    @pl.when(jnp.logical_not(is_polar()))
    def _():
        def emit(f, i, t, q, change):
            new[f, i, :, columns_of(t)] = q + STEP * change

        if inner:
            run_rolled(inner_groups, emit)
        else:
            run_rolled([edge_group(side, 3 * n) for n, side in enumerate(sides)], emit)
        pairs = [pair for f in range(4) for pair in write_out(f)]
        wait_all(start_all(pairs, sems))
        wait_all(fetched[1:])

    if not kept:
        return

    @pl.when(is_polar())
    def _():
        def emit(f, i, t, q, change):
            pair = 0 if f in PAIRS[0] else 1
            n = PAIRS[pair].index(f)
            top = change.astype(BF16)
            first = t * LANES
            kept_parts[pair][n, i, :, first : first + LANES] = top
            kept_parts[pair][n, i, :, 2 * columns + first : 2 * columns + first + LANES] = top
            rest = (change - top.astype(F32)).astype(BF16)
            kept_parts[pair][n, i, :, columns + first : columns + first + LANES] = rest

        nodal = [None] * 4
        c_all, s_all, d_all = [
            spread_waves(waves, part, sides, kept, levels) for part in range(3)
        ]

        def to_nodes(pair):
            if pair == 0:
                wait_all(fetched[1:])
            if not inner and pair == 0:
                return
            ready = [pair] if inner else [0, 1]
            parts = [kept_parts[n][...].reshape(2 * kept_items, 3 * columns) for n in ready]
            both = dot(jnp.concatenate(parts, axis=0), spread[...])
            for n, f in enumerate([f for n in ready for f in PAIRS[n]]):
                nodal[f] = both[n * kept_items : (n + 1) * kept_items]

        if inner:
            groups = inner_groups + [edge_group(1, rows - 6)] * (kept > rows - 6)
        else:
            groups = [edge_group(side, 3 * n) for n, side in enumerate(sides)]
        run(groups, emit, to_nodes)
        sent = [None] * 8
        for ready in PAIRS if inner else (PAIRS[0] + PAIRS[1],):
            turned = []
            for f in ready:
                turned += [c_all * nodal[f], s_all * nodal[f]]
            moved = dot(split(jnp.concatenate(turned, axis=0)), own[...])
            for n, f in enumerate(ready):
                of_cos = moved[2 * n * kept_items : (2 * n + 1) * kept_items]
                of_sin = moved[(2 * n + 1) * kept_items : (2 * n + 2) * kept_items]
                local[f] = s_all * of_cos[:, :NODES] - c_all * of_sin[:, :NODES] + d_all * nodal[f]
                sent[2 * f] = of_cos[:, NODES : NODES + LANES]
                sent[2 * f + 1] = of_sin[:, NODES : NODES + LANES]
        wide = lax.broadcasted_iota(jnp.int32, (kept_items, LANES), 1)
        for out, first, size in ((to_east, 0, NEAR), (to_west, NEAR, NEAR), (to_far, 2 * NEAR, FAR)):
            total = jnp.zeros((kept_items, LANES), F32)
            for g in range(7, -1, -1):
                part = sent[g]
                turn = (size * g - first) % LANES
                if turn:
                    part = pltpu.roll(part, turn, 1)
                total = jnp.where(wide < size * (g + 1), part, total)
            if size == NEAR:
                out[...] = total
            else:
                total = total.reshape(kept, 2, levels // 2, LANES)
                upper = pltpu.roll(total[:, 1].reshape(kept_items // 2, LANES), 64, 1)
                out[...] = total[:, 0].reshape(kept_items // 2, LANES) + upper


def finish_kernel(sides, count, *refs):
    inner = not sides
    fields = refs[:4]
    from_west, from_east, from_far, local, waves, take, gather = refs[4:11]
    outs = refs[15:19]
    new, sems = refs[19:]
    rows = fields[0].shape[0]
    levels, columns = new.shape[2], new.shape[3]
    items = count * levels

    @pl.when(is_polar())
    def _():
        place = lax.axis_index("lon")
        last = lax.axis_size("lon") - 1
        near_west = from_west[...] * jnp.where(place == 0, -1.0, 1.0)
        near_east = from_east[...] * jnp.where(place == last, -1.0, 1.0)
        far = from_far[...] * jnp.where(place < 2, -1.0, 1.0)
        far = far.reshape(count, 1, levels // 2, LANES)
        upper = pltpu.roll(far.reshape(items // 2, LANES), 64, 1).reshape(count, 1, levels // 2, LANES)
        far = jnp.concatenate([far, upper], axis=1).reshape(items, LANES)
        wide = lax.broadcasted_iota(jnp.int32, (items, LANES), 1)

        def turn(value, by):
            by = by % LANES
            return pltpu.roll(value, by, 1) if by else value

        come = []
        for g in range(8):
            part = jnp.where(wide < NEAR, turn(near_west, -NEAR * g), turn(near_east, NEAR - NEAR * g))
            part = jnp.where(wide < 2 * NEAR, part, turn(far, 2 * NEAR - FAR * g))
            part = jnp.where(wide < MESSAGE, part, 0.0)
            top = part.astype(BF16).astype(F32)
            come.append((top + turn(part - top, MESSAGE) + turn(top, 2 * MESSAGE)).astype(BF16))
        moved = dot(jnp.concatenate(come, axis=0), take[...])
        c_all, s_all = [spread_waves(waves, part, sides, count, levels) for part in range(2)]
        writes = []
        chunks = [(f,) for f in range(4)] if inner else [(0, 1), (2, 3)]
        for chunk in chunks:
            value = []
            for f in chunk:
                at = 2 * f * items
                value.append(
                    local[f] + (s_all * moved[at : at + items] - c_all * moved[at + items : at + 2 * items])
                )
            change = dot(split(jnp.concatenate(value, axis=0)), gather[...])
            change = change.reshape(len(chunk), count, levels, columns)
            pairs = []
            for k, f in enumerate(chunk):
                for n in range(count):
                    new[f, n] = fields[f][entry_row(sides, n, rows)] + change[k, n]
                off_edge = rows - 6 if inner else 0
                if inner:
                    pairs.append((new.at[f, 0:off_edge], outs[f].at[3 : rows - 3]))
                for n in range(off_edge, count):
                    pairs.append((new.at[f, n], outs[f].at[entry_row(sides, n, rows)]))
            writes += start_all(pairs, sems, len(writes))
        wait_all(writes)


def vmem():
    return pl.BlockSpec(memory_space=pltpu.VMEM)


def anywhere():
    return pl.BlockSpec(memory_space=pl.ANY)


def like(*shape):
    return jax.ShapeDtypeStruct(shape, F32)


def in_hbm(value):
    return pltpu.with_memory_space_constraint(value, pltpu.HBM)


def params(mebibytes):
    return pltpu.CompilerParams(vmem_limit_bytes=mebibytes * 1024 * 1024)


def row_factors(count):
    latitude = (np.arange(count).astype(np.float32) + np.float32(0.5)) * np.float32(math.pi / count)
    latitude = latitude - np.float32(math.pi / 2)
    metric = np.float32(1.0) / np.cos(latitude)
    return metric.astype(np.float32), (np.float32(SPIN) * np.sin(latitude)).astype(np.float32)


def shards(u_wind, v_wind, theta, geopot, mass, cutoffs):
    rows, levels, columns = u_wind.shape
    lat_count = lax.axis_size("lat")
    lon_count = lax.axis_size("lon")
    tables = filter_tables(columns, columns * lon_count)
    tables = {k: jnp.asarray(v) for k, v in tables.items()}
    metric, spin = [jnp.asarray(t) for t in row_factors(rows * lat_count)]
    fields = (u_wind, v_wind, theta, geopot)

    strip = 12 * levels + 8
    edge_lines = 2 * levels + rows
    far_fields = [in_hbm(q) for q in (*fields, mass)]
    to_a, to_west, to_east, waves, factors = pl.pallas_call(
        pack_kernel,
        out_shape=[
            like(strip, columns),
            *[like(edge_lines, LANES)] * 2,
            like(3, rows, 8, NODES),
            like(2, rows, 8, LANES),
        ],
        in_specs=[anywhere()] * 9,
        out_specs=[vmem()] * 5,
        scratch_shapes=[
            pltpu.VMEM((2, 4, rows, levels, LANES), F32),
            pltpu.VMEM((rows, columns), F32),
            pltpu.SMEM(cutoffs.shape, jnp.int32),
            pltpu.SMEM(metric.shape, F32),
            pltpu.SMEM(spin.shape, F32),
            pltpu.VMEM((1, NODES), F32),
            pltpu.SemaphoreType.DMA((37,)),
        ],
        compiler_params=params(8),
        name="pack_edges",
    )(*far_fields, in_hbm(cutoffs), in_hbm(metric), in_hbm(spin), in_hbm(tables["nodes"]))
    to_b = pl.pallas_call(
        pack_b_kernel,
        out_shape=like(strip, columns),
        in_specs=[anywhere()] * 6,
        out_specs=vmem(),
        scratch_shapes=[pltpu.VMEM((rows, columns), F32), pltpu.SemaphoreType.DMA((13,))],
        compiler_params=params(8),
        name="pack_b",
    )(*far_fields, to_west)

    def ring(value, step):
        return lax.ppermute(value, "lon", [(i, (i + step) % lon_count) for i in range(lon_count)])

    west = ring(to_east, 1)
    east = ring(to_west, -1)
    odd_up = [(i, i + 1) for i in range(1, lat_count - 1, 2)]
    strip_a = lax.ppermute(to_a, "lat", [(i, i ^ 1) for i in range(lat_count)])
    strip_b = lax.ppermute(to_b, "lat", odd_up + [(j, i) for i, j in odd_up])

    at_poles = lat_count == 4
    inner_count = rows - 3 if at_poles else rows - 6

    def tendencies(sides, kept, old=(), shared=()):
        inner = not sides
        count = kept if inner else 3 * len(sides)
        kept_items = kept * levels
        halos = [] if inner else [*[(strip_a, strip_b)[side] for side in sides], *shared]
        weights = [tables[k] for k in ("band", "spread", "own")]
        if inner:
            weights = [in_hbm(w) for w in weights]
        args = [*fields, mass, west, east, waves, factors, *halos, *weights]
        ahead = [tables["take"], tables["gather"]] if kept and not inner else []
        sent = [like(4, kept_items, NODES)] + [like(kept_items, LANES)] * 2 + [like(kept_items // 2, LANES)]
        tiles = columns // LANES
        results = sent * (kept > 0)
        if inner:
            results += [like(rows, 8, columns), like(tiles, 4, 6, levels, 2 * LANES)]
        part = pltpu.VMEM((2, kept, levels, 3 * columns), BF16)
        return pl.pallas_call(
            functools.partial(tend_kernel, sides, count, kept),
            out_shape=[like(rows, levels, columns)] * 4 + results,
            in_specs=[vmem()] * (len(args) - 3)
            + [anywhere() if inner else vmem()] * 3
            + [vmem()] * len(ahead)
            + [anywhere()] * len(old),
            out_specs=[anywhere()] * 4 + [vmem()] * len(results),
            scratch_shapes=[
                pltpu.VMEM((4, count, levels, columns), F32),
                pltpu.VMEM((rows if inner else count, 8, columns), F32),
                pltpu.VMEM((count, levels, columns), F32),
                pltpu.SemaphoreType.DMA((28,)),
                *[part] * (2 if kept else 0),
                *[pltpu.VMEM((4, rows, levels, columns + LANES), BF16)] * (2 if inner else 0),
                *[pltpu.VMEM((tiles, 4, rows - 6, levels, 2 * LANES), F32)] * inner,
                *[pltpu.VMEM((4, rows - 6, levels, 2 * LANES), F32)] * (tiles if inner else 0),
                *[pltpu.VMEM(w.shape, w.dtype) for w in weights if inner],
            ],
            input_output_aliases={len(args) + len(ahead) + f: f for f in range(4)} if old else {},
            compiler_params=params(40),
            cost_estimate=pl.CostEstimate(
                flops=count * levels * 4 * columns * 4000, bytes_accessed=2**22, transcendentals=0
            ),
            name="tend_inner" if inner else "tend_edge",
        )(*args, *ahead, *old)

    def exchange(east_part, west_part, far_part):
        return ring(east_part, 1), ring(west_part, -1), ring(far_part, 2)

    def finish(sides, count, received, local, old):
        weights = [tables[k] for k in ("take", "gather")]
        args = [*fields, *received, local, waves, *weights]
        return pl.pallas_call(
            functools.partial(finish_kernel, sides, count),
            out_shape=[like(rows, levels, columns)] * 4,
            in_specs=[vmem()] * len(args) + [anywhere()] * 4,
            out_specs=[anywhere()] * 4,
            scratch_shapes=[
                pltpu.VMEM((4, count, levels, columns), F32),
                pltpu.SemaphoreType.DMA((24,)),
            ],
            input_output_aliases={len(args) + f: f for f in range(4)},
            compiler_params=params(24),
            name="finish_edge" if sides else "finish_inner",
        )(*args, *old)

    *outs, local_inner, a, b, c, mass_x, edge_cross = tendencies((), inner_count)
    shared = (mass_x, edge_cross)
    received_inner = exchange(a, b, c)
    sides = (0,) if at_poles else (0, 1)
    kept = 3 * len(sides)
    *outs, local_edge, a, b, c = tendencies(sides, kept, outs, shared)
    received_edge = exchange(a, b, c)
    if at_poles:
        outs = tendencies((1,), 0, outs, shared)
    outs = finish((), inner_count, received_inner, local_inner, outs)
    outs = finish(sides, kept, received_edge, local_edge, outs)
    return tuple(outs)


def solution(mesh):
    return jax.shard_map(
        shards,
        mesh=mesh,
        in_specs=(
            P(("members", "lat"), None, "lon"),
            P(("members", "lat"), None, "lon"),
            P(("members", "lat"), None, "lon"),
            P(("members", "lat"), None, "lon"),
            P(("members", "lat"), "lon"),
            P(),
        ),
        out_specs=(
            P(("members", "lat"), None, "lon"),
            P(("members", "lat"), None, "lon"),
            P(("members", "lat"), None, "lon"),
            P(("members", "lat"), None, "lon"),
        ),
        check_vma=False,
    )
```

```python
import functools
import math

import jax
import jax.numpy as jnp
import ml_dtypes
import numpy as np
from jax import lax
from jax.experimental import pallas as pl
from jax.experimental.pallas import tpu as pltpu
from jax.sharding import PartitionSpec as P

STEP = 0.1
SPIN = 0.5
LANES = 128
NEAR = 16
FAR = 8
NODES = 256
F32 = jnp.float32
BF16 = jnp.bfloat16
MESSAGE = 2 * NEAR + FAR


def pivoted(matrix, count):
    rest = np.array(matrix)
    columns = rest.shape[1]
    tilt = 1.0 + 1e-3 * np.arange(columns) / columns
    picked = []
    tri = np.zeros((count, columns))
    for step in range(count):
        size = (rest * rest).sum(axis=0)
        best = int(np.argmax(size * tilt))
        picked.append(best)
        unit = rest[:, best] / math.sqrt(size[best])
        for _ in range(2):
            part = (unit[:, None] * rest).sum(axis=0)
            rest -= unit[:, None] * part[None, :]
            tri[step] += part
        rest[:, best] = 0.0
    left = tri[:, picked].copy()
    right = tri.copy()
    for step in range(count - 1, -1, -1):
        right[step] /= left[step, step]
        right[:step] -= left[:step, step][:, None] * right[step][None, :]
    right[:, picked] = np.eye(count)
    order = np.argsort(picked)
    return np.asarray(picked)[order], right[order]


def cauchy(target, source, circle):
    gap = target[:, None] - source[None, :]
    angle = np.where(gap == 0, 0.5 * math.pi, gap * math.pi / circle)
    return np.where(gap == 0, 0.0, 1.0 / (circle * np.sin(angle)))


def stacked_halves(table):
    table = table.astype(np.float32)
    high = table.astype(ml_dtypes.bfloat16)
    low = (table - high.astype(np.float32)).astype(ml_dtypes.bfloat16)
    return np.concatenate([high, high, low], axis=0)


def band_table():
    band = np.zeros((2 * LANES, 2 * LANES))
    slope = {-3: -1, -2: 9, -1: -45, 1: 45, 2: -9, 3: 1}
    smooth = {-3: 1, -2: -6, -1: 15, 0: -20, 1: 15, 2: -6, 3: 1}
    for j in range(LANES):
        for k, value in slope.items():
            band[j + 3 + k, j] = value
        for k, value in smooth.items():
            band[j + 3 + k, LANES + j] = value
    return np.concatenate([band, band], axis=0).astype(ml_dtypes.bfloat16)


@functools.lru_cache(maxsize=None)
def filter_tables(sector, circle):
    modes = circle // 8
    place = np.arange(sector)
    wave = np.arange(modes)
    phase = (wave[:, None] * place[None, :]) % circle * (2 * math.pi / circle)
    basis = np.concatenate([np.cos(phase), np.sin(phase[1:])], axis=0)
    nodes, spread = pivoted(basis, NODES)
    own = cauchy(nodes, nodes, circle)
    send = np.zeros((NODES, LANES))
    take = np.zeros((MESSAGE, NODES))
    at = 0
    for shift, count in ((sector, NEAR), (-sector, NEAR), (2 * sector, FAR)):
        kernel = cauchy(nodes + shift, nodes, circle)
        pick, weights = pivoted(kernel, count)
        send[:, at : at + count] = weights.T
        take[at : at + count] = kernel[:, pick].T
        at += count
    take = stacked_halves(take)
    take = np.concatenate([take, np.zeros((LANES - 3 * MESSAGE, NODES), take.dtype)], axis=0)
    return dict(
        nodes=nodes.astype(np.float32)[None],
        band=band_table(),
        spread=stacked_halves(spread.T),
        own=stacked_halves(np.concatenate([own.T, send, np.zeros((NODES, LANES))], axis=1)),
        take=take,
        gather=stacked_halves(STEP * spread),
    )


def split(value):
    high = value.astype(BF16)
    low = (value - high.astype(F32)).astype(BF16)
    return jnp.concatenate([high, low, high], axis=1)


def dot(a, b):
    return lax.dot_general(a, b, (((1,), (0,)), ((), ())), preferred_element_type=F32)


def start_all(pairs, sems, first=0):
    copies = [pltpu.make_async_copy(a, b, sems.at[first + n]) for n, (a, b) in enumerate(pairs)]
    for c in copies:
        c.start()
    return copies


def wait_all(copies):
    for c in copies:
        c.wait()


def is_polar():
    owner = lax.axis_index("lat")
    quarter = lax.axis_size("lat") // 4
    return (owner < quarter) | (owner >= lax.axis_size("lat") - quarter)


def edge_row(entry, rows):
    north = (lax.axis_index("lat") % 2 == 0) == (entry < 3)
    return jnp.where(north, rows - 1 - entry % 3, entry % 3)


def entry_row(sides, entry, rows):
    if sides:
        return edge_row(entry + 3 * sides[0], rows)
    if isinstance(entry, int):
        return entry + 3 if entry < rows - 6 else edge_row((entry - (rows - 6) + 3) % 6, rows)
    return jnp.where(entry < rows - 6, entry + 3, edge_row((entry - (rows - 6) + 3) % 6, rows))


def by_parity(even, odd):
    return jnp.where(lax.axis_index("lat") % 2 == 0, even, odd)


def strip_copies(fields, strip, side):
    rows, levels = fields[0].shape[:2]
    pairs = []
    for m in range(3):
        row = edge_row(3 * side + m, rows)
        for f, q in enumerate(fields):
            pairs.append((q.at[row], strip.at[pl.ds(levels * (3 * f + m), levels)]))
    return pairs


def mass_tail(mass, strip, side, levels):
    rows, columns = mass.shape
    tail = 12 * levels
    north = jnp.concatenate([mass[rows - 1 - m : rows - m] for m in range(3)], axis=0)
    strip[tail : tail + 3] = jnp.where(edge_row(3 * side, rows) != 0, north, mass[0:3])
    strip[tail + 3 : tail + 8] = jnp.zeros((5, columns), F32)


def pack_b_kernel(*refs):
    fields = refs[:4]
    mass, _, strip, own_mass, sems = refs[4:]
    owner = lax.axis_index("lat")

    @pl.when((owner > 0) & (owner < lax.axis_size("lat") - 1))
    def _():
        copies = start_all([(mass, own_mass)], sems)
        copies += start_all(strip_copies(fields, strip, 1), sems, 1)
        wait_all(copies[:1])
        mass_tail(own_mass, strip, 1, fields[0].shape[1])
        wait_all(copies[1:])


def pack_kernel(*refs):
    fields = refs[:4]
    mass, cutoffs_in, metric_in, spin_in, nodes_in, strip, west, east, waves, factors = refs[4:14]
    edge, own_mass, cutoffs, metric, spin, nodes, sems = refs[14:]
    rows, columns = mass.shape
    levels = edge.shape[3]
    first = start_all(
        [(cutoffs_in, cutoffs), (nodes_in, nodes), (metric_in, metric), (spin_in, spin)], sems, 33
    )
    small = start_all(
        [(mass, own_mass)]
        + [(q.at[:, :, 0:LANES], edge.at[0, f]) for f, q in enumerate(fields)]
        + [(q.at[:, :, columns - LANES : columns], edge.at[1, f]) for f, q in enumerate(fields)],
        sems,
    )
    large = start_all(strip_copies(fields, strip, 0), sems, 9)

    wait_all(first)
    lat_count = lax.axis_size("lat")
    lon_count = lax.axis_size("lon")
    owner = lax.axis_index("lat")
    circle = columns * lon_count
    start = jnp.where(owner < lat_count // 4, owner * rows, owner * rows - lat_count * rows // 2)
    start = jnp.clip(start, 0, lat_count * rows // 2 - rows)
    line = lax.broadcasted_iota(jnp.int32, (rows, NODES), 0)
    twice = jnp.zeros((rows, NODES), F32)
    for r in range(rows):
        twice = jnp.where(line == r, (2 * cutoffs[start + r] + 1).astype(F32), twice)
    place = nodes[...] + (lax.axis_index("lon") * columns).astype(F32)
    turns = twice * place
    angle = (turns - 2.0 * circle * jnp.floor(turns * (0.5 / circle))) * (math.pi / circle)
    for part, table in enumerate((jnp.cos(angle), jnp.sin(angle), twice * (1.0 / circle))):
        waves[part] = jnp.broadcast_to(table[:, None, :], (rows, 8, NODES))
    for r in range(rows):
        row = owner * rows + r
        factors[0, r] = jnp.full((8, LANES), metric[row] * (1.0 / 60.0))
        factors[1, r] = jnp.full((8, LANES), spin[row])

    wait_all(small)
    mass_tail(own_mass, strip, 0, levels)
    lane = lax.broadcasted_iota(jnp.int32, (levels, LANES), 1)
    west[2 * levels :] = own_mass[:, 0:LANES]
    east[2 * levels :] = pltpu.roll(own_mass[:, columns - LANES : columns], 3, 1)
    for parity in range(2):
        for side, out in ((0, west), (1, east)):
            total = jnp.zeros((levels, LANES), F32)
            for r in range(parity, rows, 2):
                for f in range(4):
                    lead = 16 * (r // 2) + 3 * f
                    turn = lead if side == 0 else (lead + 3) % LANES
                    tile = edge[side, f, r]
                    if turn:
                        tile = pltpu.roll(tile, turn, 1)
                    total = jnp.where((lane >= lead) & (lane < lead + 3), tile, total)
            out[parity * levels : (parity + 1) * levels] = total
    wait_all(large)


def stencil(center, plus, minus):
    p1, p2, p3 = plus
    m1, m2, m3 = minus
    slope = 45.0 * (p1 - m1) - 9.0 * (p2 - m2) + (p3 - m3)
    smooth = (p3 + m3) - 6.0 * (p2 + m2) + 15.0 * (p1 + m1) - 20.0 * center
    return slope, smooth


def over_levels(value):
    return jnp.broadcast_to(value[:, None, :], (value.shape[0], 8, value.shape[1]))


def mass_slope_x(mass, west, east, levels):
    columns = mass.shape[1]
    middle = mass[...]
    wide = jnp.concatenate(
        [pltpu.roll(west[2 * levels :], LANES - 3, 1), middle, east[2 * levels :]], axis=1
    )
    whole = columns + 2 * LANES

    def at(k):
        return pltpu.roll(wide, (-k) % whole, 1)[:, LANES : LANES + columns]

    slope = stencil(middle, [at(1), at(2), at(3)], [at(-1), at(-2), at(-3)])[0]
    return over_levels(slope / middle)


def mass_slope_y(tall):
    size = tall.shape[0] - 6
    plus = [tall[3 + k : 3 + k + size] for k in (1, 2, 3)]
    minus = [tall[3 - k : 3 - k + size] for k in (1, 2, 3)]
    middle = tall[3 : 3 + size]
    return over_levels(stencil(middle, plus, minus)[0] / middle)


def spread_waves(waves, part, sides, kept, levels):
    rows = waves.shape[1]
    numbers = [entry_row(sides, entry, rows) for entry in range(kept)]
    return jnp.concatenate([waves[part, n] for n in numbers for _ in range(levels // 8)], axis=0)


PAIRS = ((3, 0), (1, 2))


def tend_kernel(sides, count, kept, *refs):
    inner = not sides
    refs = list(refs)

    def some(n):
        taken = refs[:n]
        del refs[:n]
        return taken

    fields = some(4)
    mass, west, east, waves, factors = some(5)
    strips = dict(zip(sides, some(len(sides))))
    mass_x, edge_cross = (None, None) if inner else some(2)
    tables_in = some(3)
    if not inner:
        some(2 if kept else 0)
        some(4)
    outs = some(4)
    if kept:
        local, to_east, to_west, to_far = some(4)
    mass_x, edge_cross = some(2) if inner else (mass_x, edge_cross)
    new, mass_y, push, sems = some(4)
    kept_parts = some(2) if kept else None
    if inner:
        high, low, cross_all = some(3)
        crosses = some(mass.shape[1] // LANES)
    tables = refs if inner else tables_in
    band, spread, own = tables
    rows, columns = mass.shape
    levels = fields[0].shape[1]
    kept_items = kept * levels
    tiles = columns // LANES

    fetched = start_all(zip(tables_in, tables), sems, 24) if inner else []
    if inner:
        blank = jnp.zeros((3, columns), F32)
        mass_x[...] = mass_slope_x(mass, west, east, levels)
        mass_y[...] = mass_slope_y(jnp.concatenate([blank, mass[...], blank], axis=0))

    def edge_mass():
        for n, side in enumerate(sides):
            lines = [strips[side][12 * levels + m : 12 * levels + m + 1] for m in (2, 1, 0)]
            north = edge_row(3 * side, rows) != 0
            for m in range(6):
                lines.append(jnp.where(north, mass[rows - 1 - m : rows - m], mass[m : m + 1]))
            mass_y[3 * n : 3 * n + 3] = mass_slope_y(jnp.concatenate(lines, axis=0))

    lane = lax.broadcasted_iota(jnp.int32, (levels, LANES), 1)

    def cut(i, carry):
        row = entry_row(sides, i, rows)
        halo = pl.ds(pl.multiple_of((row % 2) * levels, levels), levels)
        for f in range(4):
            lead = 16 * (row // 2) + 3 * f
            before = pltpu.roll(west[halo, :], lax.rem(LANES - lead, LANES), 1)
            for t in range(tiles + 1):
                if t < tiles:
                    tile = pltpu.roll(fields[f][row, :, t * LANES : (t + 1) * LANES], 3, 1)
                else:
                    tile = pltpu.roll(east[halo, :], lax.rem(LANES + 3 - lead, LANES), 1)
                whole = jnp.where(lane < 3, before, tile)
                top = whole.astype(BF16)
                high[f, i, :, t * LANES : (t + 1) * LANES] = top
                low[f, i, :, t * LANES : (t + 1) * LANES] = (whole - top.astype(F32)).astype(BF16)
                before = tile
        return carry

    def cut_tile(t):
        for i in range(rows):
            row = entry_row(sides, i, rows)
            first = (row % 2) * levels
            if not isinstance(row, int):
                first = pl.multiple_of(first, levels)
            halo = pl.ds(first, levels)

            def shifted(f, n):
                lead = 16 * (row // 2) + 3 * f
                if n < 0:
                    return pltpu.roll(west[halo, :], (LANES - lead) % LANES, 1)
                if n == tiles:
                    return pltpu.roll(east[halo, :], (LANES + 3 - lead) % LANES, 1)
                return pltpu.roll(fields[f][row, :, n * LANES : (n + 1) * LANES], 3, 1)

            for f in range(4):
                whole = jnp.where(lane < 3, shifted(f, t - 1), shifted(f, t))
                top = whole.astype(BF16)
                high[f, i, :, t * LANES : (t + 1) * LANES] = top
                low[f, i, :, t * LANES : (t + 1) * LANES] = (whole - top.astype(F32)).astype(BF16)

    def columns_of(t, width=1):
        if isinstance(t, int):
            return slice(t * LANES, (t + width) * LANES)
        return pl.ds(pl.multiple_of(t * LANES, LANES), width * LANES)

    def slopes_x(t):
        span = columns_of(t, 2)
        parts = [table[:, :, :, span].reshape(4 * rows * levels, 2 * LANES) for table in (high, low)]
        product = dot(jnp.concatenate(parts, axis=1), band[...]).reshape(4, rows, levels, 2 * LANES)
        if isinstance(t, int):
            crosses[t][...] = product[:, : rows - 6]
        else:
            cross_all[t] = product[:, : rows - 6]
        edge_cross[t] = product[:, rows - 6 :]

    def cross_of(t, f, entry):
        if inner and entry < rows - 6:
            return (crosses[t], (f, entry)) if isinstance(t, int) else (cross_all, (t, f, entry))
        if inner:
            return edge_cross, (t, f, entry - (rows - 6))
        return edge_cross, (t, f, (entry + 3 * sides[0] + 3) % 6)

    def whole(lines):
        return jnp.concatenate([lines] * (levels // 8), axis=0)

    def tendency(pair, t, first, numbers, lines, row_of, emit, inward=1.0):
        size = len(numbers)
        span = columns_of(t)
        along = [whole(factors[0, n]) for n in numbers]
        centers = [[row_of(f, j, span) for j in range(size)] for f in range(3)]
        per_row = inward * (1.0 / 60.0)
        fast, fast_size, up, up_size = [], [], [], []
        for j in range(size):
            fast.append(centers[0][j] * along[j])
            fast_size.append(jnp.abs(fast[j]))
            up.append(centers[1][j] * per_row)
            up_size.append(jnp.abs(up[j]))
        push_x = [None] * size
        for f in PAIRS[pair]:
            column = [row_of(f, j, span) for j in range(-3, size + 3)]
            for j in range(size):
                q = column[j + 3]
                table, place = cross_of(t, f, first + j)
                slope_x = table[(*place, slice(None), slice(0, LANES))]
                smooth_x = table[(*place, slice(None), slice(LANES, 2 * LANES))]
                slope_y, smooth_y = stencil(q, column[j + 4 : j + 7], column[j + 2 :: -1][:3])
                change = (fast_size[j] * smooth_x - fast[j] * slope_x) + (
                    up_size[j] * smooth_y - up[j] * slope_y
                )
                if f == 3:
                    theta = centers[2][j]
                    over_x = whole(mass_x[numbers[j], :, span])
                    over_y = whole(mass_y[lines[j], :, span])
                    if inner and not isinstance(inward, float):
                        over_y = over_y * inward
                    push_x[j] = along[j] * (slope_x + theta * over_x)
                    push[first + j, :, span] = per_row * (slope_y + theta * over_y)
                elif f == 0:
                    change = change + (whole(factors[1, numbers[j]]) * centers[1][j] - push_x[j])
                elif f == 1:
                    change = change - (whole(factors[1, numbers[j]]) * centers[0][j] + push[first + j, :, span])
                emit(f, first + j, t, q, change)

    def edge_group(side, first):
        edge = edge_row(3 * side, rows)
        step = jnp.where(edge == 0, 1, -1)

        def row_of(f, j, span):
            if j >= 0:
                return fields[f][edge + step * j, :, span]
            if inner:
                return jnp.zeros((levels, LANES), F32)
            start = levels * (3 * f - j - 1)
            return strips[side][start : start + levels, span]

        numbers = [edge + step * j for j in range(3)]
        lines = numbers if inner else [first + j for j in range(3)]
        return first, numbers, lines, row_of, step.astype(F32)

    def inner_group(first, size):
        def row_of(f, j, span):
            return fields[f][3 + first + j, :, span]

        numbers = [3 + first + j for j in range(size)]
        return first, numbers, numbers, row_of, 1.0

    def run(groups, emit, then=None):
        if inner:
            cut_tile(0)
            cut_tile(1)
            wait_all(fetched[:1])
            slopes_x(0)
            cut_tile(2)
        else:
            edge_mass()
        for pair in range(2):
            for t in range(tiles):
                if inner and pair == 0 and t + 1 < tiles:
                    slopes_x(t + 1)
                    if t + 3 <= tiles:
                        cut_tile(t + 3)
                for first, numbers, lines, row_of, inward in groups:
                    tendency(pair, t, first, numbers, lines, row_of, emit, inward)
            if then:
                then(pair)

    def run_rolled(groups, emit):
        if inner:
            lax.fori_loop(0, rows, cut, 0)
            wait_all(fetched[:1])
        else:
            edge_mass()

        def step(t, carry):
            if inner:
                slopes_x(t)
            for pair in range(2):
                for first, numbers, lines, row_of, inward in groups:
                    tendency(pair, t, first, numbers, lines, row_of, emit, inward)
            return carry

        lax.fori_loop(0, tiles, step, 0)

    half = (rows - 6) // 2
    inner_groups = [inner_group(0, half), inner_group(half, rows - 6 - half)]

    def write_out(f):
        if not inner:
            return [(new.at[f, n], outs[f].at[entry_row(sides, n, rows)]) for n in range(count)]
        return [(new.at[f, 0 : rows - 6], outs[f].at[3 : rows - 3])]

    @pl.when(jnp.logical_not(is_polar()))
    def _():
        def emit(f, i, t, q, change):
            new[f, i, :, columns_of(t)] = q + STEP * change

        if inner:
            run_rolled(inner_groups, emit)
        else:
            run_rolled([edge_group(side, 3 * n) for n, side in enumerate(sides)], emit)
        pairs = [pair for f in range(4) for pair in write_out(f)]
        wait_all(start_all(pairs, sems))
        wait_all(fetched[1:])

    if not kept:
        return

    @pl.when(is_polar())
    def _():
        def emit(f, i, t, q, change):
            pair = 0 if f in PAIRS[0] else 1
            n = PAIRS[pair].index(f)
            top = change.astype(BF16)
            first = t * LANES
            kept_parts[pair][n, i, :, first : first + LANES] = top
            kept_parts[pair][n, i, :, 2 * columns + first : 2 * columns + first + LANES] = top
            rest = (change - top.astype(F32)).astype(BF16)
            kept_parts[pair][n, i, :, columns + first : columns + first + LANES] = rest

        nodal = [None] * 4
        c_all, s_all, d_all = [
            spread_waves(waves, part, sides, kept, levels) for part in range(3)
        ]

        def to_nodes(pair):
            if pair == 0:
                wait_all(fetched[1:])
            if not inner and pair == 0:
                return
            ready = [pair] if inner else [0, 1]
            parts = [kept_parts[n][...].reshape(2 * kept_items, 3 * columns) for n in ready]
            both = dot(jnp.concatenate(parts, axis=0), spread[...])
            for n, f in enumerate([f for n in ready for f in PAIRS[n]]):
                nodal[f] = both[n * kept_items : (n + 1) * kept_items]

        if inner:
            groups = inner_groups + [edge_group(1, rows - 6)] * (kept > rows - 6)
        else:
            groups = [edge_group(side, 3 * n) for n, side in enumerate(sides)]
        run(groups, emit, to_nodes)
        sent = [None] * 8
        for ready in PAIRS if inner else (PAIRS[0] + PAIRS[1],):
            turned = []
            for f in ready:
                turned += [c_all * nodal[f], s_all * nodal[f]]
            moved = dot(split(jnp.concatenate(turned, axis=0)), own[...])
            for n, f in enumerate(ready):
                of_cos = moved[2 * n * kept_items : (2 * n + 1) * kept_items]
                of_sin = moved[(2 * n + 1) * kept_items : (2 * n + 2) * kept_items]
                local[f] = s_all * of_cos[:, :NODES] - c_all * of_sin[:, :NODES] + d_all * nodal[f]
                sent[2 * f] = of_cos[:, NODES : NODES + LANES]
                sent[2 * f + 1] = of_sin[:, NODES : NODES + LANES]
        wide = lax.broadcasted_iota(jnp.int32, (kept_items, LANES), 1)
        for out, first, size in ((to_east, 0, NEAR), (to_west, NEAR, NEAR), (to_far, 2 * NEAR, FAR)):
            total = jnp.zeros((kept_items, LANES), F32)
            for g in range(7, -1, -1):
                part = sent[g]
                turn = (size * g - first) % LANES
                if turn:
                    part = pltpu.roll(part, turn, 1)
                total = jnp.where(wide < size * (g + 1), part, total)
            if size == NEAR:
                out[...] = total
            else:
                total = total.reshape(kept, 2, levels // 2, LANES)
                upper = pltpu.roll(total[:, 1].reshape(kept_items // 2, LANES), 64, 1)
                out[...] = total[:, 0].reshape(kept_items // 2, LANES) + upper


def finish_kernel(sides, count, *refs):
    inner = not sides
    fields = refs[:4]
    from_west, from_east, from_far, local, waves, take, gather = refs[4:11]
    outs = refs[15:19]
    new, sems = refs[19:]
    rows = fields[0].shape[0]
    levels, columns = new.shape[2], new.shape[3]
    items = count * levels

    @pl.when(is_polar())
    def _():
        place = lax.axis_index("lon")
        last = lax.axis_size("lon") - 1
        near_west = from_west[...] * jnp.where(place == 0, -1.0, 1.0)
        near_east = from_east[...] * jnp.where(place == last, -1.0, 1.0)
        far = from_far[...] * jnp.where(place < 2, -1.0, 1.0)
        far = far.reshape(count, 1, levels // 2, LANES)
        upper = pltpu.roll(far.reshape(items // 2, LANES), 64, 1).reshape(count, 1, levels // 2, LANES)
        far = jnp.concatenate([far, upper], axis=1).reshape(items, LANES)
        wide = lax.broadcasted_iota(jnp.int32, (items, LANES), 1)

        def turn(value, by):
            by = by % LANES
            return pltpu.roll(value, by, 1) if by else value

        def come(g):
            part = jnp.where(wide < NEAR, turn(near_west, -NEAR * g), turn(near_east, NEAR - NEAR * g))
            part = jnp.where(wide < 2 * NEAR, part, turn(far, 2 * NEAR - FAR * g))
            part = jnp.where(wide < MESSAGE, part, 0.0)
            top = part.astype(BF16).astype(F32)
            return (top + turn(part - top, MESSAGE) + turn(top, 2 * MESSAGE)).astype(BF16)

        c_all, s_all = [spread_waves(waves, part, sides, count, levels) for part in range(2)]
        writes = []
        chunks = [(f,) for f in range(4)] if inner else [(0, 1), (2, 3)]
        for chunk in chunks:
            groups = [come(2 * f + part) for f in chunk for part in range(2)]
            moved = dot(jnp.concatenate(groups, axis=0), take[...])
            value = []
            for k, f in enumerate(chunk):
                of_cos = moved[2 * k * items : (2 * k + 1) * items]
                of_sin = moved[(2 * k + 1) * items : (2 * k + 2) * items]
                value.append(local[f] + (s_all * of_cos - c_all * of_sin))
            change = dot(split(jnp.concatenate(value, axis=0)), gather[...])
            change = change.reshape(len(chunk), count, levels, columns)
            pairs = []
            for k, f in enumerate(chunk):
                for n in range(count):
                    new[f, n] = fields[f][entry_row(sides, n, rows)] + change[k, n]
                off_edge = rows - 6 if inner else 0
                if inner:
                    pairs.append((new.at[f, 0:off_edge], outs[f].at[3 : rows - 3]))
                for n in range(off_edge, count):
                    pairs.append((new.at[f, n], outs[f].at[entry_row(sides, n, rows)]))
            writes += start_all(pairs, sems, len(writes))
        wait_all(writes)


def vmem():
    return pl.BlockSpec(memory_space=pltpu.VMEM)


def anywhere():
    return pl.BlockSpec(memory_space=pl.ANY)


def like(*shape):
    return jax.ShapeDtypeStruct(shape, F32)


def in_hbm(value):
    return pltpu.with_memory_space_constraint(value, pltpu.HBM)


def params(mebibytes):
    return pltpu.CompilerParams(vmem_limit_bytes=mebibytes * 1024 * 1024)


def row_factors(count):
    latitude = (np.arange(count).astype(np.float32) + np.float32(0.5)) * np.float32(math.pi / count)
    latitude = latitude - np.float32(math.pi / 2)
    metric = np.float32(1.0) / np.cos(latitude)
    return metric.astype(np.float32), (np.float32(SPIN) * np.sin(latitude)).astype(np.float32)


def shards(u_wind, v_wind, theta, geopot, mass, cutoffs):
    rows, levels, columns = u_wind.shape
    lat_count = lax.axis_size("lat")
    lon_count = lax.axis_size("lon")
    tables = filter_tables(columns, columns * lon_count)
    tables = {k: jnp.asarray(v) for k, v in tables.items()}
    metric, spin = [jnp.asarray(t) for t in row_factors(rows * lat_count)]
    fields = (u_wind, v_wind, theta, geopot)

    strip = 12 * levels + 8
    edge_lines = 2 * levels + rows
    far_fields = [in_hbm(q) for q in (*fields, mass)]
    to_a, to_west, to_east, waves, factors = pl.pallas_call(
        pack_kernel,
        out_shape=[
            like(strip, columns),
            *[like(edge_lines, LANES)] * 2,
            like(3, rows, 8, NODES),
            like(2, rows, 8, LANES),
        ],
        in_specs=[anywhere()] * 9,
        out_specs=[vmem()] * 5,
        scratch_shapes=[
            pltpu.VMEM((2, 4, rows, levels, LANES), F32),
            pltpu.VMEM((rows, columns), F32),
            pltpu.SMEM(cutoffs.shape, jnp.int32),
            pltpu.SMEM(metric.shape, F32),
            pltpu.SMEM(spin.shape, F32),
            pltpu.VMEM((1, NODES), F32),
            pltpu.SemaphoreType.DMA((37,)),
        ],
        compiler_params=params(8),
        name="pack_edges",
    )(*far_fields, in_hbm(cutoffs), in_hbm(metric), in_hbm(spin), in_hbm(tables["nodes"]))
    to_b = pl.pallas_call(
        pack_b_kernel,
        out_shape=like(strip, columns),
        in_specs=[anywhere()] * 6,
        out_specs=vmem(),
        scratch_shapes=[pltpu.VMEM((rows, columns), F32), pltpu.SemaphoreType.DMA((13,))],
        compiler_params=params(8),
        name="pack_b",
    )(*far_fields, to_west)

    def ring(value, step):
        return lax.ppermute(value, "lon", [(i, (i + step) % lon_count) for i in range(lon_count)])

    west = ring(to_east, 1)
    east = ring(to_west, -1)
    odd_up = [(i, i + 1) for i in range(1, lat_count - 1, 2)]
    strip_a = lax.ppermute(to_a, "lat", [(i, i ^ 1) for i in range(lat_count)])
    strip_b = lax.ppermute(to_b, "lat", odd_up + [(j, i) for i, j in odd_up])

    at_poles = lat_count == 4
    inner_count = rows - 3 if at_poles else rows - 6

    def tendencies(sides, kept, old=(), shared=()):
        inner = not sides
        count = kept if inner else 3 * len(sides)
        kept_items = kept * levels
        halos = [] if inner else [*[(strip_a, strip_b)[side] for side in sides], *shared]
        weights = [tables[k] for k in ("band", "spread", "own")]
        if inner:
            weights = [in_hbm(w) for w in weights]
        args = [*fields, mass, west, east, waves, factors, *halos, *weights]
        ahead = [tables["take"], tables["gather"]] if kept and not inner else []
        sent = [like(4, kept_items, NODES)] + [like(kept_items, LANES)] * 2 + [like(kept_items // 2, LANES)]
        tiles = columns // LANES
        results = sent * (kept > 0)
        if inner:
            results += [like(rows, 8, columns), like(tiles, 4, 6, levels, 2 * LANES)]
        part = pltpu.VMEM((2, kept, levels, 3 * columns), BF16)
        return pl.pallas_call(
            functools.partial(tend_kernel, sides, count, kept),
            out_shape=[like(rows, levels, columns)] * 4 + results,
            in_specs=[vmem()] * (len(args) - 3)
            + [anywhere() if inner else vmem()] * 3
            + [vmem()] * len(ahead)
            + [anywhere()] * len(old),
            out_specs=[anywhere()] * 4 + [vmem()] * len(results),
            scratch_shapes=[
                pltpu.VMEM((4, count, levels, columns), F32),
                pltpu.VMEM((rows if inner else count, 8, columns), F32),
                pltpu.VMEM((count, levels, columns), F32),
                pltpu.SemaphoreType.DMA((28,)),
                *[part] * (2 if kept else 0),
                *[pltpu.VMEM((4, rows, levels, columns + LANES), BF16)] * (2 if inner else 0),
                *[pltpu.VMEM((tiles, 4, rows - 6, levels, 2 * LANES), F32)] * inner,
                *[pltpu.VMEM((4, rows - 6, levels, 2 * LANES), F32)] * (tiles if inner else 0),
                *[pltpu.VMEM(w.shape, w.dtype) for w in weights if inner],
            ],
            input_output_aliases={len(args) + len(ahead) + f: f for f in range(4)} if old else {},
            compiler_params=params(40),
            cost_estimate=pl.CostEstimate(
                flops=count * levels * 4 * columns * 4000, bytes_accessed=2**22, transcendentals=0
            ),
            name="tend_inner" if inner else "tend_edge",
        )(*args, *ahead, *old)

    def exchange(east_part, west_part, far_part):
        return ring(east_part, 1), ring(west_part, -1), ring(far_part, 2)

    def finish(sides, count, received, local, old):
        weights = [tables[k] for k in ("take", "gather")]
        args = [*fields, *received, local, waves, *weights]
        return pl.pallas_call(
            functools.partial(finish_kernel, sides, count),
            out_shape=[like(rows, levels, columns)] * 4,
            in_specs=[vmem()] * len(args) + [anywhere()] * 4,
            out_specs=[anywhere()] * 4,
            scratch_shapes=[
                pltpu.VMEM((4, count, levels, columns), F32),
                pltpu.SemaphoreType.DMA((24,)),
            ],
            input_output_aliases={len(args) + f: f for f in range(4)},
            compiler_params=params(24),
            name="finish_edge" if sides else "finish_inner",
        )(*args, *old)

    *outs, local_inner, a, b, c, mass_x, edge_cross = tendencies((), inner_count)
    shared = (mass_x, edge_cross)
    received_inner = exchange(a, b, c)
    sides = (0,) if at_poles else (0, 1)
    kept = 3 * len(sides)
    *outs, local_edge, a, b, c = tendencies(sides, kept, outs, shared)
    received_edge = exchange(a, b, c)
    if at_poles:
        outs = tendencies((1,), 0, outs, shared)
    outs = finish((), inner_count, received_inner, local_inner, outs)
    outs = finish(sides, kept, received_edge, local_edge, outs)
    return tuple(outs)


def solution(mesh):
    return jax.shard_map(
        shards,
        mesh=mesh,
        in_specs=(
            P(("members", "lat"), None, "lon"),
            P(("members", "lat"), None, "lon"),
            P(("members", "lat"), None, "lon"),
            P(("members", "lat"), None, "lon"),
            P(("members", "lat"), "lon"),
            P(),
        ),
        out_specs=(
            P(("members", "lat"), None, "lon"),
            P(("members", "lat"), None, "lon"),
            P(("members", "lat"), None, "lon"),
            P(("members", "lat"), None, "lon"),
        ),
        check_vma=False,
    )
```
